32 devices in a mesh: dp: 16 (over z, y, x), head: 2 (over core).
Axes of the slice: x: 2, y: 2, z: 4, core: 2. Of those that a mesh axis runs over, the one named last changes fastest.
Arguments:
- frames: bfloat16 [512, 192, 240], P(('dp', 'head')), may hold values from -6 to 6
- cotangent: bfloat16 [512, 192, 240], P(('dp', 'head')), may hold values from -6 to 6
- lengths: int32 [512], P('dp'), may hold values from 1 to 192, as said below
- head_params: float32 [2, 577968], P('head', 'dp'), may hold values from -3 to 3
- shared_params: float32 [180960], P(('dp', 'head')), may hold values from -3 to 3
- head_first: float32 [2, 577968], P('head', 'dp'), may hold values from -21.947428 to 21.947428
- head_second: float32 [2, 577968], P('head', 'dp'), may hold values from 3.93216 to 15.72864
- shared_first: float32 [180960], P(('dp', 'head')), may hold values from -21.947428 to 21.947428
- shared_second: float32 [180960], P(('dp', 'head')), may hold values from 3.93216 to 15.72864
Outputs:
- layer_out: bfloat16 [512, 192, 240], P(('dp', 'head'))
- input_grad: float32 [512, 192, 240], P(('dp', 'head'))
- head_first_new: float32 [2, 577968], P('head', 'dp')
- head_second_new: float32 [2, 577968], P('head', 'dp')
- head_new: float32 [2, 577968], P('head', 'dp')
- head_copy: bfloat16 [2, 577968], P('head', 'dp')
- shared_first_new: float32 [180960], P(('dp', 'head'))
- shared_second_new: float32 [180960], P(('dp', 'head'))
- shared_new: float32 [180960], P(('dp', 'head'))
- shared_copy: bfloat16 [180960], P(('dp', 'head'))
The draws below stay inside these ranges and needn't reach their ends.
Inputs may be any that keep to these rules, and one draw needn't show every extreme that they name: `lengths`: each utterance has 1 to 192 valid frames; the last utterance has exactly 192.
All inputs are finite; a program needn't handle non-finite values.
Results may differ from the reference program's by a relative error of at most 0.025.
Values may be sent and summed in bfloat16 or wider, within the bound.
A program may use at most 256 MiB of HBM per device.

```python
import math
import jax
import jax.numpy as jnp
import numpy as np
from jax import lax

D = 240
HEADS = 4
HD = 60
FF = 960
KW = 15
LMAX = 192
SEQ_DEV = 32
STEP = 10
BATCH = 512
TOKENS = 98304
KREL = 383
HF = 480
HH = 2
HC = 120
NHP = 577966
NHSH = 36123
NSP = 180960
NSSH = 5655
N_DP = 16
N_HEAD = 2
DEVICES = 32


def head_scale_table():
    per_head = [(D * HF, D ** (-0.5)), (HF, 0.3), (HF * D, 2.0 * FF ** (-0.5))] * 2
    per_head += [(D * HC, D ** (-0.5))] * 3 + [(HC, 0.3)] * 2
    per_head += [(HH * KREL, 1.0), (HC * D, (LMAX / (3.0 * D)) ** 0.5)]
    per_head += [(NHSH * N_DP - NHP, 0.05)]
    scales = np.concatenate([np.full(amount, spread, np.float32) for amount, spread in per_head])
    return np.tile(scales[None, :], (N_HEAD, 1))


def shared_scale_table():
    pairs = []
    for entry_index in range(13):
        if entry_index < 10 and entry_index % 2 == 0:
            pairs.append((D, 0.15, 1.0))
        else:
            pairs.append((D, 0.3, 0.0))
    pairs += [(2 * D * D, D ** (-0.5), 0.0), (2 * D, 0.3, 0.0), (KW * D, KW ** (-0.5), 0.0), (D, 0.3, 0.0), (D, 0.15, 1.0), (D, 0.3, 0.0), (D * D, D ** (-0.5), 0.0), (D, 0.3, 0.0), (NSSH * DEVICES - NSP, 0.05, 0.0)]
    scales = np.concatenate([np.full(amount, spread, np.float32) for amount, spread, centre in pairs])
    offsets = np.concatenate([np.full(amount, centre, np.float32) for amount, spread, centre in pairs])
    return (scales, offsets)


def draw_lengths(key, part):
    key = jax.random.fold_in(key, 1)
    index_all = jnp.arange(BATCH, dtype=jnp.int32)
    rank_of = index_all // (SEQ_DEV // N_HEAD)
    ceiling = LMAX // 3 + (LMAX - LMAX // 3) * rank_of // (DEVICES - 1)
    floor_len = jnp.maximum(1, ceiling // 2)
    raw_draw = jax.random.randint(key, (BATCH,), 0, 1048576, dtype=jnp.int32)
    drawn = raw_draw % (ceiling - floor_len + 1) + floor_len
    return drawn.at[BATCH - 1].set(LMAX).astype(jnp.int32)


def draw_head_params(key, part):
    key = jax.random.fold_in(key, 2)
    noise_draw = jax.random.truncated_normal(key, -3.0, 3.0, (N_HEAD, NHSH * N_DP), jnp.float32)
    return noise_draw * jnp.asarray(head_scale_table())


def draw_shared_params(key, part):
    key = jax.random.fold_in(key, 3)
    scales, offsets = shared_scale_table()
    noise_draw = jax.random.truncated_normal(key, -3.0, 3.0, (NSSH * DEVICES,), jnp.float32)
    return jnp.asarray(offsets) + noise_draw * jnp.asarray(scales)


def draw_head_first(key, part):
    key = jax.random.fold_in(key, 4)
    noise_draw = jax.random.truncated_normal(key, -3.0, 3.0, (N_HEAD, NHSH * N_DP), jnp.float32)
    return noise_draw * (0.0222 * TOKENS ** 0.5)


def draw_head_second(key, part):
    key = jax.random.fold_in(key, 5)
    factor = jax.random.uniform(key, (N_HEAD, NHSH * N_DP), jnp.float32, 1.0, 4.0)
    return factor * (4e-05 * TOKENS)


def draw_shared_first(key, part):
    key = jax.random.fold_in(key, 6)
    noise_draw = jax.random.truncated_normal(key, -3.0, 3.0, (NSSH * DEVICES,), jnp.float32)
    return noise_draw * (0.0222 * TOKENS ** 0.5)


def draw_shared_second(key, part):
    key = jax.random.fold_in(key, 7)
    factor = jax.random.uniform(key, (NSSH * DEVICES,), jnp.float32, 1.0, 4.0)
    return factor * (4e-05 * TOKENS)


def block_levels(stream_key, dims, shards, low, largest):
    level, own = 1.0, jax.random.fold_in(stream_key, 6)
    for position, parts in shards:
        steps = jnp.exp(jax.random.uniform(jax.random.fold_in(own, position), (parts,), jnp.float32, low / len(shards), largest / len(shards)))
        level = level * jnp.repeat(steps, dims[position] // parts).reshape([-1 if axis == position else 1 for axis in range(len(dims))])
    return level


def gaussian(own_key, shape, deviation, most, cuts=(), held_as=jnp.bfloat16):
    values = deviation * jax.random.normal(own_key, shape, jnp.float32)
    if cuts:
        values = values * block_levels(own_key, shape, cuts, -0.22, 0.18)
    return jnp.clip(values, -most, most).astype(held_as)


def setup_inputs(seed: int = 0) -> dict:
    seeds = jax.random.split(jax.random.key(seed), 10)
    return {
        "frames": gaussian(seeds[0], (BATCH, LMAX, D), 1.0, 6.0, ((0, 32),)),
        "cotangent": gaussian(seeds[1], (BATCH, LMAX, D), 1.0, 6.0, ((0, 32),)),
        "lengths": draw_lengths(jax.random.fold_in(seeds[9], 71), 0),
        "head_params": draw_head_params(jax.random.fold_in(seeds[9], 71), 0),
        "shared_params": draw_shared_params(jax.random.fold_in(seeds[9], 71), 0),
        "head_first": draw_head_first(jax.random.fold_in(seeds[9], 71), 0),
        "head_second": draw_head_second(jax.random.fold_in(seeds[9], 71), 0),
        "shared_first": draw_shared_first(jax.random.fold_in(seeds[9], 71), 0),
        "shared_second": draw_shared_second(jax.random.fold_in(seeds[9], 71), 0),
    }


@jax.custom_vjp
def low(v):
    return lax.optimization_barrier(v.astype(jnp.bfloat16)).astype(jnp.float32)

@jax.custom_vjp
def low_back(v):
    return v

def low_keep(v):
    return (low(v), None)

def low_pass(kept, grad):
    return (grad,)

def back_keep(v):
    return (v, None)

def back_low(kept, grad):
    return (low(grad),)
low.defvjp(low_keep, low_pass)
low_back.defvjp(back_keep, back_low)
NORM_EPS = 1e-05
BETA_ONE = 0.9
BETA_TWO = 0.999
LEARN_RATE = 0.1
WEIGHT_DECAY = 0.01
ADAM_EPS = 1e-08
HIGHEST = lax.Precision.HIGHEST
JOIN_AXIS = {'up_one': 1, 'upb_one': 0, 'down_one': 0, 'up_two': 1, 'upb_two': 0, 'down_two': 0, 'w_query': 1, 'w_key': 1, 'w_value': 1, 'b_query': 0, 'b_value': 0, 'rel_table': 0, 'w_out': 0}
VECTOR_NAMES = ('ffa_gain', 'ffa_bias', 'att_gain', 'att_bias', 'cnv_gain', 'cnv_bias', 'ffb_gain', 'ffb_bias', 'out_gain', 'out_bias', 'downb_one', 'downb_two', 'b_out')
FFN_ONE = ('ffa_gain', 'ffa_bias', 'up_one', 'upb_one', 'down_one', 'downb_one')
FFN_TWO = ('ffb_gain', 'ffb_bias', 'up_two', 'upb_two', 'down_two', 'downb_two')

def head_layout(model_dim, hidden, heads_here, head_size, rel_count):
    head_width = heads_here * head_size
    return [('up_one', (model_dim, hidden)), ('upb_one', (hidden,)), ('down_one', (hidden, model_dim)), ('up_two', (model_dim, hidden)), ('upb_two', (hidden,)), ('down_two', (hidden, model_dim)), ('w_query', (model_dim, head_width)), ('w_key', (model_dim, head_width)), ('w_value', (model_dim, head_width)), ('b_query', (head_width,)), ('b_value', (head_width,)), ('rel_table', (heads_here, rel_count)), ('w_out', (head_width, model_dim))]

def shared_layout(model_dim, kernel):
    entries = [(entry_name, (model_dim,)) for entry_name in VECTOR_NAMES]
    entries += [('point_one', (model_dim, 2 * model_dim)), ('pointb_one', (2 * model_dim,)), ('depth_kernel', (kernel, model_dim)), ('depth_bias', (model_dim,)), ('batch_gain', (model_dim,)), ('batch_bias', (model_dim,)), ('point_two', (model_dim, model_dim)), ('pointb_two', (model_dim,))]
    return entries

def unflatten(flat_vector, layout):
    result = {}
    offset = 0
    for entry_name, dims_of in layout:
        amount = math.prod(dims_of)
        result[entry_name] = flat_vector[offset:offset + amount].reshape(dims_of)
        offset += amount
    return result

def build_weights(head_flat, shared_flat):
    layout = head_layout(D, FF // N_HEAD, HEADS // N_HEAD, HD, KREL)
    pieces = [unflatten(head_flat[row_index], layout) for row_index in range(N_HEAD)]
    layer_weights = {entry_name: jnp.concatenate([piece_dict[entry_name] for piece_dict in pieces], JOIN_AXIS[entry_name]) for entry_name, dims_of in layout}
    layer_weights.update(unflatten(shared_flat, shared_layout(D, KW)))
    return layer_weights

def layer_norm(values, norm_gain, norm_bias):
    centre = values - lax.optimization_barrier(jnp.mean(values, -1, keepdims=True))
    spread = lax.optimization_barrier(jnp.mean(centre * centre, -1, keepdims=True))
    return centre * lax.rsqrt(spread + NORM_EPS) * norm_gain + norm_bias

def matmul(left_side, right_side):
    return jnp.einsum('...d,de->...e', left_side, right_side, precision=HIGHEST)

def swish_of(values):
    return values * jax.nn.sigmoid(values)

def depthwise(signal, kernel):
    tap_count = kernel.shape[0]
    half_width = tap_count // 2
    length = signal.shape[1]
    padded = jnp.pad(signal, ((0, 0), (half_width, half_width), (0, 0)))
    result = padded[:, 0:length] * kernel[0]
    for tap_index in range(1, tap_count):
        result = result + padded[:, tap_index:tap_index + length] * kernel[tap_index]
    return result

def half_ffn(values, layer_weights, names):
    gain_key, bias_key, upper_random_key, upperb_key, lower_random_key, lowerb_key = names
    normed = low(layer_norm(values, layer_weights[gain_key], layer_weights[bias_key]))
    upper_pre = low_back(matmul(normed, layer_weights[upper_random_key]) + layer_weights[upperb_key])
    active_values = low(swish_of(upper_pre))
    return values + 0.5 * low_back(matmul(active_values, layer_weights[lower_random_key]) + layer_weights[lowerb_key])

def attention(values, key_valid, layer_weights):
    count_seq, length = (values.shape[0], values.shape[1])
    normed = low(layer_norm(values, layer_weights['att_gain'], layer_weights['att_bias']))
    head_shape = (count_seq, length, HEADS, HD)
    queries = low(low_back(matmul(normed, layer_weights['w_query']) + layer_weights['b_query'])).reshape(head_shape)
    key_rows = low(low_back(matmul(normed, layer_weights['w_key']))).reshape(head_shape)
    value_rows = low(low_back(matmul(normed, layer_weights['w_value']) + layer_weights['b_value'])).reshape(head_shape)
    positions = jnp.arange(length, dtype=jnp.int32)
    rel_index = positions[None, :] - positions[:, None] + (length - 1)
    rel_bias = layer_weights['rel_table'][:, rel_index]
    scores = jnp.einsum('sihe,sjhe->shij', queries, key_rows, precision=HIGHEST) * HD ** (-0.5) + rel_bias[None]
    scores = low_back(scores)
    scores = jnp.where(key_valid[:, None, None, :], scores, -1e+30)
    row_max = lax.optimization_barrier(jnp.max(scores, -1, keepdims=True))
    exponent = jnp.exp(scores - row_max)
    soft_weights = exponent / lax.optimization_barrier(jnp.sum(exponent, -1, keepdims=True))
    mixed_head_output = jnp.einsum('shij,sjhe->sihe', low(soft_weights), value_rows, precision=HIGHEST)
    mixed_head_output = low(low_back(mixed_head_output)).reshape(count_seq, length, HEADS * HD)
    return values + low_back(matmul(mixed_head_output, layer_weights['w_out']) + layer_weights['b_out'])

def conv_front(values, piece_valid, layer_weights):
    normed = low(layer_norm(values, layer_weights['cnv_gain'], layer_weights['cnv_bias']))
    lifted = low_back(matmul(normed, layer_weights['point_one']) + layer_weights['pointb_one'])
    model_dim = values.shape[-1]
    glu_out = lifted[..., :model_dim] * jax.nn.sigmoid(lifted[..., model_dim:]) * piece_valid[..., None]
    return depthwise(glu_out, layer_weights['depth_kernel']) + layer_weights['depth_bias']

def adam_update(master, gradient, moment_one, moment_two):
    first_new = BETA_ONE * moment_one + (1.0 - BETA_ONE) * gradient
    second_new = BETA_TWO * moment_two + (1.0 - BETA_TWO) * gradient * gradient
    first_hat = first_new / (1.0 - BETA_ONE ** STEP)
    second_hat = second_new / (1.0 - BETA_TWO ** STEP)
    updated = master - LEARN_RATE * (first_hat / (jnp.sqrt(second_hat) + ADAM_EPS) + WEIGHT_DECAY * master)
    return (first_new, second_new, updated)

def reference(frames, cotangent, lengths, head_params, shared_params, head_first, head_second, shared_first, shared_second):
    inputs = frames.astype(jnp.float32)
    output_gradient = cotangent.astype(jnp.float32)
    blocks = BATCH // SEQ_DEV
    positions = jnp.arange(LMAX, dtype=jnp.int32)
    valid_frames = (positions[None, :] < lengths[:, None]).astype(jnp.float32).reshape(blocks, SEQ_DEV, LMAX)

    def forward(inputs, head_params, shared_params):
        layer_weights = build_weights(low(head_params), low(shared_params))

        def phase_one(packed):
            piece_values, piece_valid = packed
            values = half_ffn(piece_values, layer_weights, FFN_ONE)
            values = attention(values, piece_valid > 0.5, layer_weights)
            return (values, conv_front(values, piece_valid, layer_weights))
        mids, conv_outs = lax.map(jax.checkpoint(phase_one), (inputs.reshape(blocks, SEQ_DEV, LMAX, D), valid_frames))
        valid_mask = valid_frames[..., None]
        valid_count = jnp.sum(valid_frames)
        conv_mean = lax.optimization_barrier(jnp.sum(conv_outs * valid_mask, (0, 1, 2))) / valid_count
        centred = (conv_outs - conv_mean) * valid_mask
        inv_spread = lax.rsqrt(lax.optimization_barrier(jnp.sum(centred * centred, (0, 1, 2))) / valid_count + NORM_EPS)

        def phase_two(packed):
            piece_values, piece_conv = packed
            normal = (piece_conv - conv_mean) * inv_spread
            shifted = normal * layer_weights['batch_gain'] + layer_weights['batch_bias']
            active_values = low(swish_of(shifted))
            values = piece_values + low_back(matmul(active_values, layer_weights['point_two']) + layer_weights['pointb_two'])
            values = half_ffn(values, layer_weights, FFN_TWO)
            return layer_norm(values, layer_weights['out_gain'], layer_weights['out_bias'])
        finals = lax.map(jax.checkpoint(phase_two), (mids, conv_outs))
        return finals.reshape(BATCH, LMAX, D)
    result, pullback = jax.vjp(forward, inputs, head_params, shared_params)
    input_grad, head_grad, shared_grad = pullback(output_gradient)
    head_one, head_two, head_next = adam_update(head_params, head_grad, head_first, head_second)
    shared_one, shared_two, shared_next = adam_update(shared_params, shared_grad, shared_first, shared_second)
    return (result.astype(jnp.bfloat16), input_grad, head_one, head_two, head_next, head_next.astype(jnp.bfloat16), shared_one, shared_two, shared_next, shared_next.astype(jnp.bfloat16))
```

```python
import functools
import math

import jax
import jax.numpy as jnp
from jax import lax
from jax.experimental import pallas as pl
from jax.experimental.pallas import tpu as pltpu
from jax.sharding import PartitionSpec as P

BF = jnp.bfloat16
F32 = jnp.float32
LANES = 128


def up_to(count, unit):
    return -(-count // unit) * unit


def grid_place(nz):
    me = lax.axis_index("dp")
    core = lax.axis_index("head")
    zc = me // 4
    rest = me - 4 * zc
    yc = rest // 2
    xc = rest - 2 * yc
    return me, core, zc, yc, xc


def remote(src, dst, send, recv, dp, head):
    return pltpu.make_async_remote_copy(
        src_ref=src,
        dst_ref=dst,
        send_sem=send,
        recv_sem=recv,
        device_id={"dp": dp, "head": head},
        device_id_type=pl.DeviceIdType.MESH,
    )


def greet(nz, me, core, zc, yc, xc):
    barrier = pltpu.get_barrier_semaphore()

    def hello(dp, head):
        pl.semaphore_signal(
            barrier, inc=1, device_id={"dp": dp, "head": head}, device_id_type=pl.DeviceIdType.MESH
        )

    for k in range(1, nz):
        hello(lax.rem(zc + k, nz) * 4 + 2 * yc + xc, core)
    hello(4 * zc + 2 * (1 - yc) + xc, core)
    hello(4 * zc + 2 * yc + 1 - xc, core)
    hello(me, 1 - core)
    pl.semaphore_wait(barrier, nz + 2)


def gather_kernel(nz, src, out, sz, rz, s1, r1, s2, r2, sc, rc):
    rows = src.shape[0]
    row_a = up_to(rows // 2, 16)
    parts = (pl.ds(0, row_a), pl.ds(row_a, rows - row_a))
    me, core, zc, yc, xc = grid_place(nz)
    greet(nz, me, core, zc, yc, xc)
    out[me, core] = src[...]
    y_peer = 4 * zc + 2 * (1 - yc) + xc
    x_peer = 4 * zc + 2 * yc + 1 - xc
    firsts = (y_peer, x_peer)
    seconds = (x_peer, y_peer)
    pending = []

    def send(slot, p, send_sem, recv_sem, dp, head):
        block = out.at[slot, core, parts[p]]
        copy = remote(block, block, send_sem, recv_sem, dp, head)
        copy.start()
        pending.append(copy)

    def arrived(slot, which, p, send_sem, recv_sem):
        block = out.at[slot, which, parts[p]]
        remote(block, block, send_sem, recv_sem, me, 1 - core).wait_recv()

    zs = [lax.rem(zc + k, nz) for k in range(nz)]
    here = 2 * yc + xc
    first_here = (2 * (1 - yc) + xc, 2 * yc + 1 - xc)
    second_here = ((2 * yc + 1 - xc, 2 * (1 - yc) + 1 - xc), (2 * (1 - yc) + xc, 2 * (1 - yc) + 1 - xc))
    for k in range(1, nz):
        for p in (0, 1):
            send(me, p, sz.at[p, k], rz.at[p, zc], zs[k] * 4 + here, core)
    for k in range(nz):
        z = zs[k]
        slot = 4 * z + here
        for p in (0, 1):
            if k:
                arrived(slot, core, p, sz.at[p, k], rz.at[p, z])
            send(slot, p, s1.at[p, k], r1.at[p, z], firsts[p], core)
            send(slot, p, s2.at[p, k, 0], r2.at[p, z, 0], seconds[p], core)
            send(slot, p, sc.at[p, k, 0], rc.at[p, z, 0], me, 1 - core)
    for k in range(nz):
        z = zs[k]
        for p in (0, 1):
            slot = 4 * z + first_here[p]
            arrived(slot, core, p, s1.at[p, k], r1.at[p, z])
            send(slot, p, s2.at[p, k, 1], r2.at[p, z, 1], seconds[p], core)
            send(slot, p, sc.at[p, k, 1], rc.at[p, z, 1], me, 1 - core)
    for k in range(nz):
        z = zs[k]
        for p in (0, 1):
            for b in (0, 1):
                slot = 4 * z + second_here[p][b]
                arrived(slot, core, p, s2.at[p, k, b], r2.at[p, z, b])
                send(slot, p, sc.at[p, k, 2 + b], rc.at[p, z, 2 + b], me, 1 - core)
    for k in range(nz):
        z = zs[k]
        for p in (0, 1):
            for b, at in enumerate((here, first_here[p]) + second_here[p]):
                arrived(4 * z + at, 1 - core, p, sc.at[p, k, b], rc.at[p, z, b])
    for copy in pending:
        copy.wait_send()


def gather_all(block, dp, collective_id):
    rows = block.shape[0]
    nz = dp // 4
    dma = pltpu.SemaphoreType.DMA
    return pl.pallas_call(
        functools.partial(gather_kernel, nz),
        out_shape=jax.ShapeDtypeStruct((dp, 2, rows, LANES), block.dtype),
        in_specs=[pl.BlockSpec(memory_space=pltpu.VMEM)],
        out_specs=pl.BlockSpec(memory_space=pltpu.VMEM),
        scratch_shapes=[dma((2, nz)), dma((2, nz)), dma((2, nz)), dma((2, nz)), dma((2, nz, 2)), dma((2, nz, 2)), dma((2, nz, 4)), dma((2, nz, 4))],
        compiler_params=pltpu.CompilerParams(
            collective_id=collective_id, has_side_effects=True, vmem_limit_bytes=40 << 20
        ),
        name="gather_weights",
    )(block)


def scatter_kernel(nz, g, out, c1, t1, rx1, t2, rx2, t3, rx3, sc, rc, s1, r1, s2, r2, s3, r3):
    rows = g.shape[2]
    row_a = up_to(rows // 2, 16)
    starts = (0, row_a)
    sizes = (row_a, rows - row_a)
    parts = tuple(pl.ds(a, n) for a, n in zip(starts, sizes))
    me, core, zc, yc, xc = grid_place(nz)
    greet(nz, me, core, zc, yc, xc)
    y_peer = 4 * zc + 2 * (1 - yc) + xc
    x_peer = 4 * zc + 2 * yc + 1 - xc
    firsts = (x_peer, y_peer)
    seconds = (y_peer, x_peer)
    pending = []

    def send(src, dst, send_sem, recv_sem, dp, head):
        copy = remote(src, dst, send_sem, recv_sem, dp, head)
        copy.start()
        pending.append(copy)

    def arrived(block, send_sem, recv_sem):
        remote(block, block, send_sem, recv_sem, me, 1 - core).wait_recv()

    order = list(range(1, nz)) + [0]
    zs = [lax.rem(zc + k, nz) for k in range(nz)]
    give = ((1 - xc, 2 + 1 - xc), (2 * (1 - yc), 2 * (1 - yc) + 1))
    second_give = (1 - yc, 1 - xc)
    second_keep = (yc, xc)

    def place(p, b):
        return 2 * b + xc if p == 0 else 2 * yc + b

    for k in order:
        z = zs[k]
        send(g.at[1 - core, pl.ds(4 * z, 4)], c1.at[pl.ds(4 * z, 4)], sc.at[k], rc.at[z], me, 1 - core)
    for k in order:
        z = zs[k]
        arrived(c1.at[pl.ds(4 * z, 4)], sc.at[k], rc.at[z])
        for p in (0, 1):
            n = pl.ds(0, sizes[p])
            for b in (0, 1):
                slot = 4 * z + give[p][b]
                t1[p, z, b, n] = (g[core, slot, parts[p]].astype(F32) + c1[slot, parts[p]].astype(F32)).astype(BF)
            send(t1.at[p, z, :, n], rx1.at[p, z, :, n], s1.at[p, k], r1.at[p, z], firsts[p], core)

    def partial(p, z, b):
        slot = 4 * z + place(p, b)
        n = pl.ds(0, sizes[p])
        return g[core, slot, parts[p]].astype(F32) + c1[slot, parts[p]].astype(F32) + rx1[p, z, b, n].astype(F32)

    for k in order:
        z = zs[k]
        for p in (0, 1):
            n = pl.ds(0, sizes[p])
            arrived(rx1.at[p, z, :, n], s1.at[p, k], r1.at[p, z])
            t2[p, z, n] = partial(p, z, second_give[p]).astype(BF)
            send(t2.at[p, z, n], rx2.at[p, z, n], s2.at[p, k], r2.at[p, z], seconds[p], core)
    for k in order:
        z = zs[k]
        for p in (0, 1):
            n = pl.ds(0, sizes[p])
            arrived(rx2.at[p, z, n], s2.at[p, k], r2.at[p, z])
            total = partial(p, z, second_keep[p]) + rx2[p, z, n].astype(F32)
            if k:
                t3[p, z, n] = total.astype(BF)
                send(t3.at[p, z, n], rx3.at[p, zc, n], s3.at[p, k], r3.at[p, zc], 4 * z + 2 * yc + xc, core)
            else:
                out[parts[p], :] = total
    for k in order[:-1]:
        z = zs[k]
        for p in (0, 1):
            n = pl.ds(0, sizes[p])
            arrived(rx3.at[p, z, n], s3.at[p, k], r3.at[p, z])
            out[parts[p], :] += rx3[p, z, n].astype(F32)
    for copy in pending:
        copy.wait_send()


def scatter_all(g, collective_id):
    dp, rows = g.shape[1], g.shape[2]
    nz = dp // 4
    half = up_to(rows // 2, 16)
    dma = pltpu.SemaphoreType.DMA
    vm = pltpu.VMEM
    return pl.pallas_call(
        functools.partial(scatter_kernel, nz),
        out_shape=jax.ShapeDtypeStruct((rows, LANES), F32),
        in_specs=[pl.BlockSpec(memory_space=pltpu.VMEM)],
        out_specs=pl.BlockSpec(memory_space=pltpu.VMEM),
        scratch_shapes=[
            vm((dp, rows, LANES), BF),
            vm((2, nz, 2, half, LANES), BF),
            vm((2, nz, 2, half, LANES), BF),
            vm((2, nz, half, LANES), BF),
            vm((2, nz, half, LANES), BF),
            vm((2, nz, half, LANES), BF),
            vm((2, nz, half, LANES), BF),
            dma((nz,)), dma((nz,)), dma((2, nz)), dma((2, nz)), dma((2, nz)), dma((2, nz)), dma((2, nz)), dma((2, nz)),
        ],
        compiler_params=pltpu.CompilerParams(
            collective_id=collective_id, has_side_effects=True, vmem_limit_bytes=40 << 20
        ),
        name="scatter_grads",
    )(g)


def share_kernel(dp_count, src, out, ss, rs):
    me = lax.axis_index("dp")
    core = lax.axis_index("head")
    own = 2 * me + core
    total = 2 * dp_count
    barrier = pltpu.get_barrier_semaphore()

    def peer(k):
        other = lax.rem(own + k, total)
        dp = other // 2
        return other, dp, other - 2 * dp

    @pl.loop(1, total)
    def _(k):
        _, dp, head = peer(k)
        pl.semaphore_signal(
            barrier, inc=1, device_id={"dp": dp, "head": head}, device_id_type=pl.DeviceIdType.MESH
        )

    pl.semaphore_wait(barrier, total - 1)
    out[own] = src[...]

    @pl.loop(1, total)
    def _(k):
        _, dp, head = peer(k)
        remote(src, out.at[own], ss.at[k], rs.at[own], dp, head).start()

    @pl.loop(1, total)
    def _(k):
        other, dp, head = peer(k)
        remote(src, out.at[other], ss.at[k], rs.at[other], dp, head).wait()


def share_all(block, dp, collective_id):
    dma = pltpu.SemaphoreType.DMA
    return pl.pallas_call(
        functools.partial(share_kernel, dp),
        out_shape=jax.ShapeDtypeStruct((2 * dp,) + block.shape, block.dtype),
        in_specs=[pl.BlockSpec(memory_space=pltpu.VMEM)],
        out_specs=pl.BlockSpec(memory_space=pltpu.VMEM),
        scratch_shapes=[dma((2 * dp,)), dma((2 * dp,))],
        compiler_params=pltpu.CompilerParams(collective_id=collective_id, has_side_effects=True),
        name="share_sums",
    )(block)

HEADS = 4
HD = 60
FF = 960
KW = 15
STEP = 10
KREL = 383


NORM_EPS = 1e-05
BETA_ONE = 0.9
BETA_TWO = 0.999
LEARN_RATE = 0.1
WEIGHT_DECAY = 0.01
ADAM_EPS = 1e-08
(
    UP_ONE,
    UPB_ONE,
    DOWN_ONE,
    UP_TWO,
    UPB_TWO,
    DOWN_TWO,
    W_QUERY,
    W_KEY,
    W_VALUE,
    B_QUERY,
    B_VALUE,
    REL_TABLE,
    W_OUT,
    FFA_GAIN,
    FFA_BIAS,
    ATT_GAIN,
    ATT_BIAS,
    CNV_GAIN,
    CNV_BIAS,
    FFB_GAIN,
    FFB_BIAS,
    OUT_GAIN,
    OUT_BIAS,
    DOWNB_ONE,
    DOWNB_TWO,
    B_OUT,
    POINT_ONE,
    POINTB_ONE,
    DEPTH_KERNEL,
    DEPTH_BIAS,
    BATCH_GAIN,
    BATCH_BIAS,
    POINT_TWO,
    POINTB_TWO,
) = range(34)
JOIN_AXIS = {
    UP_ONE: 1,
    UPB_ONE: 0,
    DOWN_ONE: 0,
    UP_TWO: 1,
    UPB_TWO: 0,
    DOWN_TWO: 0,
    W_QUERY: 1,
    W_KEY: 1,
    W_VALUE: 1,
    B_QUERY: 0,
    B_VALUE: 0,
    REL_TABLE: 0,
    W_OUT: 0,
}
VECTOR_NAMES = (
    FFA_GAIN,
    FFA_BIAS,
    ATT_GAIN,
    ATT_BIAS,
    CNV_GAIN,
    CNV_BIAS,
    FFB_GAIN,
    FFB_BIAS,
    OUT_GAIN,
    OUT_BIAS,
    DOWNB_ONE,
    DOWNB_TWO,
    B_OUT,
)
FFN_ONE = (FFA_GAIN, FFA_BIAS, UP_ONE, UPB_ONE, DOWN_ONE, DOWNB_ONE)
FFN_TWO = (FFB_GAIN, FFB_BIAS, UP_TWO, UPB_TWO, DOWN_TWO, DOWNB_TWO)


def for_sending(x):

    def short(part):
        return part.astype(jnp.bfloat16) if part.dtype == jnp.float32 else part

    return jax.tree.map(short, x)


def head_layout(model_dim, hidden, heads_here, head_size, rel_count):
    head_width = heads_here * head_size
    return [
        (UP_ONE, (model_dim, hidden)),
        (UPB_ONE, (hidden,)),
        (DOWN_ONE, (hidden, model_dim)),
        (UP_TWO, (model_dim, hidden)),
        (UPB_TWO, (hidden,)),
        (DOWN_TWO, (hidden, model_dim)),
        (W_QUERY, (model_dim, head_width)),
        (W_KEY, (model_dim, head_width)),
        (W_VALUE, (model_dim, head_width)),
        (B_QUERY, (head_width,)),
        (B_VALUE, (head_width,)),
        (REL_TABLE, (heads_here, rel_count)),
        (W_OUT, (head_width, model_dim)),
    ]


def shared_layout(model_dim, kernel):
    entries = [(entry_name, (model_dim,)) for entry_name in VECTOR_NAMES]
    entries += [
        (POINT_ONE, (model_dim, 2 * model_dim)),
        (POINTB_ONE, (2 * model_dim,)),
        (DEPTH_KERNEL, (kernel, model_dim)),
        (DEPTH_BIAS, (model_dim,)),
        (BATCH_GAIN, (model_dim,)),
        (BATCH_BIAS, (model_dim,)),
        (POINT_TWO, (model_dim, model_dim)),
        (POINTB_TWO, (model_dim,)),
    ]
    return entries


def unflatten(flat_vector, layout):
    result = {}
    offset = 0
    for entry_name, dims_of in layout:
        amount = math.prod(dims_of)
        result[entry_name] = flat_vector[offset : offset + amount].reshape(dims_of)
        offset += amount
    return result


def flatten_dict(grads, layout, full_length):
    flat_parts = [grads[entry_name].reshape(-1) for entry_name, dims_of in layout]
    used_count = sum((math.prod(dims_of) for entry_name, dims_of in layout))
    flat_parts.append(jnp.zeros((full_length - used_count,), jnp.float32))
    return jnp.concatenate(flat_parts)


def spread_frames(normed_lower_half):
    return normed_lower_half


def collect_frames(partial_value):
    return partial_value


def spread_grads(branch_gradient):
    return branch_gradient


def collect_grads(partial_value):
    return partial_value


def norm_forward(values, norm_gain, norm_bias):
    centre = values - jnp.mean(values, -1, keepdims=True)
    inv_spread = lax.rsqrt(jnp.mean(centre * centre, -1, keepdims=True) + NORM_EPS)
    scaled = centre * inv_spread
    return (scaled * norm_gain + norm_bias, scaled, inv_spread)


def norm_backward(grad_normed, scaled, inv_spread, norm_gain):
    gain_grad = jnp.sum(grad_normed * scaled, (0, 1))
    bias_grad = jnp.sum(grad_normed, (0, 1))
    grad_scaled = grad_normed * norm_gain
    values_grad = inv_spread * (
        grad_scaled
        - jnp.mean(grad_scaled, -1, keepdims=True)
        - scaled * jnp.mean(grad_scaled * scaled, -1, keepdims=True)
    )
    return (values_grad, gain_grad, bias_grad)


def depthwise(signal, kernel):
    tap_count = kernel.shape[0]
    half_width = tap_count // 2
    length = signal.shape[1]
    padded = jnp.pad(signal, ((0, 0), (half_width, half_width), (0, 0)))
    result = padded[:, 0:length] * kernel[0]
    for tap_index in range(1, tap_count):
        result = result + padded[:, tap_index : tap_index + length] * kernel[tap_index]
    return result


def rel_expand(rel_table, length):
    heads_here = rel_table.shape[0]
    padded = jnp.pad(rel_table, ((0, 0), (1, 1)))
    tiled = jnp.tile(padded, (1, length))[:, : 2 * length * length]
    return tiled.reshape(heads_here, length, 2 * length)[:, :, length:]


def rel_collect(grid):
    heads_here, length = (grid.shape[0], grid.shape[1])
    shifted = jnp.pad(grid, ((0, 0), (0, 0), (length, 0))).reshape(heads_here, 2 * length * length)
    shifted = jnp.pad(shifted, ((0, 0), (0, length))).reshape(heads_here, length, 2 * length + 1)
    return jnp.sum(shifted, 1)[:, 1 : 2 * length]


def ffn_forward(values, layer_weights, names):
    gain_key, bias_key, upper_random_key, upperb_key, lower_random_key, lowerb_key = names
    normed, scaled, inv_spread = norm_forward(
        values,
        layer_weights[gain_key].astype(jnp.float32),
        layer_weights[bias_key].astype(jnp.float32),
    )
    gathered_params = spread_frames(normed.astype(jnp.bfloat16))
    upper_pre = jnp.einsum(
        "eav,vi->eai",
        gathered_params,
        layer_weights[upper_random_key],
        preferred_element_type=jnp.float32,
    )
    upper_pre = upper_pre + layer_weights[upperb_key].astype(jnp.float32)
    active_values = (upper_pre * jax.nn.sigmoid(upper_pre)).astype(jnp.bfloat16)
    partial_value = jnp.einsum(
        "wmp,pz->wmz",
        active_values,
        layer_weights[lower_random_key],
        preferred_element_type=jnp.float32,
    )
    branch = collect_frames(partial_value) + layer_weights[lowerb_key].astype(jnp.float32)
    return (values + 0.5 * branch, (scaled, inv_spread, gathered_params, upper_pre))


def ffn_backward(grad_out, stored, layer_weights, names):
    gain_key, bias_key, upper_random_key, upperb_key, lower_random_key, lowerb_key = names
    scaled, inv_spread, gathered_params, upper_pre = stored
    branch_gradient = (0.5 * grad_out).astype(jnp.bfloat16)
    wide_gradient = spread_grads(branch_gradient)
    sigmoid_up = jax.nn.sigmoid(upper_pre)
    active_values = (upper_pre * sigmoid_up).astype(jnp.bfloat16)
    lower_gradient = jnp.einsum(
        "mbc,mbx->cx", active_values, wide_gradient, preferred_element_type=jnp.float32
    )
    active_grad = jnp.einsum(
        "amz,tz->amt",
        wide_gradient,
        layer_weights[lower_random_key],
        preferred_element_type=jnp.float32,
    )
    upper_gradient = (active_grad * sigmoid_up * (1.0 + upper_pre * (1.0 - sigmoid_up))).astype(
        jnp.bfloat16
    )
    upperw_grad = jnp.einsum(
        "rzx,rzm->xm", gathered_params, upper_gradient, preferred_element_type=jnp.float32
    )
    normed_part = jnp.einsum(
        "rvc,hc->rvh",
        upper_gradient,
        layer_weights[upper_random_key],
        preferred_element_type=jnp.float32,
    )
    normed_grad = collect_grads(normed_part)
    values_grad, gain_grad, bias_grad = norm_backward(
        normed_grad, scaled, inv_spread, layer_weights[gain_key].astype(jnp.float32)
    )
    grads = {
        upper_random_key: upperw_grad,
        upperb_key: jnp.sum(upper_gradient, (0, 1), dtype=jnp.float32),
        lower_random_key: lower_gradient,
        lowerb_key: jnp.sum(branch_gradient, (0, 1), dtype=jnp.float32),
        gain_key: gain_grad,
        bias_key: bias_grad,
    }
    return (grad_out + values_grad, grads)


def score_block(queries, key_rows, rel_bias, key_valid):
    scores = jnp.einsum(
        "sihe,sjhe->shij", queries, key_rows, preferred_element_type=jnp.float32
    ) * HD ** (-0.5)
    scores = scores + rel_bias[None]
    return jnp.where(key_valid[:, None, None, :], scores, -1e30)


def attention_forward(values, layer_weights, key_valid):
    normed, scaled, inv_spread = norm_forward(
        values,
        layer_weights[ATT_GAIN].astype(jnp.float32),
        layer_weights[ATT_BIAS].astype(jnp.float32),
    )
    gathered_params = spread_frames(normed.astype(jnp.bfloat16))
    count_seq, length = (gathered_params.shape[0], gathered_params.shape[1])
    heads_here = layer_weights[REL_TABLE].shape[0]
    head_shape = (count_seq, length, heads_here, HD)
    queries = (
        (
            jnp.einsum(
                "yoz,zv->yov",
                gathered_params,
                layer_weights[W_QUERY],
                preferred_element_type=jnp.float32,
            )
            + layer_weights[B_QUERY].astype(jnp.float32)
        )
        .astype(jnp.bfloat16)
        .reshape(head_shape)
    )
    key_rows = (
        jnp.einsum(
            "yoz,zv->yov",
            gathered_params,
            layer_weights[W_KEY],
            preferred_element_type=jnp.float32,
        )
        .astype(jnp.bfloat16)
        .reshape(head_shape)
    )
    value_rows = (
        (
            jnp.einsum(
                "yoz,zv->yov",
                gathered_params,
                layer_weights[W_VALUE],
                preferred_element_type=jnp.float32,
            )
            + layer_weights[B_VALUE].astype(jnp.float32)
        )
        .astype(jnp.bfloat16)
        .reshape(head_shape)
    )
    rel_bias = rel_expand(layer_weights[REL_TABLE].astype(jnp.float32), length)
    scores = score_block(queries, key_rows, rel_bias, key_valid)
    row_max = jnp.max(scores, -1, keepdims=True)
    exponent = jnp.exp(scores - row_max)
    row_total = jnp.sum(exponent, -1, keepdims=True)
    soft_weights = exponent / row_total
    log_total = row_max + jnp.log(row_total)
    mixed_head_output = jnp.einsum(
        "shij,sjhe->sihe",
        soft_weights.astype(jnp.bfloat16),
        value_rows,
        preferred_element_type=jnp.float32,
    )
    mixed_head_output = mixed_head_output.astype(jnp.bfloat16).reshape(
        count_seq, length, heads_here * HD
    )
    partial_value = jnp.einsum(
        "rpa,ah->rph", mixed_head_output, layer_weights[W_OUT], preferred_element_type=jnp.float32
    )
    branch = collect_frames(partial_value) + layer_weights[B_OUT].astype(jnp.float32)
    stored = (
        scaled,
        inv_spread,
        gathered_params,
        queries,
        key_rows,
        value_rows,
        log_total,
        mixed_head_output,
        rel_bias,
    )
    return (values + branch, stored)


def attention_backward(grad_out, stored, layer_weights, key_valid):
    (
        scaled,
        inv_spread,
        gathered_params,
        queries,
        key_rows,
        value_rows,
        log_total,
        mixed_head_output,
        rel_bias,
    ) = stored
    count_seq, length = (gathered_params.shape[0], gathered_params.shape[1])
    branch_gradient = grad_out.astype(jnp.bfloat16)
    wide_gradient = spread_grads(branch_gradient)
    output_gradient = jnp.einsum(
        "yig,yif->gf", mixed_head_output, wide_gradient, preferred_element_type=jnp.float32
    )
    mixed_grad = jnp.einsum(
        "eom,vm->eov", wide_gradient, layer_weights[W_OUT], preferred_element_type=jnp.float32
    )
    mixed_grad = mixed_grad.astype(jnp.bfloat16).reshape(queries.shape)
    scores = score_block(queries, key_rows, rel_bias, key_valid)
    soft_weights = jnp.exp(scores - log_total)
    weights_grad = jnp.einsum(
        "sihe,sjhe->shij", mixed_grad, value_rows, preferred_element_type=jnp.float32
    )
    value_gradient = jnp.einsum(
        "shij,sihe->sjhe",
        soft_weights.astype(jnp.bfloat16),
        mixed_grad,
        preferred_element_type=jnp.float32,
    )
    scores_grad = soft_weights * (
        weights_grad - jnp.sum(soft_weights * weights_grad, -1, keepdims=True)
    )
    scores_grad = scores_grad.astype(jnp.bfloat16)
    query_gradient = jnp.einsum(
        "shij,sjhe->sihe", scores_grad, key_rows, preferred_element_type=jnp.float32
    )
    key_gradient = jnp.einsum(
        "shij,sihe->sjhe", scores_grad, queries, preferred_element_type=jnp.float32
    )
    flat_shape = (count_seq, length, queries.shape[2] * HD)
    query_gradient = (query_gradient * HD ** (-0.5)).astype(jnp.bfloat16).reshape(flat_shape)
    key_gradient = (key_gradient * HD ** (-0.5)).astype(jnp.bfloat16).reshape(flat_shape)
    value_gradient = value_gradient.astype(jnp.bfloat16).reshape(flat_shape)
    table_grad = rel_collect(jnp.sum(scores_grad, 0, dtype=jnp.float32))
    normed_part = jnp.einsum(
        "baz,nz->ban", query_gradient, layer_weights[W_QUERY], preferred_element_type=jnp.float32
    )
    normed_part = normed_part + jnp.einsum(
        "baz,nz->ban", key_gradient, layer_weights[W_KEY], preferred_element_type=jnp.float32
    )
    normed_part = normed_part + jnp.einsum(
        "baz,nz->ban", value_gradient, layer_weights[W_VALUE], preferred_element_type=jnp.float32
    )
    normed_grad = collect_grads(normed_part)
    values_grad, gain_grad, bias_grad = norm_backward(
        normed_grad, scaled, inv_spread, layer_weights[ATT_GAIN].astype(jnp.float32)
    )
    grads = {
        W_OUT: output_gradient,
        B_OUT: jnp.sum(branch_gradient, (0, 1), dtype=jnp.float32),
        W_QUERY: jnp.einsum(
            "exa,exn->an", gathered_params, query_gradient, preferred_element_type=jnp.float32
        ),
        W_KEY: jnp.einsum(
            "exa,exn->an", gathered_params, key_gradient, preferred_element_type=jnp.float32
        ),
        W_VALUE: jnp.einsum(
            "exa,exn->an", gathered_params, value_gradient, preferred_element_type=jnp.float32
        ),
        B_QUERY: jnp.sum(query_gradient, (0, 1), dtype=jnp.float32),
        B_VALUE: jnp.sum(value_gradient, (0, 1), dtype=jnp.float32),
        REL_TABLE: table_grad,
        ATT_GAIN: gain_grad,
        ATT_BIAS: bias_grad,
    }
    return (grad_out + values_grad, grads)


def conv_forward(values, layer_weights, own_valid):
    model_dim = values.shape[-1]
    normed, scaled, inv_spread = norm_forward(
        values,
        layer_weights[CNV_GAIN].astype(jnp.float32),
        layer_weights[CNV_BIAS].astype(jnp.float32),
    )
    normed_lower_half = normed.astype(jnp.bfloat16)
    lifted = jnp.einsum(
        "zkh,hp->zkp",
        normed_lower_half,
        layer_weights[POINT_ONE],
        preferred_element_type=jnp.float32,
    )
    lifted = lifted + layer_weights[POINTB_ONE].astype(jnp.float32)
    valid_mask = own_valid[..., None]
    linear_half = lifted[..., :model_dim]
    sigmoid_gate = jax.nn.sigmoid(lifted[..., model_dim:])
    glu_out = linear_half * sigmoid_gate * valid_mask
    kernel = layer_weights[DEPTH_KERNEL].astype(jnp.float32)
    conv_out = depthwise(glu_out, kernel) + layer_weights[DEPTH_BIAS].astype(jnp.float32)
    here = jnp.sum(own_valid)
    mean_here = jnp.sum(conv_out * valid_mask, (0, 1)) / here
    masked_centre = (conv_out - mean_here) * valid_mask
    sums = jnp.zeros((8, 256), jnp.float32)
    sums = sums.at[0, :model_dim].set(mean_here)
    sums = sums.at[1, :model_dim].set(jnp.sum(masked_centre * masked_centre, (0, 1)))
    sums = sums.at[2].set(here)
    everyone = share_all(sums, lax.axis_size("dp"), 2)
    counts = everyone[:, 2, :1]
    means = everyone[:, 0, :model_dim]
    valid_count = jnp.sum(counts)
    mean_all = jnp.sum(means * counts, 0) / valid_count
    spread = jnp.sum(everyone[:, 1, :model_dim] + counts * (means - mean_all) ** 2, 0) / valid_count
    centre = conv_out - mean_all
    inv_batch = lax.rsqrt(spread + NORM_EPS)
    normal = centre * inv_batch
    shifted = normal * layer_weights[BATCH_GAIN].astype(jnp.float32) + layer_weights[
        BATCH_BIAS
    ].astype(jnp.float32)
    active_values = (shifted * jax.nn.sigmoid(shifted)).astype(jnp.bfloat16)
    branch = jnp.einsum(
        "zkh,hp->zkp", active_values, layer_weights[POINT_TWO], preferred_element_type=jnp.float32
    )
    branch = branch + layer_weights[POINTB_TWO].astype(jnp.float32)
    stored = (
        scaled,
        inv_spread,
        normed_lower_half,
        linear_half,
        sigmoid_gate,
        glu_out,
        normal,
        shifted,
        active_values,
        inv_batch,
        valid_count,
        valid_mask,
    )
    return (values + branch, stored)


def conv_backward(grad_out, stored, layer_weights):
    (
        scaled,
        inv_spread,
        normed_lower_half,
        linear_half,
        sigmoid_gate,
        glu_out,
        normal,
        shifted,
        active_values,
        inv_batch,
        valid_count,
        valid_mask,
    ) = stored
    length = glu_out.shape[1]
    kernel = layer_weights[DEPTH_KERNEL].astype(jnp.float32)
    tap_count = kernel.shape[0]
    half_width = tap_count // 2
    branch_gradient = grad_out.astype(jnp.bfloat16)
    second_ffn_gradient = jnp.einsum(
        "qkj,qkc->jc", active_values, branch_gradient, preferred_element_type=jnp.float32
    )
    active_grad = jnp.einsum(
        "bmk,gk->bmg",
        branch_gradient,
        layer_weights[POINT_TWO],
        preferred_element_type=jnp.float32,
    )
    sigmoid_bn = jax.nn.sigmoid(shifted)
    shifted_grad = active_grad * sigmoid_bn * (1.0 + shifted * (1.0 - sigmoid_bn))
    scaled_grad = shifted_grad * layer_weights[BATCH_GAIN].astype(jnp.float32)
    model_dim = scaled_grad.shape[-1]
    sums = jnp.zeros((8, 256), jnp.float32)
    sums = sums.at[0, :model_dim].set(jnp.sum(scaled_grad, (0, 1)))
    sums = sums.at[1, :model_dim].set(jnp.sum(scaled_grad * normal, (0, 1)))
    everyone = jnp.sum(share_all(sums, lax.axis_size("dp"), 3), 0)
    sum_plain, sum_cross = everyone[0, :model_dim], everyone[1, :model_dim]
    conv_grad = inv_batch * (
        scaled_grad - valid_mask * (sum_plain + normal * sum_cross) / valid_count
    )
    padded_glu = jnp.pad(glu_out, ((0, 0), (half_width, half_width), (0, 0)))
    padded_grad = jnp.pad(conv_grad, ((0, 0), (half_width, half_width), (0, 0)))
    kernel_rows = []
    glu_grad = jnp.zeros_like(glu_out)
    for tap_index in range(tap_count):
        kernel_rows.append(
            jnp.sum(conv_grad * padded_glu[:, tap_index : tap_index + length], (0, 1))
        )
        start_at = tap_count - 1 - tap_index
        glu_grad = glu_grad + padded_grad[:, start_at : start_at + length] * kernel[tap_index]
    glu_grad = glu_grad * valid_mask
    linear_grad = glu_grad * sigmoid_gate
    gate_grad = glu_grad * linear_half * sigmoid_gate * (1.0 - sigmoid_gate)
    lifted_gradient = jnp.concatenate([linear_grad, gate_grad], -1).astype(jnp.bfloat16)
    one_grad = jnp.einsum(
        "qkj,qkc->jc", normed_lower_half, lifted_gradient, preferred_element_type=jnp.float32
    )
    normed_grad = jnp.einsum(
        "bmk,gk->bmg",
        lifted_gradient,
        layer_weights[POINT_ONE],
        preferred_element_type=jnp.float32,
    )
    values_grad, gain_grad, bias_grad = norm_backward(
        normed_grad, scaled, inv_spread, layer_weights[CNV_GAIN].astype(jnp.float32)
    )
    grads = {
        POINT_TWO: second_ffn_gradient,
        POINTB_TWO: jnp.sum(branch_gradient, (0, 1), dtype=jnp.float32),
        BATCH_GAIN: jnp.sum(shifted_grad * normal, (0, 1)),
        BATCH_BIAS: jnp.sum(shifted_grad, (0, 1)),
        DEPTH_KERNEL: jnp.stack(kernel_rows),
        DEPTH_BIAS: jnp.sum(conv_grad, (0, 1)),
        POINT_ONE: one_grad,
        POINTB_ONE: jnp.sum(lifted_gradient, (0, 1), dtype=jnp.float32),
        CNV_GAIN: gain_grad,
        CNV_BIAS: bias_grad,
    }
    return (grad_out + values_grad, grads)


def adam_update(master, gradient, moment_one, moment_two):
    first_new = BETA_ONE * moment_one + (1.0 - BETA_ONE) * gradient
    second_new = BETA_TWO * moment_two + (1.0 - BETA_TWO) * gradient * gradient
    first_hat = first_new / (1.0 - BETA_ONE**STEP)
    second_hat = second_new / (1.0 - BETA_TWO**STEP)
    updated = master - LEARN_RATE * (
        first_hat / (jnp.sqrt(second_hat) + ADAM_EPS) + WEIGHT_DECAY * master
    )
    return (first_new, second_new, updated)


def per_device(
    frames,
    cotangent,
    lengths,
    head_params,
    shared_params,
    head_first,
    head_second,
    shared_first,
    shared_second,
):
    model_dim = frames.shape[-1]
    seq_here = frames.shape[0]
    length = frames.shape[1]
    head_count = lax.axis_size("head")
    dp_count = lax.axis_size("dp")
    head_index = lax.axis_index("head")
    head_size = head_params.shape[1]
    shared_size = shared_params.shape[0]
    head_rows = up_to(up_to(head_size, LANES) // LANES, 16)
    shared_rows = up_to(up_to(shared_size, LANES) // LANES, 16)
    mine = jnp.concatenate(
        [
            jnp.pad(head_params[0], (0, head_rows * LANES - head_size)).reshape(head_rows, LANES),
            jnp.pad(shared_params, (0, shared_rows * LANES - shared_size)).reshape(shared_rows, LANES),
        ]
    ).astype(jnp.bfloat16)
    gathered = gather_all(mine, dp_count, 1)
    head_row = gathered[:, :, :head_rows].reshape(dp_count, 2, -1)[:, :, :head_size]
    head_row = head_row.transpose(1, 0, 2).reshape(2, -1)
    shared_all = gathered[:, :, head_rows:].reshape(dp_count * 2, -1)[:, :shared_size].reshape(-1)
    layout = head_layout(model_dim, FF // head_count, HEADS // head_count, HD, KREL)
    own_lengths = lax.dynamic_slice_in_dim(lengths, head_index * seq_here, seq_here)
    pieces = [unflatten(head_row[row_index], layout) for row_index in range(head_row.shape[0])]
    layer_weights = {
        entry_name: jnp.concatenate(
            [piece_dict[entry_name] for piece_dict in pieces], JOIN_AXIS[entry_name]
        )
        for entry_name, dims_of in layout
    }
    layer_weights.update(unflatten(shared_all, shared_layout(model_dim, KW)))
    positions = jnp.arange(length, dtype=jnp.int32)
    own_valid = (positions[None, :] < own_lengths[:, None]).astype(jnp.float32)
    key_valid = positions[None, :] < own_lengths[:, None]
    values = frames.astype(jnp.float32)
    values, stored_one = ffn_forward(values, layer_weights, FFN_ONE)
    values, stored_att = attention_forward(values, layer_weights, key_valid)
    values, stored_cnv = conv_forward(values, layer_weights, own_valid)
    values, stored_two = ffn_forward(values, layer_weights, FFN_TWO)
    final, out_scaled, out_inv = norm_forward(
        values,
        layer_weights[OUT_GAIN].astype(jnp.float32),
        layer_weights[OUT_BIAS].astype(jnp.float32),
    )
    gradient, gain_grad, bias_grad = norm_backward(
        cotangent.astype(jnp.float32),
        out_scaled,
        out_inv,
        layer_weights[OUT_GAIN].astype(jnp.float32),
    )
    grads = {OUT_GAIN: gain_grad, OUT_BIAS: bias_grad}
    gradient, more_grads = ffn_backward(gradient, stored_two, layer_weights, FFN_TWO)
    grads.update(more_grads)
    gradient, more_grads = conv_backward(gradient, stored_cnv, layer_weights)
    grads.update(more_grads)
    gradient, more_grads = attention_backward(gradient, stored_att, layer_weights, key_valid)
    grads.update(more_grads)
    gradient, more_grads = ffn_backward(gradient, stored_one, layer_weights, FFN_ONE)
    grads.update(more_grads)
    row_width = head_size * dp_count
    halves = [
        {name: jnp.split(grads[name], 2, JOIN_AXIS[name])[row] for name, _ in layout} for row in (0, 1)
    ]
    head_flat = jnp.stack([flatten_dict(half, layout, row_width) for half in halves])
    head_flat = jnp.pad(
        head_flat.reshape(2, dp_count, head_size), ((0, 0), (0, 0), (0, head_rows * LANES - head_size))
    ).reshape(2, dp_count, head_rows, LANES)
    shared_flat = flatten_dict(
        grads, shared_layout(model_dim, KW), shared_size * dp_count * head_count
    ).reshape(dp_count, 2, shared_size).transpose(1, 0, 2)
    shared_flat = jnp.pad(
        shared_flat, ((0, 0), (0, 0), (0, shared_rows * LANES - shared_size))
    ).reshape(2, dp_count, shared_rows, LANES)
    summed = scatter_all(jnp.concatenate([head_flat, shared_flat], 2).astype(jnp.bfloat16), 4)
    head_grad = summed[:head_rows].reshape(1, -1)[:, :head_size]
    shared_grad = summed[head_rows:].reshape(-1)[:shared_size]
    head_one, head_two, head_next = adam_update(head_params, head_grad, head_first, head_second)
    shared_one, shared_two, shared_next = adam_update(
        shared_params, shared_grad, shared_first, shared_second
    )
    return (
        final.astype(jnp.bfloat16),
        gradient,
        head_one,
        head_two,
        head_next,
        head_next.astype(jnp.bfloat16),
        shared_one,
        shared_two,
        shared_next,
        shared_next.astype(jnp.bfloat16),
    )


def solution(mesh):
    return jax.shard_map(
        per_device,
        mesh=mesh,
        in_specs=(
            P(("dp", "head"), None, None),
            P(("dp", "head"), None, None),
            P("dp"),
            P("head", "dp"),
            P(("dp", "head")),
            P("head", "dp"),
            P("head", "dp"),
            P(("dp", "head")),
            P(("dp", "head")),
        ),
        out_specs=(
            P(("dp", "head"), None, None),
            P(("dp", "head"), None, None),
            P("head", "dp"),
            P("head", "dp"),
            P("head", "dp"),
            P("head", "dp"),
            P(("dp", "head")),
            P(("dp", "head")),
            P(("dp", "head")),
            P(("dp", "head")),
        ),
        check_vma=False,
    )
```

```python
import functools
import math

import jax
import jax.numpy as jnp
from jax import lax
from jax.experimental import pallas as pl
from jax.experimental.pallas import tpu as pltpu
from jax.sharding import PartitionSpec as P

BF = jnp.bfloat16
F32 = jnp.float32
LANES = 128


def up_to(count, unit):
    return -(-count // unit) * unit


def grid_place(nz):
    me = lax.axis_index("dp")
    core = lax.axis_index("head")
    zc = me // 4
    rest = me - 4 * zc
    yc = rest // 2
    xc = rest - 2 * yc
    return me, core, zc, yc, xc


def remote(src, dst, send, recv, dp, head):
    return pltpu.make_async_remote_copy(
        src_ref=src,
        dst_ref=dst,
        send_sem=send,
        recv_sem=recv,
        device_id={"dp": dp, "head": head},
        device_id_type=pl.DeviceIdType.MESH,
    )


def greet(nz, me, core, zc, yc, xc):
    barrier = pltpu.get_barrier_semaphore()

    def hello(dp, head):
        pl.semaphore_signal(
            barrier, inc=1, device_id={"dp": dp, "head": head}, device_id_type=pl.DeviceIdType.MESH
        )

    for k in range(1, nz):
        hello(lax.rem(zc + k, nz) * 4 + 2 * yc + xc, core)
    hello(4 * zc + 2 * (1 - yc) + xc, core)
    hello(4 * zc + 2 * yc + 1 - xc, core)
    hello(me, 1 - core)
    pl.semaphore_wait(barrier, nz + 2)


def gather_kernel(nz, src, out, sz, rz, s1, r1, s2, r2, sc, rc):
    rows = src.shape[0]
    row_a = up_to(rows // 2, 16)
    parts = (pl.ds(0, row_a), pl.ds(row_a, rows - row_a))
    me, core, zc, yc, xc = grid_place(nz)
    greet(nz, me, core, zc, yc, xc)
    out[me, core] = src[...]
    y_peer = 4 * zc + 2 * (1 - yc) + xc
    x_peer = 4 * zc + 2 * yc + 1 - xc
    firsts = (y_peer, x_peer)
    seconds = (x_peer, y_peer)
    pending = []

    def send(slot, p, send_sem, recv_sem, dp, head):
        block = out.at[slot, core, parts[p]]
        copy = remote(block, block, send_sem, recv_sem, dp, head)
        copy.start()
        pending.append(copy)

    def arrived(slot, which, p, send_sem, recv_sem):
        block = out.at[slot, which, parts[p]]
        remote(block, block, send_sem, recv_sem, me, 1 - core).wait_recv()

    zs = [lax.rem(zc + k, nz) for k in range(nz)]
    here = 2 * yc + xc
    first_here = (2 * (1 - yc) + xc, 2 * yc + 1 - xc)
    second_here = ((2 * yc + 1 - xc, 2 * (1 - yc) + 1 - xc), (2 * (1 - yc) + xc, 2 * (1 - yc) + 1 - xc))
    for k in range(1, nz):
        for p in (0, 1):
            send(me, p, sz.at[p, k], rz.at[p, zc], zs[k] * 4 + here, core)
    for k in range(nz):
        z = zs[k]
        slot = 4 * z + here
        for p in (0, 1):
            if k:
                arrived(slot, core, p, sz.at[p, k], rz.at[p, z])
            send(slot, p, s1.at[p, k], r1.at[p, z], firsts[p], core)
            send(slot, p, s2.at[p, k, 0], r2.at[p, z, 0], seconds[p], core)
            send(slot, p, sc.at[p, k, 0], rc.at[p, z, 0], me, 1 - core)
    for k in range(nz):
        z = zs[k]
        for p in (0, 1):
            slot = 4 * z + first_here[p]
            arrived(slot, core, p, s1.at[p, k], r1.at[p, z])
            send(slot, p, s2.at[p, k, 1], r2.at[p, z, 1], seconds[p], core)
            send(slot, p, sc.at[p, k, 1], rc.at[p, z, 1], me, 1 - core)
    for k in range(nz):
        z = zs[k]
        for p in (0, 1):
            for b in (0, 1):
                slot = 4 * z + second_here[p][b]
                arrived(slot, core, p, s2.at[p, k, b], r2.at[p, z, b])
                send(slot, p, sc.at[p, k, 2 + b], rc.at[p, z, 2 + b], me, 1 - core)
    for k in range(nz):
        z = zs[k]
        for p in (0, 1):
            for b, at in enumerate((here, first_here[p]) + second_here[p]):
                arrived(4 * z + at, 1 - core, p, sc.at[p, k, b], rc.at[p, z, b])
    for copy in pending:
        copy.wait_send()


def gather_all(block, dp, collective_id):
    rows = block.shape[0]
    nz = dp // 4
    dma = pltpu.SemaphoreType.DMA
    return pl.pallas_call(
        functools.partial(gather_kernel, nz),
        out_shape=jax.ShapeDtypeStruct((dp, 2, rows, LANES), block.dtype),
        in_specs=[pl.BlockSpec(memory_space=pltpu.VMEM)],
        out_specs=pl.BlockSpec(memory_space=pltpu.VMEM),
        scratch_shapes=[dma((2, nz)), dma((2, nz)), dma((2, nz)), dma((2, nz)), dma((2, nz, 2)), dma((2, nz, 2)), dma((2, nz, 4)), dma((2, nz, 4))],
        compiler_params=pltpu.CompilerParams(
            collective_id=collective_id, has_side_effects=True, vmem_limit_bytes=40 << 20
        ),
        name="gather_weights",
    )(block)


def scatter_kernel(nz, g, out, c1, t1, rx1, t2, rx2, t3, rx3, sc, rc, s1, r1, s2, r2, s3, r3):
    rows = g.shape[2]
    row_a = up_to(rows // 2, 16)
    starts = (0, row_a)
    sizes = (row_a, rows - row_a)
    parts = tuple(pl.ds(a, n) for a, n in zip(starts, sizes))
    me, core, zc, yc, xc = grid_place(nz)
    greet(nz, me, core, zc, yc, xc)
    y_peer = 4 * zc + 2 * (1 - yc) + xc
    x_peer = 4 * zc + 2 * yc + 1 - xc
    firsts = (x_peer, y_peer)
    seconds = (y_peer, x_peer)
    pending = []

    def send(src, dst, send_sem, recv_sem, dp, head):
        copy = remote(src, dst, send_sem, recv_sem, dp, head)
        copy.start()
        pending.append(copy)

    def arrived(block, send_sem, recv_sem):
        remote(block, block, send_sem, recv_sem, me, 1 - core).wait_recv()

    order = list(range(1, nz)) + [0]
    zs = [lax.rem(zc + k, nz) for k in range(nz)]
    give = ((1 - xc, 2 + 1 - xc), (2 * (1 - yc), 2 * (1 - yc) + 1))
    second_give = (1 - yc, 1 - xc)
    second_keep = (yc, xc)

    def place(p, b):
        return 2 * b + xc if p == 0 else 2 * yc + b

    for k in order:
        z = zs[k]
        send(g.at[1 - core, pl.ds(4 * z, 4)], c1.at[pl.ds(4 * z, 4)], sc.at[k], rc.at[z], me, 1 - core)
    for k in order:
        z = zs[k]
        arrived(c1.at[pl.ds(4 * z, 4)], sc.at[k], rc.at[z])
        for p in (0, 1):
            n = pl.ds(0, sizes[p])
            for b in (0, 1):
                slot = 4 * z + give[p][b]
                t1[p, z, b, n] = (g[core, slot, parts[p]].astype(F32) + c1[slot, parts[p]].astype(F32)).astype(BF)
            send(t1.at[p, z, :, n], rx1.at[p, z, :, n], s1.at[p, k], r1.at[p, z], firsts[p], core)

    def partial(p, z, b):
        slot = 4 * z + place(p, b)
        n = pl.ds(0, sizes[p])
        return g[core, slot, parts[p]].astype(F32) + c1[slot, parts[p]].astype(F32) + rx1[p, z, b, n].astype(F32)

    for k in order:
        z = zs[k]
        for p in (0, 1):
            n = pl.ds(0, sizes[p])
            arrived(rx1.at[p, z, :, n], s1.at[p, k], r1.at[p, z])
            t2[p, z, n] = partial(p, z, second_give[p]).astype(BF)
            send(t2.at[p, z, n], rx2.at[p, z, n], s2.at[p, k], r2.at[p, z], seconds[p], core)
    for k in order:
        z = zs[k]
        for p in (0, 1):
            n = pl.ds(0, sizes[p])
            arrived(rx2.at[p, z, n], s2.at[p, k], r2.at[p, z])
            total = partial(p, z, second_keep[p]) + rx2[p, z, n].astype(F32)
            if k:
                t3[p, z, n] = total.astype(BF)
                send(t3.at[p, z, n], rx3.at[p, zc, n], s3.at[p, k], r3.at[p, zc], 4 * z + 2 * yc + xc, core)
            else:
                out[parts[p], :] = total
    for k in order[:-1]:
        z = zs[k]
        for p in (0, 1):
            n = pl.ds(0, sizes[p])
            arrived(rx3.at[p, z, n], s3.at[p, k], r3.at[p, z])
            out[parts[p], :] += rx3[p, z, n].astype(F32)
    for copy in pending:
        copy.wait_send()


def scatter_all(g, collective_id):
    dp, rows = g.shape[1], g.shape[2]
    nz = dp // 4
    half = up_to(rows // 2, 16)
    dma = pltpu.SemaphoreType.DMA
    vm = pltpu.VMEM
    return pl.pallas_call(
        functools.partial(scatter_kernel, nz),
        out_shape=jax.ShapeDtypeStruct((rows, LANES), F32),
        in_specs=[pl.BlockSpec(memory_space=pltpu.VMEM)],
        out_specs=pl.BlockSpec(memory_space=pltpu.VMEM),
        scratch_shapes=[
            vm((dp, rows, LANES), BF),
            vm((2, nz, 2, half, LANES), BF),
            vm((2, nz, 2, half, LANES), BF),
            vm((2, nz, half, LANES), BF),
            vm((2, nz, half, LANES), BF),
            vm((2, nz, half, LANES), BF),
            vm((2, nz, half, LANES), BF),
            dma((nz,)), dma((nz,)), dma((2, nz)), dma((2, nz)), dma((2, nz)), dma((2, nz)), dma((2, nz)), dma((2, nz)),
        ],
        compiler_params=pltpu.CompilerParams(
            collective_id=collective_id, has_side_effects=True, vmem_limit_bytes=40 << 20
        ),
        name="scatter_grads",
    )(g)


def share_kernel(dp_count, src, out, ss, rs):
    me = lax.axis_index("dp")
    core = lax.axis_index("head")
    own = 2 * me + core
    total = 2 * dp_count
    barrier = pltpu.get_barrier_semaphore()

    def peer(k):
        other = lax.rem(own + k, total)
        dp = other // 2
        return other, dp, other - 2 * dp

    @pl.loop(1, total)
    def _(k):
        _, dp, head = peer(k)
        pl.semaphore_signal(
            barrier, inc=1, device_id={"dp": dp, "head": head}, device_id_type=pl.DeviceIdType.MESH
        )

    pl.semaphore_wait(barrier, total - 1)
    out[own] = src[...]

    @pl.loop(1, total)
    def _(k):
        _, dp, head = peer(k)
        remote(src, out.at[own], ss.at[k], rs.at[own], dp, head).start()

    @pl.loop(1, total)
    def _(k):
        other, dp, head = peer(k)
        remote(src, out.at[other], ss.at[k], rs.at[other], dp, head).wait()


def share_all(block, dp, collective_id):
    dma = pltpu.SemaphoreType.DMA
    return pl.pallas_call(
        functools.partial(share_kernel, dp),
        out_shape=jax.ShapeDtypeStruct((2 * dp,) + block.shape, block.dtype),
        in_specs=[pl.BlockSpec(memory_space=pltpu.VMEM)],
        out_specs=pl.BlockSpec(memory_space=pltpu.VMEM),
        scratch_shapes=[dma((2 * dp,)), dma((2 * dp,))],
        compiler_params=pltpu.CompilerParams(collective_id=collective_id, has_side_effects=True),
        name="share_sums",
    )(block)


HEADS = 4
HD = 60
FF = 960
KW = 15
STEP = 10
KREL = 383
NORM_EPS = 1e-05
BETA_ONE = 0.9
BETA_TWO = 0.999
LEARN_RATE = 0.1
WEIGHT_DECAY = 0.01
ADAM_EPS = 1e-08
LOG2E = 1.4426950408889634
LN2 = 0.6931471805599453
SCALE = HD ** (-0.5)
UNIT = 1.28125
D = 240
DP = 256
HF = 480
HFP = 512
FFP = 1024
HC = 120
MASK_LANE = 120
NEG = -1e30
FFA, ATT, CNV, FFB, OUT = 0, 2, 4, 6, 8
DOWNB_ONE, DOWNB_TWO, B_OUT, BATCH_GAIN, BATCH_BIAS, TAPS, DEPTH_BIAS = 10, 11, 12, 13, 14, 16, 31
VEC_ROWS = 32
BIG = 60 << 20


def head_places():
    out, at = {}, 0
    for name, size in (
        ("up1", D * HF), ("upb1", HF), ("dn1", HF * D), ("up2", D * HF), ("upb2", HF), ("dn2", HF * D),
        ("wq", D * HC), ("wk", D * HC), ("wv", D * HC), ("bq", HC), ("bv", HC),
        ("rel", 2 * KREL), ("wo", HC * D),
    ):
        out[name] = at
        at += size
    return out, at


def shared_places():
    out, at = {}, 0
    for name, size in (
        ("vec", 13 * D), ("p1", 2 * D * D), ("pb1", 2 * D), ("taps", KW * D), ("db", D),
        ("bg", D), ("bb", D), ("p2", D * D), ("pb2", D),
    ):
        out[name] = at
        at += size
    return out, at


def lane_iota(shape):
    return lax.broadcasted_iota(jnp.int32, shape, len(shape) - 1)


def slot_rows(size):
    return up_to(-(-(size + LANES - 1) // LANES), 16)


def dot(a, b):
    return jnp.dot(a, b, preferred_element_type=F32)


def dot_t(a, b):
    return lax.dot_general(a, b, (((1,), (1,)), ((), ())), preferred_element_type=F32)


def t_dot(a, b):
    return lax.dot_general(a, b, (((0,), (0,)), ((), ())), preferred_element_type=F32)


def vmem_call(body, outs, ins, scratch=(), name=None, limit=BIG):
    return pl.pallas_call(
        body,
        out_shape=outs,
        in_specs=[pl.BlockSpec(memory_space=pltpu.VMEM) for _ in ins],
        out_specs=jax.tree.map(lambda _: pl.BlockSpec(memory_space=pltpu.VMEM), outs),
        scratch_shapes=list(scratch),
        compiler_params=pltpu.CompilerParams(vmem_limit_bytes=limit),
        name=name,
    )(*ins)


def own_offsets(head_size, shared_size):
    me = lax.axis_index("dp")
    core = lax.axis_index("head")
    return lax.rem(me * head_size, LANES), lax.rem((2 * me + core) * shared_size, LANES)


def push_lanes(x, shift):
    rolled = pltpu.roll(x, shift, 1)
    before = jnp.concatenate([jnp.zeros((1, LANES), F32), rolled[:-1]], 0)
    return jnp.where(lane_iota(x.shape) >= shift, rolled, before)


def pull_lanes(x, shift):
    rolled = pltpu.roll(x, lax.rem(LANES - shift, LANES), 1)
    after = jnp.concatenate([rolled[1:], jnp.zeros((1, LANES), F32)], 0)
    return jnp.where(lane_iota(x.shape) < LANES - shift, rolled, after)


def align_kernel(head_ref, shared_ref, out):
    head_size, shared_size = head_ref.shape[1], shared_ref.shape[0]
    hr, sr = slot_rows(head_size), slot_rows(shared_size)
    ho, so = own_offsets(head_size, shared_size)
    x = jnp.concatenate([head_ref[...], jnp.zeros((1, hr * LANES - head_size), F32)], 1)
    out[pl.ds(0, hr), :] = push_lanes(x.reshape(hr, LANES), ho).astype(BF)
    x = shared_ref[...].reshape(1, shared_size)
    x = jnp.concatenate([x, jnp.zeros((1, sr * LANES - shared_size), F32)], 1)
    out[pl.ds(hr, sr), :] = push_lanes(x.reshape(sr, LANES), so).astype(BF)


def adam_kernel(g_ref, hp, hf, hs, sp, sf, ss, hf_o, hs_o, hp_o, hc_o, sf_o, ss_o, sp_o, sc_o):
    head_size, shared_size = hp.shape[1], sp.shape[0]
    hr, sr = slot_rows(head_size), slot_rows(shared_size)
    ho, so = own_offsets(head_size, shared_size)

    def update(master, g, first, second):
        first_new = BETA_ONE * first + (1.0 - BETA_ONE) * g
        second_new = BETA_TWO * second + (1.0 - BETA_TWO) * g * g
        first_hat = first_new * (1.0 / (1.0 - BETA_ONE**STEP))
        second_hat = second_new * (1.0 / (1.0 - BETA_TWO**STEP))
        new = master - LEARN_RATE * (first_hat / (jnp.sqrt(second_hat) + ADAM_EPS) + WEIGHT_DECAY * master)
        return first_new, second_new, new

    g = pull_lanes(g_ref[pl.ds(0, hr), :], ho).reshape(1, hr * LANES)[:, :head_size]
    one, two, new = update(hp[...], g, hf[...], hs[...])
    hf_o[...] = one
    hs_o[...] = two
    hp_o[...] = new
    hc_o[...] = new.astype(BF)
    g = pull_lanes(g_ref[pl.ds(hr, sr), :], so).reshape(sr * LANES)[:shared_size]
    one, two, new = update(sp[...], g, sf[...], ss[...])
    sf_o[...] = one
    ss_o[...] = two
    sp_o[...] = new
    sc_o[...] = new.astype(BF)


def row_phases(rows, pitch):
    if rows == 1:
        return 1, 1, 0
    period = LANES // math.gcd(pitch, LANES)
    return period, rows // period, period * pitch // LANES


def take(flat, at, rows, pitch, col, width, dst, row0, lane0):
    period, count, stride = row_phases(rows, pitch)
    lane = lane_iota((count, LANES))
    for j in range(period):
        start = at + j * pitch + col
        q, l = divmod(start, LANES)

        def load(t):
            if count == 1:
                return flat[pl.ds(q + t, 1), :]
            return flat[pl.ds(q + t, count, stride), :]

        pieces = [load(t) for t in range(-(-(l + width) // LANES))]
        if l:
            pieces = [pltpu.roll(x, LANES - l, 1) for x in pieces]
        for t in range(-(-width // LANES)):
            value = pieces[t]
            if l and t + 1 < len(pieces):
                value = jnp.where(lane < LANES - l, value, pieces[t + 1])
            left = width - t * LANES
            if left < LANES:
                value = jnp.where(lane < left, value, 0.0)
            rows_at = pl.ds(row0 + j, 1) if count == 1 else pl.ds(row0 + j, count, period)
            dst[lane0 // LANES + t, rows_at, :] = value


def give(flat, at, rows, pitch, col, width, src, row0, lane0):
    period, count, stride = row_phases(rows, pitch)
    lane = lane_iota((count, LANES))
    for j in range(period):
        start = at + j * pitch + col
        q, l = divmod(start, LANES)
        rows_at = pl.ds(row0 + j, 1) if count == 1 else pl.ds(row0 + j, count, period)
        pieces = [src[lane0 // LANES + t, rows_at, :] for t in range(-(-width // LANES))]
        if l:
            pieces = [pltpu.roll(x, l, 1) for x in pieces]
        total = -(-(l + width) // LANES)
        for t in range(total):
            here = pl.ds(q + t, 1) if count == 1 else pl.ds(q + t, count, stride)
            if not l:
                value = pieces[t]
            elif t == 0:
                value = pieces[0]
            elif t == len(pieces):
                value = pieces[t - 1]
            else:
                value = jnp.where(lane >= l, pieces[t], pieces[t - 1])
            lo = l if t == 0 else 0
            hi = min(LANES, l + width - t * LANES)
            if lo or hi < LANES:
                keep = (lane >= lo) & (lane < hi)
                value = jnp.where(keep, value, flat[here, :])
            flat[here, :] = value


def spill(tiles, rows, dst, factor=None):
    for t in range(dst.shape[1] // LANES):
        value = tiles[t, pl.ds(0, rows), :]
        if factor:
            value = factor * value
        dst[:, pl.ds(t * LANES, LANES)] = value.astype(dst.dtype)


def load_tiles(src, tiles):
    for t in range(src.shape[1] // LANES):
        tiles[t, pl.ds(0, src.shape[0]), :] = src[:, pl.ds(t * LANES, LANES)]


def flat_rows(total, size):
    return up_to(total // LANES + slot_rows(size) + 16, 16)


def weights_kernel(sizes, got, up1, dn1, up2, dn2, qkv, wo, p1, p2, vec, rel, fh, fs, wide, tall, tmp):
    dp, head_size, shared_size = sizes
    hr, sr = slot_rows(head_size), slot_rows(shared_size)
    hp, _ = head_places()
    sp, _ = shared_places()
    row8 = lax.broadcasted_iota(jnp.int32, (8, LANES), 0)

    def merge(flat, first_row, block):
        head = flat[pl.ds(first_row, 8), :]
        flat[pl.ds(first_row, 8), :] = block[:8] + jnp.where(row8 == 0, head, 0.0)
        flat[pl.ds(first_row + 8, block.shape[0] - 8), :] = block[8:]

    for g in range(2):
        fh[g, pl.ds(0, 8), :] = jnp.zeros((8, LANES), F32)
    fs[pl.ds(0, 8), :] = jnp.zeros((8, LANES), F32)

    @pl.loop(0, dp)
    def _(i):
        for g in range(2):
            merge(fh.at[g], (i * head_size) // LANES, got[i, g, pl.ds(0, hr), :].astype(F32))
        for g in range(2):
            merge(fs, ((2 * i + g) * shared_size) // LANES, got[i, g, pl.ds(hr, sr), :].astype(F32))

    lane = lane_iota((1, LANES))

    def clear(tiles, count, row, size):
        for t in range(count):
            tiles[t, pl.ds(row, size), :] = jnp.zeros((size, LANES), F32)

    def patch(tiles, tile, row, where, value):
        part = tiles[tile, pl.ds(row, 1), :]
        tiles[tile, pl.ds(row, 1), :] = jnp.where(where, value, part)

    for dst_ref, place, bplace in ((up1, "up1", "upb1"), (up2, "up2", "upb2")):
        clear(wide, 8, 240, 16)
        for g in range(2):
            take(fh.at[g], hp[place], D, HF, 0, HF, wide, 0, g * HFP)
            take(fh.at[g], hp[bplace], 1, HF, 0, HF, wide, 240, g * HFP)
        patch(wide, 3, 240, lane == HF - 3 * LANES, UNIT)
        spill(wide, DP, dst_ref)
    for dst_ref, place, brow in ((dn1, "dn1", DOWNB_ONE), (dn2, "dn2", DOWNB_TWO)):
        for g in range(2):
            clear(tall, 2, g * HFP + HF, 32)
            take(fh.at[g], hp[place], HF, D, 0, D, tall, g * HFP, 0)
        take(fs, sp["vec"] + brow * D, 1, D, 0, D, tall, HF, 0)
        spill(tall, FFP, dst_ref, 0.5)
    clear(wide, 6, 240, 16)
    for g in range(2):
        for which, (place, bplace) in enumerate((("wq", "bq"), ("wk", None), ("wv", "bv"))):
            lane0 = which * DP + g * LANES
            take(fh.at[g], hp[place], D, HC, 0, HC, wide, 0, lane0)
            if bplace:
                take(fh.at[g], hp[bplace], 1, HC, 0, HC, wide, 240, lane0)
    patch(wide, 0, 240, lane == MASK_LANE, 1.0)
    patch(wide, 4, 240, (lane >= MASK_LANE) & (lane < MASK_LANE + 3), 1.0)
    spill(wide, DP, qkv)
    clear(tall, 2, 0, DP)
    for g in range(2):
        take(fh.at[g], hp["wo"], HC, D, 0, D, tall, g * LANES, 0)
    take(fs, sp["vec"] + B_OUT * D, 1, D, 0, D, tall, MASK_LANE, 0)
    spill(tall, DP, wo)
    clear(wide, 4, 240, 16)
    for half in range(2):
        take(fs, sp["p1"], D, 2 * D, half * D, D, wide, 0, half * DP)
        take(fs, sp["pb1"] + half * D, 1, D, 0, D, wide, 240, half * DP)
    spill(wide, DP, p1)
    clear(tall, 2, 240, 16)
    take(fs, sp["p2"], D, D, 0, D, tall, 0, 0)
    take(fs, sp["pb2"], 1, D, 0, D, tall, 240, 0)
    spill(tall, DP, p2)
    take(fs, sp["vec"], 16, D, 0, D, tall, 0, 0)
    take(fs, sp["taps"], 16, D, 0, D, tall, TAPS, 0)
    take(fs, sp["bg"], 1, D, 0, D, tall, BATCH_GAIN, 0)
    take(fs, sp["bb"], 1, D, 0, D, tall, BATCH_BIAS, 0)
    for row, value in ((FFA + 1, 1.0), (ATT + 1, 1.0), (CNV + 1, 1.0), (FFB + 1, 1.0), (BATCH_BIAS, UNIT)):
        patch(tall, 1, row, lane == D - LANES, value)
    spill(tall, VEC_ROWS, vec)
    length = rel.shape[1]
    for n in range(HEADS):
        take(fh.at[n // 2], hp["rel"] + (n % 2) * KREL, 1, KREL, 0, KREL, tmp, 0, 0)
        row = jnp.concatenate([tmp[t, pl.ds(0, 1), :] for t in range(3)] + [jnp.zeros((1, LANES), F32)], 1)
        rows = jnp.broadcast_to(row, (length, 4 * LANES))
        rows = pltpu.roll(rows, 4 * LANES - (length - 1), 1, stride=1, stride_axis=0)
        rel[n] = rows[:, :length] * LOG2E


def make_weights(got, head_size, shared_size, length):
    dp = got.shape[0]

    def s(*shape, dtype=BF):
        return jax.ShapeDtypeStruct(shape, dtype)

    outs = (
        s(DP, FFP), s(FFP, DP), s(DP, FFP), s(FFP, DP), s(DP, 3 * DP), s(DP, DP), s(DP, 2 * DP), s(DP, DP),
        s(VEC_ROWS, DP, dtype=F32), s(HEADS, length, length, dtype=F32),
    )
    vm = pltpu.VMEM
    scratch = (
        vm((2, flat_rows(head_size * dp, head_size), LANES), F32),
        vm((flat_rows(shared_size * 2 * dp, shared_size), LANES), F32),
        vm((8, DP, LANES), F32),
        vm((2, FFP, LANES), F32),
        vm((4, 8, LANES), F32),
    )
    return vmem_call(
        functools.partial(weights_kernel, (dp, head_size, shared_size)), outs, (got,), scratch, "make_weights"
    )


def flatten_kernel(sizes, up1, dn1, up2, dn2, qkv, wo, p1, p2, vec, rel, out, fh, fs, wide, tall, tmp):
    dp, head_size, shared_size = sizes
    hr, sr = slot_rows(head_size), slot_rows(shared_size)
    hp, used_h = head_places()
    sp, used_s = shared_places()
    for g in range(2):
        first = used_h // LANES // 8 * 8
        fh[g, pl.ds(first, fh.shape[1] - first), :] = jnp.zeros((fh.shape[1] - first, LANES), F32)
    first = used_s // LANES // 8 * 8
    fs[pl.ds(first, fs.shape[0] - first), :] = jnp.zeros((fs.shape[0] - first, LANES), F32)
    for src, place, bplace in ((up1, "up1", "upb1"), (up2, "up2", "upb2")):
        load_tiles(src, wide)
        for g in range(2):
            give(fh.at[g], hp[place], D, HF, 0, HF, wide, 0, g * HFP)
            give(fh.at[g], hp[bplace], 1, HF, 0, HF, wide, 240, g * HFP)
    for src, place, brow in ((dn1, "dn1", DOWNB_ONE), (dn2, "dn2", DOWNB_TWO)):
        for t in range(2):
            tall[t] = 0.5 * src[pl.ds(t * LANES, LANES), :].T
        for g in range(2):
            give(fh.at[g], hp[place], HF, D, 0, D, tall, g * HFP, 0)
        give(fs, sp["vec"] + brow * D, 1, D, 0, D, tall, HF, 0)
    load_tiles(qkv, wide)
    load_tiles(wo, tall)
    for g in range(2):
        for which, (place, bplace) in enumerate((("wq", "bq"), ("wk", None), ("wv", "bv"))):
            lane0 = which * DP + g * LANES
            give(fh.at[g], hp[place], D, HC, 0, HC, wide, 0, lane0)
            if bplace:
                give(fh.at[g], hp[bplace], 1, HC, 0, HC, wide, 240, lane0)
        give(fh.at[g], hp["wo"], HC, D, 0, D, tall, g * LANES, 0)
    give(fs, sp["vec"] + B_OUT * D, 1, D, 0, D, tall, MASK_LANE, 0)
    load_tiles(p1, wide)
    load_tiles(p2, tall)
    for half in range(2):
        give(fs, sp["p1"], D, 2 * D, half * D, D, wide, 0, half * DP)
        give(fs, sp["pb1"] + half * D, 1, D, 0, D, wide, 240, half * DP)
    give(fs, sp["p2"], D, D, 0, D, tall, 0, 0)
    give(fs, sp["pb2"], 1, D, 0, D, tall, 240, 0)
    load_tiles(vec, tall)
    for row in range(10):
        give(fs, sp["vec"] + row * D, 1, D, 0, D, tall, row, 0)
    give(fs, sp["taps"], 16, D, 0, D, tall, TAPS, 0)
    give(fs, sp["bg"], 1, D, 0, D, tall, BATCH_GAIN, 0)
    give(fs, sp["bb"], 1, D, 0, D, tall, BATCH_BIAS, 0)
    length = rel.shape[0] // HEADS
    for n in range(HEADS):
        total = jnp.zeros((8, 4 * LANES), F32)
        for block in range(length // 8):
            rows = rel[pl.ds(n * length + 8 * block, 8), :]
            rows = jnp.concatenate([rows, jnp.zeros((8, 4 * LANES - length), F32)], 1)
            total = total + pltpu.roll(rows, length - 8 - 8 * block, 1)
        row = total[7:8]
        for i in range(7):
            row = row + pltpu.roll(total[i : i + 1], 7 - i, 1)
        for t in range(4):
            tmp[t, pl.ds(0, 1), :] = row[:, t * LANES : (t + 1) * LANES]
        give(fh.at[n // 2], hp["rel"] + (n % 2) * KREL, 1, KREL, 0, KREL, tmp, 0, 0)

    @pl.loop(0, dp)
    def _(i):
        for g in range(2):
            out[g, i, pl.ds(0, hr), :] = fh[g, pl.ds((i * head_size) // LANES, hr), :].astype(BF)
            out[g, i, pl.ds(hr, sr), :] = fs[pl.ds(((2 * i + g) * shared_size) // LANES, sr), :].astype(BF)


def flatten_grads(grads, dp, head_size, shared_size):
    rows = slot_rows(head_size) + slot_rows(shared_size)
    vm = pltpu.VMEM
    scratch = (
        vm((2, flat_rows(head_size * dp, head_size), LANES), F32),
        vm((flat_rows(shared_size * 2 * dp, shared_size), LANES), F32),
        vm((8, DP, LANES), F32),
        vm((2, FFP, LANES), F32),
        vm((4, 8, LANES), F32),
    )
    return vmem_call(
        functools.partial(flatten_kernel, (dp, head_size, shared_size)),
        jax.ShapeDtypeStruct((2, dp, rows, LANES), BF),
        grads,
        scratch,
        "flatten_grads",
    )


def lane_mask():
    return jnp.where(lane_iota((1, DP)) < D, 1.0, 0.0)


def sigmoid(x):
    return 0.5 * jnp.tanh(0.5 * x) + 0.5


def row_sum(x):
    return jnp.sum(x, -1, keepdims=True)


def norm(x, gain, bias):
    centre = (x - row_sum(x) * (1.0 / D)) * lane_mask()
    inv = lax.rsqrt(row_sum(centre * centre) * (1.0 / D) + NORM_EPS)
    scaled = centre * inv
    return scaled * gain + bias, scaled, inv


def keep_norm(scaled, inv):
    return jnp.where(lane_iota(scaled.shape) == DP - 1, inv, scaled)


def norm_grad(grad, kept, gain):
    dg = grad * gain
    inv = kept[:, DP - 1 :]
    first = row_sum(dg) * (1.0 / D)
    second = row_sum(dg * kept) * (1.0 / D)
    return inv * (dg - first - kept * second) * lane_mask()


def add_rows(ref, row, value):
    ref[pl.ds(row, 1), :] += jnp.sum(value, 0, keepdims=True)


def norm_param_grads(ref, row, grad, kept):
    add_rows(ref, row, grad * kept)
    add_rows(ref, row + 1, grad)


def silu_pair(u):
    s = sigmoid(u)
    h = u * s
    return h, s + h * (1.0 - s)


def widen(x):
    rows = x.shape[0]
    return jnp.concatenate([x.astype(F32), jnp.zeros((rows, DP - D), F32)], 1)


def head_masks():
    lane = lane_iota((1, DP))
    out = []
    for n in range(HEADS):
        first = (n // 2) * LANES + (n % 2) * HD
        out.append((lane >= first) & (lane < first + HD))
    return out


def valid_rows(lengths, at, length):
    return lax.broadcasted_iota(jnp.int32, (length, 1), 0) < lengths[at]


def phase_a_kernel(
    seqs, lengths, frames, up, dn, wqkv, wo, p1, vec, rel,
    kept1_o, a1_o, h_o, sp_o, kept2_o, a2_o, qkv_o, e_o, rl_o, m_o,
    x2_o, kept3_o, a3_o, f1_o, f2_o, gl_o, w_o, stats_o,
    pad,
):
    step = pl.program_id(0)
    length = frames.shape[1]
    tokens = seqs * length
    first_seq = lax.axis_index("head") * (seqs * pl.num_programs(0)) + step * seqs

    def v(row):
        return vec[pl.ds(row, 1), :]

    x0 = widen(frames[...].reshape(tokens, D))
    a, scaled, inv = norm(x0, v(FFA), v(FFA + 1))
    a = a.astype(BF)
    a1_o[...] = a
    kept1_o[...] = keep_norm(scaled, inv)
    h, slope = silu_pair(dot(a, up[...]))
    h = h.astype(BF)
    h_o[...] = h
    sp_o[...] = slope.astype(BF)
    x1 = x0 + dot(h, dn[...])
    a, scaled, inv = norm(x1, v(ATT), v(ATT + 1))
    a = a.astype(BF)
    a2_o[...] = a
    kept2_o[...] = keep_norm(scaled, inv)
    qkv = dot(a, wqkv[...])
    lane = lane_iota((1, DP))
    masks = head_masks()
    for b in range(seqs):
        rows = pl.ds(b * length, length)
        valid = valid_rows(lengths, first_seq + b, length)
        part = qkv[b * length : (b + 1) * length]
        q = (part[:, :DP] * (SCALE * LOG2E)).astype(BF)
        k = part[:, DP : 2 * DP]
        k = jnp.where(lane == MASK_LANE, jnp.where(valid, 0.0, NEG), k).astype(BF)
        vv = part[:, 2 * DP :].astype(BF)
        qkv_o[rows, pl.ds(0, DP)] = q
        qkv_o[rows, pl.ds(DP, DP)] = k
        qkv_o[rows, pl.ds(2 * DP, DP)] = vv
        zero = jnp.zeros_like(q)
        mixed = jnp.zeros((length, DP), F32)
        shares = jnp.zeros((length, DP), F32)
        for n in range(HEADS):
            qm = jnp.where(masks[n] | (lane == MASK_LANE), q, zero)
            s = dot_t(qm, k) + rel[n]
            e = jnp.exp2(s - jnp.max(s, -1, keepdims=True)).astype(BF)
            e_o[b, pl.ds(n * length, length), :] = e
            o = dot(e, vv)
            r = 1.0 / o[:, MASK_LANE : MASK_LANE + 1]
            here = masks[n] | (lane == MASK_LANE) if n == 0 else masks[n]
            shares = jnp.where(here, r, shares)
            mixed = jnp.where(here, o, mixed)
        rl_o[rows, :] = shares
        m_o[rows, :] = (mixed * shares).astype(BF)
    x2 = x1 + dot(m_o[...], wo[...])
    x2_o[...] = x2
    a, scaled, inv = norm(x2, v(CNV), v(CNV + 1))
    a = a.astype(BF)
    a3_o[...] = a
    kept3_o[...] = keep_norm(scaled, inv)
    e = dot(a, p1[...])
    half = KW // 2

    @pl.when(step == 0)
    def _():
        pad[...] = jnp.zeros(pad.shape, F32)
        stats_o[...] = jnp.zeros(stats_o.shape, F32)

    count = jnp.float32(0.0)
    total = jnp.zeros((1, DP), F32)
    for b in range(seqs):
        rows = pl.ds(b * length, length)
        valid = jnp.where(valid_rows(lengths, first_seq + b, length), 1.0, 0.0)
        linear = e[b * length : (b + 1) * length, :DP]
        gate = sigmoid(e[b * length : (b + 1) * length, DP:])
        f1 = gate * valid
        gl = linear * f1
        f1_o[rows, :] = f1.astype(BF)
        f2_o[rows, :] = (gl * (1.0 - gate)).astype(BF)
        gl_o[rows, :] = gl.astype(BF)
        for t in range(2):
            cols = pl.ds(t * LANES, LANES)
            pad[b, t, pl.ds(8, length), :] = gl[:, t * LANES : (t + 1) * LANES]
            acc = jnp.broadcast_to(vec[pl.ds(DEPTH_BIAS, 1), cols], (length, LANES))
            for r in range(KW):
                acc = acc + pad[b, t, pl.ds(8 - half + r, length), :] * vec[pl.ds(TAPS + r, 1), cols]
            w_o[rows, cols] = acc
        total = total + jnp.sum(w_o[rows, :] * valid, 0, keepdims=True)
        count = count + lengths[first_seq + b].astype(F32)
    mean = total / count
    square = jnp.zeros((1, DP), F32)
    for b in range(seqs):
        valid = jnp.where(valid_rows(lengths, first_seq + b, length), 1.0, 0.0)
        centre = (w_o[pl.ds(b * length, length), :] - mean) * valid
        square = square + jnp.sum(centre * centre, 0, keepdims=True)
    old = stats_o[pl.ds(4, 1), :]
    new = old + count
    for t in range(2):
        cols = slice(t * LANES, (t + 1) * LANES)
        before = stats_o[pl.ds(t, 1), :]
        delta = mean[:, cols] - before
        stats_o[pl.ds(t, 1), :] = before + delta * (count / new)
        stats_o[pl.ds(2 + t, 1), :] += square[:, cols] + delta * delta * (old * count / new)
    stats_o[pl.ds(4, 1), :] = new


def batch_stats(shared, keep):
    counts = shared[:, 4:5, :]
    total = jnp.sum(counts, 0)
    means, spreads = [], []
    for t in range(2):
        each = shared[:, t : t + 1, :]
        mean = jnp.sum(each * counts, 0) / total
        spread = (jnp.sum(shared[:, 2 + t : 3 + t, :], 0) + jnp.sum(counts * (each - mean) ** 2, 0)) / total
        means.append(mean)
        spreads.append(spread)
    keep[pl.ds(0, 1), :] = jnp.concatenate(means, 1)
    keep[pl.ds(1, 1), :] = lax.rsqrt(jnp.concatenate(spreads, 1) + NORM_EPS)
    keep[pl.ds(2, 1), :] = jnp.concatenate([total, total], 1)


def phase_b_kernel(
    seqs, shared, w, x2, cotangent, p2, up, dn, vec,
    out_o, dy_o, dx3_o, dup_o, ddn_o, dp2_o, vec_o, sums_o,
    keep,
):
    step = pl.program_id(0)
    length = cotangent.shape[1]
    tokens = seqs * length

    @pl.when(step == 0)
    def _():
        batch_stats(shared[...], keep)
        for ref in (dup_o, ddn_o, dp2_o, vec_o, sums_o):
            ref[...] = jnp.zeros(ref.shape, F32)

    def v(row):
        return vec[pl.ds(row, 1), :]

    z = (w[...] - keep[pl.ds(0, 1), :]) * keep[pl.ds(1, 1), :]
    hc, slope_c = silu_pair(z * v(BATCH_GAIN) + v(BATCH_BIAS))
    hc = hc.astype(BF)
    x3 = x2[...] + dot(hc, p2[...])
    a, scaled, inv = norm(x3, v(FFB), v(FFB + 1))
    a = a.astype(BF)
    kept = keep_norm(scaled, inv)
    h, slope = silu_pair(dot(a, up[...]))
    h = h.astype(BF)
    slope = slope.astype(BF)
    x4 = x3 + dot(h, dn[...])
    final, scaled, inv = norm(x4, v(OUT), v(OUT + 1))
    out_o[...] = final[:, :D].astype(BF).reshape(seqs, length, D)
    g = widen(cotangent[...].reshape(tokens, D))
    kept4 = keep_norm(scaled, inv)
    norm_param_grads(vec_o, OUT, g, kept4)
    dx4 = norm_grad(g, kept4, v(OUT))
    do = dx4.astype(BF)
    ddn_o[...] += t_dot(do, h)
    du = (dot_t(do, dn[...]) * slope.astype(F32)).astype(BF)
    dup_o[...] += t_dot(a, du)
    da = dot_t(du, up[...])
    norm_param_grads(vec_o, FFB, da, kept)
    dx3 = dx4 + norm_grad(da, kept, v(FFB))
    dx3_o[...] = dx3
    dc = dx3.astype(BF)
    dp2_o[...] += t_dot(hc, dc)
    dy = dot_t(dc, p2[...]) * slope_c
    dy_o[...] = dy
    first = jnp.sum(dy, 0, keepdims=True)
    second = jnp.sum(dy * z, 0, keepdims=True)
    vec_o[pl.ds(BATCH_BIAS, 1), :] += first
    vec_o[pl.ds(BATCH_GAIN, 1), :] += second
    for t in range(2):
        cols = slice(t * LANES, (t + 1) * LANES)
        sums_o[pl.ds(t, 1), :] += first[:, cols]
        sums_o[pl.ds(2 + t, 1), :] += second[:, cols]


def phase_c_kernel(
    seqs, lengths, shared, shared_b, w, dy, dx3, gl, f1, f2, a3, kept3, qkv, e_all, rl, m, a2, kept2, h, slope, a1, kept1,
    p1, wo, wqkv, dn, up, vec,
    dx0_o, dp1_o, dwo_o, dqkv_o, dup_o, ddn_o, vec_o, rel_o,
    keep, padw, padg, grads,
):
    step = pl.program_id(0)
    length = dx0_o.shape[1]
    tokens = seqs * length
    first_seq = lax.axis_index("head") * (seqs * pl.num_programs(0)) + step * seqs
    half = KW // 2

    def v(row):
        return vec[pl.ds(row, 1), :]

    @pl.when(step == 0)
    def _():
        batch_stats(shared[...], keep)
        sums = jnp.sum(shared_b[...], 0)
        keep[pl.ds(3, 1), :] = jnp.concatenate([sums[0:1], sums[1:2]], 1)
        keep[pl.ds(4, 1), :] = jnp.concatenate([sums[2:3], sums[3:4]], 1)
        for ref in (dp1_o, dwo_o, dqkv_o, dup_o, ddn_o, vec_o, rel_o, padw, padg):
            ref[...] = jnp.zeros(ref.shape, F32)

    gain = v(BATCH_GAIN)
    inv_batch = keep[pl.ds(1, 1), :]
    mean = keep[pl.ds(0, 1), :]
    plain = gain * keep[pl.ds(3, 1), :] / keep[pl.ds(2, 1), :]
    cross = gain * keep[pl.ds(4, 1), :] / keep[pl.ds(2, 1), :]
    for b in range(seqs):
        rows = pl.ds(b * length, length)
        valid = jnp.where(valid_rows(lengths, first_seq + b, length), 1.0, 0.0)
        z = (w[rows, :] - mean) * inv_batch
        dw = inv_batch * (dy[rows, :] * gain - valid * (plain + z * cross))
        add_rows(vec_o, DEPTH_BIAS, dw)
        for t in range(2):
            cols = pl.ds(t * LANES, LANES)
            here = dw[:, t * LANES : (t + 1) * LANES]
            padw[b, t, pl.ds(8, length), :] = here
            padg[b, t, pl.ds(8, length), :] = gl[rows, cols].astype(F32)
            acc = jnp.zeros((length, LANES), F32)
            for r in range(KW):
                acc = acc + padw[b, t, pl.ds(8 + half - r, length), :] * vec[pl.ds(TAPS + r, 1), cols]
                tap = here * padg[b, t, pl.ds(8 - half + r, length), :]
                vec_o[pl.ds(TAPS + r, 1), cols] += jnp.sum(tap, 0, keepdims=True)
            grads[rows, cols] = (acc * f1[rows, cols].astype(F32)).astype(BF)
            grads[rows, pl.ds(DP + t * LANES, LANES)] = (acc * f2[rows, cols].astype(F32)).astype(BF)
    de = grads[:, pl.ds(0, 2 * DP)]
    dp1_o[...] += t_dot(a3[...], de)
    da = dot_t(de, p1[...])
    norm_param_grads(vec_o, CNV, da, kept3[...])
    dx2 = dx3[...] + norm_grad(da, kept3[...], v(CNV))
    db = dx2.astype(BF)
    dwo_o[...] += t_dot(m[...], db)
    dm = dot_t(db, wo[...])
    lane = lane_iota((1, DP))
    masks = head_masks()
    wide_rows = lax.broadcasted_iota(jnp.int32, (DP, LANES), 0)
    wide_lane = lane_iota((DP, LANES))
    for b in range(seqs):
        rows = pl.ds(b * length, length)
        q = qkv[rows, pl.ds(0, DP)]
        k = qkv[rows, pl.ds(DP, DP)]
        vv = qkv[rows, pl.ds(2 * DP, DP)]
        dmb = (dm[b * length : (b + 1) * length] * rl[rows, :]).astype(BF)
        product = (dmb.astype(F32) * m[rows, :].astype(F32)).astype(BF)
        zero = jnp.zeros_like(q)
        dq = jnp.zeros((length, DP), F32)
        dk = jnp.zeros((length, DP), F32)
        dv = jnp.zeros((length, DP), F32)
        for n in range(HEADS):
            first = (n // 2) * LANES + (n % 2) * HD
            pick = (wide_rows >= first) & (wide_rows < first + HD) & (wide_lane > MASK_LANE) & (wide_lane < MASK_LANE + 3)
            level = dot(product, jnp.where(pick, -1.0, 0.0).astype(BF))
            high = level.astype(BF)
            low = (level - high.astype(F32)).astype(BF)
            side = jnp.where(lane_iota((1, LANES)) == MASK_LANE + 1, high, low)
            dmm = jnp.where(masks[n], dmb, zero)
            dmm = jnp.concatenate(
                [jnp.where(lane_iota((1, LANES)) > MASK_LANE, side, dmm[:, :LANES]), dmm[:, LANES:]], 1
            )
            e = e_all[b, pl.ds(n * length, length), :]
            ds = (e.astype(F32) * dot_t(dmm, vv)).astype(BF)
            rel_o[pl.ds(n * length, length), :] += ds.astype(F32)
            dq = jnp.where(masks[n], dot(ds, k), dq)
            dk = dk + t_dot(ds, jnp.where(masks[n], q, zero))
            dv = dv + t_dot(e, dmm)
        grads[rows, pl.ds(0, DP)] = (dq * SCALE).astype(BF)
        grads[rows, pl.ds(DP, DP)] = (dk * LN2).astype(BF)
        grads[rows, pl.ds(2 * DP, DP)] = dv.astype(BF)
    dqkv = grads[...]
    dqkv_o[...] += t_dot(a2[...], dqkv)
    da = dot_t(dqkv, wqkv[...])
    norm_param_grads(vec_o, ATT, da, kept2[...])
    dx1 = dx2 + norm_grad(da, kept2[...], v(ATT))
    do = dx1.astype(BF)
    ddn_o[...] += t_dot(do, h[...])
    du = (dot_t(do, dn[...]) * slope[...].astype(F32)).astype(BF)
    dup_o[...] += t_dot(a1[...], du)
    da = dot_t(du, up[...])
    norm_param_grads(vec_o, FFA, da, kept1[...])
    dx0 = dx1 + norm_grad(da, kept1[...], v(FFA))
    dx0_o[...] = dx0[:, :D].reshape(seqs, length, D)


def layer_call(body, steps, ins, outs, scratch, name):
    def spec(item):
        kind, shape = item
        if kind == "smem":
            return pl.BlockSpec(memory_space=pltpu.SMEM)
        if kind == "tile":
            return pl.BlockSpec(shape, lambda i: (i,) + (0,) * (len(shape) - 1))
        return pl.BlockSpec(shape, lambda i: (0,) * len(shape))

    arrays = [a for _, _, a in ins]
    return pl.pallas_call(
        body,
        grid=(steps,),
        out_shape=tuple(jax.ShapeDtypeStruct(full, dtype) for _, _, full, dtype in outs),
        in_specs=[spec((kind, block)) for kind, block, _ in ins],
        out_specs=tuple(spec((kind, block)) for kind, block, _, _ in outs),
        scratch_shapes=list(scratch),
        compiler_params=pltpu.CompilerParams(vmem_limit_bytes=BIG, dimension_semantics=("arbitrary",)),
        name=name,
    )(*arrays)


def tile_in(array, steps):
    return ("tile", (array.shape[0] // steps,) + array.shape[1:], array)


def whole_in(array):
    return ("whole", array.shape, array)


def tile_out(steps, shape, dtype):
    return ("tile", (shape[0] // steps,) + shape[1:], shape, dtype)


def whole_out(shape):
    return ("whole", shape, shape, F32)


SEQS_A = 2
SEQS_B = 4
SEQS_C = 2


def per_device(
    frames, cotangent, lengths, head_params, shared_params, head_first, head_second, shared_first, shared_second
):
    seq_here, length, _ = frames.shape
    tokens = seq_here * length
    dp = lax.axis_size("dp")
    head_size, shared_size = head_params.shape[1], shared_params.shape[0]
    rows = slot_rows(head_size) + slot_rows(shared_size)
    vm = pltpu.VMEM
    mine = vmem_call(
        align_kernel, jax.ShapeDtypeStruct((rows, LANES), BF), (head_params, shared_params), name="align"
    )
    got = gather_all(mine, dp, 1)
    up1, dn1, up2, dn2, wqkv, wo, p1, p2, vec, rel = make_weights(got, head_size, shared_size, length)

    steps = seq_here // SEQS_A
    t = functools.partial(tile_out, steps)
    (
        kept1, a1, h1, slope1, kept2, a2, qkv, e_all, rl, m, x2, kept3, a3, f1, f2, gl, w, stats
    ) = layer_call(
        functools.partial(phase_a_kernel, SEQS_A),
        steps,
        [("smem", None, lengths), tile_in(frames, steps)] + [whole_in(x) for x in (up1, dn1, wqkv, wo, p1, vec, rel)],
        [
            t((tokens, DP), F32), t((tokens, DP), BF), t((tokens, FFP), BF), t((tokens, FFP), BF),
            t((tokens, DP), F32), t((tokens, DP), BF), t((tokens, 3 * DP), BF),
            t((seq_here, HEADS * length, length), BF), t((tokens, DP), F32), t((tokens, DP), BF),
            t((tokens, DP), F32), t((tokens, DP), F32), t((tokens, DP), BF), t((tokens, DP), BF),
            t((tokens, DP), BF), t((tokens, DP), BF), t((tokens, DP), F32), whole_out((8, LANES)),
        ],
        [vm((SEQS_A, 2, length + 16, LANES), F32)],
        "phase_a",
    )
    shared_a = share_all(stats, dp, 2)
    steps = seq_here // SEQS_B
    t = functools.partial(tile_out, steps)
    layer_out, dy, dx3, dup2, ddn2, dp2, vec_b, sums = layer_call(
        functools.partial(phase_b_kernel, SEQS_B),
        steps,
        [whole_in(shared_a), tile_in(w, steps), tile_in(x2, steps), tile_in(cotangent, steps)]
        + [whole_in(x) for x in (p2, up2, dn2, vec)],
        [
            t((seq_here, length, D), BF), t((tokens, DP), F32), t((tokens, DP), F32),
            whole_out((DP, FFP)), whole_out((DP, FFP)), whole_out((DP, DP)), whole_out((VEC_ROWS, DP)),
            whole_out((8, LANES)),
        ],
        [vm((8, DP), F32)],
        "phase_b",
    )
    shared_b = share_all(sums, dp, 3)
    steps = seq_here // SEQS_C
    t = functools.partial(tile_out, steps)
    input_grad, dp1, dwo, dqkv, dup1, ddn1, vec_c, rel_sum = layer_call(
        functools.partial(phase_c_kernel, SEQS_C),
        steps,
        [("smem", None, lengths), whole_in(shared_a), whole_in(shared_b)]
        + [
            tile_in(x, steps)
            for x in (w, dy, dx3, gl, f1, f2, a3, kept3, qkv, e_all, rl, m, a2, kept2, h1, slope1, a1, kept1)
        ]
        + [whole_in(x) for x in (p1, wo, wqkv, dn1, up1, vec)],
        [
            t((seq_here, length, D), F32), whole_out((DP, 2 * DP)), whole_out((DP, DP)), whole_out((DP, 3 * DP)),
            whole_out((DP, FFP)), whole_out((DP, FFP)), whole_out((VEC_ROWS, DP)), whole_out((HEADS * length, length)),
        ],
        [
            vm((8, DP), F32),
            vm((SEQS_C, 2, length + 16, LANES), F32),
            vm((SEQS_C, 2, length + 16, LANES), F32),
            vm((SEQS_C * length, 3 * DP), BF),
        ],
        "phase_c",
    )
    grads = flatten_grads((dup1, ddn1, dup2, ddn2, dqkv, dwo, dp1, dp2, vec_b + vec_c, rel_sum), dp, head_size, shared_size)
    summed = scatter_all(grads, 4)
    h_shape, s_shape = head_params.shape, shared_params.shape

    def s(shape, dtype=F32):
        return jax.ShapeDtypeStruct(shape, dtype)

    updated = vmem_call(
        adam_kernel,
        (s(h_shape), s(h_shape), s(h_shape), s(h_shape, BF), s(s_shape), s(s_shape), s(s_shape), s(s_shape, BF)),
        (summed, head_params, head_first, head_second, shared_params, shared_first, shared_second),
        name="adam",
    )
    return (layer_out, input_grad) + tuple(updated)


def solution(mesh):
    frames = P(("dp", "head"), None, None)
    heads = P("head", "dp")
    shared = P(("dp", "head"))
    return jax.shard_map(
        per_device,
        mesh=mesh,
        in_specs=(frames, frames, P("dp"), heads, shared, heads, heads, shared, shared),
        out_specs=(frames, frames) + (heads,) * 4 + (shared,) * 4,
        check_vma=False,
    )
```

```python
import functools
import math

import jax
import jax.numpy as jnp
from jax import lax
from jax.experimental import pallas as pl
from jax.experimental.pallas import tpu as pltpu
from jax.sharding import PartitionSpec as P

BF = jnp.bfloat16
F32 = jnp.float32
LANES = 128


def up_to(count, unit):
    return -(-count // unit) * unit


def grid_place(nz):
    me = lax.axis_index("dp")
    core = lax.axis_index("head")
    zc = me // 4
    rest = me - 4 * zc
    yc = rest // 2
    xc = rest - 2 * yc
    return me, core, zc, yc, xc


def remote(src, dst, send, recv, dp, head):
    return pltpu.make_async_remote_copy(
        src_ref=src,
        dst_ref=dst,
        send_sem=send,
        recv_sem=recv,
        device_id={"dp": dp, "head": head},
        device_id_type=pl.DeviceIdType.MESH,
    )


def greet(nz, me, core, zc, yc, xc):
    barrier = pltpu.get_barrier_semaphore()

    def hello(dp, head):
        pl.semaphore_signal(
            barrier, inc=1, device_id={"dp": dp, "head": head}, device_id_type=pl.DeviceIdType.MESH
        )

    for k in range(1, nz):
        hello(lax.rem(zc + k, nz) * 4 + 2 * yc + xc, core)
    hello(4 * zc + 2 * (1 - yc) + xc, core)
    hello(4 * zc + 2 * yc + 1 - xc, core)
    hello(me, 1 - core)
    pl.semaphore_wait(barrier, nz + 2)


def gather_kernel(nz, src, out, sz, rz, s1, r1, s2, r2, sc, rc):
    rows = src.shape[0]
    row_a = up_to(rows // 2, 16)
    parts = (pl.ds(0, row_a), pl.ds(row_a, rows - row_a))
    me, core, zc, yc, xc = grid_place(nz)
    greet(nz, me, core, zc, yc, xc)
    out[me, core] = src[...]
    y_peer = 4 * zc + 2 * (1 - yc) + xc
    x_peer = 4 * zc + 2 * yc + 1 - xc
    firsts = (y_peer, x_peer)
    seconds = (x_peer, y_peer)
    pending = []

    def send(slot, p, send_sem, recv_sem, dp, head):
        block = out.at[slot, core, parts[p]]
        copy = remote(block, block, send_sem, recv_sem, dp, head)
        copy.start()
        pending.append(copy)

    def arrived(slot, which, p, send_sem, recv_sem):
        block = out.at[slot, which, parts[p]]
        remote(block, block, send_sem, recv_sem, me, 1 - core).wait_recv()

    zs = [lax.rem(zc + k, nz) for k in range(nz)]
    here = 2 * yc + xc
    first_here = (2 * (1 - yc) + xc, 2 * yc + 1 - xc)
    second_here = ((2 * yc + 1 - xc, 2 * (1 - yc) + 1 - xc), (2 * (1 - yc) + xc, 2 * (1 - yc) + 1 - xc))
    for k in range(1, nz):
        for p in (0, 1):
            send(me, p, sz.at[p, k], rz.at[p, zc], zs[k] * 4 + here, core)
    for k in range(nz):
        z = zs[k]
        slot = 4 * z + here
        for p in (0, 1):
            if k:
                arrived(slot, core, p, sz.at[p, k], rz.at[p, z])
            send(slot, p, s1.at[p, k], r1.at[p, z], firsts[p], core)
            send(slot, p, s2.at[p, k, 0], r2.at[p, z, 0], seconds[p], core)
            send(slot, p, sc.at[p, k, 0], rc.at[p, z, 0], me, 1 - core)
    for k in range(nz):
        z = zs[k]
        for p in (0, 1):
            slot = 4 * z + first_here[p]
            arrived(slot, core, p, s1.at[p, k], r1.at[p, z])
            send(slot, p, s2.at[p, k, 1], r2.at[p, z, 1], seconds[p], core)
            send(slot, p, sc.at[p, k, 1], rc.at[p, z, 1], me, 1 - core)
    for k in range(nz):
        z = zs[k]
        for p in (0, 1):
            for b in (0, 1):
                slot = 4 * z + second_here[p][b]
                arrived(slot, core, p, s2.at[p, k, b], r2.at[p, z, b])
                send(slot, p, sc.at[p, k, 2 + b], rc.at[p, z, 2 + b], me, 1 - core)
    for k in range(nz):
        z = zs[k]
        for p in (0, 1):
            for b, at in enumerate((here, first_here[p]) + second_here[p]):
                arrived(4 * z + at, 1 - core, p, sc.at[p, k, b], rc.at[p, z, b])
    for copy in pending:
        copy.wait_send()


def gather_all(block, dp, collective_id):
    rows = block.shape[0]
    nz = dp // 4
    dma = pltpu.SemaphoreType.DMA
    return pl.pallas_call(
        functools.partial(gather_kernel, nz),
        out_shape=jax.ShapeDtypeStruct((dp, 2, rows, LANES), block.dtype),
        in_specs=[pl.BlockSpec(memory_space=pltpu.VMEM)],
        out_specs=pl.BlockSpec(memory_space=pltpu.VMEM),
        scratch_shapes=[dma((2, nz)), dma((2, nz)), dma((2, nz)), dma((2, nz)), dma((2, nz, 2)), dma((2, nz, 2)), dma((2, nz, 4)), dma((2, nz, 4))],
        compiler_params=pltpu.CompilerParams(
            collective_id=collective_id, has_side_effects=True, vmem_limit_bytes=40 << 20
        ),
        name="gather_weights",
    )(block)


def scatter_kernel(nz, g, out, c1, t1, rx1, t2, rx2, t3, rx3, sc, rc, s1, r1, s2, r2, s3, r3):
    rows = g.shape[2]
    row_a = up_to(rows // 2, 16)
    starts = (0, row_a)
    sizes = (row_a, rows - row_a)
    parts = tuple(pl.ds(a, n) for a, n in zip(starts, sizes))
    me, core, zc, yc, xc = grid_place(nz)
    greet(nz, me, core, zc, yc, xc)
    y_peer = 4 * zc + 2 * (1 - yc) + xc
    x_peer = 4 * zc + 2 * yc + 1 - xc
    firsts = (x_peer, y_peer)
    seconds = (y_peer, x_peer)
    pending = []

    def send(src, dst, send_sem, recv_sem, dp, head):
        copy = remote(src, dst, send_sem, recv_sem, dp, head)
        copy.start()
        pending.append(copy)

    def arrived(block, send_sem, recv_sem):
        remote(block, block, send_sem, recv_sem, me, 1 - core).wait_recv()

    order = list(range(1, nz)) + [0]
    zs = [lax.rem(zc + k, nz) for k in range(nz)]
    give = ((1 - xc, 2 + 1 - xc), (2 * (1 - yc), 2 * (1 - yc) + 1))
    second_give = (1 - yc, 1 - xc)
    second_keep = (yc, xc)

    def place(p, b):
        return 2 * b + xc if p == 0 else 2 * yc + b

    for k in order:
        z = zs[k]
        send(g.at[1 - core, pl.ds(4 * z, 4)], c1.at[pl.ds(4 * z, 4)], sc.at[k], rc.at[z], me, 1 - core)
    for k in order:
        z = zs[k]
        arrived(c1.at[pl.ds(4 * z, 4)], sc.at[k], rc.at[z])
        for p in (0, 1):
            n = pl.ds(0, sizes[p])
            for b in (0, 1):
                slot = 4 * z + give[p][b]
                t1[p, z, b, n] = (g[core, slot, parts[p]].astype(F32) + c1[slot, parts[p]].astype(F32)).astype(BF)
            send(t1.at[p, z, :, n], rx1.at[p, z, :, n], s1.at[p, k], r1.at[p, z], firsts[p], core)

    def partial(p, z, b):
        slot = 4 * z + place(p, b)
        n = pl.ds(0, sizes[p])
        return g[core, slot, parts[p]].astype(F32) + c1[slot, parts[p]].astype(F32) + rx1[p, z, b, n].astype(F32)

    for k in order:
        z = zs[k]
        for p in (0, 1):
            n = pl.ds(0, sizes[p])
            arrived(rx1.at[p, z, :, n], s1.at[p, k], r1.at[p, z])
            t2[p, z, n] = partial(p, z, second_give[p]).astype(BF)
            send(t2.at[p, z, n], rx2.at[p, z, n], s2.at[p, k], r2.at[p, z], seconds[p], core)
    for k in order:
        z = zs[k]
        for p in (0, 1):
            n = pl.ds(0, sizes[p])
            arrived(rx2.at[p, z, n], s2.at[p, k], r2.at[p, z])
            total = partial(p, z, second_keep[p]) + rx2[p, z, n].astype(F32)
            if k:
                t3[p, z, n] = total.astype(BF)
                send(t3.at[p, z, n], rx3.at[p, zc, n], s3.at[p, k], r3.at[p, zc], 4 * z + 2 * yc + xc, core)
            else:
                out[parts[p], :] = total
    for k in order[:-1]:
        z = zs[k]
        for p in (0, 1):
            n = pl.ds(0, sizes[p])
            arrived(rx3.at[p, z, n], s3.at[p, k], r3.at[p, z])
            out[parts[p], :] += rx3[p, z, n].astype(F32)
    for copy in pending:
        copy.wait_send()


def scatter_all(g, collective_id):
    dp, rows = g.shape[1], g.shape[2]
    nz = dp // 4
    half = up_to(rows // 2, 16)
    dma = pltpu.SemaphoreType.DMA
    vm = pltpu.VMEM
    return pl.pallas_call(
        functools.partial(scatter_kernel, nz),
        out_shape=jax.ShapeDtypeStruct((rows, LANES), F32),
        in_specs=[pl.BlockSpec(memory_space=pltpu.VMEM)],
        out_specs=pl.BlockSpec(memory_space=pltpu.VMEM),
        scratch_shapes=[
            vm((dp, rows, LANES), BF),
            vm((2, nz, 2, half, LANES), BF),
            vm((2, nz, 2, half, LANES), BF),
            vm((2, nz, half, LANES), BF),
            vm((2, nz, half, LANES), BF),
            vm((2, nz, half, LANES), BF),
            vm((2, nz, half, LANES), BF),
            dma((nz,)), dma((nz,)), dma((2, nz)), dma((2, nz)), dma((2, nz)), dma((2, nz)), dma((2, nz)), dma((2, nz)),
        ],
        compiler_params=pltpu.CompilerParams(
            collective_id=collective_id, has_side_effects=True, vmem_limit_bytes=40 << 20
        ),
        name="scatter_grads",
    )(g)


def peer_of(own, total, k):
    other = lax.rem(own + k, total)
    dp = other // 2
    return other, dp, other - 2 * dp


def own_number():
    return 2 * lax.axis_index("dp") + lax.axis_index("head")


def greet_all(total):
    barrier = pltpu.get_barrier_semaphore()
    own = own_number()

    @pl.loop(1, total)
    def _(k):
        _, dp, head = peer_of(own, total, k)
        pl.semaphore_signal(
            barrier, inc=1, device_id={"dp": dp, "head": head}, device_id_type=pl.DeviceIdType.MESH
        )


def share_start(total, src, inbox, ss, rs):
    pl.semaphore_wait(pltpu.get_barrier_semaphore(), total - 1)
    own = own_number()
    inbox[own] = src[...]

    @pl.loop(1, total)
    def _(k):
        _, dp, head = peer_of(own, total, k)
        remote(src, inbox.at[own], ss.at[k], rs.at[own], dp, head).start()


def share_finish(total, src, inbox, ss, rs):
    own = own_number()

    @pl.loop(1, total)
    def _(k):
        other, dp, head = peer_of(own, total, k)
        remote(src, inbox.at[other], ss.at[k], rs.at[other], dp, head).wait()


HEADS = 4
HD = 60
FF = 960
KW = 15
STEP = 10
KREL = 383
NORM_EPS = 1e-05
BETA_ONE = 0.9
BETA_TWO = 0.999
LEARN_RATE = 0.1
WEIGHT_DECAY = 0.01
ADAM_EPS = 1e-08
LOG2E = 1.4426950408889634
LN2 = 0.6931471805599453
SCALE = HD ** (-0.5)
UNIT = 1.28125
D = 240
DP = 256
HF = 480
HFP = 512
FFP = 1024
HC = 120
MASK_LANE = 120
NEG = -1e30
FFA, ATT, CNV, FFB, OUT = 0, 2, 4, 6, 8
DOWNB_ONE, DOWNB_TWO, B_OUT, BATCH_GAIN, BATCH_BIAS, TAPS, DEPTH_BIAS = 10, 11, 12, 13, 14, 16, 31
VEC_ROWS = 32
BIG = 60 << 20


def head_places():
    out, at = {}, 0
    for name, size in (
        ("up1", D * HF), ("upb1", HF), ("dn1", HF * D), ("up2", D * HF), ("upb2", HF), ("dn2", HF * D),
        ("wq", D * HC), ("wk", D * HC), ("wv", D * HC), ("bq", HC), ("bv", HC),
        ("rel", 2 * KREL), ("wo", HC * D),
    ):
        out[name] = at
        at += size
    return out, at


def shared_places():
    out, at = {}, 0
    for name, size in (
        ("vec", 13 * D), ("p1", 2 * D * D), ("pb1", 2 * D), ("taps", KW * D), ("db", D),
        ("bg", D), ("bb", D), ("p2", D * D), ("pb2", D),
    ):
        out[name] = at
        at += size
    return out, at


def lane_iota(shape):
    return lax.broadcasted_iota(jnp.int32, shape, len(shape) - 1)


def slot_rows(size):
    return up_to(-(-(size + LANES - 1) // LANES), 16)


def dot(a, b):
    return jnp.dot(a, b, preferred_element_type=F32)


def dot_t(a, b):
    return lax.dot_general(a, b, (((1,), (1,)), ((), ())), preferred_element_type=F32)


def t_dot(a, b):
    return lax.dot_general(a, b, (((0,), (0,)), ((), ())), preferred_element_type=F32)


def vmem_call(body, outs, ins, scratch=(), name=None, limit=BIG):
    return pl.pallas_call(
        body,
        out_shape=outs,
        in_specs=[pl.BlockSpec(memory_space=pltpu.VMEM) for _ in ins],
        out_specs=jax.tree.map(lambda _: pl.BlockSpec(memory_space=pltpu.VMEM), outs),
        scratch_shapes=list(scratch),
        compiler_params=pltpu.CompilerParams(vmem_limit_bytes=limit),
        name=name,
    )(*ins)


def own_offsets(head_size, shared_size):
    me = lax.axis_index("dp")
    core = lax.axis_index("head")
    return lax.rem(me * head_size, LANES), lax.rem((2 * me + core) * shared_size, LANES)


def push_lanes(x, shift):
    rolled = pltpu.roll(x, shift, 1)
    before = jnp.concatenate([jnp.zeros((1, LANES), F32), rolled[:-1]], 0)
    return jnp.where(lane_iota(x.shape) >= shift, rolled, before)


def pull_lanes(x, shift):
    rolled = pltpu.roll(x, lax.rem(LANES - shift, LANES), 1)
    after = jnp.concatenate([rolled[1:], jnp.zeros((1, LANES), F32)], 0)
    return jnp.where(lane_iota(x.shape) < LANES - shift, rolled, after)


def align_kernel(head_ref, shared_ref, out):
    head_size, shared_size = head_ref.shape[1], shared_ref.shape[0]
    hr, sr = slot_rows(head_size), slot_rows(shared_size)
    ho, so = own_offsets(head_size, shared_size)
    x = jnp.concatenate([head_ref[...], jnp.zeros((1, hr * LANES - head_size), F32)], 1)
    out[pl.ds(0, hr), :] = push_lanes(x.reshape(hr, LANES), ho).astype(BF)
    x = shared_ref[...].reshape(1, shared_size)
    x = jnp.concatenate([x, jnp.zeros((1, sr * LANES - shared_size), F32)], 1)
    out[pl.ds(hr, sr), :] = push_lanes(x.reshape(sr, LANES), so).astype(BF)


def adam_kernel(g_ref, hp, hf, hs, sp, sf, ss, hf_o, hs_o, hp_o, hc_o, sf_o, ss_o, sp_o, sc_o):
    head_size, shared_size = hp.shape[1], sp.shape[0]
    hr, sr = slot_rows(head_size), slot_rows(shared_size)
    ho, so = own_offsets(head_size, shared_size)

    def update(master, g, first, second):
        first_new = BETA_ONE * first + (1.0 - BETA_ONE) * g
        second_new = BETA_TWO * second + (1.0 - BETA_TWO) * g * g
        first_hat = first_new * (1.0 / (1.0 - BETA_ONE**STEP))
        second_hat = second_new * (1.0 / (1.0 - BETA_TWO**STEP))
        new = master - LEARN_RATE * (first_hat / (jnp.sqrt(second_hat) + ADAM_EPS) + WEIGHT_DECAY * master)
        return first_new, second_new, new

    g = pull_lanes(g_ref[pl.ds(0, hr), :], ho).reshape(1, hr * LANES)[:, :head_size]
    one, two, new = update(hp[...], g, hf[...], hs[...])
    hf_o[...] = one
    hs_o[...] = two
    hp_o[...] = new
    hc_o[...] = new.astype(BF)
    g = pull_lanes(g_ref[pl.ds(hr, sr), :], so).reshape(sr * LANES)[:shared_size]
    one, two, new = update(sp[...], g, sf[...], ss[...])
    sf_o[...] = one
    ss_o[...] = two
    sp_o[...] = new
    sc_o[...] = new.astype(BF)


def row_phases(rows, pitch):
    if rows == 1:
        return 1, 1, 0
    period = LANES // math.gcd(pitch, LANES)
    return period, rows // period, period * pitch // LANES


def take(flat, at, rows, pitch, col, width, dst, row0, lane0):
    period, count, stride = row_phases(rows, pitch)
    lane = lane_iota((count, LANES))
    for j in range(period):
        start = at + j * pitch + col
        q, l = divmod(start, LANES)

        def load(t):
            if count == 1:
                return flat[pl.ds(q + t, 1), :]
            return flat[pl.ds(q + t, count, stride), :]

        pieces = [load(t) for t in range(-(-(l + width) // LANES))]
        if l:
            pieces = [pltpu.roll(x, LANES - l, 1) for x in pieces]
        for t in range(-(-width // LANES)):
            value = pieces[t]
            if l and t + 1 < len(pieces):
                value = jnp.where(lane < LANES - l, value, pieces[t + 1])
            left = width - t * LANES
            if left < LANES:
                value = jnp.where(lane < left, value, 0.0)
            rows_at = pl.ds(row0 + j, 1) if count == 1 else pl.ds(row0 + j, count, period)
            dst[lane0 // LANES + t, rows_at, :] = value


def give(flat, at, rows, pitch, col, width, src, row0, lane0):
    period, count, stride = row_phases(rows, pitch)
    lane = lane_iota((count, LANES))
    for j in range(period):
        start = at + j * pitch + col
        q, l = divmod(start, LANES)
        rows_at = pl.ds(row0 + j, 1) if count == 1 else pl.ds(row0 + j, count, period)
        pieces = [src[lane0 // LANES + t, rows_at, :] for t in range(-(-width // LANES))]
        if l:
            pieces = [pltpu.roll(x, l, 1) for x in pieces]
        total = -(-(l + width) // LANES)
        for t in range(total):
            here = pl.ds(q + t, 1) if count == 1 else pl.ds(q + t, count, stride)
            if not l:
                value = pieces[t]
            elif t == 0:
                value = pieces[0]
            elif t == len(pieces):
                value = pieces[t - 1]
            else:
                value = jnp.where(lane >= l, pieces[t], pieces[t - 1])
            lo = l if t == 0 else 0
            hi = min(LANES, l + width - t * LANES)
            if lo or hi < LANES:
                keep = (lane >= lo) & (lane < hi)
                value = jnp.where(keep, value, flat[here, :])
            flat[here, :] = value


def spill(tiles, rows, dst, factor=None):
    for t in range(dst.shape[1] // LANES):
        value = tiles[t, pl.ds(0, rows), :]
        if factor:
            value = factor * value
        dst[:, pl.ds(t * LANES, LANES)] = value.astype(dst.dtype)


def load_tiles(src, tiles):
    for t in range(src.shape[1] // LANES):
        tiles[t, pl.ds(0, src.shape[0]), :] = src[:, pl.ds(t * LANES, LANES)]


def flat_rows(total, size):
    return up_to(total // LANES + slot_rows(size) + 16, 16)


def weights_kernel(sizes, got, up1, dn1, up2, dn2, qkv, wo, p1, p2, vec, rel, fh, fs, wide, tall, tmp):
    dp, head_size, shared_size = sizes
    hr, sr = slot_rows(head_size), slot_rows(shared_size)
    hp, _ = head_places()
    sp, _ = shared_places()
    row8 = lax.broadcasted_iota(jnp.int32, (8, LANES), 0)

    def merge(flat, first_row, block):
        head = flat[pl.ds(first_row, 8), :]
        flat[pl.ds(first_row, 8), :] = block[:8] + jnp.where(row8 == 0, head, 0.0)
        flat[pl.ds(first_row + 8, block.shape[0] - 8), :] = block[8:]

    for g in range(2):
        fh[g, pl.ds(0, 8), :] = jnp.zeros((8, LANES), F32)
    fs[pl.ds(0, 8), :] = jnp.zeros((8, LANES), F32)

    @pl.loop(0, dp)
    def _(i):
        for g in range(2):
            merge(fh.at[g], (i * head_size) // LANES, got[i, g, pl.ds(0, hr), :].astype(F32))
        for g in range(2):
            merge(fs, ((2 * i + g) * shared_size) // LANES, got[i, g, pl.ds(hr, sr), :].astype(F32))

    lane = lane_iota((1, LANES))

    def clear(tiles, count, row, size):
        for t in range(count):
            tiles[t, pl.ds(row, size), :] = jnp.zeros((size, LANES), F32)

    def patch(tiles, tile, row, where, value):
        part = tiles[tile, pl.ds(row, 1), :]
        tiles[tile, pl.ds(row, 1), :] = jnp.where(where, value, part)

    for dst_ref, place, bplace in ((up1, "up1", "upb1"), (up2, "up2", "upb2")):
        clear(wide, 8, 240, 16)
        for g in range(2):
            take(fh.at[g], hp[place], D, HF, 0, HF, wide, 0, g * HFP)
            take(fh.at[g], hp[bplace], 1, HF, 0, HF, wide, 240, g * HFP)
        patch(wide, 3, 240, lane == HF - 3 * LANES, UNIT)
        spill(wide, DP, dst_ref)
    for dst_ref, place, brow in ((dn1, "dn1", DOWNB_ONE), (dn2, "dn2", DOWNB_TWO)):
        for g in range(2):
            clear(tall, 2, g * HFP + HF, 32)
            take(fh.at[g], hp[place], HF, D, 0, D, tall, g * HFP, 0)
        take(fs, sp["vec"] + brow * D, 1, D, 0, D, tall, HF, 0)
        spill(tall, FFP, dst_ref, 0.5)
    clear(wide, 6, 240, 16)
    for g in range(2):
        for which, (place, bplace) in enumerate((("wq", "bq"), ("wk", None), ("wv", "bv"))):
            lane0 = which * DP + g * LANES
            take(fh.at[g], hp[place], D, HC, 0, HC, wide, 0, lane0)
            if bplace:
                take(fh.at[g], hp[bplace], 1, HC, 0, HC, wide, 240, lane0)
    patch(wide, 0, 240, lane == MASK_LANE, 1.0)
    patch(wide, 4, 240, (lane >= MASK_LANE) & (lane < MASK_LANE + 3), 1.0)
    spill(wide, DP, qkv)
    clear(tall, 2, 0, DP)
    for g in range(2):
        take(fh.at[g], hp["wo"], HC, D, 0, D, tall, g * LANES, 0)
    take(fs, sp["vec"] + B_OUT * D, 1, D, 0, D, tall, MASK_LANE, 0)
    spill(tall, DP, wo)
    clear(wide, 4, 240, 16)
    for half in range(2):
        take(fs, sp["p1"], D, 2 * D, half * D, D, wide, 0, half * DP)
        take(fs, sp["pb1"] + half * D, 1, D, 0, D, wide, 240, half * DP)
    spill(wide, DP, p1)
    clear(tall, 2, 240, 16)
    take(fs, sp["p2"], D, D, 0, D, tall, 0, 0)
    take(fs, sp["pb2"], 1, D, 0, D, tall, 240, 0)
    spill(tall, DP, p2)
    take(fs, sp["vec"], 16, D, 0, D, tall, 0, 0)
    take(fs, sp["taps"], 16, D, 0, D, tall, TAPS, 0)
    take(fs, sp["bg"], 1, D, 0, D, tall, BATCH_GAIN, 0)
    take(fs, sp["bb"], 1, D, 0, D, tall, BATCH_BIAS, 0)
    for row, value in ((FFA + 1, 1.0), (ATT + 1, 1.0), (CNV + 1, 1.0), (FFB + 1, 1.0), (BATCH_BIAS, UNIT)):
        patch(tall, 1, row, lane == D - LANES, value)
    spill(tall, VEC_ROWS, vec)
    length = rel.shape[1]
    for n in range(HEADS):
        take(fh.at[n // 2], hp["rel"] + (n % 2) * KREL, 1, KREL, 0, KREL, tmp, 0, 0)
        row = jnp.concatenate([tmp[t, pl.ds(0, 1), :] for t in range(3)] + [jnp.zeros((1, LANES), F32)], 1)
        rows = jnp.broadcast_to(row, (length, 4 * LANES))
        rows = pltpu.roll(rows, 4 * LANES - (length - 1), 1, stride=1, stride_axis=0)
        rel[n] = rows[:, :length] * LOG2E


def make_weights(got, head_size, shared_size, length):
    dp = got.shape[0]

    def s(*shape, dtype=BF):
        return jax.ShapeDtypeStruct(shape, dtype)

    outs = (
        s(DP, FFP), s(FFP, DP), s(DP, FFP), s(FFP, DP), s(DP, 3 * DP), s(DP, DP), s(DP, 2 * DP), s(DP, DP),
        s(VEC_ROWS, DP, dtype=F32), s(HEADS, length, length, dtype=F32),
    )
    vm = pltpu.VMEM
    scratch = (
        vm((2, flat_rows(head_size * dp, head_size), LANES), F32),
        vm((flat_rows(shared_size * 2 * dp, shared_size), LANES), F32),
        vm((8, DP, LANES), F32),
        vm((2, FFP, LANES), F32),
        vm((4, 8, LANES), F32),
    )
    return vmem_call(
        functools.partial(weights_kernel, (dp, head_size, shared_size)), outs, (got,), scratch, "make_weights"
    )


def flatten_kernel(sizes, up1, dn1, up2, dn2, qkv, wo, p1, p2, vec, rel, out, fh, fs, wide, tall, tmp):
    dp, head_size, shared_size = sizes
    hr, sr = slot_rows(head_size), slot_rows(shared_size)
    hp, used_h = head_places()
    sp, used_s = shared_places()
    for g in range(2):
        first = used_h // LANES // 8 * 8
        fh[g, pl.ds(first, fh.shape[1] - first), :] = jnp.zeros((fh.shape[1] - first, LANES), F32)
    first = used_s // LANES // 8 * 8
    fs[pl.ds(first, fs.shape[0] - first), :] = jnp.zeros((fs.shape[0] - first, LANES), F32)
    for src, place, bplace in ((up1, "up1", "upb1"), (up2, "up2", "upb2")):
        load_tiles(src, wide)
        for g in range(2):
            give(fh.at[g], hp[place], D, HF, 0, HF, wide, 0, g * HFP)
            give(fh.at[g], hp[bplace], 1, HF, 0, HF, wide, 240, g * HFP)
    for src, place, brow in ((dn1, "dn1", DOWNB_ONE), (dn2, "dn2", DOWNB_TWO)):
        for t in range(2):
            tall[t] = 0.5 * src[pl.ds(t * LANES, LANES), :].T
        for g in range(2):
            give(fh.at[g], hp[place], HF, D, 0, D, tall, g * HFP, 0)
        give(fs, sp["vec"] + brow * D, 1, D, 0, D, tall, HF, 0)
    load_tiles(qkv, wide)
    load_tiles(wo, tall)
    for g in range(2):
        for which, (place, bplace) in enumerate((("wq", "bq"), ("wk", None), ("wv", "bv"))):
            lane0 = which * DP + g * LANES
            give(fh.at[g], hp[place], D, HC, 0, HC, wide, 0, lane0)
            if bplace:
                give(fh.at[g], hp[bplace], 1, HC, 0, HC, wide, 240, lane0)
        give(fh.at[g], hp["wo"], HC, D, 0, D, tall, g * LANES, 0)
    give(fs, sp["vec"] + B_OUT * D, 1, D, 0, D, tall, MASK_LANE, 0)
    load_tiles(p1, wide)
    load_tiles(p2, tall)
    for half in range(2):
        give(fs, sp["p1"], D, 2 * D, half * D, D, wide, 0, half * DP)
        give(fs, sp["pb1"] + half * D, 1, D, 0, D, wide, 240, half * DP)
    give(fs, sp["p2"], D, D, 0, D, tall, 0, 0)
    give(fs, sp["pb2"], 1, D, 0, D, tall, 240, 0)
    load_tiles(vec, tall)
    for row in range(10):
        give(fs, sp["vec"] + row * D, 1, D, 0, D, tall, row, 0)
    give(fs, sp["taps"], 16, D, 0, D, tall, TAPS, 0)
    give(fs, sp["bg"], 1, D, 0, D, tall, BATCH_GAIN, 0)
    give(fs, sp["bb"], 1, D, 0, D, tall, BATCH_BIAS, 0)
    length = rel.shape[0] // HEADS
    for n in range(HEADS):
        total = jnp.zeros((8, 4 * LANES), F32)
        for block in range(length // 8):
            rows = rel[pl.ds(n * length + 8 * block, 8), :]
            rows = jnp.concatenate([rows, jnp.zeros((8, 4 * LANES - length), F32)], 1)
            total = total + pltpu.roll(rows, length - 8 - 8 * block, 1)
        row = total[7:8]
        for i in range(7):
            row = row + pltpu.roll(total[i : i + 1], 7 - i, 1)
        for t in range(4):
            tmp[t, pl.ds(0, 1), :] = row[:, t * LANES : (t + 1) * LANES]
        give(fh.at[n // 2], hp["rel"] + (n % 2) * KREL, 1, KREL, 0, KREL, tmp, 0, 0)

    @pl.loop(0, dp)
    def _(i):
        for g in range(2):
            out[g, i, pl.ds(0, hr), :] = fh[g, pl.ds((i * head_size) // LANES, hr), :].astype(BF)
            out[g, i, pl.ds(hr, sr), :] = fs[pl.ds(((2 * i + g) * shared_size) // LANES, sr), :].astype(BF)


def flatten_grads(grads, dp, head_size, shared_size):
    rows = slot_rows(head_size) + slot_rows(shared_size)
    vm = pltpu.VMEM
    scratch = (
        vm((2, flat_rows(head_size * dp, head_size), LANES), F32),
        vm((flat_rows(shared_size * 2 * dp, shared_size), LANES), F32),
        vm((8, DP, LANES), F32),
        vm((2, FFP, LANES), F32),
        vm((4, 8, LANES), F32),
    )
    return vmem_call(
        functools.partial(flatten_kernel, (dp, head_size, shared_size)),
        jax.ShapeDtypeStruct((2, dp, rows, LANES), BF),
        grads,
        scratch,
        "flatten_grads",
    )


def lane_mask():
    return jnp.where(lane_iota((1, DP)) < D, 1.0, 0.0)


def sigmoid(x):
    return 0.5 * jnp.tanh(0.5 * x) + 0.5


def row_sum(x):
    return jnp.sum(x, -1, keepdims=True)


def norm(x, gain, bias):
    centre = (x - row_sum(x) * (1.0 / D)) * lane_mask()
    inv = lax.rsqrt(row_sum(centre * centre) * (1.0 / D) + NORM_EPS)
    scaled = centre * inv
    return scaled * gain + bias, scaled, inv


def keep_norm(scaled, inv):
    return jnp.where(lane_iota(scaled.shape) == DP - 1, inv, scaled)


def norm_grad(grad, kept, gain):
    dg = grad * gain
    inv = kept[:, DP - 1 :]
    first = row_sum(dg) * (1.0 / D)
    second = row_sum(dg * kept) * (1.0 / D)
    return inv * (dg - first - kept * second) * lane_mask()


def add_rows(ref, row, value):
    ref[pl.ds(row, 1), :] += jnp.sum(value, 0, keepdims=True)


def norm_param_grads(ref, row, grad, kept):
    add_rows(ref, row, grad * kept)
    add_rows(ref, row + 1, grad)


def silu_pair(u):
    s = sigmoid(u)
    h = u * s
    return h, s + h * (1.0 - s)


def widen(x):
    rows = x.shape[0]
    return jnp.concatenate([x.astype(F32), jnp.zeros((rows, DP - D), F32)], 1)


def head_masks():
    lane = lane_iota((1, DP))
    out = []
    for n in range(HEADS):
        first = (n // 2) * LANES + (n % 2) * HD
        out.append((lane >= first) & (lane < first + HD))
    return out


def valid_rows(lengths, at, length):
    return lax.broadcasted_iota(jnp.int32, (length, 1), 0) < lengths[at]


def phase_a_kernel(
    seqs, lengths, frames, up, dn, wqkv, wo, p1, vec, rel,
    kept1_o, a1_o, h_o, sp_o, kept2_o, a2_o, qkv_o, e_o, rl_o, m_o,
    x2_o, kept3_o, a3_o, f1_o, f2_o, gl_o, w_o, keep_o,
    pad, stats_o, inbox, ss, rs,
):
    step = pl.program_id(0)
    total = inbox.shape[0]

    @pl.when(step == 0)
    def _():
        greet_all(total)

    length = frames.shape[1]
    tokens = seqs * length
    first_seq = lax.axis_index("head") * (seqs * pl.num_programs(0)) + step * seqs

    def v(row):
        return vec[pl.ds(row, 1), :]

    x0 = widen(frames[...].reshape(tokens, D))
    a, scaled, inv = norm(x0, v(FFA), v(FFA + 1))
    a = a.astype(BF)
    a1_o[...] = a
    kept1_o[...] = keep_norm(scaled, inv)
    h, slope = silu_pair(dot(a, up[...]))
    h = h.astype(BF)
    h_o[...] = h
    sp_o[...] = slope.astype(BF)
    x1 = x0 + dot(h, dn[...])
    a, scaled, inv = norm(x1, v(ATT), v(ATT + 1))
    a = a.astype(BF)
    a2_o[...] = a
    kept2_o[...] = keep_norm(scaled, inv)
    qkv = dot(a, wqkv[...])
    lane = lane_iota((1, DP))
    masks = head_masks()
    for b in range(seqs):
        rows = pl.ds(b * length, length)
        valid = valid_rows(lengths, first_seq + b, length)
        part = qkv[b * length : (b + 1) * length]
        q = (part[:, :DP] * (SCALE * LOG2E)).astype(BF)
        k = part[:, DP : 2 * DP]
        k = jnp.where(lane == MASK_LANE, jnp.where(valid, 0.0, NEG), k).astype(BF)
        vv = part[:, 2 * DP :].astype(BF)
        qkv_o[rows, pl.ds(0, DP)] = q
        qkv_o[rows, pl.ds(DP, DP)] = k
        qkv_o[rows, pl.ds(2 * DP, DP)] = vv
        zero = jnp.zeros_like(q)
        mixed = jnp.zeros((length, DP), F32)
        shares = jnp.zeros((length, DP), F32)
        for n in range(HEADS):
            qm = jnp.where(masks[n] | (lane == MASK_LANE), q, zero)
            s = dot_t(qm, k) + rel[n]
            e = jnp.exp2(s - jnp.max(s, -1, keepdims=True)).astype(BF)
            e_o[b, pl.ds(n * length, length), :] = e
            o = dot(e, vv)
            r = 1.0 / o[:, MASK_LANE : MASK_LANE + 1]
            here = masks[n] | (lane == MASK_LANE) if n == 0 else masks[n]
            shares = jnp.where(here, r, shares)
            mixed = jnp.where(here, o, mixed)
        rl_o[rows, :] = shares
        m_o[rows, :] = (mixed * shares).astype(BF)
    x2 = x1 + dot(m_o[...], wo[...])
    x2_o[...] = x2
    a, scaled, inv = norm(x2, v(CNV), v(CNV + 1))
    a = a.astype(BF)
    a3_o[...] = a
    kept3_o[...] = keep_norm(scaled, inv)
    e = dot(a, p1[...])
    half = KW // 2

    @pl.when(step == 0)
    def _():
        pad[...] = jnp.zeros(pad.shape, F32)
        stats_o[...] = jnp.zeros(stats_o.shape, F32)

    count = jnp.float32(0.0)
    summed = jnp.zeros((1, DP), F32)
    for b in range(seqs):
        rows = pl.ds(b * length, length)
        valid = jnp.where(valid_rows(lengths, first_seq + b, length), 1.0, 0.0)
        linear = e[b * length : (b + 1) * length, :DP]
        gate = sigmoid(e[b * length : (b + 1) * length, DP:])
        f1 = gate * valid
        gl = linear * f1
        f1_o[rows, :] = f1.astype(BF)
        f2_o[rows, :] = (gl * (1.0 - gate)).astype(BF)
        gl_o[rows, :] = gl.astype(BF)
        for t in range(2):
            cols = pl.ds(t * LANES, LANES)
            pad[b, t, pl.ds(8, length), :] = gl[:, t * LANES : (t + 1) * LANES]
            acc = jnp.broadcast_to(vec[pl.ds(DEPTH_BIAS, 1), cols], (length, LANES))
            for r in range(KW):
                acc = acc + pad[b, t, pl.ds(8 - half + r, length), :] * vec[pl.ds(TAPS + r, 1), cols]
            w_o[rows, cols] = acc
        summed = summed + jnp.sum(w_o[rows, :] * valid, 0, keepdims=True)
        count = count + lengths[first_seq + b].astype(F32)
    mean = summed / count
    square = jnp.zeros((1, DP), F32)
    for b in range(seqs):
        valid = jnp.where(valid_rows(lengths, first_seq + b, length), 1.0, 0.0)
        centre = (w_o[pl.ds(b * length, length), :] - mean) * valid
        square = square + jnp.sum(centre * centre, 0, keepdims=True)
    old = stats_o[pl.ds(4, 1), :]
    new = old + count
    for t in range(2):
        cols = slice(t * LANES, (t + 1) * LANES)
        before = stats_o[pl.ds(t, 1), :]
        delta = mean[:, cols] - before
        stats_o[pl.ds(t, 1), :] = before + delta * (count / new)
        stats_o[pl.ds(2 + t, 1), :] += square[:, cols] + delta * delta * (old * count / new)
    stats_o[pl.ds(4, 1), :] = new

    @pl.when(step == pl.num_programs(0) - 1)
    def _():
        share_start(total, stats_o, inbox, ss, rs)
        share_finish(total, stats_o, inbox, ss, rs)
        batch_stats(inbox[...], keep_o)


def batch_stats(shared, keep):
    counts = shared[:, 4:5, :]
    total = jnp.sum(counts, 0)
    means, spreads = [], []
    for t in range(2):
        each = shared[:, t : t + 1, :]
        mean = jnp.sum(each * counts, 0) / total
        spread = (jnp.sum(shared[:, 2 + t : 3 + t, :], 0) + jnp.sum(counts * (each - mean) ** 2, 0)) / total
        means.append(mean)
        spreads.append(spread)
    keep[pl.ds(0, 1), :] = jnp.concatenate(means, 1)
    keep[pl.ds(1, 1), :] = lax.rsqrt(jnp.concatenate(spreads, 1) + NORM_EPS)
    keep[pl.ds(2, 1), :] = jnp.concatenate([total, total], 1)
    keep[pl.ds(3, 5), :] = jnp.zeros((5, DP), F32)


def phase_b_kernel(
    seqs, keep, w, x2, cotangent, p2, up, dn, vec,
    out_o, dy_o, dx3_o, dup_o, ddn_o, dp2_o, vec_o, keep_o,
    sums_o, inbox, ss, rs,
):
    step = pl.program_id(0)
    total = inbox.shape[0]
    length = cotangent.shape[1]
    tokens = seqs * length

    @pl.when(step == 0)
    def _():
        greet_all(total)
        for ref in (dup_o, ddn_o, dp2_o, vec_o, sums_o):
            ref[...] = jnp.zeros(ref.shape, F32)

    def v(row):
        return vec[pl.ds(row, 1), :]

    z = (w[...] - keep[pl.ds(0, 1), :]) * keep[pl.ds(1, 1), :]
    hc, slope_c = silu_pair(z * v(BATCH_GAIN) + v(BATCH_BIAS))
    hc = hc.astype(BF)
    x3 = x2[...] + dot(hc, p2[...])
    a, scaled, inv = norm(x3, v(FFB), v(FFB + 1))
    a = a.astype(BF)
    kept = keep_norm(scaled, inv)
    h, slope = silu_pair(dot(a, up[...]))
    h = h.astype(BF)
    slope = slope.astype(BF)
    x4 = x3 + dot(h, dn[...])
    final, scaled, inv = norm(x4, v(OUT), v(OUT + 1))
    out_o[...] = final[:, :D].astype(BF).reshape(seqs, length, D)
    g = widen(cotangent[...].reshape(tokens, D))
    kept4 = keep_norm(scaled, inv)
    norm_param_grads(vec_o, OUT, g, kept4)
    dx4 = norm_grad(g, kept4, v(OUT))
    do = dx4.astype(BF)
    ddn_o[...] += t_dot(do, h)
    du = (dot_t(do, dn[...]) * slope.astype(F32)).astype(BF)
    dup_o[...] += t_dot(a, du)
    da = dot_t(du, up[...])
    norm_param_grads(vec_o, FFB, da, kept)
    dx3 = dx4 + norm_grad(da, kept, v(FFB))
    dx3_o[...] = dx3
    dc = dx3.astype(BF)
    dp2_o[...] += t_dot(hc, dc)
    dy = dot_t(dc, p2[...]) * slope_c
    dy_o[...] = dy
    first = jnp.sum(dy, 0, keepdims=True)
    second = jnp.sum(dy * z, 0, keepdims=True)
    vec_o[pl.ds(BATCH_BIAS, 1), :] += first
    vec_o[pl.ds(BATCH_GAIN, 1), :] += second
    for t in range(2):
        cols = slice(t * LANES, (t + 1) * LANES)
        sums_o[pl.ds(t, 1), :] += first[:, cols]
        sums_o[pl.ds(2 + t, 1), :] += second[:, cols]

    @pl.when(step == pl.num_programs(0) - 1)
    def _():
        share_start(total, sums_o, inbox, ss, rs)
        share_finish(total, sums_o, inbox, ss, rs)
        sums = jnp.sum(inbox[...], 0)
        keep_o[...] = keep[...]
        keep_o[pl.ds(3, 1), :] = jnp.concatenate([sums[0:1], sums[1:2]], 1)
        keep_o[pl.ds(4, 1), :] = jnp.concatenate([sums[2:3], sums[3:4]], 1)


def phase_c_kernel(
    seqs, lengths, keep, w, dy, dx3, gl, f1, f2, a3, kept3, qkv, e_all, rl, m, a2, kept2, h, slope, a1, kept1,
    p1, wo, wqkv, dn, up, vec,
    dx0_o, dp1_o, dwo_o, dqkv_o, dup_o, ddn_o, vec_o, rel_o,
    padw, padg, grads,
):
    step = pl.program_id(0)
    length = dx0_o.shape[1]
    tokens = seqs * length
    first_seq = lax.axis_index("head") * (seqs * pl.num_programs(0)) + step * seqs
    half = KW // 2

    def v(row):
        return vec[pl.ds(row, 1), :]

    @pl.when(step == 0)
    def _():
        for ref in (dp1_o, dwo_o, dqkv_o, dup_o, ddn_o, vec_o, rel_o, padw, padg):
            ref[...] = jnp.zeros(ref.shape, F32)

    gain = v(BATCH_GAIN)
    inv_batch = keep[pl.ds(1, 1), :]
    mean = keep[pl.ds(0, 1), :]
    plain = gain * keep[pl.ds(3, 1), :] / keep[pl.ds(2, 1), :]
    cross = gain * keep[pl.ds(4, 1), :] / keep[pl.ds(2, 1), :]
    for b in range(seqs):
        rows = pl.ds(b * length, length)
        valid = jnp.where(valid_rows(lengths, first_seq + b, length), 1.0, 0.0)
        z = (w[rows, :] - mean) * inv_batch
        dw = inv_batch * (dy[rows, :] * gain - valid * (plain + z * cross))
        add_rows(vec_o, DEPTH_BIAS, dw)
        for t in range(2):
            cols = pl.ds(t * LANES, LANES)
            here = dw[:, t * LANES : (t + 1) * LANES]
            padw[b, t, pl.ds(8, length), :] = here
            padg[b, t, pl.ds(8, length), :] = gl[rows, cols].astype(F32)
            acc = jnp.zeros((length, LANES), F32)
            for r in range(KW):
                acc = acc + padw[b, t, pl.ds(8 + half - r, length), :] * vec[pl.ds(TAPS + r, 1), cols]
                tap = here * padg[b, t, pl.ds(8 - half + r, length), :]
                vec_o[pl.ds(TAPS + r, 1), cols] += jnp.sum(tap, 0, keepdims=True)
            grads[rows, cols] = (acc * f1[rows, cols].astype(F32)).astype(BF)
            grads[rows, pl.ds(DP + t * LANES, LANES)] = (acc * f2[rows, cols].astype(F32)).astype(BF)
    de = grads[:, pl.ds(0, 2 * DP)]
    dp1_o[...] += t_dot(a3[...], de)
    da = dot_t(de, p1[...])
    norm_param_grads(vec_o, CNV, da, kept3[...])
    dx2 = dx3[...] + norm_grad(da, kept3[...], v(CNV))
    db = dx2.astype(BF)
    dwo_o[...] += t_dot(m[...], db)
    dm = dot_t(db, wo[...])
    lane = lane_iota((1, DP))
    masks = head_masks()
    wide_rows = lax.broadcasted_iota(jnp.int32, (DP, LANES), 0)
    wide_lane = lane_iota((DP, LANES))
    for b in range(seqs):
        rows = pl.ds(b * length, length)
        q = qkv[rows, pl.ds(0, DP)]
        k = qkv[rows, pl.ds(DP, DP)]
        vv = qkv[rows, pl.ds(2 * DP, DP)]
        dmb = (dm[b * length : (b + 1) * length] * rl[rows, :]).astype(BF)
        product = (dmb.astype(F32) * m[rows, :].astype(F32)).astype(BF)
        zero = jnp.zeros_like(q)
        dq = jnp.zeros((length, DP), F32)
        dk = jnp.zeros((length, DP), F32)
        dv = jnp.zeros((length, DP), F32)
        for n in range(HEADS):
            first = (n // 2) * LANES + (n % 2) * HD
            pick = (wide_rows >= first) & (wide_rows < first + HD) & (wide_lane > MASK_LANE) & (wide_lane < MASK_LANE + 3)
            level = dot(product, jnp.where(pick, -1.0, 0.0).astype(BF))
            high = level.astype(BF)
            low = (level - high.astype(F32)).astype(BF)
            side = jnp.where(lane_iota((1, LANES)) == MASK_LANE + 1, high, low)
            dmm = jnp.where(masks[n], dmb, zero)
            dmm = jnp.concatenate(
                [jnp.where(lane_iota((1, LANES)) > MASK_LANE, side, dmm[:, :LANES]), dmm[:, LANES:]], 1
            )
            e = e_all[b, pl.ds(n * length, length), :]
            ds = (e.astype(F32) * dot_t(dmm, vv)).astype(BF)
            rel_o[pl.ds(n * length, length), :] += ds.astype(F32)
            dq = jnp.where(masks[n], dot(ds, k), dq)
            dk = dk + t_dot(ds, jnp.where(masks[n], q, zero))
            dv = dv + t_dot(e, dmm)
        grads[rows, pl.ds(0, DP)] = (dq * SCALE).astype(BF)
        grads[rows, pl.ds(DP, DP)] = (dk * LN2).astype(BF)
        grads[rows, pl.ds(2 * DP, DP)] = dv.astype(BF)
    dqkv = grads[...]
    dqkv_o[...] += t_dot(a2[...], dqkv)
    da = dot_t(dqkv, wqkv[...])
    norm_param_grads(vec_o, ATT, da, kept2[...])
    dx1 = dx2 + norm_grad(da, kept2[...], v(ATT))
    do = dx1.astype(BF)
    ddn_o[...] += t_dot(do, h[...])
    du = (dot_t(do, dn[...]) * slope[...].astype(F32)).astype(BF)
    dup_o[...] += t_dot(a1[...], du)
    da = dot_t(du, up[...])
    norm_param_grads(vec_o, FFA, da, kept1[...])
    dx0 = dx1 + norm_grad(da, kept1[...], v(FFA))
    dx0_o[...] = dx0[:, :D].reshape(seqs, length, D)


def layer_call(body, steps, ins, outs, scratch, name, collective_id=None):
    def spec(item):
        kind, shape = item
        if kind == "smem":
            return pl.BlockSpec(memory_space=pltpu.SMEM)
        if kind == "tile":
            return pl.BlockSpec(shape, lambda i: (i,) + (0,) * (len(shape) - 1))
        return pl.BlockSpec(shape, lambda i: (0,) * len(shape))

    arrays = [a for _, _, a in ins]
    return pl.pallas_call(
        body,
        grid=(steps,),
        out_shape=tuple(jax.ShapeDtypeStruct(full, dtype) for _, _, full, dtype in outs),
        in_specs=[spec((kind, block)) for kind, block, _ in ins],
        out_specs=tuple(spec((kind, block)) for kind, block, _, _ in outs),
        scratch_shapes=list(scratch),
        compiler_params=pltpu.CompilerParams(
            vmem_limit_bytes=BIG,
            dimension_semantics=("arbitrary",),
            collective_id=collective_id,
            has_side_effects=collective_id is not None,
        ),
        name=name,
    )(*arrays)


def tile_in(array, steps):
    return ("tile", (array.shape[0] // steps,) + array.shape[1:], array)


def whole_in(array):
    return ("whole", array.shape, array)


def tile_out(steps, shape, dtype):
    return ("tile", (shape[0] // steps,) + shape[1:], shape, dtype)


def whole_out(shape):
    return ("whole", shape, shape, F32)


SEQS_A = 2
SEQS_B = 4
SEQS_C = 2


def per_device(
    frames, cotangent, lengths, head_params, shared_params, head_first, head_second, shared_first, shared_second
):
    seq_here, length, _ = frames.shape
    tokens = seq_here * length
    dp = lax.axis_size("dp")
    head_size, shared_size = head_params.shape[1], shared_params.shape[0]
    rows = slot_rows(head_size) + slot_rows(shared_size)
    vm = pltpu.VMEM
    mine = vmem_call(
        align_kernel, jax.ShapeDtypeStruct((rows, LANES), BF), (head_params, shared_params), name="align"
    )
    got = gather_all(mine, dp, 1)
    up1, dn1, up2, dn2, wqkv, wo, p1, p2, vec, rel = make_weights(got, head_size, shared_size, length)

    dma = pltpu.SemaphoreType.DMA
    sharing = [vm((8, LANES), F32), vm((2 * dp, 8, LANES), F32), dma((2 * dp,)), dma((2 * dp,))]
    steps = seq_here // SEQS_A
    t = functools.partial(tile_out, steps)
    (
        kept1, a1, h1, slope1, kept2, a2, qkv, e_all, rl, m, x2, kept3, a3, f1, f2, gl, w, keep
    ) = layer_call(
        functools.partial(phase_a_kernel, SEQS_A),
        steps,
        [("smem", None, lengths), tile_in(frames, steps)] + [whole_in(x) for x in (up1, dn1, wqkv, wo, p1, vec, rel)],
        [
            t((tokens, DP), F32), t((tokens, DP), BF), t((tokens, FFP), BF), t((tokens, FFP), BF),
            t((tokens, DP), F32), t((tokens, DP), BF), t((tokens, 3 * DP), BF),
            t((seq_here, HEADS * length, length), BF), t((tokens, DP), F32), t((tokens, DP), BF),
            t((tokens, DP), F32), t((tokens, DP), F32), t((tokens, DP), BF), t((tokens, DP), BF),
            t((tokens, DP), BF), t((tokens, DP), BF), t((tokens, DP), F32), whole_out((8, DP)),
        ],
        [vm((SEQS_A, 2, length + 16, LANES), F32)] + sharing,
        "phase_a",
        2,
    )
    steps = seq_here // SEQS_B
    t = functools.partial(tile_out, steps)
    layer_out, dy, dx3, dup2, ddn2, dp2, vec_b, keep = layer_call(
        functools.partial(phase_b_kernel, SEQS_B),
        steps,
        [whole_in(keep), tile_in(w, steps), tile_in(x2, steps), tile_in(cotangent, steps)]
        + [whole_in(x) for x in (p2, up2, dn2, vec)],
        [
            t((seq_here, length, D), BF), t((tokens, DP), F32), t((tokens, DP), F32),
            whole_out((DP, FFP)), whole_out((DP, FFP)), whole_out((DP, DP)), whole_out((VEC_ROWS, DP)),
            whole_out((8, DP)),
        ],
        sharing,
        "phase_b",
        3,
    )
    steps = seq_here // SEQS_C
    t = functools.partial(tile_out, steps)
    input_grad, dp1, dwo, dqkv, dup1, ddn1, vec_c, rel_sum = layer_call(
        functools.partial(phase_c_kernel, SEQS_C),
        steps,
        [("smem", None, lengths), whole_in(keep)]
        + [
            tile_in(x, steps)
            for x in (w, dy, dx3, gl, f1, f2, a3, kept3, qkv, e_all, rl, m, a2, kept2, h1, slope1, a1, kept1)
        ]
        + [whole_in(x) for x in (p1, wo, wqkv, dn1, up1, vec)],
        [
            t((seq_here, length, D), F32), whole_out((DP, 2 * DP)), whole_out((DP, DP)), whole_out((DP, 3 * DP)),
            whole_out((DP, FFP)), whole_out((DP, FFP)), whole_out((VEC_ROWS, DP)), whole_out((HEADS * length, length)),
        ],
        [
            vm((SEQS_C, 2, length + 16, LANES), F32),
            vm((SEQS_C, 2, length + 16, LANES), F32),
            vm((SEQS_C * length, 3 * DP), BF),
        ],
        "phase_c",
    )
    grads = flatten_grads((dup1, ddn1, dup2, ddn2, dqkv, dwo, dp1, dp2, vec_b + vec_c, rel_sum), dp, head_size, shared_size)
    summed = scatter_all(grads, 4)
    h_shape, s_shape = head_params.shape, shared_params.shape

    def s(shape, dtype=F32):
        return jax.ShapeDtypeStruct(shape, dtype)

    updated = vmem_call(
        adam_kernel,
        (s(h_shape), s(h_shape), s(h_shape), s(h_shape, BF), s(s_shape), s(s_shape), s(s_shape), s(s_shape, BF)),
        (summed, head_params, head_first, head_second, shared_params, shared_first, shared_second),
        name="adam",
    )
    return (layer_out, input_grad) + tuple(updated)


def solution(mesh):
    frames = P(("dp", "head"), None, None)
    heads = P("head", "dp")
    shared = P(("dp", "head"))
    return jax.shard_map(
        per_device,
        mesh=mesh,
        in_specs=(frames, frames, P("dp"), heads, shared, heads, heads, shared, shared),
        out_specs=(frames, frames) + (heads,) * 4 + (shared,) * 4,
        check_vma=False,
    )
```

```python
import functools
import math

import jax
import jax.numpy as jnp
from jax import lax
from jax.experimental import pallas as pl
from jax.experimental.pallas import tpu as pltpu
from jax.sharding import PartitionSpec as P

BF = jnp.bfloat16
F32 = jnp.float32
LANES = 128


def up_to(count, unit):
    return -(-count // unit) * unit


def grid_place(nz):
    me = lax.axis_index("dp")
    core = lax.axis_index("head")
    zc = me // 4
    rest = me - 4 * zc
    yc = rest // 2
    xc = rest - 2 * yc
    return me, core, zc, yc, xc


def remote(src, dst, send, recv, dp, head):
    return pltpu.make_async_remote_copy(
        src_ref=src,
        dst_ref=dst,
        send_sem=send,
        recv_sem=recv,
        device_id={"dp": dp, "head": head},
        device_id_type=pl.DeviceIdType.MESH,
    )


def greet(nz, me, core, zc, yc, xc):
    barrier = pltpu.get_barrier_semaphore()

    def hello(dp, head):
        pl.semaphore_signal(
            barrier, inc=1, device_id={"dp": dp, "head": head}, device_id_type=pl.DeviceIdType.MESH
        )

    for k in range(1, nz):
        hello(lax.rem(zc + k, nz) * 4 + 2 * yc + xc, core)
    hello(4 * zc + 2 * (1 - yc) + xc, core)
    hello(4 * zc + 2 * yc + 1 - xc, core)
    hello(me, 1 - core)


def greeted(nz):
    pl.semaphore_wait(pltpu.get_barrier_semaphore(), nz + 2)


def gather_kernel(nz, src, out, sz, rz, s1, r1, s2, r2, sc, rc):
    rows = src.shape[0]
    row_a = up_to(rows // 2, 16)
    parts = (pl.ds(0, row_a), pl.ds(row_a, rows - row_a))
    me, core, zc, yc, xc = grid_place(nz)
    greet(nz, me, core, zc, yc, xc)
    greeted(nz)
    out[me, core] = src[...]
    y_peer = 4 * zc + 2 * (1 - yc) + xc
    x_peer = 4 * zc + 2 * yc + 1 - xc
    firsts = (y_peer, x_peer)
    seconds = (x_peer, y_peer)
    pending = []

    def send(slot, p, send_sem, recv_sem, dp, head):
        block = out.at[slot, core, parts[p]]
        copy = remote(block, block, send_sem, recv_sem, dp, head)
        copy.start()
        pending.append(copy)

    def arrived(slot, which, p, send_sem, recv_sem):
        block = out.at[slot, which, parts[p]]
        remote(block, block, send_sem, recv_sem, me, 1 - core).wait_recv()

    zs = [lax.rem(zc + k, nz) for k in range(nz)]
    here = 2 * yc + xc
    first_here = (2 * (1 - yc) + xc, 2 * yc + 1 - xc)
    second_here = ((2 * yc + 1 - xc, 2 * (1 - yc) + 1 - xc), (2 * (1 - yc) + xc, 2 * (1 - yc) + 1 - xc))
    for k in range(1, nz):
        for p in (0, 1):
            send(me, p, sz.at[p, k], rz.at[p, zc], zs[k] * 4 + here, core)
    for k in range(nz):
        z = zs[k]
        slot = 4 * z + here
        for p in (0, 1):
            if k:
                arrived(slot, core, p, sz.at[p, k], rz.at[p, z])
            send(slot, p, s1.at[p, k], r1.at[p, z], firsts[p], core)
            send(slot, p, s2.at[p, k, 0], r2.at[p, z, 0], seconds[p], core)
            send(slot, p, sc.at[p, k, 0], rc.at[p, z, 0], me, 1 - core)
    for k in range(nz):
        z = zs[k]
        for p in (0, 1):
            slot = 4 * z + first_here[p]
            arrived(slot, core, p, s1.at[p, k], r1.at[p, z])
            send(slot, p, s2.at[p, k, 1], r2.at[p, z, 1], seconds[p], core)
            send(slot, p, sc.at[p, k, 1], rc.at[p, z, 1], me, 1 - core)
    for k in range(nz):
        z = zs[k]
        for p in (0, 1):
            for b in (0, 1):
                slot = 4 * z + second_here[p][b]
                arrived(slot, core, p, s2.at[p, k, b], r2.at[p, z, b])
                send(slot, p, sc.at[p, k, 2 + b], rc.at[p, z, 2 + b], me, 1 - core)
    for k in range(nz):
        z = zs[k]
        for p in (0, 1):
            for b, at in enumerate((here, first_here[p]) + second_here[p]):
                arrived(4 * z + at, 1 - core, p, sc.at[p, k, b], rc.at[p, z, b])
    for copy in pending:
        copy.wait_send()


def gather_all(block, dp, collective_id):
    rows = block.shape[0]
    nz = dp // 4
    dma = pltpu.SemaphoreType.DMA
    return pl.pallas_call(
        functools.partial(gather_kernel, nz),
        out_shape=jax.ShapeDtypeStruct((dp, 2, rows, LANES), block.dtype),
        in_specs=[pl.BlockSpec(memory_space=pltpu.VMEM)],
        out_specs=pl.BlockSpec(memory_space=pltpu.VMEM),
        scratch_shapes=[dma((2, nz)), dma((2, nz)), dma((2, nz)), dma((2, nz)), dma((2, nz, 2)), dma((2, nz, 2)), dma((2, nz, 4)), dma((2, nz, 4))],
        compiler_params=pltpu.CompilerParams(
            collective_id=collective_id, has_side_effects=True, vmem_limit_bytes=40 << 20
        ),
        name="gather_weights",
    )(block)


class Scatter:
    @staticmethod
    def scratch(dp, hr, sr):
        nz, rows = dp // 4, hr + sr
        dma, vm = pltpu.SemaphoreType.DMA, pltpu.VMEM
        return [
            vm((2, dp, rows, LANES), BF), vm((dp, rows, LANES), BF),
            vm((nz, 2, rows, LANES), BF), vm((nz, 2, rows, LANES), BF),
            vm((nz, rows, LANES), BF), vm((nz, rows, LANES), BF),
            vm((nz, rows, LANES), BF), vm((nz, rows, LANES), BF),
            dma((nz, 2)), dma((nz, 2)), dma((3, nz)), dma((3, nz)), dma((3, nz)), dma((3, nz)), dma((3, nz)), dma((3, nz)),
        ]

    def __init__(self, nz, hr, sr, mine, refs):
        self.nz, self.mine = nz, mine
        (
            self.g, self.c1, self.t1, self.rx1, self.t2, self.rx2, self.t3, self.rx3,
            self.sc, self.rc, self.s1, self.r1, self.s2, self.r2, self.s3, self.r3,
        ) = refs
        ha = up_to(hr // 2, 16)
        self.parts = (pl.ds(0, ha), pl.ds(ha, hr - ha), pl.ds(hr, sr))
        self.kinds = (pl.ds(0, hr), pl.ds(hr, sr))
        self.me, self.core, self.zc, self.yc, self.xc = grid_place(nz)
        zc, yc, xc = self.zc, self.yc, self.xc
        y_peer = 4 * zc + 2 * (1 - yc) + xc
        x_peer = 4 * zc + 2 * yc + 1 - xc
        self.firsts = (x_peer, y_peer, x_peer)
        self.seconds = (y_peer, x_peer, y_peer)
        self.second_give = (1 - yc, 1 - xc, 1 - yc)
        self.second_keep = (yc, xc, yc)

    def core_copy(self, z, kind):
        group, rows = pl.ds(4 * z, 4), self.kinds[kind]
        return remote(
            self.g.at[1 - self.core, group, rows], self.c1.at[group, rows],
            self.sc.at[z, kind], self.rc.at[z, kind], self.me, 1 - self.core,
        )

    def first_copy(self, z, p):
        rows = self.parts[p]
        return remote(
            self.t1.at[z, :, rows], self.rx1.at[z, :, rows], self.s1.at[p, z], self.r1.at[p, z], self.firsts[p], self.core
        )

    def second_copy(self, z, p):
        rows = self.parts[p]
        return remote(
            self.t2.at[z, rows], self.rx2.at[z, rows], self.s2.at[p, z], self.r2.at[p, z], self.seconds[p], self.core
        )

    def third_copy(self, z, p):
        rows = self.parts[p]
        return remote(
            self.t3.at[z, rows], self.rx3.at[self.zc, rows], self.s3.at[p, z], self.r3.at[p, self.zc],
            4 * z + 2 * self.yc + self.xc, self.core,
        )

    def place(self, p, z, b):
        return 4 * z + (2 * self.yc + b if p == 1 else 2 * b + self.xc)

    def held(self, z, p, slot):
        rows = self.parts[p]
        return self.g[self.core, slot, rows].astype(F32) + self.c1[slot, rows].astype(F32)

    def partial(self, z, p, b):
        return self.held(z, p, self.place(p, z, b)) + self.rx1[z, b, self.parts[p]].astype(F32)

    def stage_core(self, z, kind):
        self.core_copy(z, kind).start()

    def stage_first(self, z, kind):
        self.core_copy(z, kind).wait_recv()
        for p in ((0, 1), (2,))[kind]:
            for b in (0, 1):
                slot = 4 * z + (2 * (1 - self.yc) + b if p == 1 else 2 * b + 1 - self.xc)
                self.t1[z, b, self.parts[p]] = self.held(z, p, slot).astype(BF)
            self.first_copy(z, p).start()

    def stage_second(self, z, kind):
        for p in ((0, 1), (2,))[kind]:
            self.first_copy(z, p).wait_recv()
            self.t2[z, self.parts[p]] = self.partial(z, p, self.second_give[p]).astype(BF)
            self.second_copy(z, p).start()

    def stage_third(self, z, kind):
        for p in ((0, 1), (2,))[kind]:
            rows = self.parts[p]
            self.second_copy(z, p).wait_recv()
            total = self.partial(z, p, self.second_keep[p]) + self.rx2[z, rows].astype(F32)

            @pl.when(self.zc == z)
            def _():
                self.mine[rows, :] = total

            @pl.when(self.zc != z)
            def _():
                self.t3[z, rows] = total.astype(BF)
                self.third_copy(z, p).start()

    def finish(self, out):
        total = self.mine[...]
        for k in range(1, self.nz):
            sender = lax.rem(self.zc + k, self.nz)
            for p in range(3):
                rows = self.parts[p]
                remote(
                    self.t3.at[sender, rows], self.rx3.at[sender, rows], self.s3.at[p, sender], self.r3.at[p, sender],
                    self.me, 1 - self.core,
                ).wait_recv()
            total = total + self.rx3[sender].astype(F32)
        out[...] = total
        for z in range(self.nz):
            for kind in range(2):
                self.core_copy(z, kind).wait_send()
            for p in range(3):
                self.first_copy(z, p).wait_send()
                self.second_copy(z, p).wait_send()

            @pl.when(self.zc != z)
            def _():
                for p in range(3):
                    self.third_copy(z, p).wait_send()


def peer_of(own, total, k):
    other = lax.rem(own + k, total)
    dp = other // 2
    return other, dp, other - 2 * dp


def own_number():
    return 2 * lax.axis_index("dp") + lax.axis_index("head")


def greet_all(total):
    barrier = pltpu.get_barrier_semaphore()
    own = own_number()

    @pl.loop(1, total)
    def _(k):
        _, dp, head = peer_of(own, total, k)
        pl.semaphore_signal(
            barrier, inc=1, device_id={"dp": dp, "head": head}, device_id_type=pl.DeviceIdType.MESH
        )


def share_start(total, src, inbox, ss, rs):
    pl.semaphore_wait(pltpu.get_barrier_semaphore(), total - 1)
    own = own_number()
    inbox[own] = src[...]

    @pl.loop(1, total)
    def _(k):
        _, dp, head = peer_of(own, total, k)
        remote(src, inbox.at[own], ss.at[k], rs.at[own], dp, head).start()


def share_finish(total, src, inbox, ss, rs):
    own = own_number()

    @pl.loop(1, total)
    def _(k):
        other, dp, head = peer_of(own, total, k)
        remote(src, inbox.at[other], ss.at[k], rs.at[other], dp, head).wait()


HEADS = 4
HD = 60
FF = 960
KW = 15
STEP = 10
KREL = 383
NORM_EPS = 1e-05
BETA_ONE = 0.9
BETA_TWO = 0.999
LEARN_RATE = 0.1
WEIGHT_DECAY = 0.01
ADAM_EPS = 1e-08
LOG2E = 1.4426950408889634
LN2 = 0.6931471805599453
SCALE = HD ** (-0.5)
UNIT = 1.28125
D = 240
DP = 256
HF = 480
HFP = 512
FFP = 1024
HC = 120
MASK_LANE = 120
NEG = -1e30
FFA, ATT, CNV, FFB, OUT = 0, 2, 4, 6, 8
DOWNB_ONE, DOWNB_TWO, B_OUT, BATCH_GAIN, BATCH_BIAS, TAPS, DEPTH_BIAS = 10, 11, 12, 13, 14, 16, 31
VEC_ROWS = 32
BIG = 60 << 20


def head_places():
    out, at = {}, 0
    for name, size in (
        ("up1", D * HF), ("upb1", HF), ("dn1", HF * D), ("up2", D * HF), ("upb2", HF), ("dn2", HF * D),
        ("wq", D * HC), ("wk", D * HC), ("wv", D * HC), ("bq", HC), ("bv", HC),
        ("rel", 2 * KREL), ("wo", HC * D),
    ):
        out[name] = at
        at += size
    return out, at


def shared_places():
    out, at = {}, 0
    for name, size in (
        ("vec", 13 * D), ("p1", 2 * D * D), ("pb1", 2 * D), ("taps", KW * D), ("db", D),
        ("bg", D), ("bb", D), ("p2", D * D), ("pb2", D),
    ):
        out[name] = at
        at += size
    return out, at


def lane_iota(shape):
    return lax.broadcasted_iota(jnp.int32, shape, len(shape) - 1)


def slot_rows(size):
    return up_to(-(-(size + LANES - 1) // LANES), 16)


def dot(a, b):
    return jnp.dot(a, b, preferred_element_type=F32)


def dot_t(a, b):
    return lax.dot_general(a, b, (((1,), (1,)), ((), ())), preferred_element_type=F32)


def t_dot(a, b):
    return lax.dot_general(a, b, (((0,), (0,)), ((), ())), preferred_element_type=F32)


def vmem_call(body, outs, ins, scratch=(), name=None, limit=BIG):
    return pl.pallas_call(
        body,
        out_shape=outs,
        in_specs=[pl.BlockSpec(memory_space=pltpu.VMEM) for _ in ins],
        out_specs=jax.tree.map(lambda _: pl.BlockSpec(memory_space=pltpu.VMEM), outs),
        scratch_shapes=list(scratch),
        compiler_params=pltpu.CompilerParams(vmem_limit_bytes=limit),
        name=name,
    )(*ins)


def own_offsets(head_size, shared_size):
    me = lax.axis_index("dp")
    core = lax.axis_index("head")
    return lax.rem(me * head_size, LANES), lax.rem((2 * me + core) * shared_size, LANES)


def push_lanes(x, shift):
    rolled = pltpu.roll(x, shift, 1)
    before = jnp.concatenate([jnp.zeros((1, LANES), F32), rolled[:-1]], 0)
    return jnp.where(lane_iota(x.shape) >= shift, rolled, before)


def pull_lanes(x, shift):
    rolled = pltpu.roll(x, lax.rem(LANES - shift, LANES), 1)
    after = jnp.concatenate([rolled[1:], jnp.zeros((1, LANES), F32)], 0)
    return jnp.where(lane_iota(x.shape) < LANES - shift, rolled, after)


def align_kernel(head_ref, shared_ref, out):
    head_size, shared_size = head_ref.shape[1], shared_ref.shape[0]
    hr, sr = slot_rows(head_size), slot_rows(shared_size)
    ho, so = own_offsets(head_size, shared_size)
    x = jnp.concatenate([head_ref[...], jnp.zeros((1, hr * LANES - head_size), F32)], 1)
    out[pl.ds(0, hr), :] = push_lanes(x.reshape(hr, LANES), ho).astype(BF)
    x = shared_ref[...].reshape(1, shared_size)
    x = jnp.concatenate([x, jnp.zeros((1, sr * LANES - shared_size), F32)], 1)
    out[pl.ds(hr, sr), :] = push_lanes(x.reshape(sr, LANES), so).astype(BF)


def adam_kernel(
    early, grad, g_ref, hp, hf, hs, sp, sf, ss, out_o, grad_o, hf_o, hs_o, hp_o, hc_o, sf_o, ss_o, sp_o, sc_o
):
    out_o[...] = early[...]
    grad_o[...] = grad[...]

    @pl.when(pl.program_id(0) == 0)
    def _():
        adam_update(g_ref, hp, hf, hs, sp, sf, ss, hf_o, hs_o, hp_o, hc_o, sf_o, ss_o, sp_o, sc_o)


def adam_update(g_ref, hp, hf, hs, sp, sf, ss, hf_o, hs_o, hp_o, hc_o, sf_o, ss_o, sp_o, sc_o):
    head_size, shared_size = hp.shape[1], sp.shape[0]
    hr, sr = slot_rows(head_size), slot_rows(shared_size)
    ho, so = own_offsets(head_size, shared_size)

    def update(master, g, first, second):
        first_new = BETA_ONE * first + (1.0 - BETA_ONE) * g
        second_new = BETA_TWO * second + (1.0 - BETA_TWO) * g * g
        first_hat = first_new * (1.0 / (1.0 - BETA_ONE**STEP))
        second_hat = second_new * (1.0 / (1.0 - BETA_TWO**STEP))
        new = master - LEARN_RATE * (first_hat / (jnp.sqrt(second_hat) + ADAM_EPS) + WEIGHT_DECAY * master)
        return first_new, second_new, new

    g = pull_lanes(g_ref[pl.ds(0, hr), :], ho).reshape(1, hr * LANES)[:, :head_size]
    one, two, new = update(hp[...], g, hf[...], hs[...])
    hf_o[...] = one
    hs_o[...] = two
    hp_o[...] = new
    hc_o[...] = new.astype(BF)
    g = pull_lanes(g_ref[pl.ds(hr, sr), :], so).reshape(sr * LANES)[:shared_size]
    one, two, new = update(sp[...], g, sf[...], ss[...])
    sf_o[...] = one
    ss_o[...] = two
    sp_o[...] = new
    sc_o[...] = new.astype(BF)


def row_phases(rows, pitch):
    if rows == 1:
        return 1, 1, 0
    period = LANES // math.gcd(pitch, LANES)
    return period, rows // period, period * pitch // LANES


def take(flat, at, rows, pitch, col, width, dst, row0, lane0):
    period, count, stride = row_phases(rows, pitch)
    lane = lane_iota((count, LANES))
    for j in range(period):
        start = at + j * pitch + col
        q, l = divmod(start, LANES)

        def load(t):
            if count == 1:
                return flat[pl.ds(q + t, 1), :]
            return flat[pl.ds(q + t, count, stride), :]

        pieces = [load(t) for t in range(-(-(l + width) // LANES))]
        if l:
            pieces = [pltpu.roll(x, LANES - l, 1) for x in pieces]
        for t in range(-(-width // LANES)):
            value = pieces[t]
            if l and t + 1 < len(pieces):
                value = jnp.where(lane < LANES - l, value, pieces[t + 1])
            left = width - t * LANES
            if left < LANES:
                value = jnp.where(lane < left, value, 0.0)
            rows_at = pl.ds(row0 + j, 1) if count == 1 else pl.ds(row0 + j, count, period)
            dst[lane0 // LANES + t, rows_at, :] = value


def give(flat, at, rows, pitch, col, width, src, row0, lane0):
    period, count, stride = row_phases(rows, pitch)
    lane = lane_iota((count, LANES))
    for j in range(period):
        start = at + j * pitch + col
        q, l = divmod(start, LANES)
        rows_at = pl.ds(row0 + j, 1) if count == 1 else pl.ds(row0 + j, count, period)
        pieces = [src[lane0 // LANES + t, rows_at, :] for t in range(-(-width // LANES))]
        if l:
            pieces = [pltpu.roll(x, l, 1) for x in pieces]
        total = -(-(l + width) // LANES)
        for t in range(total):
            here = pl.ds(q + t, 1) if count == 1 else pl.ds(q + t, count, stride)
            if not l:
                value = pieces[t]
            elif t == 0:
                value = pieces[0]
            elif t == len(pieces):
                value = pieces[t - 1]
            else:
                value = jnp.where(lane >= l, pieces[t], pieces[t - 1])
            lo = l if t == 0 else 0
            hi = min(LANES, l + width - t * LANES)
            if lo or hi < LANES:
                keep = (lane >= lo) & (lane < hi)
                value = jnp.where(keep, value, flat[here, :])
            flat[here, :] = value


def spill(tiles, rows, dst, factor=None):
    for t in range(dst.shape[1] // LANES):
        value = tiles[t, pl.ds(0, rows), :]
        if factor:
            value = factor * value
        dst[:, pl.ds(t * LANES, LANES)] = value.astype(dst.dtype)


def load_tiles(src, tiles, factor=None):
    for t in range(src.shape[1] // LANES):
        value = src[:, pl.ds(t * LANES, LANES)]
        tiles[t, pl.ds(0, src.shape[0]), :] = factor * value if factor else value


def flat_rows(total, size):
    return up_to(total // LANES + slot_rows(size) + 16, 16)


def weights_kernel(sizes, got, up1, dn1, up2, dn2, qkv, wo, p1, p2, vec, rel, fh, fs, wide, tall, tmp):
    dp, head_size, shared_size = sizes
    hr, sr = slot_rows(head_size), slot_rows(shared_size)
    hp, _ = head_places()
    sp, _ = shared_places()
    row8 = lax.broadcasted_iota(jnp.int32, (8, LANES), 0)

    def merge(flat, first_row, block):
        head = flat[pl.ds(first_row, 8), :]
        flat[pl.ds(first_row, 8), :] = block[:8] + jnp.where(row8 == 0, head, 0.0)
        flat[pl.ds(first_row + 8, block.shape[0] - 8), :] = block[8:]

    for g in range(2):
        fh[g, pl.ds(0, 8), :] = jnp.zeros((8, LANES), F32)
    fs[pl.ds(0, 8), :] = jnp.zeros((8, LANES), F32)

    @pl.loop(0, dp)
    def _(i):
        for g in range(2):
            merge(fh.at[g], (i * head_size) // LANES, got[i, g, pl.ds(0, hr), :].astype(F32))
        for g in range(2):
            merge(fs, ((2 * i + g) * shared_size) // LANES, got[i, g, pl.ds(hr, sr), :].astype(F32))

    lane = lane_iota((1, LANES))

    def clear(tiles, count, row, size):
        for t in range(count):
            tiles[t, pl.ds(row, size), :] = jnp.zeros((size, LANES), F32)

    def patch(tiles, tile, row, where, value):
        part = tiles[tile, pl.ds(row, 1), :]
        tiles[tile, pl.ds(row, 1), :] = jnp.where(where, value, part)

    for dst_ref, place, bplace in ((up1, "up1", "upb1"), (up2, "up2", "upb2")):
        clear(wide, 8, 240, 16)
        for g in range(2):
            take(fh.at[g], hp[place], D, HF, 0, HF, wide, 0, g * HFP)
            take(fh.at[g], hp[bplace], 1, HF, 0, HF, wide, 240, g * HFP)
        patch(wide, 3, 240, lane == HF - 3 * LANES, UNIT)
        spill(wide, DP, dst_ref, 0.5)
    for dst_ref, place, brow in ((dn1, "dn1", DOWNB_ONE), (dn2, "dn2", DOWNB_TWO)):
        for g in range(2):
            clear(tall, 2, g * HFP + HF, 32)
            take(fh.at[g], hp[place], HF, D, 0, D, tall, g * HFP, 0)
        take(fs, sp["vec"] + brow * D, 1, D, 0, D, tall, HF, 0)
        spill(tall, FFP, dst_ref, 0.5)
    clear(wide, 6, 240, 16)
    for g in range(2):
        for which, (place, bplace) in enumerate((("wq", "bq"), ("wk", None), ("wv", "bv"))):
            lane0 = which * DP + g * LANES
            take(fh.at[g], hp[place], D, HC, 0, HC, wide, 0, lane0)
            if bplace:
                take(fh.at[g], hp[bplace], 1, HC, 0, HC, wide, 240, lane0)
    for tile in (0, 1, 4, 5):
        patch(wide, tile, 240, lane == MASK_LANE, 1.0)
    spill(wide, DP, qkv)
    clear(tall, 2, 0, DP)
    for g in range(2):
        take(fh.at[g], hp["wo"], HC, D, 0, D, tall, g * LANES, 0)
    take(fs, sp["vec"] + B_OUT * D, 1, D, 0, D, tall, MASK_LANE, 0)
    spill(tall, DP, wo)
    clear(wide, 4, 240, 16)
    for half in range(2):
        take(fs, sp["p1"], D, 2 * D, half * D, D, wide, 0, half * DP)
        take(fs, sp["pb1"] + half * D, 1, D, 0, D, wide, 240, half * DP)
    spill(wide, DP, p1)
    clear(tall, 2, 240, 16)
    take(fs, sp["p2"], D, D, 0, D, tall, 0, 0)
    take(fs, sp["pb2"], 1, D, 0, D, tall, 240, 0)
    spill(tall, DP, p2)
    take(fs, sp["vec"], 16, D, 0, D, tall, 0, 0)
    take(fs, sp["taps"], 16, D, 0, D, tall, TAPS, 0)
    take(fs, sp["bg"], 1, D, 0, D, tall, BATCH_GAIN, 0)
    take(fs, sp["bb"], 1, D, 0, D, tall, BATCH_BIAS, 0)
    for row, value in ((FFA + 1, 1.0), (ATT + 1, 1.0), (CNV + 1, 1.0), (FFB + 1, 1.0), (BATCH_BIAS, UNIT)):
        patch(tall, 1, row, lane == D - LANES, value)
    spill(tall, VEC_ROWS, vec)
    length = rel.shape[1]
    for n in range(HEADS):
        take(fh.at[n // 2], hp["rel"] + (n % 2) * KREL, 1, KREL, 0, KREL, tmp, 0, 0)
        row = jnp.concatenate([tmp[t, pl.ds(0, 1), :] for t in range(3)] + [jnp.zeros((1, LANES), F32)], 1)
        rows = jnp.broadcast_to(row, (length, 4 * LANES))
        rows = pltpu.roll(rows, 4 * LANES - (length - 1), 1, stride=1, stride_axis=0)
        rel[pl.ds(n * length, length), :] = rows[:, :length] * LOG2E


def make_weights(got, head_size, shared_size, length):
    dp = got.shape[0]

    def s(*shape, dtype=BF):
        return jax.ShapeDtypeStruct(shape, dtype)

    outs = (
        s(DP, FFP), s(FFP, DP), s(DP, FFP), s(FFP, DP), s(DP, 3 * DP), s(DP, DP), s(DP, 2 * DP), s(DP, DP),
        s(VEC_ROWS, DP, dtype=F32), s(HEADS * length, length, dtype=F32),
    )
    vm = pltpu.VMEM
    scratch = (
        vm((2, flat_rows(head_size * dp, head_size), LANES), F32),
        vm((flat_rows(shared_size * 2 * dp, shared_size), LANES), F32),
        vm((8, DP, LANES), F32),
        vm((2, FFP, LANES), F32),
        vm((4, 8, LANES), F32),
    )
    return vmem_call(
        functools.partial(weights_kernel, (dp, head_size, shared_size)), outs, (got,), scratch, "make_weights"
    )


class Flat:
    @staticmethod
    def scratch(dp, head_size, shared_size):
        vm = pltpu.VMEM
        return [
            vm((2, flat_rows(head_size * dp, head_size), LANES), F32),
            vm((flat_rows(shared_size * 2 * dp, shared_size), LANES), F32),
            vm((8, DP, LANES), F32),
            vm((2, FFP, LANES), F32),
            vm((4, 8, LANES), F32),
        ]

    def __init__(self, dp, head_size, shared_size, refs):
        self.dp, self.head_size, self.shared_size = dp, head_size, shared_size
        self.hr, self.sr = slot_rows(head_size), slot_rows(shared_size)
        self.fh, self.fs, self.wide, self.tall, self.tmp = refs
        self.hp, self.used_h = head_places()
        self.sp, self.used_s = shared_places()

    def clear_unused(self):
        for g in range(2):
            first = self.used_h // LANES // 8 * 8
            count = self.fh.shape[1] - first
            self.fh[g, pl.ds(first, count), :] = jnp.zeros((count, LANES), F32)
        first = self.used_s // LANES // 8 * 8
        count = self.fs.shape[0] - first
        self.fs[pl.ds(first, count), :] = jnp.zeros((count, LANES), F32)

    def head(self, g, place, rows, pitch, src, row0, lane0):
        give(self.fh.at[g], self.hp[place], rows, pitch, 0, pitch, src, row0, lane0)

    def shared(self, place, at, rows, pitch, col, src, row0, lane0):
        give(self.fs, self.sp[place] + at, rows, pitch, col, D, src, row0, lane0)

    def up(self, up, place, bias_place):
        load_tiles(up, self.wide, 0.5)
        for g in range(2):
            self.head(g, place, D, HF, self.wide, 0, g * HFP)
            self.head(g, bias_place, 1, HF, self.wide, 240, g * HFP)

    def down(self, dn, place, row):
        for t in range(2):
            self.tall[t] = (0.5 * dn[pl.ds(t * LANES, LANES), :]).astype(BF).T.astype(F32)
        for g in range(2):
            self.head(g, place, HF, D, self.tall, g * HFP, 0)
        self.shared("vec", row * D, 1, D, 0, self.tall, HF, 0)

    def attention(self, qkv, wo, rel):
        load_tiles(qkv, self.wide)
        load_tiles(wo, self.tall)
        length = rel.shape[0] // HEADS
        for g in range(2):
            for which, (place, bplace) in enumerate((("wq", "bq"), ("wk", None), ("wv", "bv"))):
                lane0 = which * DP + g * LANES
                self.head(g, place, D, HC, self.wide, 0, lane0)
                if bplace:
                    self.head(g, bplace, 1, HC, self.wide, 240, lane0)
            self.head(g, "wo", HC, D, self.tall, g * LANES, 0)
        for n in range(HEADS):
            total = jnp.zeros((8, 4 * LANES), F32)
            for block in range(length // 8):
                rows = rel[pl.ds(n * length + 8 * block, 8), :]
                rows = jnp.concatenate([rows, jnp.zeros((8, 4 * LANES - length), F32)], 1)
                total = total + pltpu.roll(rows, length - 8 - 8 * block, 1)
            row = total[7:8]
            for i in range(7):
                row = row + pltpu.roll(total[i : i + 1], 7 - i, 1)
            for t in range(4):
                self.tmp[t, pl.ds(0, 1), :] = row[:, t * LANES : (t + 1) * LANES]
            give(self.fh.at[n // 2], self.hp["rel"] + (n % 2) * KREL, 1, KREL, 0, KREL, self.tmp, 0, 0)
        self.shared("vec", B_OUT * D, 1, D, 0, self.tall, MASK_LANE, 0)

    def points(self, p1, p2):
        load_tiles(p1, self.wide)
        load_tiles(p2, self.tall)
        for half in range(2):
            self.shared("p1", 0, D, 2 * D, half * D, self.wide, 0, half * DP)
            self.shared("pb1", half * D, 1, D, 0, self.wide, 240, half * DP)
        self.shared("p2", 0, D, D, 0, self.tall, 0, 0)
        self.shared("pb2", 0, 1, D, 0, self.tall, 240, 0)

    def vectors(self, vec, vec2):
        for t in range(2):
            cols = pl.ds(t * LANES, LANES)
            self.tall[t, pl.ds(0, VEC_ROWS), :] = vec[:, cols] + vec2[:, cols]
        for row in range(2, 10):
            self.shared("vec", row * D, 1, D, 0, self.tall, row, 0)
        self.shared("taps", 0, 16, D, 0, self.tall, TAPS, 0)
        self.shared("bg", 0, 1, D, 0, self.tall, BATCH_GAIN, 0)
        self.shared("bb", 0, 1, D, 0, self.tall, BATCH_BIAS, 0)

    def first_norm(self, vec):
        for t in range(2):
            self.tall[t, pl.ds(0, 8), :] = vec[pl.ds(0, 8), pl.ds(t * LANES, LANES)]
        for row in (FFA, FFA + 1):
            self.shared("vec", row * D, 1, D, 0, self.tall, row, 0)

    def slots(self, out, z, kind):
        for i in range(4 * z, 4 * z + 4):
            for g in range(2):
                if kind == 0:
                    out[g, i, pl.ds(0, self.hr), :] = self.fh[g, pl.ds(i * self.head_size // LANES, self.hr), :].astype(BF)
                else:
                    at = (2 * i + g) * self.shared_size // LANES
                    out[g, i, pl.ds(self.hr, self.sr), :] = self.fs[pl.ds(at, self.sr), :].astype(BF)

    def groups(self):
        size = 4 * self.head_size
        every = range(self.dp // 4)
        one = [z for z in every if z * size >= self.hp["up2"] and (z + 1) * size <= self.hp["wq"]]
        two = [z for z in every if z * size >= self.hp["dn1"] and z not in one]
        late = [z for z in every if 8 * z * self.shared_size < 2 * D]
        return one, two, [z for z in every if z not in one and z not in two], [z for z in every if z not in late], late


def row_sum(x):
    return jnp.sum(x, -1, keepdims=True)


def halves(x):
    return x[:, :LANES], x[:, LANES:]


def both(lo, hi):
    return jnp.concatenate([lo, hi], 1)


def norm(x, gain, bias):
    lane = lane_iota((1, LANES))
    lo, hi = halves(x)
    mean = row_sum(lo + hi) * (1.0 / D)
    lo = lo - mean
    hi = jnp.where(lane < D - LANES, hi - mean, 0.0)
    inv = lax.rsqrt(row_sum(lo * lo + hi * hi) * (1.0 / D) + NORM_EPS)
    lo, hi = lo * inv, hi * inv
    return both(lo, hi) * gain + bias, both(lo, jnp.where(lane == LANES - 1, inv, hi))


def norm_grad(grad, kept, gain):
    dg = grad * gain
    inv = kept[:, DP - 1 :]
    first = row_sum(dg) * (1.0 / D)
    second = row_sum(dg * kept) * (1.0 / D)
    return inv * (dg - first - kept * second)


def fold_rows(x):
    return jnp.sum(x.reshape(x.shape[0] // 8, 8, x.shape[1]), 0)


def norm_param_grads(acc, row, grad, kept):
    acc[row] += fold_rows(grad * kept)
    acc[row + 1] += fold_rows(grad)


def settle(acc, out):
    for row in range(acc.shape[0]):
        out[pl.ds(row, 1), :] = jnp.sum(acc[row], 0, keepdims=True)


def silu_pair(y):
    p = jnp.tanh(y) + 1.0
    h = (y * p).astype(BF)
    p = p.astype(BF)
    return h, p + h * (2.0 - p)


def widen(x):
    rows = x.shape[0]
    return jnp.concatenate([x.astype(F32), jnp.zeros((rows, DP - D), F32)], 1)


def head_lanes():
    lane = lane_iota((1, LANES))
    return lane < HD, (lane >= HD) & (lane < 2 * HD), lane == MASK_LANE


def valid_rows(lengths, at, length):
    return lax.broadcasted_iota(jnp.int32, (length, 1), 0) < lengths[at]


def phase_a_kernel(
    seqs, lengths, frames, up, dn, wqkv, wo, p1, vec, rel,
    kept1_o, a1_o, h_o, sp_o, kept2_o, a2_o, qkv_o, e_o, rl_o, m_o,
    x2_o, kept3_o, a3_o, f1_o, f2_o, gl_o, w_o, keep_o,
    pad, stats_o, inbox, ss, rs,
):
    step = pl.program_id(0)
    total = inbox.shape[0]

    @pl.when(step == 0)
    def _():
        greet_all(total)

    length = frames.shape[1]
    tokens = seqs * length
    first_seq = lax.axis_index("head") * (seqs * pl.num_programs(0)) + step * seqs

    def v(row):
        return vec[pl.ds(row, 1), :]

    x0 = widen(frames[...].reshape(tokens, D))
    a, kept1_o[...] = norm(x0, v(FFA), v(FFA + 1))
    a = a.astype(BF)
    a1_o[...] = a
    h, slope = silu_pair(dot(a, up[...]))
    h_o[...] = h
    sp_o[...] = slope
    x1 = x0 + dot(h, dn[...])
    a, kept2_o[...] = norm(x1, v(ATT), v(ATT + 1))
    a = a.astype(BF)
    a2_o[...] = a
    qkv = dot(a, wqkv[...])
    first, second, special = head_lanes()
    for b in range(seqs):
        rows = pl.ds(b * length, length)
        fence = jnp.where(valid_rows(lengths, first_seq + b, length), 0.0, NEG)
        for g in range(2):
            def piece(which):
                at = which * DP + g * LANES
                return qkv[b * length : (b + 1) * length, at : at + LANES]

            q = (piece(0) * (SCALE * LOG2E)).astype(BF)
            k = jnp.where(special, fence, piece(1)).astype(BF)
            vv = piece(2).astype(BF)
            qkv_o[rows, pl.ds(g * LANES, LANES)] = q
            qkv_o[rows, pl.ds(DP + g * LANES, LANES)] = k
            qkv_o[rows, pl.ds(2 * DP + g * LANES, LANES)] = vv
            zero = jnp.zeros_like(q)
            pair = jnp.concatenate([jnp.where(first | special, q, zero), jnp.where(second | special, q, zero)], 0)
            at = pl.ds(2 * g * length, 2 * length)
            s = dot_t(pair, k) + rel[at, :]
            e = jnp.exp2(s - jnp.max(s, -1, keepdims=True)).astype(BF)
            e_o[b, at, :] = e
            o = dot(e, vv)
            r = 1.0 / o[:, MASK_LANE : MASK_LANE + 1]
            shares = jnp.where(second, r[length:], r[:length])
            rl_o[rows, pl.ds(g * LANES, LANES)] = shares
            m_o[rows, pl.ds(g * LANES, LANES)] = (jnp.where(second, o[length:], o[:length]) * shares).astype(BF)
    x2 = x1 + dot(m_o[...], wo[...])
    x2_o[...] = x2
    a, kept3_o[...] = norm(x2, v(CNV), v(CNV + 1))
    a = a.astype(BF)
    a3_o[...] = a
    e = dot(a, p1[...])
    half = KW // 2

    @pl.when(step == 0)
    def _():
        pad[...] = jnp.zeros(pad.shape, F32)
        stats_o[...] = jnp.zeros(stats_o.shape, F32)

    count = jnp.float32(0.0)
    summed = jnp.zeros((1, DP), F32)
    for b in range(seqs):
        rows = pl.ds(b * length, length)
        valid = jnp.where(valid_rows(lengths, first_seq + b, length), 1.0, 0.0)
        linear = e[b * length : (b + 1) * length, :DP]
        gate = 0.5 * jnp.tanh(0.5 * e[b * length : (b + 1) * length, DP:]) + 0.5
        f1 = gate * valid
        gl = linear * f1
        f1_o[rows, :] = f1.astype(BF)
        f2_o[rows, :] = (gl * (1.0 - gate)).astype(BF)
        gl_o[rows, :] = gl.astype(BF)
        for t in range(2):
            cols = pl.ds(t * LANES, LANES)
            pad[b, t, pl.ds(8, length), :] = gl[:, t * LANES : (t + 1) * LANES]
            acc = jnp.broadcast_to(vec[pl.ds(DEPTH_BIAS, 1), cols], (length, LANES))
            for r in range(KW):
                acc = acc + pad[b, t, pl.ds(8 - half + r, length), :] * vec[pl.ds(TAPS + r, 1), cols]
            w_o[rows, cols] = acc
        summed = summed + jnp.sum(w_o[rows, :] * valid, 0, keepdims=True)
        count = count + lengths[first_seq + b].astype(F32)
    mean = summed / count
    square = jnp.zeros((1, DP), F32)
    for b in range(seqs):
        valid = jnp.where(valid_rows(lengths, first_seq + b, length), 1.0, 0.0)
        centre = (w_o[pl.ds(b * length, length), :] - mean) * valid
        square = square + jnp.sum(centre * centre, 0, keepdims=True)
    old = stats_o[pl.ds(4, 1), :]
    new = old + count
    for t in range(2):
        cols = slice(t * LANES, (t + 1) * LANES)
        before = stats_o[pl.ds(t, 1), :]
        delta = mean[:, cols] - before
        stats_o[pl.ds(t, 1), :] = before + delta * (count / new)
        stats_o[pl.ds(2 + t, 1), :] += square[:, cols] + delta * delta * (old * count / new)
    stats_o[pl.ds(4, 1), :] = new

    @pl.when(step == pl.num_programs(0) - 1)
    def _():
        share_start(total, stats_o, inbox, ss, rs)
        share_finish(total, stats_o, inbox, ss, rs)
        batch_stats(inbox[...], keep_o)


def batch_stats(shared, keep):
    counts = shared[:, 4:5, :]
    total = jnp.sum(counts, 0)
    means, spreads = [], []
    for t in range(2):
        each = shared[:, t : t + 1, :]
        mean = jnp.sum(each * counts, 0) / total
        spread = (jnp.sum(shared[:, 2 + t : 3 + t, :], 0) + jnp.sum(counts * (each - mean) ** 2, 0)) / total
        means.append(mean)
        spreads.append(spread)
    keep[pl.ds(0, 1), :] = jnp.concatenate(means, 1)
    keep[pl.ds(1, 1), :] = lax.rsqrt(jnp.concatenate(spreads, 1) + NORM_EPS)
    keep[pl.ds(2, 1), :] = jnp.concatenate([total, total], 1)
    keep[pl.ds(3, 5), :] = jnp.zeros((5, DP), F32)


def phase_b_kernel(
    seqs, keep, w, x2, cotangent, p2, up, dn, vec,
    out_o, dy_o, dx3_o, dup_o, ddn_o, dp2_o, vec_o, keep_o,
    acc, a_all, du_all, do_all, h_all, hc_all, dc_all, sums_o, inbox, ss, rs,
):
    step = pl.program_id(0)
    total = inbox.shape[0]
    length = cotangent.shape[1]
    tokens = seqs * length
    at = pl.ds(pl.multiple_of(step * tokens, tokens), tokens)

    @pl.when(step == 0)
    def _():
        greet_all(total)
        for ref in (dup_o, ddn_o, dp2_o, acc):
            ref[...] = jnp.zeros(ref.shape, F32)

    def v(row):
        return vec[pl.ds(row, 1), :]

    mean, inv_batch = keep[pl.ds(0, 1), :], keep[pl.ds(1, 1), :]
    z = (w[...] - mean) * inv_batch
    hc, slope_c = silu_pair(z * (0.5 * v(BATCH_GAIN)) + 0.5 * v(BATCH_BIAS))
    x3 = x2[...] + dot(hc, p2[...])
    a, kept = norm(x3, v(FFB), v(FFB + 1))
    a = a.astype(BF)
    h, slope = silu_pair(dot(a, up[...]))
    x4 = x3 + dot(h, dn[...])
    final, kept4 = norm(x4, v(OUT), v(OUT + 1))
    out_o[...] = final[:, :D].astype(BF).reshape(seqs, length, D)
    g = widen(cotangent[...].reshape(tokens, D))
    norm_param_grads(acc, OUT, g, kept4)
    dx4 = norm_grad(g, kept4, v(OUT))
    do = dx4.astype(BF)
    do_all[at, :] = do
    h_all[at, :] = h
    du = dot_t(do, dn[...]).astype(BF) * slope
    a_all[at, :] = a
    du_all[at, :] = du
    da = dot_t(du, up[...])
    norm_param_grads(acc, FFB, da, kept)
    dx3 = dx4 + norm_grad(da, kept, v(FFB))
    dx3_o[...] = dx3
    dc = dx3.astype(BF)
    hc_all[at, :] = hc
    dc_all[at, :] = dc
    dy = dot_t(dc, p2[...]) * slope_c.astype(F32)
    dy_o[...] = dy
    acc[BATCH_BIAS] += fold_rows(dy)
    acc[BATCH_GAIN] += fold_rows(dy * z)

    @pl.when(step == pl.num_programs(0) - 1)
    def _():
        acc[BATCH_BIAS] *= 0.5
        acc[BATCH_GAIN] *= 0.5
        settle(acc, vec_o)
        for row, source in ((0, BATCH_BIAS), (2, BATCH_GAIN)):
            line = vec_o[pl.ds(source, 1), :]
            for t in range(2):
                sums_o[pl.ds(row + t, 1), :] = line[:, t * LANES : (t + 1) * LANES]

    @pl.when(step == pl.num_programs(0) - 1)
    def _():
        share_start(total, sums_o, inbox, ss, rs)

        @pl.loop(0, pl.num_programs(0))
        def _(k):
            at = pl.ds(pl.multiple_of(k * tokens, tokens), tokens)
            ddn_o[...] += t_dot(do_all[at, :], h_all[at, :])
            dup_o[...] += t_dot(a_all[at, :], du_all[at, :])
            dp2_o[...] += t_dot(hc_all[at, :], dc_all[at, :])

        share_finish(total, sums_o, inbox, ss, rs)
        sums = jnp.sum(inbox[...], 0)
        keep_o[...] = keep[...]
        keep_o[pl.ds(3, 1), :] = jnp.concatenate([sums[0:1], sums[1:2]], 1)
        keep_o[pl.ds(4, 1), :] = jnp.concatenate([sums[2:3], sums[3:4]], 1)


def phase_c_kernel(
    seqs, steps, sizes, lengths, keep, w, dy, dx3, gl, f1, f2, a3, kept3, qkv, e_all, rl, m, a2, kept2, h, slope, a1, kept1,
    p1, wo, wqkv, dn, up, vec, dup2, ddn2, dp2, vec2,
    dx0_o, sum_o,
    dp1_o, dwo_o, dqkv_o, dup_o, ddn_o, vec_o, rel_o, dx1_buf, mine,
    acc, padw, padg, grads, *refs,
):
    step = pl.program_id(0)
    length = dx0_o.shape[1]
    flat = Flat(*sizes, refs[:5])
    nz = sizes[0] // 4
    scatter = Scatter(nz, flat.hr, flat.sr, mine, refs[5:])
    one, two, rest, shared_two, shared_rest = flat.groups()

    @pl.when(step == 0)
    def _():
        greet(nz, scatter.me, scatter.core, scatter.zc, scatter.yc, scatter.xc)
        for ref in (dp1_o, dwo_o, dqkv_o, dup_o, ddn_o, acc, rel_o, padw, padg):
            ref[...] = jnp.zeros(ref.shape, F32)
        flat.clear_unused()
        flat.up(dup2, "up2", "upb2")
        flat.down(ddn2, "dn2", DOWNB_TWO)
        for z in one:
            flat.slots(scatter.g, z, 0)
        greeted(nz)
        for z in one:
            scatter.stage_core(z, 0)

    @pl.when(step < steps)
    def _():
        phase_c_first(
            seqs, step, steps, length, lengths, keep, w, dy, dx3, gl, f1, f2, a3, kept3, qkv, e_all, rl, m, a2, kept2,
            h, p1, wo, wqkv, vec, dp1_o, dwo_o, dqkv_o, ddn_o, rel_o, dx1_buf, acc, padw, padg, grads,
        )

    @pl.when(step == steps)
    def _():
        flat.attention(dqkv_o, dwo_o, rel_o)
        flat.down(ddn_o, "dn1", DOWNB_ONE)
        for z in two:
            flat.slots(scatter.g, z, 0)
            scatter.stage_core(z, 0)
        settle(acc, vec_o)
        flat.points(dp1_o, dp2)
        flat.vectors(vec_o, vec2)
        for z in shared_two:
            flat.slots(scatter.g, z, 1)
            scatter.stage_core(z, 1)

    @pl.when(step >= steps)
    def _():
        at = pl.ds(pl.multiple_of((step - steps) * (seqs * length), seqs * length), seqs * length)
        dx1 = dx1_buf[at, :]
        du = dot_t(dx1.astype(BF), dn[...]).astype(BF) * slope[...]
        dup_o[...] += t_dot(a1[...], du)
        da = dot_t(du, up[...])
        norm_param_grads(acc, FFA, da, kept1[...])
        dx0 = dx1 + norm_grad(da, kept1[...], vec[pl.ds(FFA, 1), :])
        dx0_o[...] = dx0[:, :D].reshape(seqs, length, D)

    stages = (scatter.stage_first, scatter.stage_second, scatter.stage_third)
    for at, heads, shared in (((1, 3, 5), one, []), ((steps + AT_A, steps + AT_B), two, shared_two)):
        for when, stage in zip(at, stages):
            @pl.when(step == when)
            def _():
                for z in heads:
                    stage(z, 0)
                for z in shared:
                    stage(z, 1)

    @pl.when(step == 2 * steps - 1)
    def _():
        flat.up(dup_o, "up1", "upb1")
        for z in rest:
            flat.slots(scatter.g, z, 0)
            scatter.stage_core(z, 0)
        settle(acc, vec_o)
        flat.first_norm(vec_o)
        for z in shared_rest:
            flat.slots(scatter.g, z, 1)
            scatter.stage_core(z, 1)
        for z in two:
            scatter.stage_third(z, 0)
        for z in shared_two:
            scatter.stage_third(z, 1)
        for stage in stages:
            for z in rest:
                stage(z, 0)
            for z in shared_rest:
                stage(z, 1)
        scatter.finish(sum_o)


def phase_c_first(
    seqs, step, steps, length, lengths, keep, w, dy, dx3, gl, f1, f2, a3, kept3, qkv, e_all, rl, m, a2, kept2,
    h, p1, wo, wqkv, vec, dp1_o, dwo_o, dqkv_o, ddn_o, rel_o, dx1_buf, acc, padw, padg, grads,
):
    first_seq = lax.axis_index("head") * (seqs * steps) + step * seqs
    half = KW // 2

    def v(row):
        return vec[pl.ds(row, 1), :]

    mean, inv_batch, count = (keep[pl.ds(row, 1), :] for row in range(3))
    scale = v(BATCH_GAIN) * inv_batch
    cross = inv_batch * scale * keep[pl.ds(4, 1), :] / count
    plain = scale * keep[pl.ds(3, 1), :] / count - mean * cross
    scale = 0.5 * scale
    for b in range(seqs):
        rows = pl.ds(b * length, length)
        valid = jnp.where(valid_rows(lengths, first_seq + b, length), 1.0, 0.0)
        dw = dy[rows, :] * scale - valid * (plain + w[rows, :] * cross)
        acc[DEPTH_BIAS] += fold_rows(dw)
        for t in range(2):
            cols = pl.ds(t * LANES, LANES)
            here = dw[:, t * LANES : (t + 1) * LANES]
            padw[b, t, pl.ds(8, length), :] = here
            padg[b, t, pl.ds(8, length), :] = gl[rows, cols].astype(F32)
            total = jnp.zeros((length, LANES), F32)
            for r in range(KW):
                total = total + padw[b, t, pl.ds(8 + half - r, length), :] * vec[pl.ds(TAPS + r, 1), cols]
                tap = here * padg[b, t, pl.ds(8 - half + r, length), :]
                acc[TAPS + r, :, cols] += fold_rows(tap)
            grads[rows, cols] = (total * f1[rows, cols].astype(F32)).astype(BF)
            grads[rows, pl.ds(DP + t * LANES, LANES)] = (total * f2[rows, cols].astype(F32)).astype(BF)
    de = grads[:, pl.ds(0, 2 * DP)]
    dp1_o[...] += t_dot(a3[...], de)
    da = dot_t(de, p1[...])
    norm_param_grads(acc, CNV, da, kept3[...])
    dx2 = dx3[...] + norm_grad(da, kept3[...], v(CNV))
    db = dx2.astype(BF)
    dwo_o[...] += t_dot(m[...], db)
    dm = dot_t(db, wo[...])
    first, second, special = head_lanes()
    source = lax.broadcasted_iota(jnp.int32, (LANES, 2 * LANES), 0)
    target = lane_iota((LANES, 2 * LANES)) // LANES
    spread = jnp.where((source >= target * HD) & (source < (target + 1) * HD), 1.0, 0.0).astype(BF)
    for b in range(seqs):
        rows = pl.ds(b * length, length)
        for g in range(2):
            cols = pl.ds(g * LANES, LANES)
            q = qkv[rows, cols]
            k = qkv[rows, pl.ds(DP + g * LANES, LANES)]
            vv = qkv[rows, pl.ds(2 * DP + g * LANES, LANES)]
            dmb = (dm[b * length : (b + 1) * length, g * LANES : (g + 1) * LANES] * rl[rows, cols]).astype(BF)
            level = dot(dmb * m[rows, cols], spread)
            level = jnp.concatenate([level[:, :LANES], level[:, LANES:]], 0)
            zero = jnp.zeros_like(q)
            dm_pair = jnp.concatenate([jnp.where(first, dmb, zero), jnp.where(second, dmb, zero)], 0)
            q_pair = jnp.concatenate([jnp.where(first, q, zero), jnp.where(second, q, zero)], 0)
            at = pl.ds(2 * g * length, 2 * length)
            e = e_all[b, at, :]
            dp = dot_t(dm_pair, vv)
            ds = e.astype(F32) * (dp - jnp.concatenate([level, level[:, : length - LANES]], 1))
            rel_o[at, :] += ds
            ds = ds.astype(BF)
            dq = dot(ds, k)
            dq = jnp.where(second, dq[length:], dq[:length])
            grads[rows, cols] = (dq * SCALE).astype(BF)
            grads[rows, pl.ds(DP + g * LANES, LANES)] = (t_dot(ds, q_pair) * LN2).astype(BF)
            grads[rows, pl.ds(2 * DP + g * LANES, LANES)] = t_dot(e, dm_pair).astype(BF)
    dqkv = grads[...]
    dqkv_o[...] += t_dot(a2[...], dqkv)
    da = dot_t(dqkv, wqkv[...])
    norm_param_grads(acc, ATT, da, kept2[...])
    dx1 = dx2 + norm_grad(da, kept2[...], v(ATT))
    at = pl.ds(pl.multiple_of(step * (seqs * length), seqs * length), seqs * length)
    dx1_buf[at, :] = dx1
    ddn_o[...] += t_dot(dx1.astype(BF), h[...])


def layer_call(body, steps, ins, outs, scratch, name, collective_id=None):
    def spec(item):
        kind, shape = item
        if kind == "smem":
            return pl.BlockSpec(memory_space=pltpu.SMEM)
        if kind == "tile":
            return pl.BlockSpec(shape, lambda i: (i,) + (0,) * (len(shape) - 1))
        if kind == "early":
            return pl.BlockSpec(shape, lambda i: (jnp.minimum(i, steps // 2 - 1),) + (0,) * (len(shape) - 1))
        if kind == "late":
            return pl.BlockSpec(shape, lambda i: (jnp.maximum(i - steps // 2, 0),) + (0,) * (len(shape) - 1))
        return pl.BlockSpec(shape, lambda i: (0,) * len(shape))

    arrays = [a for _, _, a in ins]
    return pl.pallas_call(
        body,
        grid=(steps,),
        out_shape=tuple(jax.ShapeDtypeStruct(full, dtype) for _, _, full, dtype in outs),
        in_specs=[spec((kind, block)) for kind, block, _ in ins],
        out_specs=tuple(spec((kind, block)) for kind, block, _, _ in outs),
        scratch_shapes=list(scratch),
        compiler_params=pltpu.CompilerParams(
            vmem_limit_bytes=BIG,
            dimension_semantics=("arbitrary",),
            collective_id=collective_id,
            has_side_effects=collective_id is not None,
        ),
        name=name,
    )(*arrays)


def tile_in(array, steps, kind="tile"):
    return (kind, (array.shape[0] // steps,) + array.shape[1:], array)


def whole_in(array):
    return ("whole", array.shape, array)


def tile_out(steps, shape, dtype, kind="tile"):
    return (kind, (shape[0] // steps,) + shape[1:], shape, dtype)


def whole_out(shape, dtype=F32):
    return ("whole", shape, shape, dtype)


SEQS_A = 2
SEQS_B = 4
SEQS_C = 2
AT_A = 4
AT_B = 7


def per_device(
    frames, cotangent, lengths, head_params, shared_params, head_first, head_second, shared_first, shared_second
):
    seq_here, length, _ = frames.shape
    tokens = seq_here * length
    dp = lax.axis_size("dp")
    head_size, shared_size = head_params.shape[1], shared_params.shape[0]
    rows = slot_rows(head_size) + slot_rows(shared_size)
    vm = pltpu.VMEM
    mine = vmem_call(
        align_kernel, jax.ShapeDtypeStruct((rows, LANES), BF), (head_params, shared_params), name="align"
    )
    got = gather_all(mine, dp, 1)
    up1, dn1, up2, dn2, wqkv, wo, p1, p2, vec, rel = make_weights(got, head_size, shared_size, length)

    dma = pltpu.SemaphoreType.DMA
    sharing = [vm((8, LANES), F32), vm((2 * dp, 8, LANES), F32), dma((2 * dp,)), dma((2 * dp,))]
    steps = seq_here // SEQS_A
    t = functools.partial(tile_out, steps)
    (
        kept1, a1, h1, slope1, kept2, a2, qkv, e_all, rl, m, x2, kept3, a3, f1, f2, gl, w, keep
    ) = layer_call(
        functools.partial(phase_a_kernel, SEQS_A),
        steps,
        [("smem", None, lengths), tile_in(frames, steps)] + [whole_in(x) for x in (up1, dn1, wqkv, wo, p1, vec, rel)],
        [
            t((tokens, DP), F32), t((tokens, DP), BF), t((tokens, FFP), BF), t((tokens, FFP), BF),
            t((tokens, DP), F32), t((tokens, DP), BF), t((tokens, 3 * DP), BF),
            t((seq_here, HEADS * length, length), BF), t((tokens, DP), F32), t((tokens, DP), BF),
            t((tokens, DP), F32), t((tokens, DP), F32), t((tokens, DP), BF), t((tokens, DP), BF),
            t((tokens, DP), BF), t((tokens, DP), BF), t((tokens, DP), F32), whole_out((8, DP)),
        ],
        [vm((SEQS_A, 2, length + 16, LANES), F32)] + sharing,
        "phase_a",
        2,
    )
    steps = seq_here // SEQS_B
    t = functools.partial(tile_out, steps)
    early, dy, dx3, dup2, ddn2, dp2, vec_b, keep = layer_call(
        functools.partial(phase_b_kernel, SEQS_B),
        steps,
        [whole_in(keep), tile_in(w, steps), tile_in(x2, steps), tile_in(cotangent, steps)]
        + [whole_in(x) for x in (p2, up2, dn2, vec)],
        [
            t((seq_here, length, D), BF), t((tokens, DP), F32), t((tokens, DP), F32),
            whole_out((DP, FFP)), whole_out((DP, FFP)), whole_out((DP, DP)), whole_out((VEC_ROWS, DP)),
            whole_out((8, DP)),
        ],
        [
            vm((VEC_ROWS, 8, DP), F32), vm((tokens, DP), BF), vm((tokens, FFP), BF), vm((tokens, DP), BF),
            vm((tokens, FFP), BF), vm((tokens, DP), BF), vm((tokens, DP), BF),
        ]
        + sharing,
        "phase_b",
        3,
    )
    steps = seq_here // SEQS_C
    slot = (slot_rows(head_size), slot_rows(shared_size))
    block = SEQS_C * length
    input_grad, summed = layer_call(
        functools.partial(phase_c_kernel, SEQS_C, steps, (dp, head_size, shared_size)),
        2 * steps,
        [("smem", None, lengths), whole_in(keep)]
        + [tile_in(x, steps, "early") for x in (w, dy, dx3, gl, f1, f2, a3, kept3, qkv, e_all, rl, m, a2, kept2, h1)]
        + [tile_in(x, steps, "late") for x in (slope1, a1, kept1)]
        + [whole_in(x) for x in (p1, wo, wqkv, dn1, up1, vec, dup2, ddn2, dp2, vec_b)],
        [tile_out(steps, (seq_here, length, D), F32, "late"), whole_out((rows, LANES))],
        [
            vm((DP, 2 * DP), F32), vm((DP, DP), F32), vm((DP, 3 * DP), F32), vm((DP, FFP), F32), vm((DP, FFP), F32),
            vm((VEC_ROWS, DP), F32), vm((HEADS * length, length), F32), vm((tokens, DP), F32), vm((rows, LANES), F32),
            vm((VEC_ROWS, 8, DP), F32),
            vm((SEQS_C, 2, length + 16, LANES), F32),
            vm((SEQS_C, 2, length + 16, LANES), F32),
            vm((block, 3 * DP), BF),
        ]
        + Flat.scratch(dp, head_size, shared_size)
        + Scatter.scratch(dp, *slot),
        "phase_c",
        4,
    )
    h_shape, s_shape = head_params.shape, shared_params.shape
    steps = 4
    return layer_call(
        adam_kernel,
        steps,
        [tile_in(x, steps) for x in (early, input_grad)]
        + [whole_in(x) for x in (summed, head_params, head_first, head_second, shared_params, shared_first, shared_second)],
        [tile_out(steps, early.shape, BF), tile_out(steps, early.shape, F32)]
        + [whole_out(h_shape)] * 3
        + [whole_out(h_shape, BF)]
        + [whole_out(s_shape)] * 3
        + [whole_out(s_shape, BF)],
        [],
        "adam",
    )


def solution(mesh):
    frames = P(("dp", "head"), None, None)
    heads = P("head", "dp")
    shared = P(("dp", "head"))
    return jax.shard_map(
        per_device,
        mesh=mesh,
        in_specs=(frames, frames, P("dp"), heads, shared, heads, heads, shared, shared),
        out_specs=(frames, frames) + (heads,) * 4 + (shared,) * 4,
        check_vma=False,
    )
```

```python
import functools
import math

import jax
import jax.numpy as jnp
from jax import lax
from jax.experimental import pallas as pl
from jax.experimental.pallas import tpu as pltpu
from jax.sharding import PartitionSpec as P

BF = jnp.bfloat16
F32 = jnp.float32
LANES = 128


def up_to(count, unit):
    return -(-count // unit) * unit


def grid_place(nz):
    me = lax.axis_index("dp")
    core = lax.axis_index("head")
    zc = me // 4
    rest = me - 4 * zc
    yc = rest // 2
    xc = rest - 2 * yc
    return me, core, zc, yc, xc


def remote(src, dst, send, recv, dp, head):
    return pltpu.make_async_remote_copy(
        src_ref=src,
        dst_ref=dst,
        send_sem=send,
        recv_sem=recv,
        device_id={"dp": dp, "head": head},
        device_id_type=pl.DeviceIdType.MESH,
    )


def greet(nz, me, core, zc, yc, xc):
    barrier = pltpu.get_barrier_semaphore()

    def hello(dp, head):
        pl.semaphore_signal(
            barrier, inc=1, device_id={"dp": dp, "head": head}, device_id_type=pl.DeviceIdType.MESH
        )

    for k in range(1, nz):
        hello(lax.rem(zc + k, nz) * 4 + 2 * yc + xc, core)
    hello(4 * zc + 2 * (1 - yc) + xc, core)
    hello(4 * zc + 2 * yc + 1 - xc, core)
    hello(me, 1 - core)


def greeted(nz):
    pl.semaphore_wait(pltpu.get_barrier_semaphore(), nz + 2)


def gather(nz, src, out, sems, merge):
    sz, rz, s1, r1, s2, r2, sc, rc = sems
    rows = src.shape[0]
    row_a = up_to(rows // 2, 16)
    parts = (pl.ds(0, row_a), pl.ds(row_a, rows - row_a))
    me, core, zc, yc, xc = grid_place(nz)
    out[me, core] = src[...]
    y_peer = 4 * zc + 2 * (1 - yc) + xc
    x_peer = 4 * zc + 2 * yc + 1 - xc
    firsts = (y_peer, x_peer)
    seconds = (x_peer, y_peer)
    pending = []

    def send(slot, p, send_sem, recv_sem, dp, head):
        block = out.at[slot, core, parts[p]]
        copy = remote(block, block, send_sem, recv_sem, dp, head)
        copy.start()
        pending.append(copy)

    def arrived(slot, which, p, send_sem, recv_sem):
        block = out.at[slot, which, parts[p]]
        remote(block, block, send_sem, recv_sem, me, 1 - core).wait_recv()

    zs = [lax.rem(zc + k, nz) for k in range(nz)]
    here = 2 * yc + xc
    first_here = (2 * (1 - yc) + xc, 2 * yc + 1 - xc)
    second_here = ((2 * yc + 1 - xc, 2 * (1 - yc) + 1 - xc), (2 * (1 - yc) + xc, 2 * (1 - yc) + 1 - xc))
    for k in range(1, nz):
        for p in (0, 1):
            send(me, p, sz.at[p, k], rz.at[p, zc], zs[k] * 4 + here, core)
    for k in range(nz):
        z = zs[k]
        slot = 4 * z + here
        for p in (0, 1):
            if k:
                arrived(slot, core, p, sz.at[p, k], rz.at[p, z])
            send(slot, p, s1.at[p, k], r1.at[p, z], firsts[p], core)
            send(slot, p, s2.at[p, k, 0], r2.at[p, z, 0], seconds[p], core)
            send(slot, p, sc.at[p, k, 0], rc.at[p, z, 0], me, 1 - core)
    for k in range(nz):
        for p in (0, 1):
            merge(4 * zs[k] + here, core, p)
    for k in range(nz):
        z = zs[k]
        for p in (0, 1):
            slot = 4 * z + first_here[p]
            arrived(slot, core, p, s1.at[p, k], r1.at[p, z])
            send(slot, p, s2.at[p, k, 1], r2.at[p, z, 1], seconds[p], core)
            send(slot, p, sc.at[p, k, 1], rc.at[p, z, 1], me, 1 - core)
    for k in range(nz):
        for p in (0, 1):
            merge(4 * zs[k] + first_here[p], core, p)
    for k in range(nz):
        z = zs[k]
        for b in (0, 1):
            for p in (0, 1):
                slot = 4 * z + second_here[p][b]
                arrived(slot, core, p, s2.at[p, k, b], r2.at[p, z, b])
                send(slot, p, sc.at[p, k, 2 + b], rc.at[p, z, 2 + b], me, 1 - core)
        for b in (0, 1):
            for p in (0, 1):
                merge(4 * z + second_here[p][b], core, p)
    for k in range(nz):
        z = zs[k]
        for p in (0, 1):
            for b, at in enumerate((here, first_here[p]) + second_here[p]):
                arrived(4 * z + at, 1 - core, p, sc.at[p, k, b], rc.at[p, z, b])
                merge(4 * z + at, 1 - core, p)
    for copy in pending:
        copy.wait_send()


def gather_sems(nz):
    dma = pltpu.SemaphoreType.DMA
    return [
        dma((2, nz)), dma((2, nz)), dma((2, nz)), dma((2, nz)),
        dma((2, nz, 2)), dma((2, nz, 2)), dma((2, nz, 4)), dma((2, nz, 4)),
    ]


class Scatter:
    @staticmethod
    def scratch(dp, hr, sr):
        nz, rows = dp // 4, hr + sr
        dma, vm = pltpu.SemaphoreType.DMA, pltpu.VMEM
        return [
            vm((2, dp, rows, LANES), BF), vm((dp, rows, LANES), BF),
            vm((nz, 2, rows, LANES), BF), vm((nz, 2, rows, LANES), BF),
            vm((nz, rows, LANES), BF), vm((nz, rows, LANES), BF),
            vm((nz, rows, LANES), BF), vm((nz, rows, LANES), BF),
            dma((nz, 2)), dma((nz, 2)), dma((3, nz)), dma((3, nz)), dma((3, nz)), dma((3, nz)), dma((3, nz)), dma((3, nz)),
        ]

    def __init__(self, nz, hr, sr, mine, refs):
        self.nz, self.mine = nz, mine
        (
            self.g, self.c1, self.t1, self.rx1, self.t2, self.rx2, self.t3, self.rx3,
            self.sc, self.rc, self.s1, self.r1, self.s2, self.r2, self.s3, self.r3,
        ) = refs
        ha = up_to(hr // 2, 16)
        self.parts = (pl.ds(0, ha), pl.ds(ha, hr - ha), pl.ds(hr, sr))
        self.kinds = (pl.ds(0, hr), pl.ds(hr, sr))
        self.me, self.core, self.zc, self.yc, self.xc = grid_place(nz)
        zc, yc, xc = self.zc, self.yc, self.xc
        y_peer = 4 * zc + 2 * (1 - yc) + xc
        x_peer = 4 * zc + 2 * yc + 1 - xc
        self.firsts = (x_peer, y_peer, x_peer)
        self.seconds = (y_peer, x_peer, y_peer)
        self.second_give = (1 - yc, 1 - xc, 1 - yc)
        self.second_keep = (yc, xc, yc)

    def core_copy(self, z, kind):
        group, rows = pl.ds(4 * z, 4), self.kinds[kind]
        return remote(
            self.g.at[1 - self.core, group, rows], self.c1.at[group, rows],
            self.sc.at[z, kind], self.rc.at[z, kind], self.me, 1 - self.core,
        )

    def first_copy(self, z, p):
        rows = self.parts[p]
        return remote(
            self.t1.at[z, :, rows], self.rx1.at[z, :, rows], self.s1.at[p, z], self.r1.at[p, z], self.firsts[p], self.core
        )

    def second_copy(self, z, p):
        rows = self.parts[p]
        return remote(
            self.t2.at[z, rows], self.rx2.at[z, rows], self.s2.at[p, z], self.r2.at[p, z], self.seconds[p], self.core
        )

    def third_copy(self, z, p):
        rows = self.parts[p]
        return remote(
            self.t3.at[z, rows], self.rx3.at[self.zc, rows], self.s3.at[p, z], self.r3.at[p, self.zc],
            4 * z + 2 * self.yc + self.xc, self.core,
        )

    def place(self, p, z, b):
        return 4 * z + (2 * self.yc + b if p == 1 else 2 * b + self.xc)

    def held(self, z, p, slot):
        rows = self.parts[p]
        return self.g[self.core, slot, rows].astype(F32) + self.c1[slot, rows].astype(F32)

    def partial(self, z, p, b):
        return self.held(z, p, self.place(p, z, b)) + self.rx1[z, b, self.parts[p]].astype(F32)

    def stage_core(self, z, kind):
        self.core_copy(z, kind).start()

    def stage_first(self, z, kind):
        self.core_copy(z, kind).wait_recv()
        for p in ((0, 1), (2,))[kind]:
            for b in (0, 1):
                slot = 4 * z + (2 * (1 - self.yc) + b if p == 1 else 2 * b + 1 - self.xc)
                self.t1[z, b, self.parts[p]] = self.held(z, p, slot).astype(BF)
            self.first_copy(z, p).start()

    def stage_second(self, z, kind):
        for p in ((0, 1), (2,))[kind]:
            self.first_copy(z, p).wait_recv()
            self.t2[z, self.parts[p]] = self.partial(z, p, self.second_give[p]).astype(BF)
            self.second_copy(z, p).start()

    def stage_third(self, z, kind):
        for p in ((0, 1), (2,))[kind]:
            rows = self.parts[p]
            self.second_copy(z, p).wait_recv()
            total = self.partial(z, p, self.second_keep[p]) + self.rx2[z, rows].astype(F32)

            @pl.when(self.zc == z)
            def _():
                self.mine[rows, :] = total

            @pl.when(self.zc != z)
            def _():
                self.t3[z, rows] = total.astype(BF)
                self.third_copy(z, p).start()

    def finish(self, out):
        total = self.mine[...]
        for k in range(1, self.nz):
            sender = lax.rem(self.zc + k, self.nz)
            for p in range(3):
                rows = self.parts[p]
                remote(
                    self.t3.at[sender, rows], self.rx3.at[sender, rows], self.s3.at[p, sender], self.r3.at[p, sender],
                    self.me, 1 - self.core,
                ).wait_recv()
            total = total + self.rx3[sender].astype(F32)
        out[...] = total
        for z in range(self.nz):
            for kind in range(2):
                self.core_copy(z, kind).wait_send()
            for p in range(3):
                self.first_copy(z, p).wait_send()
                self.second_copy(z, p).wait_send()

            @pl.when(self.zc != z)
            def _():
                for p in range(3):
                    self.third_copy(z, p).wait_send()


def peer_of(own, total, k):
    other = lax.rem(own + k, total)
    dp = other // 2
    return other, dp, other - 2 * dp


def own_number():
    return 2 * lax.axis_index("dp") + lax.axis_index("head")


def greet_all(total):
    barrier = pltpu.get_barrier_semaphore()
    own = own_number()

    @pl.loop(1, total)
    def _(k):
        _, dp, head = peer_of(own, total, k)
        pl.semaphore_signal(
            barrier, inc=1, device_id={"dp": dp, "head": head}, device_id_type=pl.DeviceIdType.MESH
        )


def greeted_all(total):
    pl.semaphore_wait(pltpu.get_barrier_semaphore(), total - 1)


def share_start(total, src, inbox, ss, rs):
    own = own_number()
    inbox[own] = src[...]

    @pl.loop(1, total)
    def _(k):
        _, dp, head = peer_of(own, total, k)
        remote(src, inbox.at[own], ss.at[k], rs.at[own], dp, head).start()


def share_finish(total, src, inbox, ss, rs):
    own = own_number()

    @pl.loop(1, total)
    def _(k):
        other, dp, head = peer_of(own, total, k)
        remote(src, inbox.at[other], ss.at[k], rs.at[other], dp, head).wait()


HEADS = 4
HD = 60
FF = 960
KW = 15
STEP = 10
KREL = 383
NORM_EPS = 1e-05
BETA_ONE = 0.9
BETA_TWO = 0.999
LEARN_RATE = 0.1
WEIGHT_DECAY = 0.01
ADAM_EPS = 1e-08
LOG2E = 1.4426950408889634
LN2 = 0.6931471805599453
SCALE = HD ** (-0.5)
UNIT = 1.28125
D = 240
DP = 256
HF = 480
HFP = 512
FFP = 1024
HC = 120
MASK_LANE = 120
NEG = -1e30
FFA, ATT, CNV, FFB, OUT = 0, 2, 4, 6, 8
DOWNB_ONE, DOWNB_TWO, B_OUT, BATCH_GAIN, BATCH_BIAS, TAPS, DEPTH_BIAS = 10, 11, 12, 13, 14, 16, 31
VEC_ROWS = 32
BIG = 60 << 20


def head_places():
    out, at = {}, 0
    for name, size in (
        ("up1", D * HF), ("upb1", HF), ("dn1", HF * D), ("up2", D * HF), ("upb2", HF), ("dn2", HF * D),
        ("wq", D * HC), ("wk", D * HC), ("wv", D * HC), ("bq", HC), ("bv", HC),
        ("rel", 2 * KREL), ("wo", HC * D),
    ):
        out[name] = at
        at += size
    return out, at


def shared_places():
    out, at = {}, 0
    for name, size in (
        ("vec", 13 * D), ("p1", 2 * D * D), ("pb1", 2 * D), ("taps", KW * D), ("db", D),
        ("bg", D), ("bb", D), ("p2", D * D), ("pb2", D),
    ):
        out[name] = at
        at += size
    return out, at


def lane_iota(shape):
    return lax.broadcasted_iota(jnp.int32, shape, len(shape) - 1)


def slot_rows(size):
    return up_to(-(-(size + LANES - 1) // LANES), 16)


def dot(a, b):
    return jnp.dot(a, b, preferred_element_type=F32)


def dot_t(a, b):
    return lax.dot_general(a, b, (((1,), (1,)), ((), ())), preferred_element_type=F32)


def t_dot(a, b):
    return lax.dot_general(a, b, (((0,), (0,)), ((), ())), preferred_element_type=F32)


def vmem_call(body, outs, ins, scratch=(), name=None, limit=BIG):
    return pl.pallas_call(
        body,
        out_shape=outs,
        in_specs=[pl.BlockSpec(memory_space=pltpu.VMEM) for _ in ins],
        out_specs=jax.tree.map(lambda _: pl.BlockSpec(memory_space=pltpu.VMEM), outs),
        scratch_shapes=list(scratch),
        compiler_params=pltpu.CompilerParams(vmem_limit_bytes=limit),
        name=name,
    )(*ins)


def own_offsets(head_size, shared_size):
    me = lax.axis_index("dp")
    core = lax.axis_index("head")
    return lax.rem(me * head_size, LANES), lax.rem((2 * me + core) * shared_size, LANES)


def push_lanes(x, shift):
    rolled = pltpu.roll(x, shift, 1)
    before = jnp.concatenate([jnp.zeros((1, LANES), F32), rolled[:-1]], 0)
    return jnp.where(lane_iota(x.shape) >= shift, rolled, before)


def pull_lanes(x, shift):
    rolled = pltpu.roll(x, lax.rem(LANES - shift, LANES), 1)
    after = jnp.concatenate([rolled[1:], jnp.zeros((1, LANES), F32)], 0)
    return jnp.where(lane_iota(x.shape) < LANES - shift, rolled, after)


def align(head_ref, shared_ref, out):
    head_size, shared_size = head_ref.shape[1], shared_ref.shape[0]
    hr, sr = slot_rows(head_size), slot_rows(shared_size)
    ho, so = own_offsets(head_size, shared_size)
    x = jnp.concatenate([head_ref[...], jnp.zeros((1, hr * LANES - head_size), F32)], 1)
    out[pl.ds(0, hr), :] = push_lanes(x.reshape(hr, LANES), ho).astype(BF)
    x = shared_ref[...].reshape(1, shared_size)
    x = jnp.concatenate([x, jnp.zeros((1, sr * LANES - shared_size), F32)], 1)
    out[pl.ds(hr, sr), :] = push_lanes(x.reshape(sr, LANES), so).astype(BF)


def adam_kernel(
    early, grad, g_ref, hp, hf, hs, sp, sf, ss, out_o, grad_o, hf_o, hs_o, hp_o, hc_o, sf_o, ss_o, sp_o, sc_o
):
    out_o[...] = early[...]
    grad_o[...] = grad[...]

    @pl.when(pl.program_id(0) == 0)
    def _():
        adam_update(g_ref, hp, hf, hs, sp, sf, ss, hf_o, hs_o, hp_o, hc_o, sf_o, ss_o, sp_o, sc_o)


def adam_update(g_ref, hp, hf, hs, sp, sf, ss, hf_o, hs_o, hp_o, hc_o, sf_o, ss_o, sp_o, sc_o):
    head_size, shared_size = hp.shape[1], sp.shape[0]
    hr, sr = slot_rows(head_size), slot_rows(shared_size)
    ho, so = own_offsets(head_size, shared_size)

    def update(master, g, first, second):
        first_new = BETA_ONE * first + (1.0 - BETA_ONE) * g
        second_new = BETA_TWO * second + (1.0 - BETA_TWO) * g * g
        first_hat = first_new * (1.0 / (1.0 - BETA_ONE**STEP))
        second_hat = second_new * (1.0 / (1.0 - BETA_TWO**STEP))
        new = master - LEARN_RATE * (first_hat / (jnp.sqrt(second_hat) + ADAM_EPS) + WEIGHT_DECAY * master)
        return first_new, second_new, new

    g = pull_lanes(g_ref[pl.ds(0, hr), :], ho).reshape(1, hr * LANES)[:, :head_size]
    one, two, new = update(hp[...], g, hf[...], hs[...])
    hf_o[...] = one
    hs_o[...] = two
    hp_o[...] = new
    hc_o[...] = new.astype(BF)
    g = pull_lanes(g_ref[pl.ds(hr, sr), :], so).reshape(sr * LANES)[:shared_size]
    one, two, new = update(sp[...], g, sf[...], ss[...])
    sf_o[...] = one
    ss_o[...] = two
    sp_o[...] = new
    sc_o[...] = new.astype(BF)


def row_phases(rows, pitch):
    if rows == 1:
        return 1, 1, 0
    period = LANES // math.gcd(pitch, LANES)
    return period, rows // period, period * pitch // LANES


def take(flat, at, rows, pitch, col, width, dst, row0, lane0):
    period, count, stride = row_phases(rows, pitch)
    lane = lane_iota((count, LANES))
    for j in range(period):
        start = at + j * pitch + col
        q, l = divmod(start, LANES)

        def load(t):
            if count == 1:
                return flat[pl.ds(q + t, 1), :]
            return flat[pl.ds(q + t, count, stride), :]

        pieces = [load(t) for t in range(-(-(l + width) // LANES))]
        if l:
            pieces = [pltpu.roll(x, LANES - l, 1) for x in pieces]
        for t in range(-(-width // LANES)):
            value = pieces[t]
            if l and t + 1 < len(pieces):
                value = jnp.where(lane < LANES - l, value, pieces[t + 1])
            left = width - t * LANES
            if left < LANES:
                value = jnp.where(lane < left, value, 0.0)
            rows_at = pl.ds(row0 + j, 1) if count == 1 else pl.ds(row0 + j, count, period)
            dst[lane0 // LANES + t, rows_at, :] = value


def give(flat, at, rows, pitch, col, width, src, row0, lane0):
    period, count, stride = row_phases(rows, pitch)
    lane = lane_iota((count, LANES))
    for j in range(period):
        start = at + j * pitch + col
        q, l = divmod(start, LANES)
        rows_at = pl.ds(row0 + j, 1) if count == 1 else pl.ds(row0 + j, count, period)
        pieces = [src[lane0 // LANES + t, rows_at, :] for t in range(-(-width // LANES))]
        if l:
            pieces = [pltpu.roll(x, l, 1) for x in pieces]
        total = -(-(l + width) // LANES)
        for t in range(total):
            here = pl.ds(q + t, 1) if count == 1 else pl.ds(q + t, count, stride)
            if not l:
                value = pieces[t]
            elif t == 0:
                value = pieces[0]
            elif t == len(pieces):
                value = pieces[t - 1]
            else:
                value = jnp.where(lane >= l, pieces[t], pieces[t - 1])
            lo = l if t == 0 else 0
            hi = min(LANES, l + width - t * LANES)
            if lo or hi < LANES:
                keep = (lane >= lo) & (lane < hi)
                value = jnp.where(keep, value, flat[here, :])
            flat[here, :] = value


def spill(tiles, rows, dst, factor=None):
    for t in range(dst.shape[1] // LANES):
        value = tiles[t, pl.ds(0, rows), :]
        if factor:
            value = factor * value
        dst[:, pl.ds(t * LANES, LANES)] = value.astype(dst.dtype)


def load_tiles(src, tiles, factor=None):
    for t in range(src.shape[1] // LANES):
        value = src[:, pl.ds(t * LANES, LANES)]
        tiles[t, pl.ds(0, src.shape[0]), :] = factor * value if factor else value


def flat_rows(total, size):
    return up_to(total // LANES + slot_rows(size) + 16, 16)


class Weights:
    def __init__(self, dp, head_size, shared_size, got, refs):
        self.dp, self.head_size, self.shared_size, self.got = dp, head_size, shared_size, got
        self.hr, self.sr = slot_rows(head_size), slot_rows(shared_size)
        self.fh, self.fs, self.wide, self.tall, self.tmp = refs
        self.hp, _ = head_places()
        self.sp, _ = shared_places()

    def clear_flat(self):
        self.fh[...] = jnp.zeros(self.fh.shape, F32)
        self.fs[...] = jnp.zeros(self.fs.shape, F32)

    def merge(self, slot, core, p):
        rows = self.hr + self.sr
        cut = up_to(rows // 2, 16)
        first = (slot * self.head_size) // LANES
        low, high = ((0, min(cut, self.hr)), (min(cut, self.hr), self.hr))[p]
        if high > low:
            at = pl.ds(first + low, high - low)
            self.fh[core, at, :] += self.got[slot, core, pl.ds(low, high - low), :].astype(F32)
        low, high = ((self.hr, max(cut, self.hr)), (max(cut, self.hr), rows))[p]
        if high > low:
            at = pl.ds(((2 * slot + core) * self.shared_size) // LANES + low - self.hr, high - low)
            self.fs[at, :] += self.got[slot, core, pl.ds(low, high - low), :].astype(F32)

    def clear(self, tiles, count, row, size):
        for t in range(count):
            tiles[t, pl.ds(row, size), :] = jnp.zeros((size, LANES), F32)

    def patch(self, tiles, tile, row, where, value):
        part = tiles[tile, pl.ds(row, 1), :]
        tiles[tile, pl.ds(row, 1), :] = jnp.where(where, value, part)

    def ffn(self, up, dn, up_place, bias_place, dn_place, row):
        wide, tall, hp = self.wide, self.tall, self.hp
        self.clear(wide, 8, 240, 16)
        for g in range(2):
            take(self.fh.at[g], hp[up_place], D, HF, 0, HF, wide, 0, g * HFP)
            take(self.fh.at[g], hp[bias_place], 1, HF, 0, HF, wide, 240, g * HFP)
        self.patch(wide, 3, 240, lane_iota((1, LANES)) == HF - 3 * LANES, UNIT)
        spill(wide, DP, up, 0.5)
        for g in range(2):
            self.clear(tall, 2, g * HFP + HF, 32)
            take(self.fh.at[g], hp[dn_place], HF, D, 0, D, tall, g * HFP, 0)
        take(self.fs, self.sp["vec"] + row * D, 1, D, 0, D, tall, HF, 0)
        spill(tall, FFP, dn, 0.5)

    def point_two(self, p2):
        self.clear(self.tall, 2, 240, 16)
        take(self.fs, self.sp["p2"], D, D, 0, D, self.tall, 0, 0)
        take(self.fs, self.sp["pb2"], 1, D, 0, D, self.tall, 240, 0)
        spill(self.tall, DP, p2)

    def others(self, qkv, wo, p1, vec, rel):
        wide, tall, tmp, fh, fs, hp, sp = self.wide, self.tall, self.tmp, self.fh, self.fs, self.hp, self.sp
        lane = lane_iota((1, LANES))
        self.clear(wide, 6, 240, 16)
        for g in range(2):
            for which, (place, bplace) in enumerate((("wq", "bq"), ("wk", None), ("wv", "bv"))):
                lane0 = which * DP + g * LANES
                take(fh.at[g], hp[place], D, HC, 0, HC, wide, 0, lane0)
                if bplace:
                    take(fh.at[g], hp[bplace], 1, HC, 0, HC, wide, 240, lane0)
        for tile in (0, 1, 4, 5):
            self.patch(wide, tile, 240, lane == MASK_LANE, 1.0)
        spill(wide, DP, qkv)
        self.clear(tall, 2, 0, DP)
        for g in range(2):
            take(fh.at[g], hp["wo"], HC, D, 0, D, tall, g * LANES, 0)
        take(fs, sp["vec"] + B_OUT * D, 1, D, 0, D, tall, MASK_LANE, 0)
        spill(tall, DP, wo)
        self.clear(wide, 4, 240, 16)
        for half in range(2):
            take(fs, sp["p1"], D, 2 * D, half * D, D, wide, 0, half * DP)
            take(fs, sp["pb1"] + half * D, 1, D, 0, D, wide, 240, half * DP)
        spill(wide, DP, p1)
        take(fs, sp["vec"], 16, D, 0, D, tall, 0, 0)
        take(fs, sp["taps"], 16, D, 0, D, tall, TAPS, 0)
        take(fs, sp["bg"], 1, D, 0, D, tall, BATCH_GAIN, 0)
        take(fs, sp["bb"], 1, D, 0, D, tall, BATCH_BIAS, 0)
        for row, value in ((FFA + 1, 1.0), (ATT + 1, 1.0), (CNV + 1, 1.0), (FFB + 1, 1.0), (BATCH_BIAS, UNIT)):
            self.patch(tall, 1, row, lane == D - LANES, value)
        spill(tall, VEC_ROWS, vec)
        length = rel.shape[1]
        for n in range(HEADS):
            take(fh.at[n // 2], hp["rel"] + (n % 2) * KREL, 1, KREL, 0, KREL, tmp, 0, 0)
            row = jnp.concatenate([tmp[t, pl.ds(0, 1), :] for t in range(3)] + [jnp.zeros((1, LANES), F32)], 1)
            rows = jnp.broadcast_to(row, (length, 4 * LANES))
            rows = pltpu.roll(rows, 4 * LANES - (length - 1), 1, stride=1, stride_axis=0)
            rel[pl.ds(n * length, length), :] = rows[:, :length] * LOG2E


class Flat:
    @staticmethod
    def scratch(dp, head_size, shared_size):
        vm = pltpu.VMEM
        return [
            vm((2, flat_rows(head_size * dp, head_size), LANES), F32),
            vm((flat_rows(shared_size * 2 * dp, shared_size), LANES), F32),
            vm((8, DP, LANES), F32),
            vm((2, FFP, LANES), F32),
            vm((4, 8, LANES), F32),
        ]

    def __init__(self, dp, head_size, shared_size, refs):
        self.dp, self.head_size, self.shared_size = dp, head_size, shared_size
        self.hr, self.sr = slot_rows(head_size), slot_rows(shared_size)
        self.fh, self.fs, self.wide, self.tall, self.tmp = refs
        self.hp, self.used_h = head_places()
        self.sp, self.used_s = shared_places()

    def clear_unused(self):
        for g in range(2):
            first = self.used_h // LANES // 8 * 8
            count = self.fh.shape[1] - first
            self.fh[g, pl.ds(first, count), :] = jnp.zeros((count, LANES), F32)
        first = self.used_s // LANES // 8 * 8
        count = self.fs.shape[0] - first
        self.fs[pl.ds(first, count), :] = jnp.zeros((count, LANES), F32)

    def head(self, g, place, rows, pitch, src, row0, lane0):
        give(self.fh.at[g], self.hp[place], rows, pitch, 0, pitch, src, row0, lane0)

    def shared(self, place, at, rows, pitch, col, src, row0, lane0):
        give(self.fs, self.sp[place] + at, rows, pitch, col, D, src, row0, lane0)

    def up(self, up, place, bias_place):
        load_tiles(up, self.wide, 0.5)
        for g in range(2):
            self.head(g, place, D, HF, self.wide, 0, g * HFP)
            self.head(g, bias_place, 1, HF, self.wide, 240, g * HFP)

    def down(self, dn, place, row):
        for t in range(2):
            self.tall[t] = (0.5 * dn[pl.ds(t * LANES, LANES), :]).astype(BF).T.astype(F32)
        for g in range(2):
            self.head(g, place, HF, D, self.tall, g * HFP, 0)
        self.shared("vec", row * D, 1, D, 0, self.tall, HF, 0)

    def attention(self, qkv, wo, rel):
        load_tiles(qkv, self.wide)
        load_tiles(wo, self.tall)
        length = rel.shape[0] // HEADS
        for g in range(2):
            for which, (place, bplace) in enumerate((("wq", "bq"), ("wk", None), ("wv", "bv"))):
                lane0 = which * DP + g * LANES
                self.head(g, place, D, HC, self.wide, 0, lane0)
                if bplace:
                    self.head(g, bplace, 1, HC, self.wide, 240, lane0)
            self.head(g, "wo", HC, D, self.tall, g * LANES, 0)
        for n in range(HEADS):
            total = jnp.zeros((8, 4 * LANES), F32)
            for block in range(length // 8):
                rows = rel[pl.ds(n * length + 8 * block, 8), :]
                rows = jnp.concatenate([rows, jnp.zeros((8, 4 * LANES - length), F32)], 1)
                total = total + pltpu.roll(rows, length - 8 - 8 * block, 1)
            row = total[7:8]
            for i in range(7):
                row = row + pltpu.roll(total[i : i + 1], 7 - i, 1)
            for t in range(4):
                self.tmp[t, pl.ds(0, 1), :] = row[:, t * LANES : (t + 1) * LANES]
            give(self.fh.at[n // 2], self.hp["rel"] + (n % 2) * KREL, 1, KREL, 0, KREL, self.tmp, 0, 0)
        self.shared("vec", B_OUT * D, 1, D, 0, self.tall, MASK_LANE, 0)

    def points(self, p1, p2):
        load_tiles(p1, self.wide)
        load_tiles(p2, self.tall)
        for half in range(2):
            self.shared("p1", 0, D, 2 * D, half * D, self.wide, 0, half * DP)
            self.shared("pb1", half * D, 1, D, 0, self.wide, 240, half * DP)
        self.shared("p2", 0, D, D, 0, self.tall, 0, 0)
        self.shared("pb2", 0, 1, D, 0, self.tall, 240, 0)

    def vectors(self, vec, vec2):
        for t in range(2):
            cols = pl.ds(t * LANES, LANES)
            self.tall[t, pl.ds(0, VEC_ROWS), :] = vec[:, cols] + vec2[:, cols]
        for row in range(2, 10):
            self.shared("vec", row * D, 1, D, 0, self.tall, row, 0)
        self.shared("taps", 0, 16, D, 0, self.tall, TAPS, 0)
        self.shared("bg", 0, 1, D, 0, self.tall, BATCH_GAIN, 0)
        self.shared("bb", 0, 1, D, 0, self.tall, BATCH_BIAS, 0)

    def first_norm(self, vec):
        for t in range(2):
            self.tall[t, pl.ds(0, 8), :] = vec[pl.ds(0, 8), pl.ds(t * LANES, LANES)]
        for row in (FFA, FFA + 1):
            self.shared("vec", row * D, 1, D, 0, self.tall, row, 0)

    def slots(self, out, z, kind):
        for i in range(4 * z, 4 * z + 4):
            for g in range(2):
                if kind == 0:
                    out[g, i, pl.ds(0, self.hr), :] = self.fh[g, pl.ds(i * self.head_size // LANES, self.hr), :].astype(BF)
                else:
                    at = (2 * i + g) * self.shared_size // LANES
                    out[g, i, pl.ds(self.hr, self.sr), :] = self.fs[pl.ds(at, self.sr), :].astype(BF)

    def groups(self):
        size = 4 * self.head_size
        every = range(self.dp // 4)
        one = [z for z in every if z * size >= self.hp["up2"] and (z + 1) * size <= self.hp["wq"]]
        two = [z for z in every if z * size >= self.hp["dn1"] and z not in one]
        late = [z for z in every if 8 * z * self.shared_size < 2 * D]
        return one, two, [z for z in every if z not in one and z not in two], [z for z in every if z not in late], late


def row_sum(x):
    return jnp.sum(x, -1, keepdims=True)


def halves(x):
    return x[:, :LANES], x[:, LANES:]


def both(lo, hi):
    return jnp.concatenate([lo, hi], 1)


def norm(x, gain, bias):
    lane = lane_iota((1, LANES))
    lo, hi = halves(x)
    mean = row_sum(lo + hi) * (1.0 / D)
    lo = lo - mean
    hi = jnp.where(lane < D - LANES, hi - mean, 0.0)
    inv = lax.rsqrt(row_sum(lo * lo + hi * hi) * (1.0 / D) + NORM_EPS)
    lo, hi = lo * inv, hi * inv
    return both(lo, hi) * gain + bias, both(lo, jnp.where(lane == LANES - 1, inv, hi))


def norm_grad(grad, kept, gain):
    dg = grad * gain
    inv = kept[:, DP - 1 :]
    first = row_sum(dg) * (1.0 / D)
    second = row_sum(dg * kept) * (1.0 / D)
    return inv * (dg - first - kept * second)


def fold_rows(x):
    return jnp.sum(x.reshape(x.shape[0] // 8, 8, x.shape[1]), 0)


def norm_param_grads(acc, row, grad, kept):
    acc[row] += fold_rows(grad * kept)
    acc[row + 1] += fold_rows(grad)


def settle(acc, out):
    for row in range(acc.shape[0]):
        out[pl.ds(row, 1), :] = jnp.sum(acc[row], 0, keepdims=True)


def silu_pair(y):
    p = jnp.tanh(y) + 1.0
    h = (y * p).astype(BF)
    p = p.astype(BF)
    return h, p + h * (2.0 - p)


def widen(x):
    rows = x.shape[0]
    return jnp.concatenate([x.astype(F32), jnp.zeros((rows, DP - D), F32)], 1)


def head_lanes():
    lane = lane_iota((1, LANES))
    return lane < HD, (lane >= HD) & (lane < 2 * HD), lane == MASK_LANE


def valid_rows(lengths, at, length):
    return lax.broadcasted_iota(jnp.int32, (length, 1), 0) < lengths[at]


def phase_a_kernel(
    seqs, sizes, lengths, frames, head_ref, shared_ref,
    kept1_o, a1_o, h_o, sp_o, kept2_o, a2_o, qkv_o, e_o, rl_o, m_o,
    x2_o, kept3_o, a3_o, f1_o, f2_o, gl_o, w_o, keep_o, up, dn, up2, dn2, wqkv, wo, p1, p2, vec, rel,
    pad, stats_o, inbox, ss, rs, own_slot, got, fh, fs, wide, tall, tmp, *sems,
):
    step = pl.program_id(0)
    total = inbox.shape[0]
    weights = Weights(*sizes, got, (fh, fs, wide, tall, tmp))

    @pl.when(step == 0)
    def _():
        greet_all(total)
        align(head_ref, shared_ref, own_slot)
        weights.clear_flat()
        greeted_all(total)
        gather(sizes[0] // 4, own_slot, got, sems, weights.merge)
        weights.ffn(up, dn, "up1", "upb1", "dn1", DOWNB_ONE)
        weights.others(wqkv, wo, p1, vec, rel)

    length = frames.shape[1]
    tokens = seqs * length
    first_seq = lax.axis_index("head") * (seqs * pl.num_programs(0)) + step * seqs

    def v(row):
        return vec[pl.ds(row, 1), :]

    x0 = widen(frames[...].reshape(tokens, D))
    a, kept1_o[...] = norm(x0, v(FFA), v(FFA + 1))
    a = a.astype(BF)
    a1_o[...] = a
    h, slope = silu_pair(dot(a, up[...]))
    h_o[...] = h
    sp_o[...] = slope
    x1 = x0 + dot(h, dn[...])
    a, kept2_o[...] = norm(x1, v(ATT), v(ATT + 1))
    a = a.astype(BF)
    a2_o[...] = a
    qkv = dot(a, wqkv[...])
    first, second, special = head_lanes()
    for b in range(seqs):
        rows = pl.ds(b * length, length)
        fence = jnp.where(valid_rows(lengths, first_seq + b, length), 0.0, NEG)
        for g in range(2):
            def piece(which):
                at = which * DP + g * LANES
                return qkv[b * length : (b + 1) * length, at : at + LANES]

            q = (piece(0) * (SCALE * LOG2E)).astype(BF)
            k = jnp.where(special, fence, piece(1)).astype(BF)
            vv = piece(2).astype(BF)
            qkv_o[rows, pl.ds(g * LANES, LANES)] = q
            qkv_o[rows, pl.ds(DP + g * LANES, LANES)] = k
            qkv_o[rows, pl.ds(2 * DP + g * LANES, LANES)] = vv
            zero = jnp.zeros_like(q)
            pair = jnp.concatenate([jnp.where(first | special, q, zero), jnp.where(second | special, q, zero)], 0)
            at = pl.ds(2 * g * length, 2 * length)
            s = dot_t(pair, k) + rel[at, :]
            e = jnp.exp2(s - jnp.max(s, -1, keepdims=True)).astype(BF)
            e_o[b, at, :] = e
            o = dot(e, vv)
            r = 1.0 / o[:, MASK_LANE : MASK_LANE + 1]
            shares = jnp.where(second, r[length:], r[:length])
            rl_o[rows, pl.ds(g * LANES, LANES)] = shares
            m_o[rows, pl.ds(g * LANES, LANES)] = (jnp.where(second, o[length:], o[:length]) * shares).astype(BF)
    x2 = x1 + dot(m_o[...], wo[...])
    x2_o[...] = x2
    a, kept3_o[...] = norm(x2, v(CNV), v(CNV + 1))
    a = a.astype(BF)
    a3_o[...] = a
    e = dot(a, p1[...])
    half = KW // 2

    @pl.when(step == 0)
    def _():
        pad[...] = jnp.zeros(pad.shape, F32)
        stats_o[...] = jnp.zeros(stats_o.shape, F32)

    count = jnp.float32(0.0)
    summed = jnp.zeros((1, DP), F32)
    for b in range(seqs):
        rows = pl.ds(b * length, length)
        valid = jnp.where(valid_rows(lengths, first_seq + b, length), 1.0, 0.0)
        linear = e[b * length : (b + 1) * length, :DP]
        gate = 0.5 * jnp.tanh(0.5 * e[b * length : (b + 1) * length, DP:]) + 0.5
        f1 = gate * valid
        gl = linear * f1
        f1_o[rows, :] = f1.astype(BF)
        f2_o[rows, :] = (gl * (1.0 - gate)).astype(BF)
        gl_o[rows, :] = gl.astype(BF)
        for t in range(2):
            cols = pl.ds(t * LANES, LANES)
            pad[b, t, pl.ds(8, length), :] = gl[:, t * LANES : (t + 1) * LANES]
            acc = jnp.broadcast_to(vec[pl.ds(DEPTH_BIAS, 1), cols], (length, LANES))
            for r in range(KW):
                acc = acc + pad[b, t, pl.ds(8 - half + r, length), :] * vec[pl.ds(TAPS + r, 1), cols]
            w_o[rows, cols] = acc
        summed = summed + jnp.sum(w_o[rows, :] * valid, 0, keepdims=True)
        count = count + lengths[first_seq + b].astype(F32)
    mean = summed / count
    square = jnp.zeros((1, DP), F32)
    for b in range(seqs):
        valid = jnp.where(valid_rows(lengths, first_seq + b, length), 1.0, 0.0)
        centre = (w_o[pl.ds(b * length, length), :] - mean) * valid
        square = square + jnp.sum(centre * centre, 0, keepdims=True)
    old = stats_o[pl.ds(4, 1), :]
    new = old + count
    for t in range(2):
        cols = slice(t * LANES, (t + 1) * LANES)
        before = stats_o[pl.ds(t, 1), :]
        delta = mean[:, cols] - before
        stats_o[pl.ds(t, 1), :] = before + delta * (count / new)
        stats_o[pl.ds(2 + t, 1), :] += square[:, cols] + delta * delta * (old * count / new)
    stats_o[pl.ds(4, 1), :] = new

    @pl.when(step == pl.num_programs(0) - 1)
    def _():
        share_start(total, stats_o, inbox, ss, rs)
        weights.ffn(up2, dn2, "up2", "upb2", "dn2", DOWNB_TWO)
        weights.point_two(p2)
        share_finish(total, stats_o, inbox, ss, rs)
        batch_stats(inbox[...], keep_o)


def batch_stats(shared, keep):
    counts = shared[:, 4:5, :]
    total = jnp.sum(counts, 0)
    means, spreads = [], []
    for t in range(2):
        each = shared[:, t : t + 1, :]
        mean = jnp.sum(each * counts, 0) / total
        spread = (jnp.sum(shared[:, 2 + t : 3 + t, :], 0) + jnp.sum(counts * (each - mean) ** 2, 0)) / total
        means.append(mean)
        spreads.append(spread)
    keep[pl.ds(0, 1), :] = jnp.concatenate(means, 1)
    keep[pl.ds(1, 1), :] = lax.rsqrt(jnp.concatenate(spreads, 1) + NORM_EPS)
    keep[pl.ds(2, 1), :] = jnp.concatenate([total, total], 1)
    keep[pl.ds(3, 5), :] = jnp.zeros((5, DP), F32)


def phase_b_kernel(
    seqs, keep, w, x2, cotangent, p2, up, dn, vec,
    out_o, dy_o, dx3_o, dup_o, ddn_o, dp2_o, vec_o, keep_o,
    acc, a_all, du_all, do_all, h_all, hc_all, dc_all, sums_o, inbox, ss, rs,
):
    step = pl.program_id(0)
    total = inbox.shape[0]
    length = cotangent.shape[1]
    tokens = seqs * length
    at = pl.ds(pl.multiple_of(step * tokens, tokens), tokens)

    @pl.when(step == 0)
    def _():
        greet_all(total)
        for ref in (dup_o, ddn_o, dp2_o, acc):
            ref[...] = jnp.zeros(ref.shape, F32)

    def v(row):
        return vec[pl.ds(row, 1), :]

    mean, inv_batch = keep[pl.ds(0, 1), :], keep[pl.ds(1, 1), :]
    z = (w[...] - mean) * inv_batch
    hc, slope_c = silu_pair(z * (0.5 * v(BATCH_GAIN)) + 0.5 * v(BATCH_BIAS))
    x3 = x2[...] + dot(hc, p2[...])
    a, kept = norm(x3, v(FFB), v(FFB + 1))
    a = a.astype(BF)
    h, slope = silu_pair(dot(a, up[...]))
    x4 = x3 + dot(h, dn[...])
    final, kept4 = norm(x4, v(OUT), v(OUT + 1))
    out_o[...] = final[:, :D].astype(BF).reshape(seqs, length, D)
    g = widen(cotangent[...].reshape(tokens, D))
    norm_param_grads(acc, OUT, g, kept4)
    dx4 = norm_grad(g, kept4, v(OUT))
    do = dx4.astype(BF)
    do_all[at, :] = do
    h_all[at, :] = h
    du = dot_t(do, dn[...]).astype(BF) * slope
    a_all[at, :] = a
    du_all[at, :] = du
    da = dot_t(du, up[...])
    norm_param_grads(acc, FFB, da, kept)
    dx3 = dx4 + norm_grad(da, kept, v(FFB))
    dx3_o[...] = dx3
    dc = dx3.astype(BF)
    hc_all[at, :] = hc
    dc_all[at, :] = dc
    dy = dot_t(dc, p2[...]) * slope_c.astype(F32)
    dy_o[...] = dy
    acc[BATCH_BIAS] += fold_rows(dy)
    acc[BATCH_GAIN] += fold_rows(dy * z)

    @pl.when(step == pl.num_programs(0) - 1)
    def _():
        acc[BATCH_BIAS] *= 0.5
        acc[BATCH_GAIN] *= 0.5
        settle(acc, vec_o)
        for row, source in ((0, BATCH_BIAS), (2, BATCH_GAIN)):
            line = vec_o[pl.ds(source, 1), :]
            for t in range(2):
                sums_o[pl.ds(row + t, 1), :] = line[:, t * LANES : (t + 1) * LANES]

    @pl.when(step == pl.num_programs(0) - 1)
    def _():
        greeted_all(total)
        share_start(total, sums_o, inbox, ss, rs)

        @pl.loop(0, pl.num_programs(0))
        def _(k):
            at = pl.ds(pl.multiple_of(k * tokens, tokens), tokens)
            ddn_o[...] += t_dot(do_all[at, :], h_all[at, :])
            dup_o[...] += t_dot(a_all[at, :], du_all[at, :])
            dp2_o[...] += t_dot(hc_all[at, :], dc_all[at, :])

        share_finish(total, sums_o, inbox, ss, rs)
        sums = jnp.sum(inbox[...], 0)
        keep_o[...] = keep[...]
        keep_o[pl.ds(3, 1), :] = jnp.concatenate([sums[0:1], sums[1:2]], 1)
        keep_o[pl.ds(4, 1), :] = jnp.concatenate([sums[2:3], sums[3:4]], 1)


def phase_c_kernel(
    seqs, steps, sizes, lengths, keep, w, dy, dx3, gl, f1, f2, a3, kept3, qkv, e_all, rl, m, a2, kept2, h, slope, a1, kept1,
    p1, wo, wqkv, dn, up, vec, dup2, ddn2, dp2, vec2,
    dx0_o, sum_o,
    dp1_o, dwo_o, dqkv_o, dup_o, ddn_o, vec_o, rel_o, dx1_buf, mine,
    acc, padw, padg, grads, *refs,
):
    step = pl.program_id(0)
    length = dx0_o.shape[1]
    flat = Flat(*sizes, refs[:5])
    nz = sizes[0] // 4
    scatter = Scatter(nz, flat.hr, flat.sr, mine, refs[5:])
    one, two, rest, shared_two, shared_rest = flat.groups()

    @pl.when(step == 0)
    def _():
        greet(nz, scatter.me, scatter.core, scatter.zc, scatter.yc, scatter.xc)
        for ref in (dp1_o, dwo_o, dqkv_o, dup_o, ddn_o, acc, rel_o, padw, padg):
            ref[...] = jnp.zeros(ref.shape, F32)
        flat.clear_unused()
        flat.up(dup2, "up2", "upb2")
        flat.down(ddn2, "dn2", DOWNB_TWO)
        for z in one:
            flat.slots(scatter.g, z, 0)
        greeted(nz)
        for z in one:
            scatter.stage_core(z, 0)

    @pl.when(step < steps)
    def _():
        phase_c_first(
            seqs, step, steps, length, lengths, keep, w, dy, dx3, gl, f1, f2, a3, kept3, qkv, e_all, rl, m, a2, kept2,
            h, p1, wo, wqkv, vec, dp1_o, dwo_o, dqkv_o, ddn_o, rel_o, dx1_buf, acc, padw, padg, grads,
        )

    @pl.when(step == steps)
    def _():
        flat.attention(dqkv_o, dwo_o, rel_o)
        flat.down(ddn_o, "dn1", DOWNB_ONE)
        for z in two:
            flat.slots(scatter.g, z, 0)
            scatter.stage_core(z, 0)
        settle(acc, vec_o)
        flat.points(dp1_o, dp2)
        flat.vectors(vec_o, vec2)
        for z in shared_two:
            flat.slots(scatter.g, z, 1)
            scatter.stage_core(z, 1)

    @pl.when(step >= steps)
    def _():
        at = pl.ds(pl.multiple_of((step - steps) * (seqs * length), seqs * length), seqs * length)
        dx1 = dx1_buf[at, :]
        du = dot_t(dx1.astype(BF), dn[...]).astype(BF) * slope[...]
        dup_o[...] += t_dot(a1[...], du)
        da = dot_t(du, up[...])
        norm_param_grads(acc, FFA, da, kept1[...])
        dx0 = dx1 + norm_grad(da, kept1[...], vec[pl.ds(FFA, 1), :])
        dx0_o[...] = dx0[:, :D].reshape(seqs, length, D)

    stages = (scatter.stage_first, scatter.stage_second, scatter.stage_third)
    for at, heads, shared in (((1, 3, 5), one, []), ((steps + AT_A, steps + AT_B), two, shared_two)):
        for when, stage in zip(at, stages):
            @pl.when(step == when)
            def _():
                for z in heads:
                    stage(z, 0)
                for z in shared:
                    stage(z, 1)

    @pl.when(step == 2 * steps - 1)
    def _():
        flat.up(dup_o, "up1", "upb1")
        for z in rest:
            flat.slots(scatter.g, z, 0)
            scatter.stage_core(z, 0)
        settle(acc, vec_o)
        flat.first_norm(vec_o)
        for z in shared_rest:
            flat.slots(scatter.g, z, 1)
            scatter.stage_core(z, 1)
        for z in two:
            scatter.stage_third(z, 0)
        for z in shared_two:
            scatter.stage_third(z, 1)
        for stage in stages:
            for z in rest:
                stage(z, 0)
            for z in shared_rest:
                stage(z, 1)
        scatter.finish(sum_o)


def phase_c_first(
    seqs, step, steps, length, lengths, keep, w, dy, dx3, gl, f1, f2, a3, kept3, qkv, e_all, rl, m, a2, kept2,
    h, p1, wo, wqkv, vec, dp1_o, dwo_o, dqkv_o, ddn_o, rel_o, dx1_buf, acc, padw, padg, grads,
):
    first_seq = lax.axis_index("head") * (seqs * steps) + step * seqs
    half = KW // 2

    def v(row):
        return vec[pl.ds(row, 1), :]

    mean, inv_batch, count = (keep[pl.ds(row, 1), :] for row in range(3))
    scale = v(BATCH_GAIN) * inv_batch
    cross = inv_batch * scale * keep[pl.ds(4, 1), :] / count
    plain = scale * keep[pl.ds(3, 1), :] / count - mean * cross
    scale = 0.5 * scale
    for b in range(seqs):
        rows = pl.ds(b * length, length)
        valid = jnp.where(valid_rows(lengths, first_seq + b, length), 1.0, 0.0)
        dw = dy[rows, :] * scale - valid * (plain + w[rows, :] * cross)
        acc[DEPTH_BIAS] += fold_rows(dw)
        for t in range(2):
            cols = pl.ds(t * LANES, LANES)
            here = dw[:, t * LANES : (t + 1) * LANES]
            padw[b, t, pl.ds(8, length), :] = here
            padg[b, t, pl.ds(8, length), :] = gl[rows, cols].astype(F32)
            total = jnp.zeros((length, LANES), F32)
            for r in range(KW):
                total = total + padw[b, t, pl.ds(8 + half - r, length), :] * vec[pl.ds(TAPS + r, 1), cols]
                tap = here * padg[b, t, pl.ds(8 - half + r, length), :]
                acc[TAPS + r, :, cols] += fold_rows(tap)
            grads[rows, cols] = (total * f1[rows, cols].astype(F32)).astype(BF)
            grads[rows, pl.ds(DP + t * LANES, LANES)] = (total * f2[rows, cols].astype(F32)).astype(BF)
    de = grads[:, pl.ds(0, 2 * DP)]
    dp1_o[...] += t_dot(a3[...], de)
    da = dot_t(de, p1[...])
    norm_param_grads(acc, CNV, da, kept3[...])
    dx2 = dx3[...] + norm_grad(da, kept3[...], v(CNV))
    db = dx2.astype(BF)
    dwo_o[...] += t_dot(m[...], db)
    dm = dot_t(db, wo[...])
    first, second, special = head_lanes()
    source = lax.broadcasted_iota(jnp.int32, (LANES, 2 * LANES), 0)
    target = lane_iota((LANES, 2 * LANES)) // LANES
    spread = jnp.where((source >= target * HD) & (source < (target + 1) * HD), 1.0, 0.0).astype(BF)
    for b in range(seqs):
        rows = pl.ds(b * length, length)
        for g in range(2):
            cols = pl.ds(g * LANES, LANES)
            q = qkv[rows, cols]
            k = qkv[rows, pl.ds(DP + g * LANES, LANES)]
            vv = qkv[rows, pl.ds(2 * DP + g * LANES, LANES)]
            dmb = (dm[b * length : (b + 1) * length, g * LANES : (g + 1) * LANES] * rl[rows, cols]).astype(BF)
            level = dot(dmb * m[rows, cols], spread)
            level = jnp.concatenate([level[:, :LANES], level[:, LANES:]], 0)
            zero = jnp.zeros_like(q)
            dm_pair = jnp.concatenate([jnp.where(first, dmb, zero), jnp.where(second, dmb, zero)], 0)
            q_pair = jnp.concatenate([jnp.where(first, q, zero), jnp.where(second, q, zero)], 0)
            at = pl.ds(2 * g * length, 2 * length)
            e = e_all[b, at, :]
            dp = dot_t(dm_pair, vv)
            ds = e.astype(F32) * (dp - jnp.concatenate([level, level[:, : length - LANES]], 1))
            rel_o[at, :] += ds
            ds = ds.astype(BF)
            dq = dot(ds, k)
            dq = jnp.where(second, dq[length:], dq[:length])
            grads[rows, cols] = (dq * SCALE).astype(BF)
            grads[rows, pl.ds(DP + g * LANES, LANES)] = (t_dot(ds, q_pair) * LN2).astype(BF)
            grads[rows, pl.ds(2 * DP + g * LANES, LANES)] = t_dot(e, dm_pair).astype(BF)
    dqkv = grads[...]
    dqkv_o[...] += t_dot(a2[...], dqkv)
    da = dot_t(dqkv, wqkv[...])
    norm_param_grads(acc, ATT, da, kept2[...])
    dx1 = dx2 + norm_grad(da, kept2[...], v(ATT))
    at = pl.ds(pl.multiple_of(step * (seqs * length), seqs * length), seqs * length)
    dx1_buf[at, :] = dx1
    ddn_o[...] += t_dot(dx1.astype(BF), h[...])


def layer_call(body, steps, ins, outs, scratch, name, collective_id=None):
    def spec(item):
        kind, shape = item
        if kind == "smem":
            return pl.BlockSpec(memory_space=pltpu.SMEM)
        if kind == "tile":
            return pl.BlockSpec(shape, lambda i: (i,) + (0,) * (len(shape) - 1))
        if kind == "early":
            return pl.BlockSpec(shape, lambda i: (jnp.minimum(i, steps // 2 - 1),) + (0,) * (len(shape) - 1))
        if kind == "late":
            return pl.BlockSpec(shape, lambda i: (jnp.maximum(i - steps // 2, 0),) + (0,) * (len(shape) - 1))
        return pl.BlockSpec(shape, lambda i: (0,) * len(shape))

    arrays = [a for _, _, a in ins]
    return pl.pallas_call(
        body,
        grid=(steps,),
        out_shape=tuple(jax.ShapeDtypeStruct(full, dtype) for _, _, full, dtype in outs),
        in_specs=[spec((kind, block)) for kind, block, _ in ins],
        out_specs=tuple(spec((kind, block)) for kind, block, _, _ in outs),
        scratch_shapes=list(scratch),
        compiler_params=pltpu.CompilerParams(
            vmem_limit_bytes=BIG,
            dimension_semantics=("arbitrary",),
            collective_id=collective_id,
            has_side_effects=collective_id is not None,
        ),
        name=name,
    )(*arrays)


def tile_in(array, steps, kind="tile"):
    return (kind, (array.shape[0] // steps,) + array.shape[1:], array)


def whole_in(array):
    return ("whole", array.shape, array)


def tile_out(steps, shape, dtype, kind="tile"):
    return (kind, (shape[0] // steps,) + shape[1:], shape, dtype)


def whole_out(shape, dtype=F32):
    return ("whole", shape, shape, dtype)


SEQS_A = 2
SEQS_B = 4
SEQS_C = 2
AT_A = 4
AT_B = 7


def per_device(
    frames, cotangent, lengths, head_params, shared_params, head_first, head_second, shared_first, shared_second
):
    seq_here, length, _ = frames.shape
    tokens = seq_here * length
    dp = lax.axis_size("dp")
    head_size, shared_size = head_params.shape[1], shared_params.shape[0]
    rows = slot_rows(head_size) + slot_rows(shared_size)
    vm = pltpu.VMEM
    dma = pltpu.SemaphoreType.DMA
    sharing = [vm((8, LANES), F32), vm((2 * dp, 8, LANES), F32), dma((2 * dp,)), dma((2 * dp,))]
    steps = seq_here // SEQS_A
    t = functools.partial(tile_out, steps)
    (
        kept1, a1, h1, slope1, kept2, a2, qkv, e_all, rl, m, x2, kept3, a3, f1, f2, gl, w, keep,
        up1, dn1, up2, dn2, wqkv, wo, p1, p2, vec, rel
    ) = layer_call(
        functools.partial(phase_a_kernel, SEQS_A, (dp, head_size, shared_size)),
        steps,
        [("smem", None, lengths), tile_in(frames, steps), whole_in(head_params), whole_in(shared_params)],
        [
            t((tokens, DP), F32), t((tokens, DP), BF), t((tokens, FFP), BF), t((tokens, FFP), BF),
            t((tokens, DP), F32), t((tokens, DP), BF), t((tokens, 3 * DP), BF),
            t((seq_here, HEADS * length, length), BF), t((tokens, DP), F32), t((tokens, DP), BF),
            t((tokens, DP), F32), t((tokens, DP), F32), t((tokens, DP), BF), t((tokens, DP), BF),
            t((tokens, DP), BF), t((tokens, DP), BF), t((tokens, DP), F32), whole_out((8, DP)),
            whole_out((DP, FFP), BF), whole_out((FFP, DP), BF), whole_out((DP, FFP), BF), whole_out((FFP, DP), BF),
            whole_out((DP, 3 * DP), BF), whole_out((DP, DP), BF), whole_out((DP, 2 * DP), BF), whole_out((DP, DP), BF),
            whole_out((VEC_ROWS, DP)), whole_out((HEADS * length, length)),
        ],
        [vm((SEQS_A, 2, length + 16, LANES), F32)]
        + sharing
        + [vm((rows, LANES), BF), vm((dp, 2, rows, LANES), BF)]
        + Flat.scratch(dp, head_size, shared_size)
        + gather_sems(dp // 4),
        "phase_a",
        1,
    )
    steps = seq_here // SEQS_B
    t = functools.partial(tile_out, steps)
    early, dy, dx3, dup2, ddn2, dp2, vec_b, keep = layer_call(
        functools.partial(phase_b_kernel, SEQS_B),
        steps,
        [whole_in(keep), tile_in(w, steps), tile_in(x2, steps), tile_in(cotangent, steps)]
        + [whole_in(x) for x in (p2, up2, dn2, vec)],
        [
            t((seq_here, length, D), BF), t((tokens, DP), F32), t((tokens, DP), F32),
            whole_out((DP, FFP)), whole_out((DP, FFP)), whole_out((DP, DP)), whole_out((VEC_ROWS, DP)),
            whole_out((8, DP)),
        ],
        [
            vm((VEC_ROWS, 8, DP), F32), vm((tokens, DP), BF), vm((tokens, FFP), BF), vm((tokens, DP), BF),
            vm((tokens, FFP), BF), vm((tokens, DP), BF), vm((tokens, DP), BF),
        ]
        + sharing,
        "phase_b",
        3,
    )
    steps = seq_here // SEQS_C
    slot = (slot_rows(head_size), slot_rows(shared_size))
    block = SEQS_C * length
    input_grad, summed = layer_call(
        functools.partial(phase_c_kernel, SEQS_C, steps, (dp, head_size, shared_size)),
        2 * steps,
        [("smem", None, lengths), whole_in(keep)]
        + [tile_in(x, steps, "early") for x in (w, dy, dx3, gl, f1, f2, a3, kept3, qkv, e_all, rl, m, a2, kept2, h1)]
        + [tile_in(x, steps, "late") for x in (slope1, a1, kept1)]
        + [whole_in(x) for x in (p1, wo, wqkv, dn1, up1, vec, dup2, ddn2, dp2, vec_b)],
        [tile_out(steps, (seq_here, length, D), F32, "late"), whole_out((rows, LANES))],
        [
            vm((DP, 2 * DP), F32), vm((DP, DP), F32), vm((DP, 3 * DP), F32), vm((DP, FFP), F32), vm((DP, FFP), F32),
            vm((VEC_ROWS, DP), F32), vm((HEADS * length, length), F32), vm((tokens, DP), F32), vm((rows, LANES), F32),
            vm((VEC_ROWS, 8, DP), F32),
            vm((SEQS_C, 2, length + 16, LANES), F32),
            vm((SEQS_C, 2, length + 16, LANES), F32),
            vm((block, 3 * DP), BF),
        ]
        + Flat.scratch(dp, head_size, shared_size)
        + Scatter.scratch(dp, *slot),
        "phase_c",
        4,
    )
    h_shape, s_shape = head_params.shape, shared_params.shape
    steps = 4
    return layer_call(
        adam_kernel,
        steps,
        [tile_in(x, steps) for x in (early, input_grad)]
        + [whole_in(x) for x in (summed, head_params, head_first, head_second, shared_params, shared_first, shared_second)],
        [tile_out(steps, early.shape, BF), tile_out(steps, early.shape, F32)]
        + [whole_out(h_shape)] * 3
        + [whole_out(h_shape, BF)]
        + [whole_out(s_shape)] * 3
        + [whole_out(s_shape, BF)],
        [],
        "adam",
    )


def solution(mesh):
    frames = P(("dp", "head"), None, None)
    heads = P("head", "dp")
    shared = P(("dp", "head"))
    return jax.shard_map(
        per_device,
        mesh=mesh,
        in_specs=(frames, frames, P("dp"), heads, shared, heads, heads, shared, shared),
        out_specs=(frames, frames) + (heads,) * 4 + (shared,) * 4,
        check_vma=False,
    )
```

```python
import functools
import math

import jax
import jax.numpy as jnp
from jax import lax
from jax.experimental import pallas as pl
from jax.experimental.pallas import tpu as pltpu
from jax.sharding import PartitionSpec as P

BF = jnp.bfloat16
F32 = jnp.float32
LANES = 128


def up_to(count, unit):
    return -(-count // unit) * unit


def grid_place(nz):
    me = lax.axis_index("dp")
    core = lax.axis_index("head")
    zc = me // 4
    rest = me - 4 * zc
    yc = rest // 2
    xc = rest - 2 * yc
    return me, core, zc, yc, xc


def remote(src, dst, send, recv, dp, head):
    return pltpu.make_async_remote_copy(
        src_ref=src,
        dst_ref=dst,
        send_sem=send,
        recv_sem=recv,
        device_id={"dp": dp, "head": head},
        device_id_type=pl.DeviceIdType.MESH,
    )


def greet(nz, me, core, zc, yc, xc):
    barrier = pltpu.get_barrier_semaphore()

    def hello(dp, head):
        pl.semaphore_signal(
            barrier, inc=1, device_id={"dp": dp, "head": head}, device_id_type=pl.DeviceIdType.MESH
        )

    for k in range(1, nz):
        hello(lax.rem(zc + k, nz) * 4 + 2 * yc + xc, core)
    hello(4 * zc + 2 * (1 - yc) + xc, core)
    hello(4 * zc + 2 * yc + 1 - xc, core)
    hello(me, 1 - core)


def greeted(nz):
    pl.semaphore_wait(pltpu.get_barrier_semaphore(), nz + 2)


def gather(nz, src, out, sems, merge):
    sz, rz, s1, r1, s2, r2, sc, rc = sems
    rows = src.shape[0]
    row_a = up_to(rows // 2, 16)
    parts = (pl.ds(0, row_a), pl.ds(row_a, rows - row_a))
    me, core, zc, yc, xc = grid_place(nz)
    out[me, core] = src[...]
    y_peer = 4 * zc + 2 * (1 - yc) + xc
    x_peer = 4 * zc + 2 * yc + 1 - xc
    firsts = (y_peer, x_peer)
    seconds = (x_peer, y_peer)
    pending = []

    def send(slot, p, send_sem, recv_sem, dp, head):
        block = out.at[slot, core, parts[p]]
        copy = remote(block, block, send_sem, recv_sem, dp, head)
        copy.start()
        pending.append(copy)

    def arrived(slot, which, p, send_sem, recv_sem):
        block = out.at[slot, which, parts[p]]
        remote(block, block, send_sem, recv_sem, me, 1 - core).wait_recv()

    zs = [lax.rem(zc + k, nz) for k in range(nz)]
    here = 2 * yc + xc
    first_here = (2 * (1 - yc) + xc, 2 * yc + 1 - xc)
    second_here = ((2 * yc + 1 - xc, 2 * (1 - yc) + 1 - xc), (2 * (1 - yc) + xc, 2 * (1 - yc) + 1 - xc))
    for k in range(1, nz):
        for p in (0, 1):
            send(me, p, sz.at[p, k], rz.at[p, zc], zs[k] * 4 + here, core)
    for k in range(nz):
        z = zs[k]
        slot = 4 * z + here
        for p in (0, 1):
            if k:
                arrived(slot, core, p, sz.at[p, k], rz.at[p, z])
            send(slot, p, s1.at[p, k], r1.at[p, z], firsts[p], core)
            send(slot, p, s2.at[p, k, 0], r2.at[p, z, 0], seconds[p], core)
            send(slot, p, sc.at[p, k, 0], rc.at[p, z, 0], me, 1 - core)
    for k in range(nz):
        for p in (0, 1):
            merge(4 * zs[k] + here, core, p)
    for k in range(nz):
        z = zs[k]
        for p in (0, 1):
            slot = 4 * z + first_here[p]
            arrived(slot, core, p, s1.at[p, k], r1.at[p, z])
            send(slot, p, s2.at[p, k, 1], r2.at[p, z, 1], seconds[p], core)
            send(slot, p, sc.at[p, k, 1], rc.at[p, z, 1], me, 1 - core)
    for k in range(nz):
        for p in (0, 1):
            merge(4 * zs[k] + first_here[p], core, p)
    for k in range(nz):
        z = zs[k]
        for b in (0, 1):
            for p in (0, 1):
                slot = 4 * z + second_here[p][b]
                arrived(slot, core, p, s2.at[p, k, b], r2.at[p, z, b])
                send(slot, p, sc.at[p, k, 2 + b], rc.at[p, z, 2 + b], me, 1 - core)
        for b in (0, 1):
            for p in (0, 1):
                merge(4 * z + second_here[p][b], core, p)
    for k in range(nz):
        z = zs[k]
        for p in (0, 1):
            for b, at in enumerate((here, first_here[p]) + second_here[p]):
                arrived(4 * z + at, 1 - core, p, sc.at[p, k, b], rc.at[p, z, b])
                merge(4 * z + at, 1 - core, p)
    for copy in pending:
        copy.wait_send()


def gather_sems(nz):
    dma = pltpu.SemaphoreType.DMA
    return [
        dma((2, nz)), dma((2, nz)), dma((2, nz)), dma((2, nz)),
        dma((2, nz, 2)), dma((2, nz, 2)), dma((2, nz, 4)), dma((2, nz, 4)),
    ]


class Scatter:
    @staticmethod
    def scratch(dp, hr, sr):
        nz, rows = dp // 4, hr + sr
        dma, vm = pltpu.SemaphoreType.DMA, pltpu.VMEM
        return [
            vm((2, dp, rows, LANES), BF), vm((dp, rows, LANES), BF),
            vm((nz, 2, rows, LANES), BF), vm((nz, 2, rows, LANES), BF),
            vm((nz, rows, LANES), BF), vm((nz, rows, LANES), BF),
            vm((nz, rows, LANES), BF), vm((nz, rows, LANES), BF),
            dma((nz, 2)), dma((nz, 2)), dma((3, nz)), dma((3, nz)), dma((3, nz)), dma((3, nz)), dma((3, nz)), dma((3, nz)),
        ]

    def __init__(self, nz, hr, sr, mine, refs):
        self.nz, self.mine = nz, mine
        (
            self.g, self.c1, self.t1, self.rx1, self.t2, self.rx2, self.t3, self.rx3,
            self.sc, self.rc, self.s1, self.r1, self.s2, self.r2, self.s3, self.r3,
        ) = refs
        ha = up_to(hr // 2, 16)
        self.parts = (pl.ds(0, ha), pl.ds(ha, hr - ha), pl.ds(hr, sr))
        self.kinds = (pl.ds(0, hr), pl.ds(hr, sr))
        self.me, self.core, self.zc, self.yc, self.xc = grid_place(nz)
        zc, yc, xc = self.zc, self.yc, self.xc
        y_peer = 4 * zc + 2 * (1 - yc) + xc
        x_peer = 4 * zc + 2 * yc + 1 - xc
        self.firsts = (x_peer, y_peer, x_peer)
        self.seconds = (y_peer, x_peer, y_peer)
        self.second_give = (1 - yc, 1 - xc, 1 - yc)
        self.second_keep = (yc, xc, yc)

    def core_copy(self, z, kind):
        group, rows = pl.ds(4 * z, 4), self.kinds[kind]
        return remote(
            self.g.at[1 - self.core, group, rows], self.c1.at[group, rows],
            self.sc.at[z, kind], self.rc.at[z, kind], self.me, 1 - self.core,
        )

    def first_copy(self, z, p):
        rows = self.parts[p]
        return remote(
            self.t1.at[z, :, rows], self.rx1.at[z, :, rows], self.s1.at[p, z], self.r1.at[p, z], self.firsts[p], self.core
        )

    def second_copy(self, z, p):
        rows = self.parts[p]
        return remote(
            self.t2.at[z, rows], self.rx2.at[z, rows], self.s2.at[p, z], self.r2.at[p, z], self.seconds[p], self.core
        )

    def third_copy(self, z, p):
        rows = self.parts[p]
        return remote(
            self.t3.at[z, rows], self.rx3.at[self.zc, rows], self.s3.at[p, z], self.r3.at[p, self.zc],
            4 * z + 2 * self.yc + self.xc, self.core,
        )

    def place(self, p, z, b):
        return 4 * z + (2 * self.yc + b if p == 1 else 2 * b + self.xc)

    def held(self, z, p, slot):
        rows = self.parts[p]
        return self.g[self.core, slot, rows].astype(F32) + self.c1[slot, rows].astype(F32)

    def partial(self, z, p, b):
        return self.held(z, p, self.place(p, z, b)) + self.rx1[z, b, self.parts[p]].astype(F32)

    def stage_core(self, z, kind):
        self.core_copy(z, kind).start()

    def stage_first(self, z, kind):
        self.core_copy(z, kind).wait_recv()
        for p in ((0, 1), (2,))[kind]:
            for b in (0, 1):
                slot = 4 * z + (2 * (1 - self.yc) + b if p == 1 else 2 * b + 1 - self.xc)
                self.t1[z, b, self.parts[p]] = self.held(z, p, slot).astype(BF)
            self.first_copy(z, p).start()

    def stage_second(self, z, kind):
        for p in ((0, 1), (2,))[kind]:
            self.first_copy(z, p).wait_recv()
            self.t2[z, self.parts[p]] = self.partial(z, p, self.second_give[p]).astype(BF)
            self.second_copy(z, p).start()

    def stage_third(self, z, kind):
        for p in ((0, 1), (2,))[kind]:
            rows = self.parts[p]
            self.second_copy(z, p).wait_recv()
            total = self.partial(z, p, self.second_keep[p]) + self.rx2[z, rows].astype(F32)

            @pl.when(self.zc == z)
            def _():
                self.mine[rows, :] = total

            @pl.when(self.zc != z)
            def _():
                self.t3[z, rows] = total.astype(BF)
                self.third_copy(z, p).start()

    def finish(self, out):
        total = self.mine[...]
        for k in range(1, self.nz):
            sender = lax.rem(self.zc + k, self.nz)
            for p in range(3):
                rows = self.parts[p]
                remote(
                    self.t3.at[sender, rows], self.rx3.at[sender, rows], self.s3.at[p, sender], self.r3.at[p, sender],
                    self.me, 1 - self.core,
                ).wait_recv()
            total = total + self.rx3[sender].astype(F32)
        out[...] = total
        for z in range(self.nz):
            for kind in range(2):
                self.core_copy(z, kind).wait_send()
            for p in range(3):
                self.first_copy(z, p).wait_send()
                self.second_copy(z, p).wait_send()

            @pl.when(self.zc != z)
            def _():
                for p in range(3):
                    self.third_copy(z, p).wait_send()


def peer_of(own, total, k):
    other = lax.rem(own + k, total)
    dp = other // 2
    return other, dp, other - 2 * dp


def own_number():
    return 2 * lax.axis_index("dp") + lax.axis_index("head")


def greet_all(total):
    barrier = pltpu.get_barrier_semaphore()
    own = own_number()

    @pl.loop(1, total)
    def _(k):
        _, dp, head = peer_of(own, total, k)
        pl.semaphore_signal(
            barrier, inc=1, device_id={"dp": dp, "head": head}, device_id_type=pl.DeviceIdType.MESH
        )


def greeted_all(total):
    pl.semaphore_wait(pltpu.get_barrier_semaphore(), total - 1)


def share_start(total, src, inbox, ss, rs):
    own = own_number()
    inbox[own] = src[...]

    @pl.loop(1, total)
    def _(k):
        _, dp, head = peer_of(own, total, k)
        remote(src, inbox.at[own], ss.at[k], rs.at[own], dp, head).start()


def share_finish(total, src, inbox, ss, rs):
    own = own_number()

    @pl.loop(1, total)
    def _(k):
        other, dp, head = peer_of(own, total, k)
        remote(src, inbox.at[other], ss.at[k], rs.at[other], dp, head).wait()


HEADS = 4
HD = 60
FF = 960
KW = 15
STEP = 10
KREL = 383
NORM_EPS = 1e-05
BETA_ONE = 0.9
BETA_TWO = 0.999
LEARN_RATE = 0.1
WEIGHT_DECAY = 0.01
ADAM_EPS = 1e-08
LOG2E = 1.4426950408889634
LN2 = 0.6931471805599453
SCALE = HD ** (-0.5)
UNIT = 1.28125
D = 240
DP = 256
HF = 480
HFP = 512
FFP = 1024
HC = 120
MASK_LANE = 120
NEG = -1e30
FFA, ATT, CNV, FFB, OUT = 0, 2, 4, 6, 8
DOWNB_ONE, DOWNB_TWO, B_OUT, BATCH_GAIN, BATCH_BIAS, TAPS, DEPTH_BIAS = 10, 11, 12, 13, 14, 16, 31
VEC_ROWS = 32
BIG = 60 << 20


def head_places():
    out, at = {}, 0
    for name, size in (
        ("up1", D * HF), ("upb1", HF), ("dn1", HF * D), ("up2", D * HF), ("upb2", HF), ("dn2", HF * D),
        ("wq", D * HC), ("wk", D * HC), ("wv", D * HC), ("bq", HC), ("bv", HC),
        ("rel", 2 * KREL), ("wo", HC * D),
    ):
        out[name] = at
        at += size
    return out, at


def shared_places():
    out, at = {}, 0
    for name, size in (
        ("vec", 13 * D), ("p1", 2 * D * D), ("pb1", 2 * D), ("taps", KW * D), ("db", D),
        ("bg", D), ("bb", D), ("p2", D * D), ("pb2", D),
    ):
        out[name] = at
        at += size
    return out, at


def lane_iota(shape):
    return lax.broadcasted_iota(jnp.int32, shape, len(shape) - 1)


def slot_rows(size):
    return up_to(-(-(size + LANES - 1) // LANES), 16)


def dot(a, b):
    return jnp.dot(a, b, preferred_element_type=F32)


def dot_t(a, b):
    return lax.dot_general(a, b, (((1,), (1,)), ((), ())), preferred_element_type=F32)


def t_dot(a, b):
    return lax.dot_general(a, b, (((0,), (0,)), ((), ())), preferred_element_type=F32)


def vmem_call(body, outs, ins, scratch=(), name=None, limit=BIG):
    return pl.pallas_call(
        body,
        out_shape=outs,
        in_specs=[pl.BlockSpec(memory_space=pltpu.VMEM) for _ in ins],
        out_specs=jax.tree.map(lambda _: pl.BlockSpec(memory_space=pltpu.VMEM), outs),
        scratch_shapes=list(scratch),
        compiler_params=pltpu.CompilerParams(vmem_limit_bytes=limit),
        name=name,
    )(*ins)


def own_offsets(head_size, shared_size):
    me = lax.axis_index("dp")
    core = lax.axis_index("head")
    return lax.rem(me * head_size, LANES), lax.rem((2 * me + core) * shared_size, LANES)


def push_lanes(x, shift):
    rolled = pltpu.roll(x, shift, 1)
    before = jnp.concatenate([jnp.zeros((1, LANES), F32), rolled[:-1]], 0)
    return jnp.where(lane_iota(x.shape) >= shift, rolled, before)


def pull_lanes(x, shift):
    rolled = pltpu.roll(x, lax.rem(LANES - shift, LANES), 1)
    after = jnp.concatenate([rolled[1:], jnp.zeros((1, LANES), F32)], 0)
    return jnp.where(lane_iota(x.shape) < LANES - shift, rolled, after)


def align(head_ref, shared_ref, out):
    head_size, shared_size = head_ref.shape[1], shared_ref.shape[0]
    hr, sr = slot_rows(head_size), slot_rows(shared_size)
    ho, so = own_offsets(head_size, shared_size)
    x = jnp.concatenate([head_ref[...], jnp.zeros((1, hr * LANES - head_size), F32)], 1)
    out[pl.ds(0, hr), :] = push_lanes(x.reshape(hr, LANES), ho).astype(BF)
    x = shared_ref[...].reshape(1, shared_size)
    x = jnp.concatenate([x, jnp.zeros((1, sr * LANES - shared_size), F32)], 1)
    out[pl.ds(hr, sr), :] = push_lanes(x.reshape(sr, LANES), so).astype(BF)


def adam_kernel(
    early, grad, g_ref, hp, hf, hs, sp, sf, ss, out_o, grad_o, hf_o, hs_o, hp_o, hc_o, sf_o, ss_o, sp_o, sc_o
):
    out_o[...] = early[...]
    grad_o[...] = grad[...]

    @pl.when(pl.program_id(0) == 0)
    def _():
        adam_update(g_ref, hp, hf, hs, sp, sf, ss, hf_o, hs_o, hp_o, hc_o, sf_o, ss_o, sp_o, sc_o)


def adam_update(g_ref, hp, hf, hs, sp, sf, ss, hf_o, hs_o, hp_o, hc_o, sf_o, ss_o, sp_o, sc_o):
    head_size, shared_size = hp.shape[1], sp.shape[0]
    hr, sr = slot_rows(head_size), slot_rows(shared_size)
    ho, so = own_offsets(head_size, shared_size)

    def update(master, g, first, second):
        first_new = BETA_ONE * first + (1.0 - BETA_ONE) * g
        second_new = BETA_TWO * second + (1.0 - BETA_TWO) * g * g
        first_hat = first_new * (1.0 / (1.0 - BETA_ONE**STEP))
        second_hat = second_new * (1.0 / (1.0 - BETA_TWO**STEP))
        new = master - LEARN_RATE * (first_hat / (jnp.sqrt(second_hat) + ADAM_EPS) + WEIGHT_DECAY * master)
        return first_new, second_new, new

    g = pull_lanes(g_ref[pl.ds(0, hr), :], ho).reshape(1, hr * LANES)[:, :head_size]
    one, two, new = update(hp[...], g, hf[...], hs[...])
    hf_o[...] = one
    hs_o[...] = two
    hp_o[...] = new
    hc_o[...] = new.astype(BF)
    g = pull_lanes(g_ref[pl.ds(hr, sr), :], so).reshape(sr * LANES)[:shared_size]
    one, two, new = update(sp[...], g, sf[...], ss[...])
    sf_o[...] = one
    ss_o[...] = two
    sp_o[...] = new
    sc_o[...] = new.astype(BF)


def row_phases(rows, pitch):
    if rows == 1:
        return 1, 1, 0
    period = LANES // math.gcd(pitch, LANES)
    return period, rows // period, period * pitch // LANES


def take(flat, at, rows, pitch, col, width, dst, row0, lane0):
    period, count, stride = row_phases(rows, pitch)
    lane = lane_iota((count, LANES))
    for j in range(period):
        start = at + j * pitch + col
        q, l = divmod(start, LANES)

        def load(t):
            if count == 1:
                return flat[pl.ds(q + t, 1), :]
            return flat[pl.ds(q + t, count, stride), :]

        pieces = [load(t) for t in range(-(-(l + width) // LANES))]
        if l:
            pieces = [pltpu.roll(x, LANES - l, 1) for x in pieces]
        for t in range(-(-width // LANES)):
            value = pieces[t]
            if l and t + 1 < len(pieces):
                value = jnp.where(lane < LANES - l, value, pieces[t + 1])
            left = width - t * LANES
            if left < LANES:
                value = jnp.where(lane < left, value, 0.0)
            rows_at = pl.ds(row0 + j, 1) if count == 1 else pl.ds(row0 + j, count, period)
            dst[lane0 // LANES + t, rows_at, :] = value


def give(flat, at, rows, pitch, col, width, src, row0, lane0):
    period, count, stride = row_phases(rows, pitch)
    lane = lane_iota((count, LANES))
    for j in range(period):
        start = at + j * pitch + col
        q, l = divmod(start, LANES)
        rows_at = pl.ds(row0 + j, 1) if count == 1 else pl.ds(row0 + j, count, period)
        pieces = [src[lane0 // LANES + t, rows_at, :] for t in range(-(-width // LANES))]
        if l:
            pieces = [pltpu.roll(x, l, 1) for x in pieces]
        total = -(-(l + width) // LANES)
        for t in range(total):
            here = pl.ds(q + t, 1) if count == 1 else pl.ds(q + t, count, stride)
            if not l:
                value = pieces[t]
            elif t == 0:
                value = pieces[0]
            elif t == len(pieces):
                value = pieces[t - 1]
            else:
                value = jnp.where(lane >= l, pieces[t], pieces[t - 1])
            lo = l if t == 0 else 0
            hi = min(LANES, l + width - t * LANES)
            if lo or hi < LANES:
                keep = (lane >= lo) & (lane < hi)
                value = jnp.where(keep, value, flat[here, :])
            flat[here, :] = value


def spill(tiles, rows, dst, factor=None):
    for t in range(dst.shape[1] // LANES):
        value = tiles[t, pl.ds(0, rows), :]
        if factor:
            value = factor * value
        dst[:, pl.ds(t * LANES, LANES)] = value.astype(dst.dtype)


def load_tiles(src, tiles, factor=None):
    for t in range(src.shape[1] // LANES):
        value = src[:, pl.ds(t * LANES, LANES)]
        tiles[t, pl.ds(0, src.shape[0]), :] = factor * value if factor else value


def flat_rows(total, size):
    return up_to(total // LANES + slot_rows(size) + 16, 16)


class Weights:
    def __init__(self, dp, head_size, shared_size, got, refs):
        self.dp, self.head_size, self.shared_size, self.got = dp, head_size, shared_size, got
        self.hr, self.sr = slot_rows(head_size), slot_rows(shared_size)
        self.fh, self.fs, self.wide, self.tall, self.tmp = refs
        self.hp, _ = head_places()
        self.sp, _ = shared_places()

    def clear_flat(self):
        self.fh[...] = jnp.zeros(self.fh.shape, F32)
        self.fs[...] = jnp.zeros(self.fs.shape, F32)

    def merge(self, slot, core, p):
        rows = self.hr + self.sr
        cut = up_to(rows // 2, 16)
        first = (slot * self.head_size) // LANES
        low, high = ((0, min(cut, self.hr)), (min(cut, self.hr), self.hr))[p]
        if high > low:
            at = pl.ds(first + low, high - low)
            self.fh[core, at, :] += self.got[slot, core, pl.ds(low, high - low), :].astype(F32)
        low, high = ((self.hr, max(cut, self.hr)), (max(cut, self.hr), rows))[p]
        if high > low:
            at = pl.ds(((2 * slot + core) * self.shared_size) // LANES + low - self.hr, high - low)
            self.fs[at, :] += self.got[slot, core, pl.ds(low, high - low), :].astype(F32)

    def clear(self, tiles, count, row, size):
        for t in range(count):
            tiles[t, pl.ds(row, size), :] = jnp.zeros((size, LANES), F32)

    def patch(self, tiles, tile, row, where, value):
        part = tiles[tile, pl.ds(row, 1), :]
        tiles[tile, pl.ds(row, 1), :] = jnp.where(where, value, part)

    def ffn(self, up, dn, up_place, bias_place, dn_place, row):
        wide, tall, hp = self.wide, self.tall, self.hp
        self.clear(wide, 8, 240, 16)
        for g in range(2):
            take(self.fh.at[g], hp[up_place], D, HF, 0, HF, wide, 0, g * HFP)
            take(self.fh.at[g], hp[bias_place], 1, HF, 0, HF, wide, 240, g * HFP)
        self.patch(wide, 3, 240, lane_iota((1, LANES)) == HF - 3 * LANES, UNIT)
        spill(wide, DP, up, 0.5)
        for g in range(2):
            self.clear(tall, 2, g * HFP + HF, 32)
            take(self.fh.at[g], hp[dn_place], HF, D, 0, D, tall, g * HFP, 0)
        take(self.fs, self.sp["vec"] + row * D, 1, D, 0, D, tall, HF, 0)
        spill(tall, FFP, dn, 0.5)

    def point_two(self, p2):
        self.clear(self.tall, 2, 240, 16)
        take(self.fs, self.sp["p2"], D, D, 0, D, self.tall, 0, 0)
        take(self.fs, self.sp["pb2"], 1, D, 0, D, self.tall, 240, 0)
        spill(self.tall, DP, p2)

    def others(self, qkv, wo, p1, vec, rel):
        wide, tall, tmp, fh, fs, hp, sp = self.wide, self.tall, self.tmp, self.fh, self.fs, self.hp, self.sp
        lane = lane_iota((1, LANES))
        self.clear(wide, 6, 240, 16)
        for g in range(2):
            for which, (place, bplace) in enumerate((("wq", "bq"), ("wk", None), ("wv", "bv"))):
                lane0 = which * DP + g * LANES
                take(fh.at[g], hp[place], D, HC, 0, HC, wide, 0, lane0)
                if bplace:
                    take(fh.at[g], hp[bplace], 1, HC, 0, HC, wide, 240, lane0)
        for tile in (0, 1, 4, 5):
            self.patch(wide, tile, 240, lane == MASK_LANE, 1.0)
        spill(wide, DP, qkv)
        self.clear(tall, 2, 0, DP)
        for g in range(2):
            take(fh.at[g], hp["wo"], HC, D, 0, D, tall, g * LANES, 0)
        take(fs, sp["vec"] + B_OUT * D, 1, D, 0, D, tall, MASK_LANE, 0)
        spill(tall, DP, wo)
        self.clear(wide, 4, 240, 16)
        for half in range(2):
            take(fs, sp["p1"], D, 2 * D, half * D, D, wide, 0, half * DP)
            take(fs, sp["pb1"] + half * D, 1, D, 0, D, wide, 240, half * DP)
        spill(wide, DP, p1)
        take(fs, sp["vec"], 16, D, 0, D, tall, 0, 0)
        take(fs, sp["taps"], 16, D, 0, D, tall, TAPS, 0)
        take(fs, sp["bg"], 1, D, 0, D, tall, BATCH_GAIN, 0)
        take(fs, sp["bb"], 1, D, 0, D, tall, BATCH_BIAS, 0)
        for row, value in ((FFA + 1, 1.0), (ATT + 1, 1.0), (CNV + 1, 1.0), (FFB + 1, 1.0), (BATCH_BIAS, UNIT)):
            self.patch(tall, 1, row, lane == D - LANES, value)
        spill(tall, VEC_ROWS, vec)
        length = rel.shape[1]
        for n in range(HEADS):
            take(fh.at[n // 2], hp["rel"] + (n % 2) * KREL, 1, KREL, 0, KREL, tmp, 0, 0)
            row = jnp.concatenate([tmp[t, pl.ds(0, 1), :] for t in range(3)] + [jnp.zeros((1, LANES), F32)], 1)
            rows = jnp.broadcast_to(row, (length, 4 * LANES))
            rows = pltpu.roll(rows, 4 * LANES - (length - 1), 1, stride=1, stride_axis=0)
            rel[pl.ds(n * length, length), :] = rows[:, :length] * LOG2E


class Flat:
    @staticmethod
    def scratch(dp, head_size, shared_size):
        vm = pltpu.VMEM
        return [
            vm((2, flat_rows(head_size * dp, head_size), LANES), F32),
            vm((flat_rows(shared_size * 2 * dp, shared_size), LANES), F32),
            vm((8, DP, LANES), F32),
            vm((2, FFP, LANES), F32),
            vm((4, 8, LANES), F32),
        ]

    def __init__(self, dp, head_size, shared_size, refs):
        self.dp, self.head_size, self.shared_size = dp, head_size, shared_size
        self.hr, self.sr = slot_rows(head_size), slot_rows(shared_size)
        self.fh, self.fs, self.wide, self.tall, self.tmp = refs
        self.hp, self.used_h = head_places()
        self.sp, self.used_s = shared_places()

    def clear_unused(self):
        for g in range(2):
            first = self.used_h // LANES // 8 * 8
            count = self.fh.shape[1] - first
            self.fh[g, pl.ds(first, count), :] = jnp.zeros((count, LANES), F32)
        first = self.used_s // LANES // 8 * 8
        count = self.fs.shape[0] - first
        self.fs[pl.ds(first, count), :] = jnp.zeros((count, LANES), F32)

    def head(self, g, place, rows, pitch, src, row0, lane0):
        give(self.fh.at[g], self.hp[place], rows, pitch, 0, pitch, src, row0, lane0)

    def shared(self, place, at, rows, pitch, col, src, row0, lane0):
        give(self.fs, self.sp[place] + at, rows, pitch, col, D, src, row0, lane0)

    def up(self, up, place, bias_place):
        load_tiles(up, self.wide, 0.5)
        for g in range(2):
            self.head(g, place, D, HF, self.wide, 0, g * HFP)
            self.head(g, bias_place, 1, HF, self.wide, 240, g * HFP)

    def down(self, dn, place, row):
        for t in range(2):
            self.tall[t] = (0.5 * dn[pl.ds(t * LANES, LANES), :]).astype(BF).T.astype(F32)
        for g in range(2):
            self.head(g, place, HF, D, self.tall, g * HFP, 0)
        self.shared("vec", row * D, 1, D, 0, self.tall, HF, 0)

    def attention(self, qkv, wo, rel):
        load_tiles(qkv, self.wide)
        load_tiles(wo, self.tall)
        length = rel.shape[0] // HEADS
        for g in range(2):
            for which, (place, bplace) in enumerate((("wq", "bq"), ("wk", None), ("wv", "bv"))):
                lane0 = which * DP + g * LANES
                self.head(g, place, D, HC, self.wide, 0, lane0)
                if bplace:
                    self.head(g, bplace, 1, HC, self.wide, 240, lane0)
            self.head(g, "wo", HC, D, self.tall, g * LANES, 0)
        for n in range(HEADS):
            total = jnp.zeros((8, 4 * LANES), F32)
            for block in range(length // 8):
                rows = rel[pl.ds(n * length + 8 * block, 8), :]
                rows = jnp.concatenate([rows, jnp.zeros((8, 4 * LANES - length), F32)], 1)
                total = total + pltpu.roll(rows, length - 8 - 8 * block, 1)
            row = total[7:8]
            for i in range(7):
                row = row + pltpu.roll(total[i : i + 1], 7 - i, 1)
            for t in range(4):
                self.tmp[t, pl.ds(0, 1), :] = row[:, t * LANES : (t + 1) * LANES]
            give(self.fh.at[n // 2], self.hp["rel"] + (n % 2) * KREL, 1, KREL, 0, KREL, self.tmp, 0, 0)
        self.shared("vec", B_OUT * D, 1, D, 0, self.tall, MASK_LANE, 0)

    def points(self, p1, p2):
        load_tiles(p1, self.wide)
        load_tiles(p2, self.tall)
        for half in range(2):
            self.shared("p1", 0, D, 2 * D, half * D, self.wide, 0, half * DP)
            self.shared("pb1", half * D, 1, D, 0, self.wide, 240, half * DP)
        self.shared("p2", 0, D, D, 0, self.tall, 0, 0)
        self.shared("pb2", 0, 1, D, 0, self.tall, 240, 0)

    def vectors(self, vec, vec2):
        for t in range(2):
            cols = pl.ds(t * LANES, LANES)
            self.tall[t, pl.ds(0, VEC_ROWS), :] = vec[:, cols] + vec2[:, cols]
        for row in range(2, 10):
            self.shared("vec", row * D, 1, D, 0, self.tall, row, 0)
        self.shared("taps", 0, 16, D, 0, self.tall, TAPS, 0)
        self.shared("bg", 0, 1, D, 0, self.tall, BATCH_GAIN, 0)
        self.shared("bb", 0, 1, D, 0, self.tall, BATCH_BIAS, 0)

    def first_norm(self, vec):
        for t in range(2):
            self.tall[t, pl.ds(0, 8), :] = vec[pl.ds(0, 8), pl.ds(t * LANES, LANES)]
        for row in (FFA, FFA + 1):
            self.shared("vec", row * D, 1, D, 0, self.tall, row, 0)

    def slots(self, out, z, kind):
        for i in range(4 * z, 4 * z + 4):
            for g in range(2):
                if kind == 0:
                    out[g, i, pl.ds(0, self.hr), :] = self.fh[g, pl.ds(i * self.head_size // LANES, self.hr), :].astype(BF)
                else:
                    at = (2 * i + g) * self.shared_size // LANES
                    out[g, i, pl.ds(self.hr, self.sr), :] = self.fs[pl.ds(at, self.sr), :].astype(BF)

    def groups(self):
        size = 4 * self.head_size
        every = range(self.dp // 4)
        one = [z for z in every if z * size >= self.hp["up2"] and (z + 1) * size <= self.hp["wq"]]
        two = [z for z in every if z * size >= self.hp["dn1"] and z not in one]
        late = [z for z in every if 8 * z * self.shared_size < 2 * D]
        return one, two, [z for z in every if z not in one and z not in two], [z for z in every if z not in late], late


def row_sum(x):
    return jnp.sum(x, -1, keepdims=True)


def halves(x):
    return x[:, :LANES], x[:, LANES:]


def both(lo, hi):
    return jnp.concatenate([lo, hi], 1)


def norm(x, gain, bias):
    lane = lane_iota((1, LANES))
    lo, hi = halves(x)
    mean = row_sum(lo + hi) * (1.0 / D)
    lo = lo - mean
    hi = jnp.where(lane < D - LANES, hi - mean, 0.0)
    inv = lax.rsqrt(row_sum(lo * lo + hi * hi) * (1.0 / D) + NORM_EPS)
    lo, hi = lo * inv, hi * inv
    return both(lo, hi) * gain + bias, both(lo, jnp.where(lane == LANES - 1, inv, hi))


def norm_grad(grad, kept, gain):
    dg = grad * gain
    inv = kept[:, DP - 1 :]
    first = row_sum(dg) * (1.0 / D)
    second = row_sum(dg * kept) * (1.0 / D)
    return inv * (dg - first - kept * second)


def fold_rows(x):
    return jnp.sum(x.reshape(x.shape[0] // 8, 8, x.shape[1]), 0)


def norm_param_grads(acc, row, grad, kept):
    acc[row] += fold_rows(grad * kept)
    acc[row + 1] += fold_rows(grad)


def settle(acc, out):
    for row in range(acc.shape[0]):
        out[pl.ds(row, 1), :] = jnp.sum(acc[row], 0, keepdims=True)


def silu_pair(y):
    p = jnp.tanh(y) + 1.0
    h = (y * p).astype(BF)
    p = p.astype(BF)
    return h, p + h * (2.0 - p)


def widen(x):
    rows = x.shape[0]
    return jnp.concatenate([x.astype(F32), jnp.zeros((rows, DP - D), F32)], 1)


SHORT = (1, 1, 1, 1, 3, 1, 1, 4)
LATE = (4, 1)
LONG = (1, 1, 1)
PAIR = (1, 1)


def columns(ref, widths):
    out, at = [], 0
    for width in widths:
        out.append(ref.at[:, pl.ds(at * DP, width * DP)])
        at += width
    return out


def head_lanes():
    lane = lane_iota((1, LANES))
    return lane < HD, (lane >= HD) & (lane < 2 * HD), lane == MASK_LANE


def valid_rows(lengths, at, length):
    return lax.broadcasted_iota(jnp.int32, (length, 1), 0) < lengths[at]


def phase_a_kernel(
    seqs, sizes, lengths, frames, head_ref, shared_ref,
    short_far, late_far, long_far, kept1_far, xw_far, e_far, keep_o, up, dn, up2, dn2, wqkv, wo, p1, p2, vec, rel,
    pad, stats_o, inbox, ss, rs, own_slot, got, fh, fs, wide, tall, tmp,
    short_b, late_b, long_b, kept1_b, xw_b, e_b, out_sem, *sems,
):
    step = pl.program_id(0)
    slot = lax.rem(step, 2)
    far = (short_far, late_far, long_far, kept1_far, xw_far, e_far)
    near = (short_b, late_b, long_b, kept1_b, xw_b, e_b)

    def moves(k):
        side = lax.rem(k, 2)
        out = []
        for j, (here, there) in enumerate(zip(near, far)):
            size = here.shape[1]
            rows = pl.ds(pl.multiple_of(k * size, size), size)
            out.append(pltpu.make_async_copy(here.at[side], there.at[rows], out_sem.at[side, j]))
        return out

    @pl.when(step >= 2)
    def _():
        for move in moves(step - 2):
            move.wait()

    short_o, late_o, long_o, kept1_o, xw_o, e_o = (ref.at[slot] for ref in near)
    total = inbox.shape[0]
    weights = Weights(*sizes, got, (fh, fs, wide, tall, tmp))
    gl_o, f1_o, f2_o, a3_o, qkv_o, m_o, a2_o, h_o = columns(short_o, SHORT)
    sp_o, a1_o = columns(late_o, LATE)
    kept3_o, kept2_o, rl_o = columns(long_o, LONG)
    x2_o, w_o = columns(xw_o, PAIR)

    @pl.when(step == 0)
    def _():
        greet_all(total)
        align(head_ref, shared_ref, own_slot)
        weights.clear_flat()
        greeted_all(total)
        gather(sizes[0] // 4, own_slot, got, sems, weights.merge)
        weights.ffn(up, dn, "up1", "upb1", "dn1", DOWNB_ONE)
        weights.others(wqkv, wo, p1, vec, rel)

    length = frames.shape[1]
    tokens = seqs * length
    first_seq = lax.axis_index("head") * (seqs * pl.num_programs(0)) + step * seqs

    def v(row):
        return vec[pl.ds(row, 1), :]

    x0 = widen(frames[...].reshape(tokens, D))
    a, kept1_o[...] = norm(x0, v(FFA), v(FFA + 1))
    a = a.astype(BF)
    a1_o[...] = a
    h, slope = silu_pair(dot(a, up[...]))
    h_o[...] = h
    sp_o[...] = slope
    x1 = x0 + dot(h, dn[...])
    a, kept = norm(x1, v(ATT), v(ATT + 1))
    kept2_o[...] = kept.astype(BF)
    a = a.astype(BF)
    a2_o[...] = a
    qkv = dot(a, wqkv[...])
    first, second, special = head_lanes()
    for b in range(seqs):
        rows = pl.ds(b * length, length)
        fence = jnp.where(valid_rows(lengths, first_seq + b, length), 0.0, NEG)
        for g in range(2):
            def piece(which):
                at = which * DP + g * LANES
                return qkv[b * length : (b + 1) * length, at : at + LANES]

            q = (piece(0) * (SCALE * LOG2E)).astype(BF)
            k = jnp.where(special, fence, piece(1)).astype(BF)
            vv = piece(2).astype(BF)
            qkv_o[rows, pl.ds(g * LANES, LANES)] = q
            qkv_o[rows, pl.ds(DP + g * LANES, LANES)] = k
            qkv_o[rows, pl.ds(2 * DP + g * LANES, LANES)] = vv
            zero = jnp.zeros_like(q)
            pair = jnp.concatenate([jnp.where(first | special, q, zero), jnp.where(second | special, q, zero)], 0)
            at = pl.ds(2 * g * length, 2 * length)
            s = dot_t(pair, k) + rel[at, :]
            e = jnp.exp2(s - jnp.max(s, -1, keepdims=True)).astype(BF)
            e_o[b, at, :] = e
            o = dot(e, vv)
            r = 1.0 / o[:, MASK_LANE : MASK_LANE + 1]
            shares = jnp.where(second, r[length:], r[:length])
            rl_o[rows, pl.ds(g * LANES, LANES)] = shares.astype(BF)
            m_o[rows, pl.ds(g * LANES, LANES)] = (jnp.where(second, o[length:], o[:length]) * shares).astype(BF)
    x2 = x1 + dot(m_o[...], wo[...])
    x2_o[...] = x2
    a, kept = norm(x2, v(CNV), v(CNV + 1))
    kept3_o[...] = kept.astype(BF)
    a = a.astype(BF)
    a3_o[...] = a
    e = dot(a, p1[...])
    half = KW // 2

    @pl.when(step == 0)
    def _():
        pad[...] = jnp.zeros(pad.shape, F32)
        stats_o[...] = jnp.zeros(stats_o.shape, F32)

    count = jnp.float32(0.0)
    summed = jnp.zeros((1, DP), F32)
    for b in range(seqs):
        rows = pl.ds(b * length, length)
        valid = jnp.where(valid_rows(lengths, first_seq + b, length), 1.0, 0.0)
        linear = e[b * length : (b + 1) * length, :DP]
        gate = 0.5 * jnp.tanh(0.5 * e[b * length : (b + 1) * length, DP:]) + 0.5
        f1 = gate * valid
        gl = linear * f1
        f1_o[rows, :] = f1.astype(BF)
        f2_o[rows, :] = (gl * (1.0 - gate)).astype(BF)
        gl_o[rows, :] = gl.astype(BF)
        for t in range(2):
            cols = pl.ds(t * LANES, LANES)
            pad[b, t, pl.ds(8, length), :] = gl[:, t * LANES : (t + 1) * LANES]
            acc = jnp.broadcast_to(vec[pl.ds(DEPTH_BIAS, 1), cols], (length, LANES))
            for r in range(KW):
                acc = acc + pad[b, t, pl.ds(8 - half + r, length), :] * vec[pl.ds(TAPS + r, 1), cols]
            w_o[rows, cols] = acc
        summed = summed + jnp.sum(w_o[rows, :] * valid, 0, keepdims=True)
        count = count + lengths[first_seq + b].astype(F32)
    mean = summed / count
    square = jnp.zeros((1, DP), F32)
    for b in range(seqs):
        valid = jnp.where(valid_rows(lengths, first_seq + b, length), 1.0, 0.0)
        centre = (w_o[pl.ds(b * length, length), :] - mean) * valid
        square = square + jnp.sum(centre * centre, 0, keepdims=True)
    old = stats_o[pl.ds(4, 1), :]
    new = old + count
    for t in range(2):
        cols = slice(t * LANES, (t + 1) * LANES)
        before = stats_o[pl.ds(t, 1), :]
        delta = mean[:, cols] - before
        stats_o[pl.ds(t, 1), :] = before + delta * (count / new)
        stats_o[pl.ds(2 + t, 1), :] += square[:, cols] + delta * delta * (old * count / new)
    stats_o[pl.ds(4, 1), :] = new
    for move in moves(step):
        move.start()

    @pl.when(step == pl.num_programs(0) - 1)
    def _():
        share_start(total, stats_o, inbox, ss, rs)
        weights.ffn(up2, dn2, "up2", "upb2", "dn2", DOWNB_TWO)
        weights.point_two(p2)
        share_finish(total, stats_o, inbox, ss, rs)
        batch_stats(inbox[...], keep_o)
        for move in moves(step - 1) + moves(step):
            move.wait()


def batch_stats(shared, keep):
    counts = shared[:, 4:5, :]
    total = jnp.sum(counts, 0)
    means, spreads = [], []
    for t in range(2):
        each = shared[:, t : t + 1, :]
        mean = jnp.sum(each * counts, 0) / total
        spread = (jnp.sum(shared[:, 2 + t : 3 + t, :], 0) + jnp.sum(counts * (each - mean) ** 2, 0)) / total
        means.append(mean)
        spreads.append(spread)
    keep[pl.ds(0, 1), :] = jnp.concatenate(means, 1)
    keep[pl.ds(1, 1), :] = lax.rsqrt(jnp.concatenate(spreads, 1) + NORM_EPS)
    keep[pl.ds(2, 1), :] = jnp.concatenate([total, total], 1)
    keep[pl.ds(3, 5), :] = jnp.zeros((5, DP), F32)


def phase_b_kernel(
    seqs, keep, xw, cotangent, p2, up, dn, vec,
    out_o, back_o, dup_o, ddn_o, dp2_o, vec_o, keep_o,
    acc, a_all, du_all, do_all, h_all, hc_all, dc_all, sums_o, inbox, ss, rs,
):
    step = pl.program_id(0)
    total = inbox.shape[0]
    length = cotangent.shape[1]
    tokens = seqs * length
    at = pl.ds(pl.multiple_of(step * tokens, tokens), tokens)
    x2, w = columns(xw, PAIR)
    dy_o, dx3_o = columns(back_o, PAIR)

    @pl.when(step == 0)
    def _():
        greet_all(total)
        for ref in (dup_o, ddn_o, dp2_o, acc):
            ref[...] = jnp.zeros(ref.shape, F32)

    def v(row):
        return vec[pl.ds(row, 1), :]

    mean, inv_batch = keep[pl.ds(0, 1), :], keep[pl.ds(1, 1), :]
    z = (w[...] - mean) * inv_batch
    hc, slope_c = silu_pair(z * (0.5 * v(BATCH_GAIN)) + 0.5 * v(BATCH_BIAS))
    x3 = x2[...] + dot(hc, p2[...])
    a, kept = norm(x3, v(FFB), v(FFB + 1))
    a = a.astype(BF)
    h, slope = silu_pair(dot(a, up[...]))
    x4 = x3 + dot(h, dn[...])
    final, kept4 = norm(x4, v(OUT), v(OUT + 1))
    out_o[...] = final[:, :D].astype(BF).reshape(seqs, length, D)
    g = widen(cotangent[...].reshape(tokens, D))
    norm_param_grads(acc, OUT, g, kept4)
    dx4 = norm_grad(g, kept4, v(OUT))
    do = dx4.astype(BF)
    do_all[at, :] = do
    h_all[at, :] = h
    du = dot_t(do, dn[...]).astype(BF) * slope
    a_all[at, :] = a
    du_all[at, :] = du
    da = dot_t(du, up[...])
    norm_param_grads(acc, FFB, da, kept)
    dx3 = dx4 + norm_grad(da, kept, v(FFB))
    dx3_o[...] = dx3
    dc = dx3.astype(BF)
    hc_all[at, :] = hc
    dc_all[at, :] = dc
    dy = dot_t(dc, p2[...]) * slope_c.astype(F32)
    dy_o[...] = dy
    acc[BATCH_BIAS] += fold_rows(dy)
    acc[BATCH_GAIN] += fold_rows(dy * z)

    @pl.when(step == pl.num_programs(0) - 1)
    def _():
        acc[BATCH_BIAS] *= 0.5
        acc[BATCH_GAIN] *= 0.5
        settle(acc, vec_o)
        for row, source in ((0, BATCH_BIAS), (2, BATCH_GAIN)):
            line = vec_o[pl.ds(source, 1), :]
            for t in range(2):
                sums_o[pl.ds(row + t, 1), :] = line[:, t * LANES : (t + 1) * LANES]

    @pl.when(step == pl.num_programs(0) - 1)
    def _():
        greeted_all(total)
        share_start(total, sums_o, inbox, ss, rs)

        @pl.loop(0, pl.num_programs(0))
        def _(k):
            at = pl.ds(pl.multiple_of(k * tokens, tokens), tokens)
            ddn_o[...] += t_dot(do_all[at, :], h_all[at, :])
            dup_o[...] += t_dot(a_all[at, :], du_all[at, :])
            dp2_o[...] += t_dot(hc_all[at, :], dc_all[at, :])

        share_finish(total, sums_o, inbox, ss, rs)
        sums = jnp.sum(inbox[...], 0)
        keep_o[...] = keep[...]
        keep_o[pl.ds(3, 1), :] = jnp.concatenate([sums[0:1], sums[1:2]], 1)
        keep_o[pl.ds(4, 1), :] = jnp.concatenate([sums[2:3], sums[3:4]], 1)


def phase_c_kernel(
    seqs, steps, sizes, lengths, keep, xw_far, back_far, short_far, long_far, e_far, late_far, kept1_far,
    p1, wo, wqkv, dn, up, vec, dup2, ddn2, dp2, vec2,
    dx0_o, sum_o,
    dp1_o, dwo_o, dqkv_o, dup_o, ddn_o, vec_o, rel_o, dx1_buf, mine,
    acc, padw, padg, grads, w_b, back_b, short_b, long_b, e_b, late_b, kept1_b, in_sem, *refs,
):
    step = pl.program_id(0)
    length = dx0_o.shape[1]
    side = lax.rem(step, 2)
    cut = 3 * DP

    def fetch(k, names):
        to = lax.rem(k, 2)
        size = seqs * length
        rows = pl.ds(pl.multiple_of(k * size, size), size)
        make = pltpu.make_async_copy
        every = (
            lambda j: make(xw_far.at[rows, pl.ds(DP, DP)], w_b.at[to], in_sem.at[to, j]),
            lambda j: make(back_far.at[rows], back_b.at[to], in_sem.at[to, j]),
            lambda j: make(short_far.at[rows, pl.ds(0, cut)], short_b.at[to, :, pl.ds(0, cut)], in_sem.at[to, j]),
            lambda j: make(
                short_far.at[rows, pl.ds(cut, short_b.shape[2] - cut)],
                short_b.at[to, :, pl.ds(cut, short_b.shape[2] - cut)],
                in_sem.at[to, j],
            ),
            lambda j: make(long_far.at[rows], long_b.at[to], in_sem.at[to, j]),
            lambda j: make(e_far.at[pl.ds(k * seqs, seqs)], e_b.at[to], in_sem.at[to, j]),
            lambda j: make(late_far.at[rows], late_b.at[to], in_sem.at[to, j]),
            lambda j: make(kept1_far.at[rows], kept1_b.at[to], in_sem.at[to, j]),
        )
        return [every[j](j) for j in names]

    conv_names, rest_names, late_names = (0, 1, 2), (3, 4, 5), (6, 7)

    @pl.when(step == 0)
    def _():
        for move in fetch(step, conv_names + rest_names):
            move.start()

    @pl.when(step < steps - 1)
    def _():
        for move in fetch(step + 1, conv_names + rest_names):
            move.start()

    @pl.when(step == steps - 1)
    def _():
        for move in fetch(step * 0, late_names):
            move.start()

    @pl.when((step >= steps) & (step < 2 * steps - 1))
    def _():
        for move in fetch(step + 1 - steps, late_names):
            move.start()

    w, back, short, long, e_all = (ref.at[side] for ref in (w_b, back_b, short_b, long_b, e_b))
    late_side = lax.rem(jnp.maximum(step - steps, 0), 2)
    late, kept1 = late_b.at[late_side], kept1_b.at[late_side]
    flat = Flat(*sizes, refs[:5])
    nz = sizes[0] // 4
    scatter = Scatter(nz, flat.hr, flat.sr, mine, refs[5:])
    one, two, rest, shared_two, shared_rest = flat.groups()
    dy, dx3 = columns(back, PAIR)
    gl, f1, f2, a3, qkv, m, a2, h = columns(short, SHORT)
    kept3, kept2, rl = columns(long, LONG)
    slope, a1 = columns(late, LATE)

    @pl.when(step == 0)
    def _():
        greet(nz, scatter.me, scatter.core, scatter.zc, scatter.yc, scatter.xc)
        for ref in (dp1_o, dwo_o, dqkv_o, dup_o, ddn_o, acc, rel_o, padw, padg):
            ref[...] = jnp.zeros(ref.shape, F32)
        flat.clear_unused()
        flat.up(dup2, "up2", "upb2")
        flat.down(ddn2, "dn2", DOWNB_TWO)
        for z in one:
            flat.slots(scatter.g, z, 0)
        greeted(nz)
        for z in one:
            scatter.stage_core(z, 0)

    @pl.when(step < steps)
    def _():
        def ready(names):
            for move in fetch(step, names):
                move.wait()

        ready(conv_names)
        phase_c_first(
            functools.partial(ready, rest_names), seqs, step, steps, length, lengths, keep, w, dy, dx3, gl, f1, f2, a3, kept3, qkv, e_all, rl, m, a2, kept2,
            h, p1, wo, wqkv, vec, dp1_o, dwo_o, dqkv_o, ddn_o, rel_o, dx1_buf, acc, padw, padg, grads,
        )

    @pl.when(step == steps)
    def _():
        flat.attention(dqkv_o, dwo_o, rel_o)
        flat.down(ddn_o, "dn1", DOWNB_ONE)
        for z in two:
            flat.slots(scatter.g, z, 0)
            scatter.stage_core(z, 0)
        settle(acc, vec_o)
        flat.points(dp1_o, dp2)
        flat.vectors(vec_o, vec2)
        for z in shared_two:
            flat.slots(scatter.g, z, 1)
            scatter.stage_core(z, 1)

    @pl.when(step >= steps)
    def _():
        for move in fetch(step - steps, late_names):
            move.wait()
        at = pl.ds(pl.multiple_of((step - steps) * (seqs * length), seqs * length), seqs * length)
        dx1 = dx1_buf[at, :]
        du = dot_t(dx1.astype(BF), dn[...]).astype(BF) * slope[...]
        dup_o[...] += t_dot(a1[...], du)
        da = dot_t(du, up[...])
        norm_param_grads(acc, FFA, da, kept1[...])
        dx0 = dx1 + norm_grad(da, kept1[...], vec[pl.ds(FFA, 1), :])
        dx0_o[...] = dx0[:, :D].reshape(seqs, length, D)

    stages = (scatter.stage_first, scatter.stage_second, scatter.stage_third)
    for at, heads, shared in (((1, 2, 3), one, []), ((steps + AT_A, steps + AT_B), two, shared_two)):
        for when, stage in zip(at, stages):
            @pl.when(step == when)
            def _():
                for z in heads:
                    stage(z, 0)
                for z in shared:
                    stage(z, 1)

    @pl.when(step == 2 * steps - 1)
    def _():
        flat.up(dup_o, "up1", "upb1")
        for z in rest:
            flat.slots(scatter.g, z, 0)
            scatter.stage_core(z, 0)
        settle(acc, vec_o)
        flat.first_norm(vec_o)
        for z in shared_rest:
            flat.slots(scatter.g, z, 1)
            scatter.stage_core(z, 1)
        for z in two:
            scatter.stage_third(z, 0)
        for z in shared_two:
            scatter.stage_third(z, 1)
        for stage in stages:
            for z in rest:
                stage(z, 0)
            for z in shared_rest:
                stage(z, 1)
        scatter.finish(sum_o)


def phase_c_first(
    ready, seqs, step, steps, length, lengths, keep, w, dy, dx3, gl, f1, f2, a3, kept3, qkv, e_all, rl, m, a2, kept2,
    h, p1, wo, wqkv, vec, dp1_o, dwo_o, dqkv_o, ddn_o, rel_o, dx1_buf, acc, padw, padg, grads,
):
    first_seq = lax.axis_index("head") * (seqs * steps) + step * seqs
    half = KW // 2

    def v(row):
        return vec[pl.ds(row, 1), :]

    mean, inv_batch, count = (keep[pl.ds(row, 1), :] for row in range(3))
    scale = v(BATCH_GAIN) * inv_batch
    cross = inv_batch * scale * keep[pl.ds(4, 1), :] / count
    plain = scale * keep[pl.ds(3, 1), :] / count - mean * cross
    scale = 0.5 * scale
    for b in range(seqs):
        rows = pl.ds(b * length, length)
        valid = jnp.where(valid_rows(lengths, first_seq + b, length), 1.0, 0.0)
        dw = dy[rows, :] * scale - valid * (plain + w[rows, :] * cross)
        acc[DEPTH_BIAS] += fold_rows(dw)
        for t in range(2):
            cols = pl.ds(t * LANES, LANES)
            here = dw[:, t * LANES : (t + 1) * LANES]
            padw[b, t, pl.ds(8, length), :] = here
            padg[b, t, pl.ds(8, length), :] = gl[rows, cols].astype(F32)
            total = jnp.zeros((length, LANES), F32)
            for r in range(KW):
                total = total + padw[b, t, pl.ds(8 + half - r, length), :] * vec[pl.ds(TAPS + r, 1), cols]
                tap = here * padg[b, t, pl.ds(8 - half + r, length), :]
                acc[TAPS + r, :, cols] += fold_rows(tap)
            grads[rows, cols] = (total * f1[rows, cols].astype(F32)).astype(BF)
            grads[rows, pl.ds(DP + t * LANES, LANES)] = (total * f2[rows, cols].astype(F32)).astype(BF)
    ready()
    de = grads[:, pl.ds(0, 2 * DP)]
    dp1_o[...] += t_dot(a3[...], de)
    da = dot_t(de, p1[...])
    kept = kept3[...].astype(F32)
    norm_param_grads(acc, CNV, da, kept)
    dx2 = dx3[...] + norm_grad(da, kept, v(CNV))
    db = dx2.astype(BF)
    dwo_o[...] += t_dot(m[...], db)
    dm = dot_t(db, wo[...])
    first, second, special = head_lanes()
    source = lax.broadcasted_iota(jnp.int32, (LANES, 2 * LANES), 0)
    target = lane_iota((LANES, 2 * LANES)) // LANES
    spread = jnp.where((source >= target * HD) & (source < (target + 1) * HD), 1.0, 0.0).astype(BF)
    for b in range(seqs):
        rows = pl.ds(b * length, length)
        for g in range(2):
            cols = pl.ds(g * LANES, LANES)
            q = qkv[rows, cols]
            k = qkv[rows, pl.ds(DP + g * LANES, LANES)]
            vv = qkv[rows, pl.ds(2 * DP + g * LANES, LANES)]
            dmb = (dm[b * length : (b + 1) * length, g * LANES : (g + 1) * LANES] * rl[rows, cols].astype(F32)).astype(BF)
            level = dot(dmb * m[rows, cols], spread)
            level = jnp.concatenate([level[:, :LANES], level[:, LANES:]], 0)
            zero = jnp.zeros_like(q)
            dm_pair = jnp.concatenate([jnp.where(first, dmb, zero), jnp.where(second, dmb, zero)], 0)
            q_pair = jnp.concatenate([jnp.where(first, q, zero), jnp.where(second, q, zero)], 0)
            at = pl.ds(2 * g * length, 2 * length)
            e = e_all[b, at, :]
            dp = dot_t(dm_pair, vv)
            ds = e.astype(F32) * (dp - jnp.concatenate([level, level[:, : length - LANES]], 1))
            rel_o[at, :] += ds
            ds = ds.astype(BF)
            dq = dot(ds, k)
            dq = jnp.where(second, dq[length:], dq[:length])
            grads[rows, cols] = (dq * SCALE).astype(BF)
            grads[rows, pl.ds(DP + g * LANES, LANES)] = (t_dot(ds, q_pair) * LN2).astype(BF)
            grads[rows, pl.ds(2 * DP + g * LANES, LANES)] = t_dot(e, dm_pair).astype(BF)
    dqkv = grads[...]
    dqkv_o[...] += t_dot(a2[...], dqkv)
    da = dot_t(dqkv, wqkv[...])
    kept = kept2[...].astype(F32)
    norm_param_grads(acc, ATT, da, kept)
    dx1 = dx2 + norm_grad(da, kept, v(ATT))
    at = pl.ds(pl.multiple_of(step * (seqs * length), seqs * length), seqs * length)
    dx1_buf[at, :] = dx1
    ddn_o[...] += t_dot(dx1.astype(BF), h[...])


def layer_call(body, steps, ins, outs, scratch, name, collective_id=None):
    def spec(item):
        kind, shape = item
        if kind == "far":
            return pl.BlockSpec(memory_space=pl.ANY)
        if kind == "smem":
            return pl.BlockSpec(memory_space=pltpu.SMEM)
        if kind == "tile":
            return pl.BlockSpec(shape, lambda i: (i,) + (0,) * (len(shape) - 1))
        if kind == "early":
            return pl.BlockSpec(shape, lambda i: (jnp.minimum(i, steps // 2 - 1),) + (0,) * (len(shape) - 1))
        if kind == "late":
            return pl.BlockSpec(shape, lambda i: (jnp.maximum(i - steps // 2, 0),) + (0,) * (len(shape) - 1))
        return pl.BlockSpec(shape, lambda i: (0,) * len(shape))

    arrays = [a for _, _, a in ins]
    return pl.pallas_call(
        body,
        grid=(steps,),
        out_shape=tuple(jax.ShapeDtypeStruct(full, dtype) for _, _, full, dtype in outs),
        in_specs=[spec((kind, block)) for kind, block, _ in ins],
        out_specs=tuple(spec((kind, block)) for kind, block, _, _ in outs),
        scratch_shapes=list(scratch),
        compiler_params=pltpu.CompilerParams(
            vmem_limit_bytes=BIG,
            dimension_semantics=("arbitrary",),
            collective_id=collective_id,
            has_side_effects=collective_id is not None,
        ),
        name=name,
    )(*arrays)


def tile_in(array, steps, kind="tile"):
    return (kind, (array.shape[0] // steps,) + array.shape[1:], array)


def whole_in(array):
    return ("whole", array.shape, array)


def tile_out(steps, shape, dtype, kind="tile"):
    return (kind, (shape[0] // steps,) + shape[1:], shape, dtype)


def far_in(array):
    return ("far", None, array)


def far_out(shape, dtype):
    return ("far", None, shape, dtype)


def whole_out(shape, dtype=F32):
    return ("whole", shape, shape, dtype)


SEQS_A = 4
SEQS_B = 4
SEQS_C = 4
AT_A = 2
AT_B = 3


def per_device(
    frames, cotangent, lengths, head_params, shared_params, head_first, head_second, shared_first, shared_second
):
    seq_here, length, _ = frames.shape
    tokens = seq_here * length
    dp = lax.axis_size("dp")
    head_size, shared_size = head_params.shape[1], shared_params.shape[0]
    rows = slot_rows(head_size) + slot_rows(shared_size)
    vm = pltpu.VMEM
    dma = pltpu.SemaphoreType.DMA
    sharing = [vm((8, LANES), F32), vm((2 * dp, 8, LANES), F32), dma((2 * dp,)), dma((2 * dp,))]
    steps = seq_here // SEQS_A
    block = SEQS_A * length
    t = functools.partial(tile_out, steps)
    (
        short, late, long, kept1, xw, e_all, keep,
        up1, dn1, up2, dn2, wqkv, wo, p1, p2, vec, rel
    ) = layer_call(
        functools.partial(phase_a_kernel, SEQS_A, (dp, head_size, shared_size)),
        steps,
        [("smem", None, lengths), tile_in(frames, steps), whole_in(head_params), whole_in(shared_params)],
        [
            far_out((tokens, sum(SHORT) * DP), BF), far_out((tokens, sum(LATE) * DP), BF),
            far_out((tokens, sum(LONG) * DP), BF), far_out((tokens, DP), F32), far_out((tokens, sum(PAIR) * DP), F32),
            far_out((seq_here, HEADS * length, length), BF),
            whole_out((8, DP)),
            whole_out((DP, FFP), BF), whole_out((FFP, DP), BF), whole_out((DP, FFP), BF), whole_out((FFP, DP), BF),
            whole_out((DP, 3 * DP), BF), whole_out((DP, DP), BF), whole_out((DP, 2 * DP), BF), whole_out((DP, DP), BF),
            whole_out((VEC_ROWS, DP)), whole_out((HEADS * length, length)),
        ],
        [vm((SEQS_A, 2, length + 16, LANES), F32)]
        + sharing
        + [vm((rows, LANES), BF), vm((dp, 2, rows, LANES), BF)]
        + Flat.scratch(dp, head_size, shared_size)
        + [
            vm((2, block, sum(SHORT) * DP), BF), vm((2, block, sum(LATE) * DP), BF), vm((2, block, sum(LONG) * DP), BF),
            vm((2, block, DP), F32), vm((2, block, sum(PAIR) * DP), F32), vm((2, SEQS_A, HEADS * length, length), BF),
            dma((2, 6)),
        ]
        + gather_sems(dp // 4),
        "phase_a",
        1,
    )
    steps = seq_here // SEQS_B
    t = functools.partial(tile_out, steps)
    early, back, dup2, ddn2, dp2, vec_b, keep = layer_call(
        functools.partial(phase_b_kernel, SEQS_B),
        steps,
        [whole_in(keep), tile_in(xw, steps), tile_in(cotangent, steps)]
        + [whole_in(x) for x in (p2, up2, dn2, vec)],
        [
            t((seq_here, length, D), BF), t((tokens, sum(PAIR) * DP), F32),
            whole_out((DP, FFP)), whole_out((DP, FFP)), whole_out((DP, DP)), whole_out((VEC_ROWS, DP)),
            whole_out((8, DP)),
        ],
        [
            vm((VEC_ROWS, 8, DP), F32), vm((tokens, DP), BF), vm((tokens, FFP), BF), vm((tokens, DP), BF),
            vm((tokens, FFP), BF), vm((tokens, DP), BF), vm((tokens, DP), BF),
        ]
        + sharing,
        "phase_b",
        3,
    )
    steps = seq_here // SEQS_C
    slot = (slot_rows(head_size), slot_rows(shared_size))
    block = SEQS_C * length
    input_grad, summed = layer_call(
        functools.partial(phase_c_kernel, SEQS_C, steps, (dp, head_size, shared_size)),
        2 * steps,
        [("smem", None, lengths), whole_in(keep)]
        + [far_in(x) for x in (xw, back, short, long, e_all, late, kept1)]
        + [whole_in(x) for x in (p1, wo, wqkv, dn1, up1, vec, dup2, ddn2, dp2, vec_b)],
        [tile_out(steps, (seq_here, length, D), F32, "late"), whole_out((rows, LANES))],
        [
            vm((DP, 2 * DP), F32), vm((DP, DP), F32), vm((DP, 3 * DP), F32), vm((DP, FFP), F32), vm((DP, FFP), F32),
            vm((VEC_ROWS, DP), F32), vm((HEADS * length, length), F32), vm((tokens, DP), F32), vm((rows, LANES), F32),
            vm((VEC_ROWS, 8, DP), F32),
            vm((SEQS_C, 2, length + 16, LANES), F32),
            vm((SEQS_C, 2, length + 16, LANES), F32),
            vm((block, 3 * DP), BF),
            vm((2, block, DP), F32), vm((2, block, sum(PAIR) * DP), F32), vm((2, block, sum(SHORT) * DP), BF),
            vm((2, block, sum(LONG) * DP), BF), vm((2, SEQS_C, HEADS * length, length), BF),
            vm((2, block, sum(LATE) * DP), BF), vm((2, block, DP), F32), dma((2, 8)),
        ]
        + Flat.scratch(dp, head_size, shared_size)
        + Scatter.scratch(dp, *slot),
        "phase_c",
        4,
    )
    h_shape, s_shape = head_params.shape, shared_params.shape
    steps = 4
    return layer_call(
        adam_kernel,
        steps,
        [tile_in(x, steps) for x in (early, input_grad)]
        + [whole_in(x) for x in (summed, head_params, head_first, head_second, shared_params, shared_first, shared_second)],
        [tile_out(steps, early.shape, BF), tile_out(steps, early.shape, F32)]
        + [whole_out(h_shape)] * 3
        + [whole_out(h_shape, BF)]
        + [whole_out(s_shape)] * 3
        + [whole_out(s_shape, BF)],
        [],
        "adam",
    )


def solution(mesh):
    frames = P(("dp", "head"), None, None)
    heads = P("head", "dp")
    shared = P(("dp", "head"))
    return jax.shard_map(
        per_device,
        mesh=mesh,
        in_specs=(frames, frames, P("dp"), heads, shared, heads, heads, shared, shared),
        out_specs=(frames, frames) + (heads,) * 4 + (shared,) * 4,
        check_vma=False,
    )
```

```python
import functools
import math

import jax
import jax.numpy as jnp
from jax import lax
from jax.experimental import pallas as pl
from jax.experimental.pallas import tpu as pltpu
from jax.sharding import PartitionSpec as P

BF = jnp.bfloat16
F32 = jnp.float32
LANES = 128


def up_to(count, unit):
    return -(-count // unit) * unit


def grid_place(nz):
    me = lax.axis_index("dp")
    core = lax.axis_index("head")
    zc = me // 4
    rest = me - 4 * zc
    yc = rest // 2
    xc = rest - 2 * yc
    return me, core, zc, yc, xc


def remote(src, dst, send, recv, dp, head):
    return pltpu.make_async_remote_copy(
        src_ref=src,
        dst_ref=dst,
        send_sem=send,
        recv_sem=recv,
        device_id={"dp": dp, "head": head},
        device_id_type=pl.DeviceIdType.MESH,
    )


def greet(nz, me, core, zc, yc, xc):
    barrier = pltpu.get_barrier_semaphore()

    def hello(dp, head):
        pl.semaphore_signal(
            barrier, inc=1, device_id={"dp": dp, "head": head}, device_id_type=pl.DeviceIdType.MESH
        )

    for k in range(1, nz):
        hello(lax.rem(zc + k, nz) * 4 + 2 * yc + xc, core)
    hello(4 * zc + 2 * (1 - yc) + xc, core)
    hello(4 * zc + 2 * yc + 1 - xc, core)
    hello(me, 1 - core)


def greeted(nz):
    pl.semaphore_wait(pltpu.get_barrier_semaphore(), nz + 2)


def gather(nz, src, out, sems, merge):
    sz, rz, s1, r1, s2, r2, sc, rc = sems
    rows = src.shape[0]
    row_a = up_to(rows // 2, 16)
    parts = (pl.ds(0, row_a), pl.ds(row_a, rows - row_a))
    me, core, zc, yc, xc = grid_place(nz)
    out[me, core] = src[...]
    y_peer = 4 * zc + 2 * (1 - yc) + xc
    x_peer = 4 * zc + 2 * yc + 1 - xc
    firsts = (y_peer, x_peer)
    seconds = (x_peer, y_peer)
    pending = []

    def send(slot, p, send_sem, recv_sem, dp, head):
        block = out.at[slot, core, parts[p]]
        copy = remote(block, block, send_sem, recv_sem, dp, head)
        copy.start()
        pending.append(copy)

    def arrived(slot, which, p, send_sem, recv_sem):
        block = out.at[slot, which, parts[p]]
        remote(block, block, send_sem, recv_sem, me, 1 - core).wait_recv()

    zs = [lax.rem(zc + k, nz) for k in range(nz)]
    here = 2 * yc + xc
    first_here = (2 * (1 - yc) + xc, 2 * yc + 1 - xc)
    second_here = ((2 * yc + 1 - xc, 2 * (1 - yc) + 1 - xc), (2 * (1 - yc) + xc, 2 * (1 - yc) + 1 - xc))
    for k in range(1, nz):
        for p in (0, 1):
            send(me, p, sz.at[p, k], rz.at[p, zc], zs[k] * 4 + here, core)
    for k in range(nz):
        z = zs[k]
        slot = 4 * z + here
        for p in (0, 1):
            if k:
                arrived(slot, core, p, sz.at[p, k], rz.at[p, z])
            send(slot, p, s1.at[p, k], r1.at[p, z], firsts[p], core)
            send(slot, p, s2.at[p, k, 0], r2.at[p, z, 0], seconds[p], core)
            send(slot, p, sc.at[p, k, 0], rc.at[p, z, 0], me, 1 - core)
    for k in range(nz):
        for p in (0, 1):
            merge(4 * zs[k] + here, core, p)
    for k in range(nz):
        z = zs[k]
        for p in (0, 1):
            slot = 4 * z + first_here[p]
            arrived(slot, core, p, s1.at[p, k], r1.at[p, z])
            send(slot, p, s2.at[p, k, 1], r2.at[p, z, 1], seconds[p], core)
            send(slot, p, sc.at[p, k, 1], rc.at[p, z, 1], me, 1 - core)
    for k in range(nz):
        for p in (0, 1):
            merge(4 * zs[k] + first_here[p], core, p)
    for k in range(nz):
        z = zs[k]
        for b in (0, 1):
            for p in (0, 1):
                slot = 4 * z + second_here[p][b]
                arrived(slot, core, p, s2.at[p, k, b], r2.at[p, z, b])
                send(slot, p, sc.at[p, k, 2 + b], rc.at[p, z, 2 + b], me, 1 - core)
        for b in (0, 1):
            for p in (0, 1):
                merge(4 * z + second_here[p][b], core, p)
    for k in range(nz):
        z = zs[k]
        for p in (0, 1):
            for b, at in enumerate((here, first_here[p]) + second_here[p]):
                arrived(4 * z + at, 1 - core, p, sc.at[p, k, b], rc.at[p, z, b])
                merge(4 * z + at, 1 - core, p)
    for copy in pending:
        copy.wait_send()


def gather_sems(nz):
    dma = pltpu.SemaphoreType.DMA
    return [
        dma((2, nz)), dma((2, nz)), dma((2, nz)), dma((2, nz)),
        dma((2, nz, 2)), dma((2, nz, 2)), dma((2, nz, 4)), dma((2, nz, 4)),
    ]


class Scatter:
    @staticmethod
    def scratch(dp, hr, sr):
        nz, rows = dp // 4, hr + sr
        dma, vm = pltpu.SemaphoreType.DMA, pltpu.VMEM
        return [
            vm((2, dp, rows, LANES), BF), vm((dp, rows, LANES), BF),
            vm((nz, 2, rows, LANES), BF), vm((nz, 2, rows, LANES), BF),
            vm((nz, rows, LANES), BF), vm((nz, rows, LANES), BF),
            vm((nz, rows, LANES), BF), vm((nz, rows, LANES), BF),
            dma((nz, 2)), dma((nz, 2)), dma((3, nz)), dma((3, nz)), dma((3, nz)), dma((3, nz)), dma((3, nz)), dma((3, nz)),
        ]

    def __init__(self, nz, hr, sr, mine, refs):
        self.nz, self.mine = nz, mine
        (
            self.g, self.c1, self.t1, self.rx1, self.t2, self.rx2, self.t3, self.rx3,
            self.sc, self.rc, self.s1, self.r1, self.s2, self.r2, self.s3, self.r3,
        ) = refs
        ha = up_to(hr // 2, 16)
        self.parts = (pl.ds(0, ha), pl.ds(ha, hr - ha), pl.ds(hr, sr))
        self.kinds = (pl.ds(0, hr), pl.ds(hr, sr))
        self.me, self.core, self.zc, self.yc, self.xc = grid_place(nz)
        zc, yc, xc = self.zc, self.yc, self.xc
        y_peer = 4 * zc + 2 * (1 - yc) + xc
        x_peer = 4 * zc + 2 * yc + 1 - xc
        self.firsts = (x_peer, y_peer, x_peer)
        self.seconds = (y_peer, x_peer, y_peer)
        self.second_give = (1 - yc, 1 - xc, 1 - yc)
        self.second_keep = (yc, xc, yc)

    def core_copy(self, z, kind):
        group, rows = pl.ds(4 * z, 4), self.kinds[kind]
        return remote(
            self.g.at[1 - self.core, group, rows], self.c1.at[group, rows],
            self.sc.at[z, kind], self.rc.at[z, kind], self.me, 1 - self.core,
        )

    def first_copy(self, z, p):
        rows = self.parts[p]
        return remote(
            self.t1.at[z, :, rows], self.rx1.at[z, :, rows], self.s1.at[p, z], self.r1.at[p, z], self.firsts[p], self.core
        )

    def second_copy(self, z, p):
        rows = self.parts[p]
        return remote(
            self.t2.at[z, rows], self.rx2.at[z, rows], self.s2.at[p, z], self.r2.at[p, z], self.seconds[p], self.core
        )

    def third_copy(self, z, p):
        rows = self.parts[p]
        return remote(
            self.t3.at[z, rows], self.rx3.at[self.zc, rows], self.s3.at[p, z], self.r3.at[p, self.zc],
            4 * z + 2 * self.yc + self.xc, self.core,
        )

    def place(self, p, z, b):
        return 4 * z + (2 * self.yc + b if p == 1 else 2 * b + self.xc)

    def held(self, z, p, slot):
        rows = self.parts[p]
        return self.g[self.core, slot, rows].astype(F32) + self.c1[slot, rows].astype(F32)

    def partial(self, z, p, b):
        return self.held(z, p, self.place(p, z, b)) + self.rx1[z, b, self.parts[p]].astype(F32)

    def stage_core(self, z, kind):
        self.core_copy(z, kind).start()

    def stage_first(self, z, kind):
        self.core_copy(z, kind).wait_recv()
        for p in ((0, 1), (2,))[kind]:
            for b in (0, 1):
                slot = 4 * z + (2 * (1 - self.yc) + b if p == 1 else 2 * b + 1 - self.xc)
                self.t1[z, b, self.parts[p]] = self.held(z, p, slot).astype(BF)
            self.first_copy(z, p).start()

    def stage_second(self, z, kind):
        for p in ((0, 1), (2,))[kind]:
            self.first_copy(z, p).wait_recv()
            self.t2[z, self.parts[p]] = self.partial(z, p, self.second_give[p]).astype(BF)
            self.second_copy(z, p).start()

    def stage_third(self, z, kind):
        for p in ((0, 1), (2,))[kind]:
            rows = self.parts[p]
            self.second_copy(z, p).wait_recv()
            total = self.partial(z, p, self.second_keep[p]) + self.rx2[z, rows].astype(F32)

            @pl.when(self.zc == z)
            def _():
                self.mine[rows, :] = total

            @pl.when(self.zc != z)
            def _():
                self.t3[z, rows] = total.astype(BF)
                self.third_copy(z, p).start()

    def finish(self, out):
        total = self.mine[...]
        for k in range(1, self.nz):
            sender = lax.rem(self.zc + k, self.nz)
            for p in range(3):
                rows = self.parts[p]
                remote(
                    self.t3.at[sender, rows], self.rx3.at[sender, rows], self.s3.at[p, sender], self.r3.at[p, sender],
                    self.me, 1 - self.core,
                ).wait_recv()
            total = total + self.rx3[sender].astype(F32)
        out[...] = total
        for z in range(self.nz):
            for kind in range(2):
                self.core_copy(z, kind).wait_send()
            for p in range(3):
                self.first_copy(z, p).wait_send()
                self.second_copy(z, p).wait_send()

            @pl.when(self.zc != z)
            def _():
                for p in range(3):
                    self.third_copy(z, p).wait_send()


def peer_of(own, total, k):
    other = lax.rem(own + k, total)
    dp = other // 2
    return other, dp, other - 2 * dp


def own_number():
    return 2 * lax.axis_index("dp") + lax.axis_index("head")


def greet_all(total):
    barrier = pltpu.get_barrier_semaphore()
    own = own_number()

    @pl.loop(1, total)
    def _(k):
        _, dp, head = peer_of(own, total, k)
        pl.semaphore_signal(
            barrier, inc=1, device_id={"dp": dp, "head": head}, device_id_type=pl.DeviceIdType.MESH
        )


def greeted_all(total):
    pl.semaphore_wait(pltpu.get_barrier_semaphore(), total - 1)


def share_start(total, src, inbox, ss, rs):
    own = own_number()
    inbox[own] = src[...]

    @pl.loop(1, total)
    def _(k):
        _, dp, head = peer_of(own, total, k)
        remote(src, inbox.at[own], ss.at[k], rs.at[own], dp, head).start()


def share_finish(total, src, inbox, ss, rs):
    own = own_number()

    @pl.loop(1, total)
    def _(k):
        other, dp, head = peer_of(own, total, k)
        remote(src, inbox.at[other], ss.at[k], rs.at[other], dp, head).wait()


HEADS = 4
HD = 60
FF = 960
KW = 15
STEP = 10
KREL = 383
NORM_EPS = 1e-05
BETA_ONE = 0.9
BETA_TWO = 0.999
LEARN_RATE = 0.1
WEIGHT_DECAY = 0.01
ADAM_EPS = 1e-08
LOG2E = 1.4426950408889634
LN2 = 0.6931471805599453
SCALE = HD ** (-0.5)
UNIT = 1.28125
D = 240
DP = 256
HF = 480
HFP = 512
FFP = 1024
HC = 120
MASK_LANE = 120
NEG = -1e30
FFA, ATT, CNV, FFB, OUT = 0, 2, 4, 6, 8
DOWNB_ONE, DOWNB_TWO, B_OUT, BATCH_GAIN, BATCH_BIAS, TAPS, DEPTH_BIAS = 10, 11, 12, 13, 14, 16, 31
VEC_ROWS = 32
BIG = 60 << 20


def head_places():
    out, at = {}, 0
    for name, size in (
        ("up1", D * HF), ("upb1", HF), ("dn1", HF * D), ("up2", D * HF), ("upb2", HF), ("dn2", HF * D),
        ("wq", D * HC), ("wk", D * HC), ("wv", D * HC), ("bq", HC), ("bv", HC),
        ("rel", 2 * KREL), ("wo", HC * D),
    ):
        out[name] = at
        at += size
    return out, at


def shared_places():
    out, at = {}, 0
    for name, size in (
        ("vec", 13 * D), ("p1", 2 * D * D), ("pb1", 2 * D), ("taps", KW * D), ("db", D),
        ("bg", D), ("bb", D), ("p2", D * D), ("pb2", D),
    ):
        out[name] = at
        at += size
    return out, at


def lane_iota(shape):
    return lax.broadcasted_iota(jnp.int32, shape, len(shape) - 1)


def slot_rows(size):
    return up_to(-(-(size + LANES - 1) // LANES), 16)


def dot(a, b):
    return jnp.dot(a, b, preferred_element_type=F32)


def dot_t(a, b):
    return lax.dot_general(a, b, (((1,), (1,)), ((), ())), preferred_element_type=F32)


def t_dot(a, b):
    return lax.dot_general(a, b, (((0,), (0,)), ((), ())), preferred_element_type=F32)


def vmem_call(body, outs, ins, scratch=(), name=None, limit=BIG):
    return pl.pallas_call(
        body,
        out_shape=outs,
        in_specs=[pl.BlockSpec(memory_space=pltpu.VMEM) for _ in ins],
        out_specs=jax.tree.map(lambda _: pl.BlockSpec(memory_space=pltpu.VMEM), outs),
        scratch_shapes=list(scratch),
        compiler_params=pltpu.CompilerParams(vmem_limit_bytes=limit),
        name=name,
    )(*ins)


def own_offsets(head_size, shared_size):
    me = lax.axis_index("dp")
    core = lax.axis_index("head")
    return lax.rem(me * head_size, LANES), lax.rem((2 * me + core) * shared_size, LANES)


def push_lanes(x, shift):
    rolled = pltpu.roll(x, shift, 1)
    before = jnp.concatenate([jnp.zeros((1, LANES), F32), rolled[:-1]], 0)
    return jnp.where(lane_iota(x.shape) >= shift, rolled, before)


def pull_lanes(x, shift):
    rolled = pltpu.roll(x, lax.rem(LANES - shift, LANES), 1)
    after = jnp.concatenate([rolled[1:], jnp.zeros((1, LANES), F32)], 0)
    return jnp.where(lane_iota(x.shape) < LANES - shift, rolled, after)


def align(head_ref, shared_ref, out):
    head_size, shared_size = head_ref.shape[1], shared_ref.shape[0]
    hr, sr = slot_rows(head_size), slot_rows(shared_size)
    ho, so = own_offsets(head_size, shared_size)
    x = jnp.concatenate([head_ref[...], jnp.zeros((1, hr * LANES - head_size), F32)], 1)
    out[pl.ds(0, hr), :] = push_lanes(x.reshape(hr, LANES), ho).astype(BF)
    x = shared_ref[...].reshape(1, shared_size)
    x = jnp.concatenate([x, jnp.zeros((1, sr * LANES - shared_size), F32)], 1)
    out[pl.ds(hr, sr), :] = push_lanes(x.reshape(sr, LANES), so).astype(BF)


def adam_kernel(
    early, grad, g_ref, hp, hf, hs, sp, sf, ss, out_o, grad_o, hf_o, hs_o, hp_o, hc_o, sf_o, ss_o, sp_o, sc_o
):
    out_o[...] = early[...]
    grad_o[...] = grad[...]

    @pl.when(pl.program_id(0) == 0)
    def _():
        adam_update(g_ref, hp, hf, hs, sp, sf, ss, hf_o, hs_o, hp_o, hc_o, sf_o, ss_o, sp_o, sc_o)


def adam_update(g_ref, hp, hf, hs, sp, sf, ss, hf_o, hs_o, hp_o, hc_o, sf_o, ss_o, sp_o, sc_o):
    head_size, shared_size = hp.shape[1], sp.shape[0]
    hr, sr = slot_rows(head_size), slot_rows(shared_size)
    ho, so = own_offsets(head_size, shared_size)

    def update(master, g, first, second):
        first_new = BETA_ONE * first + (1.0 - BETA_ONE) * g
        second_new = BETA_TWO * second + (1.0 - BETA_TWO) * g * g
        first_hat = first_new * (1.0 / (1.0 - BETA_ONE**STEP))
        second_hat = second_new * (1.0 / (1.0 - BETA_TWO**STEP))
        new = master - LEARN_RATE * (first_hat / (jnp.sqrt(second_hat) + ADAM_EPS) + WEIGHT_DECAY * master)
        return first_new, second_new, new

    g = pull_lanes(g_ref[pl.ds(0, hr), :], ho).reshape(1, hr * LANES)[:, :head_size]
    one, two, new = update(hp[...], g, hf[...], hs[...])
    hf_o[...] = one
    hs_o[...] = two
    hp_o[...] = new
    hc_o[...] = new.astype(BF)
    g = pull_lanes(g_ref[pl.ds(hr, sr), :], so).reshape(sr * LANES)[:shared_size]
    one, two, new = update(sp[...], g, sf[...], ss[...])
    sf_o[...] = one
    ss_o[...] = two
    sp_o[...] = new
    sc_o[...] = new.astype(BF)


def row_phases(rows, pitch):
    if rows == 1:
        return 1, 1, 0
    period = LANES // math.gcd(pitch, LANES)
    return period, rows // period, period * pitch // LANES


def take(flat, at, rows, pitch, col, width, dst, row0, lane0):
    period, count, stride = row_phases(rows, pitch)
    lane = lane_iota((count, LANES))
    for j in range(period):
        start = at + j * pitch + col
        q, l = divmod(start, LANES)

        def load(t):
            if count == 1:
                return flat[pl.ds(q + t, 1), :]
            return flat[pl.ds(q + t, count, stride), :]

        pieces = [load(t) for t in range(-(-(l + width) // LANES))]
        if l:
            pieces = [pltpu.roll(x, LANES - l, 1) for x in pieces]
        for t in range(-(-width // LANES)):
            value = pieces[t]
            if l and t + 1 < len(pieces):
                value = jnp.where(lane < LANES - l, value, pieces[t + 1])
            left = width - t * LANES
            if left < LANES:
                value = jnp.where(lane < left, value, 0.0)
            rows_at = pl.ds(row0 + j, 1) if count == 1 else pl.ds(row0 + j, count, period)
            dst[lane0 // LANES + t, rows_at, :] = value


def give(flat, at, rows, pitch, col, width, src, row0, lane0):
    period, count, stride = row_phases(rows, pitch)
    lane = lane_iota((count, LANES))
    for j in range(period):
        start = at + j * pitch + col
        q, l = divmod(start, LANES)
        rows_at = pl.ds(row0 + j, 1) if count == 1 else pl.ds(row0 + j, count, period)
        pieces = [src[lane0 // LANES + t, rows_at, :] for t in range(-(-width // LANES))]
        if l:
            pieces = [pltpu.roll(x, l, 1) for x in pieces]
        total = -(-(l + width) // LANES)
        for t in range(total):
            here = pl.ds(q + t, 1) if count == 1 else pl.ds(q + t, count, stride)
            if not l:
                value = pieces[t]
            elif t == 0:
                value = pieces[0]
            elif t == len(pieces):
                value = pieces[t - 1]
            else:
                value = jnp.where(lane >= l, pieces[t], pieces[t - 1])
            lo = l if t == 0 else 0
            hi = min(LANES, l + width - t * LANES)
            if lo or hi < LANES:
                keep = (lane >= lo) & (lane < hi)
                value = jnp.where(keep, value, flat[here, :])
            flat[here, :] = value


def spill(tiles, rows, dst, factor=None):
    for t in range(dst.shape[1] // LANES):
        value = tiles[t, pl.ds(0, rows), :]
        if factor:
            value = factor * value
        dst[:, pl.ds(t * LANES, LANES)] = value.astype(dst.dtype)


def load_tiles(src, tiles, factor=None):
    for t in range(src.shape[1] // LANES):
        value = src[:, pl.ds(t * LANES, LANES)]
        tiles[t, pl.ds(0, src.shape[0]), :] = factor * value if factor else value


def flat_rows(total, size):
    return up_to(total // LANES + slot_rows(size) + 16, 16)


class Weights:
    def __init__(self, dp, head_size, shared_size, got, refs):
        self.dp, self.head_size, self.shared_size, self.got = dp, head_size, shared_size, got
        self.hr, self.sr = slot_rows(head_size), slot_rows(shared_size)
        self.fh, self.fs, self.wide, self.tall, self.tmp = refs
        self.hp, _ = head_places()
        self.sp, _ = shared_places()

    def clear_flat(self):
        self.fh[...] = jnp.zeros(self.fh.shape, F32)
        self.fs[...] = jnp.zeros(self.fs.shape, F32)

    def merge(self, slot, core, p):
        rows = self.hr + self.sr
        cut = up_to(rows // 2, 16)
        first = (slot * self.head_size) // LANES
        low, high = ((0, min(cut, self.hr)), (min(cut, self.hr), self.hr))[p]
        if high > low:
            at = pl.ds(first + low, high - low)
            self.fh[core, at, :] += self.got[slot, core, pl.ds(low, high - low), :].astype(F32)
        low, high = ((self.hr, max(cut, self.hr)), (max(cut, self.hr), rows))[p]
        if high > low:
            at = pl.ds(((2 * slot + core) * self.shared_size) // LANES + low - self.hr, high - low)
            self.fs[at, :] += self.got[slot, core, pl.ds(low, high - low), :].astype(F32)

    def clear(self, tiles, count, row, size):
        for t in range(count):
            tiles[t, pl.ds(row, size), :] = jnp.zeros((size, LANES), F32)

    def patch(self, tiles, tile, row, where, value):
        part = tiles[tile, pl.ds(row, 1), :]
        tiles[tile, pl.ds(row, 1), :] = jnp.where(where, value, part)

    def ffn(self, up, dn, up_place, bias_place, dn_place, row):
        wide, tall, hp = self.wide, self.tall, self.hp
        self.clear(wide, 8, 240, 16)
        for g in range(2):
            take(self.fh.at[g], hp[up_place], D, HF, 0, HF, wide, 0, g * HFP)
            take(self.fh.at[g], hp[bias_place], 1, HF, 0, HF, wide, 240, g * HFP)
        self.patch(wide, 3, 240, lane_iota((1, LANES)) == HF - 3 * LANES, UNIT)
        spill(wide, DP, up, 0.5)
        for g in range(2):
            self.clear(tall, 2, g * HFP + HF, 32)
            take(self.fh.at[g], hp[dn_place], HF, D, 0, D, tall, g * HFP, 0)
        take(self.fs, self.sp["vec"] + row * D, 1, D, 0, D, tall, HF, 0)
        spill(tall, FFP, dn, 0.5)

    def point_two(self, p2):
        self.clear(self.tall, 2, 240, 16)
        take(self.fs, self.sp["p2"], D, D, 0, D, self.tall, 0, 0)
        take(self.fs, self.sp["pb2"], 1, D, 0, D, self.tall, 240, 0)
        spill(self.tall, DP, p2)

    def others(self, qkv, wo, p1, vec, rel):
        wide, tall, tmp, fh, fs, hp, sp = self.wide, self.tall, self.tmp, self.fh, self.fs, self.hp, self.sp
        lane = lane_iota((1, LANES))
        self.clear(wide, 6, 240, 16)
        for g in range(2):
            for which, (place, bplace) in enumerate((("wq", "bq"), ("wk", None), ("wv", "bv"))):
                lane0 = which * DP + g * LANES
                take(fh.at[g], hp[place], D, HC, 0, HC, wide, 0, lane0)
                if bplace:
                    take(fh.at[g], hp[bplace], 1, HC, 0, HC, wide, 240, lane0)
        for tile in (0, 1, 4, 5):
            self.patch(wide, tile, 240, lane == MASK_LANE, 1.0)
        spill(wide, DP, qkv)
        self.clear(tall, 2, 0, DP)
        for g in range(2):
            take(fh.at[g], hp["wo"], HC, D, 0, D, tall, g * LANES, 0)
        take(fs, sp["vec"] + B_OUT * D, 1, D, 0, D, tall, MASK_LANE, 0)
        spill(tall, DP, wo)
        self.clear(wide, 4, 240, 16)
        for half in range(2):
            take(fs, sp["p1"], D, 2 * D, half * D, D, wide, 0, half * DP)
            take(fs, sp["pb1"] + half * D, 1, D, 0, D, wide, 240, half * DP)
        spill(wide, DP, p1)
        take(fs, sp["vec"], 16, D, 0, D, tall, 0, 0)
        take(fs, sp["taps"], 16, D, 0, D, tall, TAPS, 0)
        take(fs, sp["bg"], 1, D, 0, D, tall, BATCH_GAIN, 0)
        take(fs, sp["bb"], 1, D, 0, D, tall, BATCH_BIAS, 0)
        for row, value in ((FFA + 1, 1.0), (ATT + 1, 1.0), (CNV + 1, 1.0), (FFB + 1, 1.0), (BATCH_BIAS, UNIT)):
            self.patch(tall, 1, row, lane == D - LANES, value)
        spill(tall, VEC_ROWS, vec)
        length = rel.shape[1]
        for n in range(HEADS):
            take(fh.at[n // 2], hp["rel"] + (n % 2) * KREL, 1, KREL, 0, KREL, tmp, 0, 0)
            row = jnp.concatenate([tmp[t, pl.ds(0, 1), :] for t in range(3)] + [jnp.zeros((1, LANES), F32)], 1)
            rows = jnp.broadcast_to(row, (length, 4 * LANES))
            rows = pltpu.roll(rows, 4 * LANES - (length - 1), 1, stride=1, stride_axis=0)
            rel[pl.ds(n * length, length), :] = rows[:, :length] * LOG2E


class Flat:
    @staticmethod
    def scratch(dp, head_size, shared_size):
        vm = pltpu.VMEM
        return [
            vm((2, flat_rows(head_size * dp, head_size), LANES), F32),
            vm((flat_rows(shared_size * 2 * dp, shared_size), LANES), F32),
            vm((8, DP, LANES), F32),
            vm((2, FFP, LANES), F32),
            vm((4, 8, LANES), F32),
        ]

    def __init__(self, dp, head_size, shared_size, refs):
        self.dp, self.head_size, self.shared_size = dp, head_size, shared_size
        self.hr, self.sr = slot_rows(head_size), slot_rows(shared_size)
        self.fh, self.fs, self.wide, self.tall, self.tmp = refs
        self.hp, self.used_h = head_places()
        self.sp, self.used_s = shared_places()

    def clear_unused(self):
        for g in range(2):
            first = self.used_h // LANES // 8 * 8
            count = self.fh.shape[1] - first
            self.fh[g, pl.ds(first, count), :] = jnp.zeros((count, LANES), F32)
        first = self.used_s // LANES // 8 * 8
        count = self.fs.shape[0] - first
        self.fs[pl.ds(first, count), :] = jnp.zeros((count, LANES), F32)

    def head(self, g, place, rows, pitch, src, row0, lane0):
        give(self.fh.at[g], self.hp[place], rows, pitch, 0, pitch, src, row0, lane0)

    def shared(self, place, at, rows, pitch, col, src, row0, lane0):
        give(self.fs, self.sp[place] + at, rows, pitch, col, D, src, row0, lane0)

    def up(self, up, place, bias_place):
        load_tiles(up, self.wide, 0.5)
        for g in range(2):
            self.head(g, place, D, HF, self.wide, 0, g * HFP)
            self.head(g, bias_place, 1, HF, self.wide, 240, g * HFP)

    def down(self, dn, place, row):
        for t in range(2):
            self.tall[t] = (0.5 * dn[pl.ds(t * LANES, LANES), :]).astype(BF).T.astype(F32)
        for g in range(2):
            self.head(g, place, HF, D, self.tall, g * HFP, 0)
        self.shared("vec", row * D, 1, D, 0, self.tall, HF, 0)

    def attention(self, qkv, wo, rel):
        load_tiles(qkv, self.wide)
        load_tiles(wo, self.tall)
        length = rel.shape[0] // HEADS
        for g in range(2):
            for which, (place, bplace) in enumerate((("wq", "bq"), ("wk", None), ("wv", "bv"))):
                lane0 = which * DP + g * LANES
                self.head(g, place, D, HC, self.wide, 0, lane0)
                if bplace:
                    self.head(g, bplace, 1, HC, self.wide, 240, lane0)
            self.head(g, "wo", HC, D, self.tall, g * LANES, 0)
        for n in range(HEADS):
            total = jnp.zeros((8, 4 * LANES), F32)
            for block in range(length // 8):
                rows = rel[pl.ds(n * length + 8 * block, 8), :]
                rows = jnp.concatenate([rows, jnp.zeros((8, 4 * LANES - length), F32)], 1)
                total = total + pltpu.roll(rows, length - 8 - 8 * block, 1)
            row = total[7:8]
            for i in range(7):
                row = row + pltpu.roll(total[i : i + 1], 7 - i, 1)
            for t in range(4):
                self.tmp[t, pl.ds(0, 1), :] = row[:, t * LANES : (t + 1) * LANES]
            give(self.fh.at[n // 2], self.hp["rel"] + (n % 2) * KREL, 1, KREL, 0, KREL, self.tmp, 0, 0)
        self.shared("vec", B_OUT * D, 1, D, 0, self.tall, MASK_LANE, 0)

    def points(self, p1, p2):
        load_tiles(p1, self.wide)
        load_tiles(p2, self.tall)
        for half in range(2):
            self.shared("p1", 0, D, 2 * D, half * D, self.wide, 0, half * DP)
            self.shared("pb1", half * D, 1, D, 0, self.wide, 240, half * DP)
        self.shared("p2", 0, D, D, 0, self.tall, 0, 0)
        self.shared("pb2", 0, 1, D, 0, self.tall, 240, 0)

    def vectors(self, vec, vec2):
        for t in range(2):
            cols = pl.ds(t * LANES, LANES)
            self.tall[t, pl.ds(0, VEC_ROWS), :] = vec[:, cols] + vec2[:, cols]
        for row in range(2, 10):
            self.shared("vec", row * D, 1, D, 0, self.tall, row, 0)
        self.shared("taps", 0, 16, D, 0, self.tall, TAPS, 0)
        self.shared("bg", 0, 1, D, 0, self.tall, BATCH_GAIN, 0)
        self.shared("bb", 0, 1, D, 0, self.tall, BATCH_BIAS, 0)

    def first_norm(self, vec):
        for t in range(2):
            self.tall[t, pl.ds(0, 8), :] = vec[pl.ds(0, 8), pl.ds(t * LANES, LANES)]
        for row in (FFA, FFA + 1):
            self.shared("vec", row * D, 1, D, 0, self.tall, row, 0)

    def slots(self, out, z, kind):
        for i in range(4 * z, 4 * z + 4):
            for g in range(2):
                if kind == 0:
                    out[g, i, pl.ds(0, self.hr), :] = self.fh[g, pl.ds(i * self.head_size // LANES, self.hr), :].astype(BF)
                else:
                    at = (2 * i + g) * self.shared_size // LANES
                    out[g, i, pl.ds(self.hr, self.sr), :] = self.fs[pl.ds(at, self.sr), :].astype(BF)

    def groups(self):
        size = 4 * self.head_size
        every = range(self.dp // 4)
        one = [z for z in every if z * size >= self.hp["up2"] and (z + 1) * size <= self.hp["wq"]]
        two = [z for z in every if z * size >= self.hp["dn1"] and z not in one]
        late = [z for z in every if 8 * z * self.shared_size < 2 * D]
        return one, two, [z for z in every if z not in one and z not in two], [z for z in every if z not in late], late


def row_sum(x):
    return jnp.sum(x, -1, keepdims=True)


def halves(x):
    return x[:, :LANES], x[:, LANES:]


def both(lo, hi):
    return jnp.concatenate([lo, hi], 1)


def norm(x, gain, bias):
    lane = lane_iota((1, LANES))
    lo, hi = halves(x)
    mean = row_sum(lo + hi) * (1.0 / D)
    lo = lo - mean
    hi = jnp.where(lane < D - LANES, hi - mean, 0.0)
    inv = lax.rsqrt(row_sum(lo * lo + hi * hi) * (1.0 / D) + NORM_EPS)
    lo, hi = lo * inv, hi * inv
    return both(lo, hi) * gain + bias, both(lo, jnp.where(lane == LANES - 1, inv, hi))


def norm_grad(grad, kept, gain):
    dg = grad * gain
    inv = kept[:, DP - 1 :]
    first = row_sum(dg) * (1.0 / D)
    second = row_sum(dg * kept) * (1.0 / D)
    return inv * (dg - first - kept * second)


def fold_rows(x):
    return jnp.sum(x.reshape(x.shape[0] // 8, 8, x.shape[1]), 0)


def norm_param_grads(acc, row, grad, kept):
    acc[row] += fold_rows(grad * kept)
    acc[row + 1] += fold_rows(grad)


def settle(acc, out):
    for row in range(acc.shape[0]):
        out[pl.ds(row, 1), :] = jnp.sum(acc[row], 0, keepdims=True)


def silu_pair(y):
    p = jnp.tanh(y) + 1.0
    h = (y * p).astype(BF)
    p = p.astype(BF)
    return h, p + h * (2.0 - p)


def widen(x):
    rows = x.shape[0]
    return jnp.concatenate([x.astype(F32), jnp.zeros((rows, DP - D), F32)], 1)


SHORT = (1, 1, 1, 1, 3, 1, 1, 4)
LATE = (4, 1)
LONG = (1, 1, 1)
PAIR = (1, 1)


def columns(ref, widths):
    out, at = [], 0
    for width in widths:
        out.append(ref.at[:, pl.ds(at * DP, width * DP)])
        at += width
    return out


def head_lanes():
    lane = lane_iota((1, LANES))
    return lane < HD, (lane >= HD) & (lane < 2 * HD), lane == MASK_LANE


def valid_rows(lengths, at, length):
    return lax.broadcasted_iota(jnp.int32, (length, 1), 0) < lengths[at]


def phase_a_kernel(
    seqs, sizes, lengths, frames, head_ref, shared_ref,
    short_far, late_far, long_far, kept1_far, xw_far, e_far, keep_o, up, dn, up2, dn2, wqkv, wo, p1, p2, vec, rel,
    pad, stats_o, inbox, ss, rs, own_slot, got, fh, fs, wide, tall, tmp,
    short_b, late_b, long_b, kept1_b, xw_b, e_b, out_sem, *sems,
):
    step = pl.program_id(0)
    slot = lax.rem(step, 2)
    far = (short_far, late_far, long_far, kept1_far, xw_far, e_far)
    near = (short_b, late_b, long_b, kept1_b, xw_b, e_b)

    def moves(k):
        side = lax.rem(k, 2)
        out = []
        for j, (here, there) in enumerate(zip(near, far)):
            size = here.shape[1]
            rows = pl.ds(pl.multiple_of(k * size, size), size)
            out.append(pltpu.make_async_copy(here.at[side], there.at[rows], out_sem.at[side, j]))
        return out

    @pl.when(step >= 2)
    def _():
        for move in moves(step - 2):
            move.wait()

    short_o, late_o, long_o, kept1_o, xw_o, e_o = (ref.at[slot] for ref in near)
    total = inbox.shape[0]
    weights = Weights(*sizes, got, (fh, fs, wide, tall, tmp))
    gl_o, f1_o, f2_o, a3_o, qkv_o, m_o, a2_o, h_o = columns(short_o, SHORT)
    sp_o, a1_o = columns(late_o, LATE)
    kept3_o, kept2_o, rl_o = columns(long_o, LONG)
    x2_o, w_o = columns(xw_o, PAIR)

    @pl.when(step == 0)
    def _():
        greet_all(total)
        align(head_ref, shared_ref, own_slot)
        weights.clear_flat()
        greeted_all(total)
        gather(sizes[0] // 4, own_slot, got, sems, weights.merge)
        weights.ffn(up, dn, "up1", "upb1", "dn1", DOWNB_ONE)
        weights.others(wqkv, wo, p1, vec, rel)

    length = frames.shape[1]
    tokens = seqs * length
    first_seq = lax.axis_index("head") * (seqs * pl.num_programs(0)) + step * seqs

    def v(row):
        return vec[pl.ds(row, 1), :]

    x0 = widen(frames[...].reshape(tokens, D))
    a, kept1_o[...] = norm(x0, v(FFA), v(FFA + 1))
    a = a.astype(BF)
    a1_o[...] = a
    h, slope = silu_pair(dot(a, up[...]))
    h_o[...] = h
    sp_o[...] = slope
    x1 = x0 + dot(h, dn[...])
    a, kept = norm(x1, v(ATT), v(ATT + 1))
    kept2_o[...] = kept.astype(BF)
    a = a.astype(BF)
    a2_o[...] = a
    qkv = dot(a, wqkv[...])
    first, second, special = head_lanes()
    for b in range(seqs):
        rows = pl.ds(b * length, length)
        fence = jnp.where(valid_rows(lengths, first_seq + b, length), 0.0, NEG)
        for g in range(2):
            def piece(which):
                at = which * DP + g * LANES
                return qkv[b * length : (b + 1) * length, at : at + LANES]

            q = (piece(0) * (SCALE * LOG2E)).astype(BF)
            k = jnp.where(special, fence, piece(1)).astype(BF)
            vv = piece(2).astype(BF)
            qkv_o[rows, pl.ds(g * LANES, LANES)] = q
            qkv_o[rows, pl.ds(DP + g * LANES, LANES)] = k
            qkv_o[rows, pl.ds(2 * DP + g * LANES, LANES)] = vv
            zero = jnp.zeros_like(q)
            pair = jnp.concatenate([jnp.where(first | special, q, zero), jnp.where(second | special, q, zero)], 0)
            at = pl.ds(2 * g * length, 2 * length)
            s = dot_t(pair, k) + rel[at, :]
            e = jnp.exp2(s - jnp.max(s, -1, keepdims=True)).astype(BF)
            e_o[b, at, :] = e
            o = dot(e, vv)
            r = 1.0 / o[:, MASK_LANE : MASK_LANE + 1]
            shares = jnp.where(second, r[length:], r[:length])
            rl_o[rows, pl.ds(g * LANES, LANES)] = shares.astype(BF)
            m_o[rows, pl.ds(g * LANES, LANES)] = (jnp.where(second, o[length:], o[:length]) * shares).astype(BF)
    x2 = x1 + dot(m_o[...], wo[...])
    x2_o[...] = x2
    a, kept = norm(x2, v(CNV), v(CNV + 1))
    kept3_o[...] = kept.astype(BF)
    a = a.astype(BF)
    a3_o[...] = a
    e = dot(a, p1[...])
    half = KW // 2

    @pl.when(step == 0)
    def _():
        pad[...] = jnp.zeros(pad.shape, F32)
        stats_o[...] = jnp.zeros(stats_o.shape, F32)

    count = jnp.float32(0.0)
    summed = jnp.zeros((1, DP), F32)
    for b in range(seqs):
        rows = pl.ds(b * length, length)
        valid = jnp.where(valid_rows(lengths, first_seq + b, length), 1.0, 0.0)
        linear = e[b * length : (b + 1) * length, :DP]
        gate = 0.5 * jnp.tanh(0.5 * e[b * length : (b + 1) * length, DP:]) + 0.5
        f1 = gate * valid
        gl = linear * f1
        f1_o[rows, :] = f1.astype(BF)
        f2_o[rows, :] = (gl * (1.0 - gate)).astype(BF)
        gl_o[rows, :] = gl.astype(BF)
        for t in range(2):
            cols = pl.ds(t * LANES, LANES)
            pad[b, t, pl.ds(8, length), :] = gl[:, t * LANES : (t + 1) * LANES]
            acc = jnp.broadcast_to(vec[pl.ds(DEPTH_BIAS, 1), cols], (length, LANES))
            for r in range(KW):
                acc = acc + pad[b, t, pl.ds(8 - half + r, length), :] * vec[pl.ds(TAPS + r, 1), cols]
            w_o[rows, cols] = acc
        summed = summed + jnp.sum(w_o[rows, :] * valid, 0, keepdims=True)
        count = count + lengths[first_seq + b].astype(F32)
    mean = summed / count
    square = jnp.zeros((1, DP), F32)
    for b in range(seqs):
        valid = jnp.where(valid_rows(lengths, first_seq + b, length), 1.0, 0.0)
        centre = (w_o[pl.ds(b * length, length), :] - mean) * valid
        square = square + jnp.sum(centre * centre, 0, keepdims=True)
    old = stats_o[pl.ds(4, 1), :]
    new = old + count
    for t in range(2):
        cols = slice(t * LANES, (t + 1) * LANES)
        before = stats_o[pl.ds(t, 1), :]
        delta = mean[:, cols] - before
        stats_o[pl.ds(t, 1), :] = before + delta * (count / new)
        stats_o[pl.ds(2 + t, 1), :] += square[:, cols] + delta * delta * (old * count / new)
    stats_o[pl.ds(4, 1), :] = new
    for move in moves(step):
        move.start()

    @pl.when(step == pl.num_programs(0) - 1)
    def _():
        share_start(total, stats_o, inbox, ss, rs)
        weights.ffn(up2, dn2, "up2", "upb2", "dn2", DOWNB_TWO)
        weights.point_two(p2)
        share_finish(total, stats_o, inbox, ss, rs)
        batch_stats(inbox[...], keep_o)
        for move in moves(step - 1) + moves(step):
            move.wait()


def batch_stats(shared, keep):
    counts = shared[:, 4:5, :]
    total = jnp.sum(counts, 0)
    means, spreads = [], []
    for t in range(2):
        each = shared[:, t : t + 1, :]
        mean = jnp.sum(each * counts, 0) / total
        spread = (jnp.sum(shared[:, 2 + t : 3 + t, :], 0) + jnp.sum(counts * (each - mean) ** 2, 0)) / total
        means.append(mean)
        spreads.append(spread)
    keep[pl.ds(0, 1), :] = jnp.concatenate(means, 1)
    keep[pl.ds(1, 1), :] = lax.rsqrt(jnp.concatenate(spreads, 1) + NORM_EPS)
    keep[pl.ds(2, 1), :] = jnp.concatenate([total, total], 1)
    keep[pl.ds(3, 5), :] = jnp.zeros((5, DP), F32)


def phase_b_kernel(
    seqs, keep, xw, cotangent, p2, up, dn, vec,
    out_o, back_o, dup_o, ddn_o, dp2_o, vec_o, keep_o,
    acc, a_all, du_all, do_all, h_all, hc_all, dc_all, sums_o, inbox, ss, rs,
):
    step = pl.program_id(0)
    total = inbox.shape[0]
    length = cotangent.shape[1]
    tokens = seqs * length
    at = pl.ds(pl.multiple_of(step * tokens, tokens), tokens)
    x2, w = columns(xw, PAIR)
    dy_o, dx3_o = columns(back_o, PAIR)

    @pl.when(step == 0)
    def _():
        greet_all(total)
        for ref in (dup_o, ddn_o, dp2_o, acc):
            ref[...] = jnp.zeros(ref.shape, F32)

    def v(row):
        return vec[pl.ds(row, 1), :]

    mean, inv_batch = keep[pl.ds(0, 1), :], keep[pl.ds(1, 1), :]
    z = (w[...] - mean) * inv_batch
    hc, slope_c = silu_pair(z * (0.5 * v(BATCH_GAIN)) + 0.5 * v(BATCH_BIAS))
    x3 = x2[...] + dot(hc, p2[...])
    a, kept = norm(x3, v(FFB), v(FFB + 1))
    a = a.astype(BF)
    h, slope = silu_pair(dot(a, up[...]))
    x4 = x3 + dot(h, dn[...])
    final, kept4 = norm(x4, v(OUT), v(OUT + 1))
    out_o[...] = final[:, :D].astype(BF).reshape(seqs, length, D)
    g = widen(cotangent[...].reshape(tokens, D))
    norm_param_grads(acc, OUT, g, kept4)
    dx4 = norm_grad(g, kept4, v(OUT))
    do = dx4.astype(BF)
    do_all[at, :] = do
    h_all[at, :] = h
    du = dot_t(do, dn[...]).astype(BF) * slope
    a_all[at, :] = a
    du_all[at, :] = du
    da = dot_t(du, up[...])
    norm_param_grads(acc, FFB, da, kept)
    dx3 = dx4 + norm_grad(da, kept, v(FFB))
    dx3_o[...] = dx3
    dc = dx3.astype(BF)
    hc_all[at, :] = hc
    dc_all[at, :] = dc
    dy = dot_t(dc, p2[...]) * slope_c.astype(F32)
    dy_o[...] = dy
    acc[BATCH_BIAS] += fold_rows(dy)
    acc[BATCH_GAIN] += fold_rows(dy * z)

    @pl.when(step == pl.num_programs(0) - 1)
    def _():
        acc[BATCH_BIAS] *= 0.5
        acc[BATCH_GAIN] *= 0.5
        settle(acc, vec_o)
        for row, source in ((0, BATCH_BIAS), (2, BATCH_GAIN)):
            line = vec_o[pl.ds(source, 1), :]
            for t in range(2):
                sums_o[pl.ds(row + t, 1), :] = line[:, t * LANES : (t + 1) * LANES]

    @pl.when(step == pl.num_programs(0) - 1)
    def _():
        greeted_all(total)
        share_start(total, sums_o, inbox, ss, rs)

        @pl.loop(0, pl.num_programs(0))
        def _(k):
            at = pl.ds(pl.multiple_of(k * tokens, tokens), tokens)
            ddn_o[...] += t_dot(do_all[at, :], h_all[at, :])
            dup_o[...] += t_dot(a_all[at, :], du_all[at, :])
            dp2_o[...] += t_dot(hc_all[at, :], dc_all[at, :])

        share_finish(total, sums_o, inbox, ss, rs)
        sums = jnp.sum(inbox[...], 0)
        keep_o[...] = keep[...]
        keep_o[pl.ds(3, 1), :] = jnp.concatenate([sums[0:1], sums[1:2]], 1)
        keep_o[pl.ds(4, 1), :] = jnp.concatenate([sums[2:3], sums[3:4]], 1)


def phase_c_kernel(
    seqs, steps, sizes, lengths, keep, xw_far, back_far, short_far, long_far, e_far, late_far, kept1_far,
    p1, wo, wqkv, dn, up, vec, dup2, ddn2, dp2, vec2,
    dx0_o, sum_o,
    dp1_o, dwo_o, dqkv_o, dup_o, ddn_o, vec_o, rel_o, dx1_buf, mine,
    acc, padw, padg, grads, w_b, back_b, short_b, long_b, e_b, late_b, kept1_b, in_sem, *refs,
):
    step = pl.program_id(0)
    length = dx0_o.shape[1]
    side = lax.rem(step, 2)
    cut = 3 * DP

    def fetch(k, names):
        to = lax.rem(k, 2)
        size = seqs * length
        rows = pl.ds(pl.multiple_of(k * size, size), size)
        make = pltpu.make_async_copy
        every = (
            lambda j: make(xw_far.at[rows, pl.ds(DP, DP)], w_b.at[to], in_sem.at[to, j]),
            lambda j: make(back_far.at[rows], back_b.at[to], in_sem.at[to, j]),
            lambda j: make(short_far.at[rows, pl.ds(0, cut)], short_b.at[to, :, pl.ds(0, cut)], in_sem.at[to, j]),
            lambda j: make(
                short_far.at[rows, pl.ds(cut, short_b.shape[2] - cut)],
                short_b.at[to, :, pl.ds(cut, short_b.shape[2] - cut)],
                in_sem.at[to, j],
            ),
            lambda j: make(long_far.at[rows], long_b.at[to], in_sem.at[to, j]),
            lambda j: make(e_far.at[pl.ds(k * seqs, seqs)], e_b.at[to], in_sem.at[to, j]),
            lambda j: make(late_far.at[rows], late_b.at[to], in_sem.at[to, j]),
            lambda j: make(kept1_far.at[rows], kept1_b.at[to], in_sem.at[to, j]),
        )
        return [every[j](j) for j in names]

    conv_names, rest_names, late_names = (0, 1, 2), (3, 4, 5), (6, 7)

    @pl.when(step == 0)
    def _():
        for move in fetch(step, conv_names + rest_names):
            move.start()

    @pl.when(step < steps - 1)
    def _():
        for move in fetch(step + 1, conv_names + rest_names):
            move.start()

    @pl.when(step == steps - 1)
    def _():
        for move in fetch(step * 0, late_names):
            move.start()

    @pl.when((step >= steps) & (step < 2 * steps - 1))
    def _():
        for move in fetch(step + 1 - steps, late_names):
            move.start()

    w, back, short, long, e_all = (ref.at[side] for ref in (w_b, back_b, short_b, long_b, e_b))
    late_side = lax.rem(jnp.maximum(step - steps, 0), 2)
    late, kept1 = late_b.at[late_side], kept1_b.at[late_side]
    flat = Flat(*sizes, refs[:5])
    nz = sizes[0] // 4
    scatter = Scatter(nz, flat.hr, flat.sr, mine, refs[5:])
    one, two, rest, shared_two, shared_rest = flat.groups()
    dy, dx3 = columns(back, PAIR)
    gl, f1, f2, a3, qkv, m, a2, h = columns(short, SHORT)
    kept3, kept2, rl = columns(long, LONG)
    slope, a1 = columns(late, LATE)

    @pl.when(step == 0)
    def _():
        greet(nz, scatter.me, scatter.core, scatter.zc, scatter.yc, scatter.xc)
        for ref in (dp1_o, dwo_o, dqkv_o, dup_o, ddn_o, acc, rel_o, padw, padg):
            ref[...] = jnp.zeros(ref.shape, F32)
        flat.clear_unused()
        flat.up(dup2, "up2", "upb2")
        flat.down(ddn2, "dn2", DOWNB_TWO)
        for z in one:
            flat.slots(scatter.g, z, 0)
        greeted(nz)
        for z in one:
            scatter.stage_core(z, 0)

    @pl.when(step < steps)
    def _():
        def ready(names):
            for move in fetch(step, names):
                move.wait()

        ready(conv_names)
        phase_c_first(
            functools.partial(ready, rest_names), seqs, step, steps, length, lengths, keep, w, dy, dx3, gl, f1, f2, a3, kept3, qkv, e_all, rl, m, a2, kept2,
            h, p1, wo, wqkv, vec, dp1_o, dwo_o, dqkv_o, ddn_o, rel_o, dx1_buf, acc, padw, padg, grads,
        )

    @pl.when(step == steps)
    def _():
        flat.attention(dqkv_o, dwo_o, rel_o)
        flat.down(ddn_o, "dn1", DOWNB_ONE)
        for z in two:
            flat.slots(scatter.g, z, 0)
            scatter.stage_core(z, 0)
        settle(acc, vec_o)
        flat.points(dp1_o, dp2)
        flat.vectors(vec_o, vec2)
        for z in shared_two:
            flat.slots(scatter.g, z, 1)
            scatter.stage_core(z, 1)

    @pl.when(step >= steps)
    def _():
        for move in fetch(step - steps, late_names):
            move.wait()
        at = pl.ds(pl.multiple_of((step - steps) * (seqs * length), seqs * length), seqs * length)
        dx1 = dx1_buf[at, :]
        du = dot_t(dx1.astype(BF), dn[...]).astype(BF) * slope[...]
        dup_o[...] += t_dot(a1[...], du)
        da = dot_t(du, up[...])
        norm_param_grads(acc, FFA, da, kept1[...])
        dx0 = dx1 + norm_grad(da, kept1[...], vec[pl.ds(FFA, 1), :])
        dx0_o[...] = dx0[:, :D].reshape(seqs, length, D)

    stages = (scatter.stage_first, scatter.stage_second, scatter.stage_third)
    for at, heads, shared in (((1, 2, 3), one, []), (tuple(steps + k for k in TWO_AT), two, shared_two)):
        for when, stage in zip(at, stages):
            @pl.when(step == when)
            def _():
                for z in heads:
                    stage(z, 0)
                for z in shared:
                    stage(z, 1)

    @pl.when(step == 2 * steps - 1)
    def _():
        flat.up(dup_o, "up1", "upb1")
        for z in rest:
            flat.slots(scatter.g, z, 0)
            scatter.stage_core(z, 0)
        settle(acc, vec_o)
        flat.first_norm(vec_o)
        for z in shared_rest:
            flat.slots(scatter.g, z, 1)
            scatter.stage_core(z, 1)
        waiting = [(stage, two, shared_two) for stage in stages[len(TWO_AT) :]]
        last = [(stage, rest, shared_rest) for stage in stages]
        for stage, heads, shared in [x for pair in zip(waiting, last) for x in pair] + last[len(waiting) :]:
            for z in heads:
                stage(z, 0)
            for z in shared:
                stage(z, 1)
        scatter.finish(sum_o)


def phase_c_first(
    ready, seqs, step, steps, length, lengths, keep, w, dy, dx3, gl, f1, f2, a3, kept3, qkv, e_all, rl, m, a2, kept2,
    h, p1, wo, wqkv, vec, dp1_o, dwo_o, dqkv_o, ddn_o, rel_o, dx1_buf, acc, padw, padg, grads,
):
    first_seq = lax.axis_index("head") * (seqs * steps) + step * seqs
    half = KW // 2

    def v(row):
        return vec[pl.ds(row, 1), :]

    mean, inv_batch, count = (keep[pl.ds(row, 1), :] for row in range(3))
    scale = v(BATCH_GAIN) * inv_batch
    cross = inv_batch * scale * keep[pl.ds(4, 1), :] / count
    plain = scale * keep[pl.ds(3, 1), :] / count - mean * cross
    scale = 0.5 * scale
    for b in range(seqs):
        rows = pl.ds(b * length, length)
        valid = jnp.where(valid_rows(lengths, first_seq + b, length), 1.0, 0.0)
        dw = dy[rows, :] * scale - valid * (plain + w[rows, :] * cross)
        acc[DEPTH_BIAS] += fold_rows(dw)
        for t in range(2):
            cols = pl.ds(t * LANES, LANES)
            here = dw[:, t * LANES : (t + 1) * LANES]
            padw[b, t, pl.ds(8, length), :] = here
            padg[b, t, pl.ds(8, length), :] = gl[rows, cols].astype(F32)
            total = jnp.zeros((length, LANES), F32)
            for r in range(KW):
                total = total + padw[b, t, pl.ds(8 + half - r, length), :] * vec[pl.ds(TAPS + r, 1), cols]
                tap = here * padg[b, t, pl.ds(8 - half + r, length), :]
                acc[TAPS + r, :, cols] += fold_rows(tap)
            grads[rows, cols] = (total * f1[rows, cols].astype(F32)).astype(BF)
            grads[rows, pl.ds(DP + t * LANES, LANES)] = (total * f2[rows, cols].astype(F32)).astype(BF)
    ready()
    de = grads[:, pl.ds(0, 2 * DP)]
    dp1_o[...] += t_dot(a3[...], de)
    da = dot_t(de, p1[...])
    kept = kept3[...].astype(F32)
    norm_param_grads(acc, CNV, da, kept)
    dx2 = dx3[...] + norm_grad(da, kept, v(CNV))
    db = dx2.astype(BF)
    dwo_o[...] += t_dot(m[...], db)
    dm = dot_t(db, wo[...])
    first, second, special = head_lanes()
    source = lax.broadcasted_iota(jnp.int32, (LANES, 2 * LANES), 0)
    target = lane_iota((LANES, 2 * LANES)) // LANES
    spread = jnp.where((source >= target * HD) & (source < (target + 1) * HD), 1.0, 0.0).astype(BF)
    for b in range(seqs):
        rows = pl.ds(b * length, length)
        for g in range(2):
            cols = pl.ds(g * LANES, LANES)
            q = qkv[rows, cols]
            k = qkv[rows, pl.ds(DP + g * LANES, LANES)]
            vv = qkv[rows, pl.ds(2 * DP + g * LANES, LANES)]
            dmb = (dm[b * length : (b + 1) * length, g * LANES : (g + 1) * LANES] * rl[rows, cols].astype(F32)).astype(BF)
            level = dot(dmb * m[rows, cols], spread)
            level = jnp.concatenate([level[:, :LANES], level[:, LANES:]], 0)
            zero = jnp.zeros_like(q)
            dm_pair = jnp.concatenate([jnp.where(first, dmb, zero), jnp.where(second, dmb, zero)], 0)
            q_pair = jnp.concatenate([jnp.where(first, q, zero), jnp.where(second, q, zero)], 0)
            at = pl.ds(2 * g * length, 2 * length)
            e = e_all[b, at, :]
            dp = dot_t(dm_pair, vv)
            ds = e.astype(F32) * (dp - jnp.concatenate([level, level[:, : length - LANES]], 1))
            rel_o[at, :] += ds
            ds = ds.astype(BF)
            dq = dot(ds, k)
            dq = jnp.where(second, dq[length:], dq[:length])
            grads[rows, cols] = (dq * SCALE).astype(BF)
            grads[rows, pl.ds(DP + g * LANES, LANES)] = (t_dot(ds, q_pair) * LN2).astype(BF)
            grads[rows, pl.ds(2 * DP + g * LANES, LANES)] = t_dot(e, dm_pair).astype(BF)
    dqkv = grads[...]
    dqkv_o[...] += t_dot(a2[...], dqkv)
    da = dot_t(dqkv, wqkv[...])
    kept = kept2[...].astype(F32)
    norm_param_grads(acc, ATT, da, kept)
    dx1 = dx2 + norm_grad(da, kept, v(ATT))
    at = pl.ds(pl.multiple_of(step * (seqs * length), seqs * length), seqs * length)
    dx1_buf[at, :] = dx1
    ddn_o[...] += t_dot(dx1.astype(BF), h[...])


def layer_call(body, steps, ins, outs, scratch, name, collective_id=None):
    def spec(item):
        kind, shape = item
        if kind == "far":
            return pl.BlockSpec(memory_space=pl.ANY)
        if kind == "smem":
            return pl.BlockSpec(memory_space=pltpu.SMEM)
        if kind == "tile":
            return pl.BlockSpec(shape, lambda i: (i,) + (0,) * (len(shape) - 1))
        if kind == "early":
            return pl.BlockSpec(shape, lambda i: (jnp.minimum(i, steps // 2 - 1),) + (0,) * (len(shape) - 1))
        if kind == "late":
            return pl.BlockSpec(shape, lambda i: (jnp.maximum(i - steps // 2, 0),) + (0,) * (len(shape) - 1))
        return pl.BlockSpec(shape, lambda i: (0,) * len(shape))

    arrays = [a for _, _, a in ins]
    return pl.pallas_call(
        body,
        grid=(steps,),
        out_shape=tuple(jax.ShapeDtypeStruct(full, dtype) for _, _, full, dtype in outs),
        in_specs=[spec((kind, block)) for kind, block, _ in ins],
        out_specs=tuple(spec((kind, block)) for kind, block, _, _ in outs),
        scratch_shapes=list(scratch),
        compiler_params=pltpu.CompilerParams(
            vmem_limit_bytes=BIG,
            dimension_semantics=("arbitrary",),
            collective_id=collective_id,
            has_side_effects=collective_id is not None,
        ),
        name=name,
    )(*arrays)


def tile_in(array, steps, kind="tile"):
    return (kind, (array.shape[0] // steps,) + array.shape[1:], array)


def whole_in(array):
    return ("whole", array.shape, array)


def tile_out(steps, shape, dtype, kind="tile"):
    return (kind, (shape[0] // steps,) + shape[1:], shape, dtype)


def far_in(array):
    return ("far", None, array)


def far_out(shape, dtype):
    return ("far", None, shape, dtype)


def whole_out(shape, dtype=F32):
    return ("whole", shape, shape, dtype)


SEQS_A = 4
SEQS_B = 4
SEQS_C = 4
TWO_AT = (1,)


def per_device(
    frames, cotangent, lengths, head_params, shared_params, head_first, head_second, shared_first, shared_second
):
    seq_here, length, _ = frames.shape
    tokens = seq_here * length
    dp = lax.axis_size("dp")
    head_size, shared_size = head_params.shape[1], shared_params.shape[0]
    rows = slot_rows(head_size) + slot_rows(shared_size)
    vm = pltpu.VMEM
    dma = pltpu.SemaphoreType.DMA
    sharing = [vm((8, LANES), F32), vm((2 * dp, 8, LANES), F32), dma((2 * dp,)), dma((2 * dp,))]
    steps = seq_here // SEQS_A
    block = SEQS_A * length
    t = functools.partial(tile_out, steps)
    (
        short, late, long, kept1, xw, e_all, keep,
        up1, dn1, up2, dn2, wqkv, wo, p1, p2, vec, rel
    ) = layer_call(
        functools.partial(phase_a_kernel, SEQS_A, (dp, head_size, shared_size)),
        steps,
        [("smem", None, lengths), tile_in(frames, steps), whole_in(head_params), whole_in(shared_params)],
        [
            far_out((tokens, sum(SHORT) * DP), BF), far_out((tokens, sum(LATE) * DP), BF),
            far_out((tokens, sum(LONG) * DP), BF), far_out((tokens, DP), F32), far_out((tokens, sum(PAIR) * DP), F32),
            far_out((seq_here, HEADS * length, length), BF),
            whole_out((8, DP)),
            whole_out((DP, FFP), BF), whole_out((FFP, DP), BF), whole_out((DP, FFP), BF), whole_out((FFP, DP), BF),
            whole_out((DP, 3 * DP), BF), whole_out((DP, DP), BF), whole_out((DP, 2 * DP), BF), whole_out((DP, DP), BF),
            whole_out((VEC_ROWS, DP)), whole_out((HEADS * length, length)),
        ],
        [vm((SEQS_A, 2, length + 16, LANES), F32)]
        + sharing
        + [vm((rows, LANES), BF), vm((dp, 2, rows, LANES), BF)]
        + Flat.scratch(dp, head_size, shared_size)
        + [
            vm((2, block, sum(SHORT) * DP), BF), vm((2, block, sum(LATE) * DP), BF), vm((2, block, sum(LONG) * DP), BF),
            vm((2, block, DP), F32), vm((2, block, sum(PAIR) * DP), F32), vm((2, SEQS_A, HEADS * length, length), BF),
            dma((2, 6)),
        ]
        + gather_sems(dp // 4),
        "phase_a",
        1,
    )
    steps = seq_here // SEQS_B
    t = functools.partial(tile_out, steps)
    early, back, dup2, ddn2, dp2, vec_b, keep = layer_call(
        functools.partial(phase_b_kernel, SEQS_B),
        steps,
        [whole_in(keep), tile_in(xw, steps), tile_in(cotangent, steps)]
        + [whole_in(x) for x in (p2, up2, dn2, vec)],
        [
            t((seq_here, length, D), BF), t((tokens, sum(PAIR) * DP), F32),
            whole_out((DP, FFP)), whole_out((DP, FFP)), whole_out((DP, DP)), whole_out((VEC_ROWS, DP)),
            whole_out((8, DP)),
        ],
        [
            vm((VEC_ROWS, 8, DP), F32), vm((tokens, DP), BF), vm((tokens, FFP), BF), vm((tokens, DP), BF),
            vm((tokens, FFP), BF), vm((tokens, DP), BF), vm((tokens, DP), BF),
        ]
        + sharing,
        "phase_b",
        3,
    )
    steps = seq_here // SEQS_C
    slot = (slot_rows(head_size), slot_rows(shared_size))
    block = SEQS_C * length
    input_grad, summed = layer_call(
        functools.partial(phase_c_kernel, SEQS_C, steps, (dp, head_size, shared_size)),
        2 * steps,
        [("smem", None, lengths), whole_in(keep)]
        + [far_in(x) for x in (xw, back, short, long, e_all, late, kept1)]
        + [whole_in(x) for x in (p1, wo, wqkv, dn1, up1, vec, dup2, ddn2, dp2, vec_b)],
        [tile_out(steps, (seq_here, length, D), F32, "late"), whole_out((rows, LANES))],
        [
            vm((DP, 2 * DP), F32), vm((DP, DP), F32), vm((DP, 3 * DP), F32), vm((DP, FFP), F32), vm((DP, FFP), F32),
            vm((VEC_ROWS, DP), F32), vm((HEADS * length, length), F32), vm((tokens, DP), F32), vm((rows, LANES), F32),
            vm((VEC_ROWS, 8, DP), F32),
            vm((SEQS_C, 2, length + 16, LANES), F32),
            vm((SEQS_C, 2, length + 16, LANES), F32),
            vm((block, 3 * DP), BF),
            vm((2, block, DP), F32), vm((2, block, sum(PAIR) * DP), F32), vm((2, block, sum(SHORT) * DP), BF),
            vm((2, block, sum(LONG) * DP), BF), vm((2, SEQS_C, HEADS * length, length), BF),
            vm((2, block, sum(LATE) * DP), BF), vm((2, block, DP), F32), dma((2, 8)),
        ]
        + Flat.scratch(dp, head_size, shared_size)
        + Scatter.scratch(dp, *slot),
        "phase_c",
        4,
    )
    h_shape, s_shape = head_params.shape, shared_params.shape
    steps = 2
    return layer_call(
        adam_kernel,
        steps,
        [tile_in(x, steps) for x in (early, input_grad)]
        + [whole_in(x) for x in (summed, head_params, head_first, head_second, shared_params, shared_first, shared_second)],
        [tile_out(steps, early.shape, BF), tile_out(steps, early.shape, F32)]
        + [whole_out(h_shape)] * 3
        + [whole_out(h_shape, BF)]
        + [whole_out(s_shape)] * 3
        + [whole_out(s_shape, BF)],
        [],
        "adam",
    )


def solution(mesh):
    frames = P(("dp", "head"), None, None)
    heads = P("head", "dp")
    shared = P(("dp", "head"))
    return jax.shard_map(
        per_device,
        mesh=mesh,
        in_specs=(frames, frames, P("dp"), heads, shared, heads, heads, shared, shared),
        out_specs=(frames, frames) + (heads,) * 4 + (shared,) * 4,
        check_vma=False,
    )
```

```python
import functools
import math

import jax
import jax.numpy as jnp
from jax import lax
from jax.experimental import pallas as pl
from jax.experimental.pallas import tpu as pltpu
from jax.sharding import PartitionSpec as P

BF = jnp.bfloat16
F32 = jnp.float32
LANES = 128


def up_to(count, unit):
    return -(-count // unit) * unit


def grid_place(nz):
    me = lax.axis_index("dp")
    core = lax.axis_index("head")
    zc = me // 4
    rest = me - 4 * zc
    yc = rest // 2
    xc = rest - 2 * yc
    return me, core, zc, yc, xc


def remote(src, dst, send, recv, dp, head):
    return pltpu.make_async_remote_copy(
        src_ref=src,
        dst_ref=dst,
        send_sem=send,
        recv_sem=recv,
        device_id={"dp": dp, "head": head},
        device_id_type=pl.DeviceIdType.MESH,
    )


def greet(nz, me, core, zc, yc, xc):
    barrier = pltpu.get_barrier_semaphore()

    def hello(dp, head):
        pl.semaphore_signal(
            barrier, inc=1, device_id={"dp": dp, "head": head}, device_id_type=pl.DeviceIdType.MESH
        )

    for k in range(1, nz):
        hello(lax.rem(zc + k, nz) * 4 + 2 * yc + xc, core)
    hello(4 * zc + 2 * (1 - yc) + xc, core)
    hello(4 * zc + 2 * yc + 1 - xc, core)
    hello(me, 1 - core)


def greeted(nz):
    pl.semaphore_wait(pltpu.get_barrier_semaphore(), nz + 2)


def gather(nz, src, out, sems, merge):
    sz, rz, s1, r1, s2, r2, sc, rc = sems
    rows = src.shape[0]
    row_a = up_to(rows // 2, 16)
    parts = (pl.ds(0, row_a), pl.ds(row_a, rows - row_a))
    me, core, zc, yc, xc = grid_place(nz)
    out[me, core] = src[...]
    y_peer = 4 * zc + 2 * (1 - yc) + xc
    x_peer = 4 * zc + 2 * yc + 1 - xc
    firsts = (y_peer, x_peer)
    seconds = (x_peer, y_peer)
    pending = []

    def send(slot, p, send_sem, recv_sem, dp, head):
        block = out.at[slot, core, parts[p]]
        copy = remote(block, block, send_sem, recv_sem, dp, head)
        copy.start()
        pending.append(copy)

    def arrived(slot, which, p, send_sem, recv_sem):
        block = out.at[slot, which, parts[p]]
        remote(block, block, send_sem, recv_sem, me, 1 - core).wait_recv()

    zs = [lax.rem(zc + k, nz) for k in range(nz)]
    here = 2 * yc + xc
    first_here = (2 * (1 - yc) + xc, 2 * yc + 1 - xc)
    second_here = ((2 * yc + 1 - xc, 2 * (1 - yc) + 1 - xc), (2 * (1 - yc) + xc, 2 * (1 - yc) + 1 - xc))
    for k in range(1, nz):
        for p in (0, 1):
            send(me, p, sz.at[p, k], rz.at[p, zc], zs[k] * 4 + here, core)
    for k in range(nz):
        z = zs[k]
        slot = 4 * z + here
        for p in (0, 1):
            if k:
                arrived(slot, core, p, sz.at[p, k], rz.at[p, z])
            send(slot, p, s1.at[p, k], r1.at[p, z], firsts[p], core)
            send(slot, p, s2.at[p, k, 0], r2.at[p, z, 0], seconds[p], core)
            send(slot, p, sc.at[p, k, 0], rc.at[p, z, 0], me, 1 - core)
    for k in range(nz):
        for p in (0, 1):
            merge(4 * zs[k] + here, core, p)
    for k in range(nz):
        z = zs[k]
        for p in (0, 1):
            slot = 4 * z + first_here[p]
            arrived(slot, core, p, s1.at[p, k], r1.at[p, z])
            send(slot, p, s2.at[p, k, 1], r2.at[p, z, 1], seconds[p], core)
            send(slot, p, sc.at[p, k, 1], rc.at[p, z, 1], me, 1 - core)
    for k in range(nz):
        for p in (0, 1):
            merge(4 * zs[k] + first_here[p], core, p)
    for k in range(nz):
        z = zs[k]
        for b in (0, 1):
            for p in (0, 1):
                slot = 4 * z + second_here[p][b]
                arrived(slot, core, p, s2.at[p, k, b], r2.at[p, z, b])
                send(slot, p, sc.at[p, k, 2 + b], rc.at[p, z, 2 + b], me, 1 - core)
        for b in (0, 1):
            for p in (0, 1):
                merge(4 * z + second_here[p][b], core, p)
    for k in range(nz):
        z = zs[k]
        for p in (0, 1):
            for b, at in enumerate((here, first_here[p]) + second_here[p]):
                arrived(4 * z + at, 1 - core, p, sc.at[p, k, b], rc.at[p, z, b])
                merge(4 * z + at, 1 - core, p)
    for copy in pending:
        copy.wait_send()


def gather_sems(nz):
    dma = pltpu.SemaphoreType.DMA
    return [
        dma((2, nz)), dma((2, nz)), dma((2, nz)), dma((2, nz)),
        dma((2, nz, 2)), dma((2, nz, 2)), dma((2, nz, 4)), dma((2, nz, 4)),
    ]


class Scatter:
    @staticmethod
    def scratch(dp, hr, sr):
        nz, rows = dp // 4, hr + sr
        dma, vm = pltpu.SemaphoreType.DMA, pltpu.VMEM
        return [
            vm((2, dp, rows, LANES), BF), vm((dp, rows, LANES), BF),
            vm((nz, 2, rows, LANES), BF), vm((nz, 2, rows, LANES), BF),
            vm((nz, rows, LANES), BF), vm((nz, rows, LANES), BF),
            vm((nz, rows, LANES), BF), vm((nz, rows, LANES), BF),
            dma((nz, 2)), dma((nz, 2)), dma((3, nz)), dma((3, nz)), dma((3, nz)), dma((3, nz)), dma((3, nz)), dma((3, nz)),
        ]

    def __init__(self, nz, hr, sr, mine, refs):
        self.nz, self.mine = nz, mine
        (
            self.g, self.c1, self.t1, self.rx1, self.t2, self.rx2, self.t3, self.rx3,
            self.sc, self.rc, self.s1, self.r1, self.s2, self.r2, self.s3, self.r3,
        ) = refs
        ha = up_to(hr // 2, 16)
        self.parts = (pl.ds(0, ha), pl.ds(ha, hr - ha), pl.ds(hr, sr))
        self.kinds = (pl.ds(0, hr), pl.ds(hr, sr))
        self.me, self.core, self.zc, self.yc, self.xc = grid_place(nz)
        zc, yc, xc = self.zc, self.yc, self.xc
        y_peer = 4 * zc + 2 * (1 - yc) + xc
        x_peer = 4 * zc + 2 * yc + 1 - xc
        self.firsts = (x_peer, y_peer, x_peer)
        self.seconds = (y_peer, x_peer, y_peer)
        self.second_give = (1 - yc, 1 - xc, 1 - yc)
        self.second_keep = (yc, xc, yc)

    def core_copy(self, z, kind):
        group, rows = pl.ds(4 * z, 4), self.kinds[kind]
        return remote(
            self.g.at[1 - self.core, group, rows], self.c1.at[group, rows],
            self.sc.at[z, kind], self.rc.at[z, kind], self.me, 1 - self.core,
        )

    def first_copy(self, z, p):
        rows = self.parts[p]
        return remote(
            self.t1.at[z, :, rows], self.rx1.at[z, :, rows], self.s1.at[p, z], self.r1.at[p, z], self.firsts[p], self.core
        )

    def second_copy(self, z, p):
        rows = self.parts[p]
        return remote(
            self.t2.at[z, rows], self.rx2.at[z, rows], self.s2.at[p, z], self.r2.at[p, z], self.seconds[p], self.core
        )

    def third_copy(self, z, p):
        rows = self.parts[p]
        return remote(
            self.t3.at[z, rows], self.rx3.at[self.zc, rows], self.s3.at[p, z], self.r3.at[p, self.zc],
            4 * z + 2 * self.yc + self.xc, self.core,
        )

    def place(self, p, z, b):
        return 4 * z + (2 * self.yc + b if p == 1 else 2 * b + self.xc)

    def held(self, z, p, slot):
        rows = self.parts[p]
        return self.g[self.core, slot, rows].astype(F32) + self.c1[slot, rows].astype(F32)

    def partial(self, z, p, b):
        return self.held(z, p, self.place(p, z, b)) + self.rx1[z, b, self.parts[p]].astype(F32)

    def stage_core(self, z, kind):
        self.core_copy(z, kind).start()

    def stage_first(self, z, kind):
        self.core_copy(z, kind).wait_recv()
        for p in ((0, 1), (2,))[kind]:
            for b in (0, 1):
                slot = 4 * z + (2 * (1 - self.yc) + b if p == 1 else 2 * b + 1 - self.xc)
                self.t1[z, b, self.parts[p]] = self.held(z, p, slot).astype(BF)
            self.first_copy(z, p).start()

    def stage_second(self, z, kind):
        for p in ((0, 1), (2,))[kind]:
            self.first_copy(z, p).wait_recv()
            self.t2[z, self.parts[p]] = self.partial(z, p, self.second_give[p]).astype(BF)
            self.second_copy(z, p).start()

    def stage_third(self, z, kind):
        for p in ((0, 1), (2,))[kind]:
            rows = self.parts[p]
            self.second_copy(z, p).wait_recv()
            total = self.partial(z, p, self.second_keep[p]) + self.rx2[z, rows].astype(F32)

            @pl.when(self.zc == z)
            def _():
                self.mine[rows, :] = total

            @pl.when(self.zc != z)
            def _():
                self.t3[z, rows] = total.astype(BF)
                self.third_copy(z, p).start()

    def finish(self, out):
        total = self.mine[...]
        for k in range(1, self.nz):
            sender = lax.rem(self.zc + k, self.nz)
            for p in range(3):
                rows = self.parts[p]
                remote(
                    self.t3.at[sender, rows], self.rx3.at[sender, rows], self.s3.at[p, sender], self.r3.at[p, sender],
                    self.me, 1 - self.core,
                ).wait_recv()
            total = total + self.rx3[sender].astype(F32)
        out[...] = total
        for z in range(self.nz):
            for kind in range(2):
                self.core_copy(z, kind).wait_send()
            for p in range(3):
                self.first_copy(z, p).wait_send()
                self.second_copy(z, p).wait_send()

            @pl.when(self.zc != z)
            def _():
                for p in range(3):
                    self.third_copy(z, p).wait_send()


def peer_of(own, total, k):
    other = lax.rem(own + k, total)
    dp = other // 2
    return other, dp, other - 2 * dp


def own_number():
    return 2 * lax.axis_index("dp") + lax.axis_index("head")


def greet_all(total):
    barrier = pltpu.get_barrier_semaphore()
    own = own_number()

    @pl.loop(1, total)
    def _(k):
        _, dp, head = peer_of(own, total, k)
        pl.semaphore_signal(
            barrier, inc=1, device_id={"dp": dp, "head": head}, device_id_type=pl.DeviceIdType.MESH
        )


def greeted_all(total):
    pl.semaphore_wait(pltpu.get_barrier_semaphore(), total - 1)


def share_start(total, src, inbox, ss, rs):
    own = own_number()
    inbox[own] = src[...]

    @pl.loop(1, total)
    def _(k):
        _, dp, head = peer_of(own, total, k)
        remote(src, inbox.at[own], ss.at[k], rs.at[own], dp, head).start()


def share_finish(total, src, inbox, ss, rs):
    own = own_number()

    @pl.loop(1, total)
    def _(k):
        other, dp, head = peer_of(own, total, k)
        remote(src, inbox.at[other], ss.at[k], rs.at[other], dp, head).wait()


HEADS = 4
HD = 60
FF = 960
KW = 15
STEP = 10
KREL = 383
NORM_EPS = 1e-05
BETA_ONE = 0.9
BETA_TWO = 0.999
LEARN_RATE = 0.1
WEIGHT_DECAY = 0.01
ADAM_EPS = 1e-08
LOG2E = 1.4426950408889634
LN2 = 0.6931471805599453
SCALE = HD ** (-0.5)
UNIT = 1.28125
D = 240
DP = 256
HF = 480
HFP = 512
FFP = 1024
HC = 120
MASK_LANE = 120
NEG = -1e30
FFA, ATT, CNV, FFB, OUT = 0, 2, 4, 6, 8
DOWNB_ONE, DOWNB_TWO, B_OUT, BATCH_GAIN, BATCH_BIAS, TAPS, DEPTH_BIAS = 10, 11, 12, 13, 14, 16, 31
VEC_ROWS = 32
BIG = 60 << 20


def head_places():
    out, at = {}, 0
    for name, size in (
        ("up1", D * HF), ("upb1", HF), ("dn1", HF * D), ("up2", D * HF), ("upb2", HF), ("dn2", HF * D),
        ("wq", D * HC), ("wk", D * HC), ("wv", D * HC), ("bq", HC), ("bv", HC),
        ("rel", 2 * KREL), ("wo", HC * D),
    ):
        out[name] = at
        at += size
    return out, at


def shared_places():
    out, at = {}, 0
    for name, size in (
        ("vec", 13 * D), ("p1", 2 * D * D), ("pb1", 2 * D), ("taps", KW * D), ("db", D),
        ("bg", D), ("bb", D), ("p2", D * D), ("pb2", D),
    ):
        out[name] = at
        at += size
    return out, at


def lane_iota(shape):
    return lax.broadcasted_iota(jnp.int32, shape, len(shape) - 1)


def slot_rows(size):
    return up_to(-(-(size + LANES - 1) // LANES), 16)


def dot(a, b):
    return jnp.dot(a, b, preferred_element_type=F32)


def dot_t(a, b):
    return lax.dot_general(a, b, (((1,), (1,)), ((), ())), preferred_element_type=F32)


def t_dot(a, b):
    return lax.dot_general(a, b, (((0,), (0,)), ((), ())), preferred_element_type=F32)


def vmem_call(body, outs, ins, scratch=(), name=None, limit=BIG):
    return pl.pallas_call(
        body,
        out_shape=outs,
        in_specs=[pl.BlockSpec(memory_space=pltpu.VMEM) for _ in ins],
        out_specs=jax.tree.map(lambda _: pl.BlockSpec(memory_space=pltpu.VMEM), outs),
        scratch_shapes=list(scratch),
        compiler_params=pltpu.CompilerParams(vmem_limit_bytes=limit),
        name=name,
    )(*ins)


def own_offsets(head_size, shared_size):
    me = lax.axis_index("dp")
    core = lax.axis_index("head")
    return lax.rem(me * head_size, LANES), lax.rem((2 * me + core) * shared_size, LANES)


def push_lanes(x, shift):
    rolled = pltpu.roll(x, shift, 1)
    before = jnp.concatenate([jnp.zeros((1, LANES), F32), rolled[:-1]], 0)
    return jnp.where(lane_iota(x.shape) >= shift, rolled, before)


def pull_lanes(x, shift):
    rolled = pltpu.roll(x, lax.rem(LANES - shift, LANES), 1)
    after = jnp.concatenate([rolled[1:], jnp.zeros((1, LANES), F32)], 0)
    return jnp.where(lane_iota(x.shape) < LANES - shift, rolled, after)


def align(head_ref, shared_ref, out):
    head_size, shared_size = head_ref.shape[1], shared_ref.shape[0]
    hr, sr = slot_rows(head_size), slot_rows(shared_size)
    ho, so = own_offsets(head_size, shared_size)
    x = jnp.concatenate([head_ref[...], jnp.zeros((1, hr * LANES - head_size), F32)], 1)
    out[pl.ds(0, hr), :] = push_lanes(x.reshape(hr, LANES), ho).astype(BF)
    x = shared_ref[...].reshape(1, shared_size)
    x = jnp.concatenate([x, jnp.zeros((1, sr * LANES - shared_size), F32)], 1)
    out[pl.ds(hr, sr), :] = push_lanes(x.reshape(sr, LANES), so).astype(BF)


def adam_kernel(
    early, grad, g_ref, hp, hf, hs, sp, sf, ss, out_o, grad_o, hf_o, hs_o, hp_o, hc_o, sf_o, ss_o, sp_o, sc_o
):
    out_o[...] = early[...]
    grad_o[...] = grad[...]

    @pl.when(pl.program_id(0) == 0)
    def _():
        adam_update(g_ref, hp, hf, hs, sp, sf, ss, hf_o, hs_o, hp_o, hc_o, sf_o, ss_o, sp_o, sc_o)


def adam_update(g_ref, hp, hf, hs, sp, sf, ss, hf_o, hs_o, hp_o, hc_o, sf_o, ss_o, sp_o, sc_o):
    head_size, shared_size = hp.shape[1], sp.shape[0]
    hr, sr = slot_rows(head_size), slot_rows(shared_size)
    ho, so = own_offsets(head_size, shared_size)

    def update(master, g, first, second):
        first_new = BETA_ONE * first + (1.0 - BETA_ONE) * g
        second_new = BETA_TWO * second + (1.0 - BETA_TWO) * g * g
        first_hat = first_new * (1.0 / (1.0 - BETA_ONE**STEP))
        second_hat = second_new * (1.0 / (1.0 - BETA_TWO**STEP))
        new = master - LEARN_RATE * (first_hat / (jnp.sqrt(second_hat) + ADAM_EPS) + WEIGHT_DECAY * master)
        return first_new, second_new, new

    g = pull_lanes(g_ref[pl.ds(0, hr), :], ho).reshape(1, hr * LANES)[:, :head_size]
    one, two, new = update(hp[...], g, hf[...], hs[...])
    hf_o[...] = one
    hs_o[...] = two
    hp_o[...] = new
    hc_o[...] = new.astype(BF)
    g = pull_lanes(g_ref[pl.ds(hr, sr), :], so).reshape(sr * LANES)[:shared_size]
    one, two, new = update(sp[...], g, sf[...], ss[...])
    sf_o[...] = one
    ss_o[...] = two
    sp_o[...] = new
    sc_o[...] = new.astype(BF)


def row_phases(rows, pitch):
    if rows == 1:
        return 1, 1, 0
    period = LANES // math.gcd(pitch, LANES)
    return period, rows // period, period * pitch // LANES


def take(flat, at, rows, pitch, col, width, dst, row0, lane0):
    period, count, stride = row_phases(rows, pitch)
    lane = lane_iota((count, LANES))
    for j in range(period):
        start = at + j * pitch + col
        q, l = divmod(start, LANES)

        def load(t):
            if count == 1:
                return flat[pl.ds(q + t, 1), :]
            return flat[pl.ds(q + t, count, stride), :]

        pieces = [load(t) for t in range(-(-(l + width) // LANES))]
        if l:
            pieces = [pltpu.roll(x, LANES - l, 1) for x in pieces]
        for t in range(-(-width // LANES)):
            value = pieces[t]
            if l and t + 1 < len(pieces):
                value = jnp.where(lane < LANES - l, value, pieces[t + 1])
            left = width - t * LANES
            if left < LANES:
                value = jnp.where(lane < left, value, 0.0)
            rows_at = pl.ds(row0 + j, 1) if count == 1 else pl.ds(row0 + j, count, period)
            dst[lane0 // LANES + t, rows_at, :] = value


def give(flat, at, rows, pitch, col, width, src, row0, lane0):
    period, count, stride = row_phases(rows, pitch)
    lane = lane_iota((count, LANES))
    for j in range(period):
        start = at + j * pitch + col
        q, l = divmod(start, LANES)
        rows_at = pl.ds(row0 + j, 1) if count == 1 else pl.ds(row0 + j, count, period)
        pieces = [src[lane0 // LANES + t, rows_at, :] for t in range(-(-width // LANES))]
        if l:
            pieces = [pltpu.roll(x, l, 1) for x in pieces]
        total = -(-(l + width) // LANES)
        for t in range(total):
            here = pl.ds(q + t, 1) if count == 1 else pl.ds(q + t, count, stride)
            if not l:
                value = pieces[t]
            elif t == 0:
                value = pieces[0]
            elif t == len(pieces):
                value = pieces[t - 1]
            else:
                value = jnp.where(lane >= l, pieces[t], pieces[t - 1])
            lo = l if t == 0 else 0
            hi = min(LANES, l + width - t * LANES)
            if lo or hi < LANES:
                keep = (lane >= lo) & (lane < hi)
                value = jnp.where(keep, value, flat[here, :])
            flat[here, :] = value


def spill(tiles, rows, dst, factor=None):
    for t in range(dst.shape[1] // LANES):
        value = tiles[t, pl.ds(0, rows), :]
        if factor:
            value = factor * value
        dst[:, pl.ds(t * LANES, LANES)] = value.astype(dst.dtype)


def load_tiles(src, tiles, factor=None):
    for t in range(src.shape[1] // LANES):
        value = src[:, pl.ds(t * LANES, LANES)]
        tiles[t, pl.ds(0, src.shape[0]), :] = factor * value if factor else value


def flat_rows(total, size):
    return up_to(total // LANES + slot_rows(size) + 16, 16)


class Weights:
    def __init__(self, dp, head_size, shared_size, got, refs):
        self.dp, self.head_size, self.shared_size, self.got = dp, head_size, shared_size, got
        self.hr, self.sr = slot_rows(head_size), slot_rows(shared_size)
        self.fh, self.fs, self.wide, self.tall, self.tmp = refs
        self.hp, _ = head_places()
        self.sp, _ = shared_places()

    def clear_flat(self):
        self.fh[...] = jnp.zeros(self.fh.shape, F32)
        self.fs[...] = jnp.zeros(self.fs.shape, F32)

    def merge(self, slot, core, p):
        rows = self.hr + self.sr
        cut = up_to(rows // 2, 16)
        first = (slot * self.head_size) // LANES
        low, high = ((0, min(cut, self.hr)), (min(cut, self.hr), self.hr))[p]
        if high > low:
            at = pl.ds(first + low, high - low)
            self.fh[core, at, :] += self.got[slot, core, pl.ds(low, high - low), :].astype(F32)
        low, high = ((self.hr, max(cut, self.hr)), (max(cut, self.hr), rows))[p]
        if high > low:
            at = pl.ds(((2 * slot + core) * self.shared_size) // LANES + low - self.hr, high - low)
            self.fs[at, :] += self.got[slot, core, pl.ds(low, high - low), :].astype(F32)

    def clear(self, tiles, count, row, size):
        for t in range(count):
            tiles[t, pl.ds(row, size), :] = jnp.zeros((size, LANES), F32)

    def patch(self, tiles, tile, row, where, value):
        part = tiles[tile, pl.ds(row, 1), :]
        tiles[tile, pl.ds(row, 1), :] = jnp.where(where, value, part)

    def ffn(self, up, dn, up_place, bias_place, dn_place, row):
        wide, tall, hp = self.wide, self.tall, self.hp
        self.clear(wide, 8, 240, 16)
        for g in range(2):
            take(self.fh.at[g], hp[up_place], D, HF, 0, HF, wide, 0, g * HFP)
            take(self.fh.at[g], hp[bias_place], 1, HF, 0, HF, wide, 240, g * HFP)
        self.patch(wide, 3, 240, lane_iota((1, LANES)) == HF - 3 * LANES, UNIT)
        spill(wide, DP, up, 0.5)
        for g in range(2):
            self.clear(tall, 2, g * HFP + HF, 32)
            take(self.fh.at[g], hp[dn_place], HF, D, 0, D, tall, g * HFP, 0)
        take(self.fs, self.sp["vec"] + row * D, 1, D, 0, D, tall, HF, 0)
        spill(tall, FFP, dn, 0.5)

    def point_two(self, p2):
        self.clear(self.tall, 2, 240, 16)
        take(self.fs, self.sp["p2"], D, D, 0, D, self.tall, 0, 0)
        take(self.fs, self.sp["pb2"], 1, D, 0, D, self.tall, 240, 0)
        spill(self.tall, DP, p2)

    def others(self, qkv, wo, p1, vec, rel):
        wide, tall, tmp, fh, fs, hp, sp = self.wide, self.tall, self.tmp, self.fh, self.fs, self.hp, self.sp
        lane = lane_iota((1, LANES))
        self.clear(wide, 6, 240, 16)
        for g in range(2):
            for which, (place, bplace) in enumerate((("wq", "bq"), ("wk", None), ("wv", "bv"))):
                lane0 = which * DP + g * LANES
                take(fh.at[g], hp[place], D, HC, 0, HC, wide, 0, lane0)
                if bplace:
                    take(fh.at[g], hp[bplace], 1, HC, 0, HC, wide, 240, lane0)
        for tile in (0, 1, 4, 5):
            self.patch(wide, tile, 240, lane == MASK_LANE, 1.0)
        spill(wide, DP, qkv)
        self.clear(tall, 2, 0, DP)
        for g in range(2):
            take(fh.at[g], hp["wo"], HC, D, 0, D, tall, g * LANES, 0)
        take(fs, sp["vec"] + B_OUT * D, 1, D, 0, D, tall, MASK_LANE, 0)
        spill(tall, DP, wo)
        self.clear(wide, 4, 240, 16)
        for half in range(2):
            take(fs, sp["p1"], D, 2 * D, half * D, D, wide, 0, half * DP)
            take(fs, sp["pb1"] + half * D, 1, D, 0, D, wide, 240, half * DP)
        spill(wide, DP, p1)
        take(fs, sp["vec"], 16, D, 0, D, tall, 0, 0)
        take(fs, sp["taps"], 16, D, 0, D, tall, TAPS, 0)
        take(fs, sp["bg"], 1, D, 0, D, tall, BATCH_GAIN, 0)
        take(fs, sp["bb"], 1, D, 0, D, tall, BATCH_BIAS, 0)
        for row, value in ((FFA + 1, 1.0), (ATT + 1, 1.0), (CNV + 1, 1.0), (FFB + 1, 1.0), (BATCH_BIAS, UNIT)):
            self.patch(tall, 1, row, lane == D - LANES, value)
        spill(tall, VEC_ROWS, vec)
        length = rel.shape[1]
        for n in range(HEADS):
            take(fh.at[n // 2], hp["rel"] + (n % 2) * KREL, 1, KREL, 0, KREL, tmp, 0, 0)
            row = jnp.concatenate([tmp[t, pl.ds(0, 1), :] for t in range(3)] + [jnp.zeros((1, LANES), F32)], 1)
            rows = jnp.broadcast_to(row, (length, 4 * LANES))
            rows = pltpu.roll(rows, 4 * LANES - (length - 1), 1, stride=1, stride_axis=0)
            rel[pl.ds(n * length, length), :] = rows[:, :length] * LOG2E


class Flat:
    @staticmethod
    def scratch(dp, head_size, shared_size):
        vm = pltpu.VMEM
        return [
            vm((2, flat_rows(head_size * dp, head_size), LANES), F32),
            vm((flat_rows(shared_size * 2 * dp, shared_size), LANES), F32),
            vm((8, DP, LANES), F32),
            vm((2, FFP, LANES), F32),
            vm((4, 8, LANES), F32),
        ]

    def __init__(self, dp, head_size, shared_size, refs):
        self.dp, self.head_size, self.shared_size = dp, head_size, shared_size
        self.hr, self.sr = slot_rows(head_size), slot_rows(shared_size)
        self.fh, self.fs, self.wide, self.tall, self.tmp = refs
        self.hp, self.used_h = head_places()
        self.sp, self.used_s = shared_places()

    def clear_unused(self):
        for g in range(2):
            first = self.used_h // LANES // 8 * 8
            count = self.fh.shape[1] - first
            self.fh[g, pl.ds(first, count), :] = jnp.zeros((count, LANES), F32)
        first = self.used_s // LANES // 8 * 8
        count = self.fs.shape[0] - first
        self.fs[pl.ds(first, count), :] = jnp.zeros((count, LANES), F32)

    def head(self, g, place, rows, pitch, src, row0, lane0):
        give(self.fh.at[g], self.hp[place], rows, pitch, 0, pitch, src, row0, lane0)

    def shared(self, place, at, rows, pitch, col, src, row0, lane0):
        give(self.fs, self.sp[place] + at, rows, pitch, col, D, src, row0, lane0)

    def up(self, up, place, bias_place):
        load_tiles(up, self.wide, 0.5)
        for g in range(2):
            self.head(g, place, D, HF, self.wide, 0, g * HFP)
            self.head(g, bias_place, 1, HF, self.wide, 240, g * HFP)

    def down(self, dn, place, row):
        for t in range(2):
            self.tall[t] = (0.5 * dn[pl.ds(t * LANES, LANES), :]).astype(BF).T.astype(F32)
        for g in range(2):
            self.head(g, place, HF, D, self.tall, g * HFP, 0)
        self.shared("vec", row * D, 1, D, 0, self.tall, HF, 0)

    def attention(self, qkv, wo, rel):
        load_tiles(qkv, self.wide)
        load_tiles(wo, self.tall)
        length = rel.shape[0] // HEADS
        for g in range(2):
            for which, (place, bplace) in enumerate((("wq", "bq"), ("wk", None), ("wv", "bv"))):
                lane0 = which * DP + g * LANES
                self.head(g, place, D, HC, self.wide, 0, lane0)
                if bplace:
                    self.head(g, bplace, 1, HC, self.wide, 240, lane0)
            self.head(g, "wo", HC, D, self.tall, g * LANES, 0)
        for n in range(HEADS):
            total = jnp.zeros((8, 4 * LANES), F32)
            for block in range(length // 8):
                rows = rel[pl.ds(n * length + 8 * block, 8), :]
                rows = jnp.concatenate([rows, jnp.zeros((8, 4 * LANES - length), F32)], 1)
                total = total + pltpu.roll(rows, length - 8 - 8 * block, 1)
            row = total[7:8]
            for i in range(7):
                row = row + pltpu.roll(total[i : i + 1], 7 - i, 1)
            for t in range(4):
                self.tmp[t, pl.ds(0, 1), :] = row[:, t * LANES : (t + 1) * LANES]
            give(self.fh.at[n // 2], self.hp["rel"] + (n % 2) * KREL, 1, KREL, 0, KREL, self.tmp, 0, 0)
        self.shared("vec", B_OUT * D, 1, D, 0, self.tall, MASK_LANE, 0)

    def points(self, p1, p2):
        load_tiles(p1, self.wide)
        load_tiles(p2, self.tall)
        for half in range(2):
            self.shared("p1", 0, D, 2 * D, half * D, self.wide, 0, half * DP)
            self.shared("pb1", half * D, 1, D, 0, self.wide, 240, half * DP)
        self.shared("p2", 0, D, D, 0, self.tall, 0, 0)
        self.shared("pb2", 0, 1, D, 0, self.tall, 240, 0)

    def vectors(self, vec, vec2):
        for t in range(2):
            cols = pl.ds(t * LANES, LANES)
            self.tall[t, pl.ds(0, VEC_ROWS), :] = vec[:, cols] + vec2[:, cols]
        for row in range(2, 10):
            self.shared("vec", row * D, 1, D, 0, self.tall, row, 0)
        self.shared("taps", 0, 16, D, 0, self.tall, TAPS, 0)
        self.shared("bg", 0, 1, D, 0, self.tall, BATCH_GAIN, 0)
        self.shared("bb", 0, 1, D, 0, self.tall, BATCH_BIAS, 0)

    def first_norm(self, vec):
        for t in range(2):
            self.tall[t, pl.ds(0, 8), :] = vec[pl.ds(0, 8), pl.ds(t * LANES, LANES)]
        for row in (FFA, FFA + 1):
            self.shared("vec", row * D, 1, D, 0, self.tall, row, 0)

    def slots(self, out, z, kind):
        for i in range(4 * z, 4 * z + 4):
            for g in range(2):
                if kind == 0:
                    out[g, i, pl.ds(0, self.hr), :] = self.fh[g, pl.ds(i * self.head_size // LANES, self.hr), :].astype(BF)
                else:
                    at = (2 * i + g) * self.shared_size // LANES
                    out[g, i, pl.ds(self.hr, self.sr), :] = self.fs[pl.ds(at, self.sr), :].astype(BF)

    def groups(self):
        size = 4 * self.head_size
        every = range(self.dp // 4)
        one = [z for z in every if z * size >= self.hp["up2"] and (z + 1) * size <= self.hp["wq"]]
        two = [z for z in every if z * size >= self.hp["dn1"] and z not in one]
        late = [z for z in every if 8 * z * self.shared_size < 2 * D]
        return one, two, [z for z in every if z not in one and z not in two], [z for z in every if z not in late], late


def row_sum(x):
    return jnp.sum(x, -1, keepdims=True)


def halves(x):
    return x[:, :LANES], x[:, LANES:]


def both(lo, hi):
    return jnp.concatenate([lo, hi], 1)


def norm(x, gain, bias):
    lane = lane_iota((1, LANES))
    lo, hi = halves(x)
    mean = row_sum(lo + hi) * (1.0 / D)
    lo = lo - mean
    hi = jnp.where(lane < D - LANES, hi - mean, 0.0)
    inv = lax.rsqrt(row_sum(lo * lo + hi * hi) * (1.0 / D) + NORM_EPS)
    lo, hi = lo * inv, hi * inv
    return both(lo, hi) * gain + bias, both(lo, jnp.where(lane == LANES - 1, inv, hi))


def norm_grad(grad, kept, gain):
    dg = grad * gain
    inv = kept[:, DP - 1 :]
    first = row_sum(dg) * (1.0 / D)
    second = row_sum(dg * kept) * (1.0 / D)
    return inv * (dg - first - kept * second)


def fold_rows(x):
    return jnp.sum(x.reshape(x.shape[0] // 8, 8, x.shape[1]), 0)


def norm_param_grads(acc, row, grad, kept):
    acc[row] += fold_rows(grad * kept)
    acc[row + 1] += fold_rows(grad)


def settle(acc, out):
    for row in range(acc.shape[0]):
        out[pl.ds(row, 1), :] = jnp.sum(acc[row], 0, keepdims=True)


def silu_pair(y):
    p = jnp.tanh(y) + 1.0
    h = (y * p).astype(BF)
    p = p.astype(BF)
    return h, p + h * (2.0 - p)


def widen(x):
    rows = x.shape[0]
    return jnp.concatenate([x.astype(F32), jnp.zeros((rows, DP - D), F32)], 1)


SHORT = (1, 1, 1, 1, 3, 1, 1, 4)
LATE = (4, 1)
LONG = (1, 1, 1)
PAIR = (1, 1)


def columns(ref, widths):
    out, at = [], 0
    for width in widths:
        out.append(ref.at[:, pl.ds(at * DP, width * DP)])
        at += width
    return out


def head_lanes():
    lane = lane_iota((1, LANES))
    return lane < HD, (lane >= HD) & (lane < 2 * HD), lane == MASK_LANE


def valid_rows(lengths, at, length):
    return lax.broadcasted_iota(jnp.int32, (length, 1), 0) < lengths[at]


def phase_a_kernel(
    seqs, sizes, lengths, frames, head_ref, shared_ref,
    short_far, late_far, long_far, kept1_far, xw_far, e_far, keep_o, up, dn, up2, dn2, wqkv, wo, p1, p2, vec, rel,
    pad, stats_o, inbox, ss, rs, own_slot, got, fh, fs, wide, tall, tmp,
    short_b, late_b, long_b, kept1_b, xw_b, e_b, out_sem, *sems,
):
    step = pl.program_id(0)
    slot = lax.rem(step, 2)
    far = (short_far, late_far, long_far, kept1_far, xw_far, e_far)
    near = (short_b, late_b, long_b, kept1_b, xw_b, e_b)

    def moves(k):
        side = lax.rem(k, 2)
        out = []
        for j, (here, there) in enumerate(zip(near, far)):
            size = here.shape[1]
            rows = pl.ds(pl.multiple_of(k * size, size), size)
            out.append(pltpu.make_async_copy(here.at[side], there.at[rows], out_sem.at[side, j]))
        return out

    @pl.when(step >= 2)
    def _():
        for move in moves(step - 2):
            move.wait()

    short_o, late_o, long_o, kept1_o, xw_o, e_o = (ref.at[slot] for ref in near)
    total = inbox.shape[0]
    weights = Weights(*sizes, got, (fh, fs, wide, tall, tmp))
    gl_o, f1_o, f2_o, a3_o, qkv_o, m_o, a2_o, h_o = columns(short_o, SHORT)
    sp_o, a1_o = columns(late_o, LATE)
    kept3_o, kept2_o, rl_o = columns(long_o, LONG)
    x2_o, w_o = columns(xw_o, PAIR)

    @pl.when(step == 0)
    def _():
        greet_all(total)
        align(head_ref, shared_ref, own_slot)
        weights.clear_flat()
        greeted_all(total)
        gather(sizes[0] // 4, own_slot, got, sems, weights.merge)
        weights.ffn(up, dn, "up1", "upb1", "dn1", DOWNB_ONE)
        weights.others(wqkv, wo, p1, vec, rel)

    length = frames.shape[1]
    tokens = seqs * length
    first_seq = lax.axis_index("head") * (seqs * pl.num_programs(0)) + step * seqs

    def v(row):
        return vec[pl.ds(row, 1), :]

    x0 = widen(frames[...].reshape(tokens, D))
    a, kept1_o[...] = norm(x0, v(FFA), v(FFA + 1))
    a = a.astype(BF)
    a1_o[...] = a
    h, slope = silu_pair(dot(a, up[...]))
    h_o[...] = h
    sp_o[...] = slope
    x1 = x0 + dot(h, dn[...])
    a, kept = norm(x1, v(ATT), v(ATT + 1))
    kept2_o[...] = kept.astype(BF)
    a = a.astype(BF)
    a2_o[...] = a
    qkv = dot(a, wqkv[...])
    first, second, special = head_lanes()
    for b in range(seqs):
        rows = pl.ds(b * length, length)
        fence = jnp.where(valid_rows(lengths, first_seq + b, length), 0.0, NEG)
        for g in range(2):
            def piece(which):
                at = which * DP + g * LANES
                return qkv[b * length : (b + 1) * length, at : at + LANES]

            q = (piece(0) * (SCALE * LOG2E)).astype(BF)
            k = jnp.where(special, fence, piece(1)).astype(BF)
            vv = piece(2).astype(BF)
            qkv_o[rows, pl.ds(g * LANES, LANES)] = q
            qkv_o[rows, pl.ds(DP + g * LANES, LANES)] = k
            qkv_o[rows, pl.ds(2 * DP + g * LANES, LANES)] = vv
            zero = jnp.zeros_like(q)
            pair = jnp.concatenate([jnp.where(first | special, q, zero), jnp.where(second | special, q, zero)], 0)
            at = pl.ds(2 * g * length, 2 * length)
            s = dot_t(pair, k) + rel[at, :]
            e = jnp.exp2(s - jnp.max(s, -1, keepdims=True)).astype(BF)
            e_o[b, at, :] = e
            o = dot(e, vv)
            r = 1.0 / o[:, MASK_LANE : MASK_LANE + 1]
            shares = jnp.where(second, r[length:], r[:length])
            rl_o[rows, pl.ds(g * LANES, LANES)] = shares.astype(BF)
            m_o[rows, pl.ds(g * LANES, LANES)] = (jnp.where(second, o[length:], o[:length]) * shares).astype(BF)
    x2 = x1 + dot(m_o[...], wo[...])
    x2_o[...] = x2
    a, kept = norm(x2, v(CNV), v(CNV + 1))
    kept3_o[...] = kept.astype(BF)
    a = a.astype(BF)
    a3_o[...] = a
    e = dot(a, p1[...])
    half = KW // 2

    @pl.when(step == 0)
    def _():
        pad[...] = jnp.zeros(pad.shape, F32)
        stats_o[...] = jnp.zeros(stats_o.shape, F32)

    count = jnp.float32(0.0)
    summed = jnp.zeros((1, DP), F32)
    for b in range(seqs):
        rows = pl.ds(b * length, length)
        valid = jnp.where(valid_rows(lengths, first_seq + b, length), 1.0, 0.0)
        linear = e[b * length : (b + 1) * length, :DP]
        gate = 0.5 * jnp.tanh(0.5 * e[b * length : (b + 1) * length, DP:]) + 0.5
        f1 = gate * valid
        gl = linear * f1
        f1_o[rows, :] = f1.astype(BF)
        f2_o[rows, :] = (gl * (1.0 - gate)).astype(BF)
        gl_o[rows, :] = gl.astype(BF)
        for t in range(2):
            cols = pl.ds(t * LANES, LANES)
            pad[b, t, pl.ds(8, length), :] = gl[:, t * LANES : (t + 1) * LANES]
            acc = jnp.broadcast_to(vec[pl.ds(DEPTH_BIAS, 1), cols], (length, LANES))
            for r in range(KW):
                acc = acc + pad[b, t, pl.ds(8 - half + r, length), :] * vec[pl.ds(TAPS + r, 1), cols]
            w_o[rows, cols] = acc
        summed = summed + jnp.sum(w_o[rows, :] * valid, 0, keepdims=True)
        count = count + lengths[first_seq + b].astype(F32)
    mean = summed / count
    square = jnp.zeros((1, DP), F32)
    for b in range(seqs):
        valid = jnp.where(valid_rows(lengths, first_seq + b, length), 1.0, 0.0)
        centre = (w_o[pl.ds(b * length, length), :] - mean) * valid
        square = square + jnp.sum(centre * centre, 0, keepdims=True)
    old = stats_o[pl.ds(4, 1), :]
    new = old + count
    for t in range(2):
        cols = slice(t * LANES, (t + 1) * LANES)
        before = stats_o[pl.ds(t, 1), :]
        delta = mean[:, cols] - before
        stats_o[pl.ds(t, 1), :] = before + delta * (count / new)
        stats_o[pl.ds(2 + t, 1), :] += square[:, cols] + delta * delta * (old * count / new)
    stats_o[pl.ds(4, 1), :] = new
    for move in moves(step):
        move.start()

    @pl.when(step == pl.num_programs(0) - 1)
    def _():
        unused = lane_iota((1, LANES)) == LANES - 1
        stats_o[pl.ds(1, 1), :] = jnp.where(unused, stats_o[pl.ds(4, 1), :], stats_o[pl.ds(1, 1), :])
        share_start(total, stats_o.at[pl.ds(0, 4)], inbox, ss, rs)
        weights.ffn(up2, dn2, "up2", "upb2", "dn2", DOWNB_TWO)
        weights.point_two(p2)
        share_finish(total, stats_o.at[pl.ds(0, 4)], inbox, ss, rs)
        batch_stats(inbox[...], keep_o)
        for move in moves(step - 1) + moves(step):
            move.wait()


def batch_stats(shared, keep):
    counts = jnp.broadcast_to(shared[:, 1:2, LANES - 1 :], (shared.shape[0], 1, LANES))
    total = jnp.sum(counts, 0)
    means, spreads = [], []
    for t in range(2):
        each = shared[:, t : t + 1, :]
        mean = jnp.sum(each * counts, 0) / total
        spread = (jnp.sum(shared[:, 2 + t : 3 + t, :], 0) + jnp.sum(counts * (each - mean) ** 2, 0)) / total
        means.append(mean)
        spreads.append(spread)
    keep[pl.ds(0, 1), :] = jnp.concatenate(means, 1)
    keep[pl.ds(1, 1), :] = lax.rsqrt(jnp.concatenate(spreads, 1) + NORM_EPS)
    keep[pl.ds(2, 1), :] = jnp.concatenate([total, total], 1)
    keep[pl.ds(3, 5), :] = jnp.zeros((5, DP), F32)


def phase_b_kernel(
    seqs, keep, xw, cotangent, p2, up, dn, vec,
    out_o, back_o, dup_far, ddn_far, dp2_far, vec_o, keep_o,
    dup_o, ddn_o, dp2_o, out_sem, acc, a_all, du_all, do_all, h_all, hc_all, dc_all, sums_o, inbox, ss, rs,
):
    step = pl.program_id(0)
    total = inbox.shape[0]
    length = cotangent.shape[1]
    tokens = seqs * length
    at = pl.ds(pl.multiple_of(step * tokens, tokens), tokens)
    x2, w = columns(xw, PAIR)
    dy_o, dx3_o = columns(back_o, PAIR)

    @pl.when(step == 0)
    def _():
        greet_all(total)
        for ref in (dup_o, ddn_o, dp2_o, acc):
            ref[...] = jnp.zeros(ref.shape, F32)

    def v(row):
        return vec[pl.ds(row, 1), :]

    mean, inv_batch = keep[pl.ds(0, 1), :], keep[pl.ds(1, 1), :]
    z = (w[...] - mean) * inv_batch
    hc, slope_c = silu_pair(z * (0.5 * v(BATCH_GAIN)) + 0.5 * v(BATCH_BIAS))
    x3 = x2[...] + dot(hc, p2[...])
    a, kept = norm(x3, v(FFB), v(FFB + 1))
    a = a.astype(BF)
    h, slope = silu_pair(dot(a, up[...]))
    x4 = x3 + dot(h, dn[...])
    final, kept4 = norm(x4, v(OUT), v(OUT + 1))
    out_o[...] = final[:, :D].astype(BF).reshape(seqs, length, D)
    g = widen(cotangent[...].reshape(tokens, D))
    norm_param_grads(acc, OUT, g, kept4)
    dx4 = norm_grad(g, kept4, v(OUT))
    do = dx4.astype(BF)
    do_all[at, :] = do
    h_all[at, :] = h
    du = dot_t(do, dn[...]).astype(BF) * slope
    a_all[at, :] = a
    du_all[at, :] = du
    da = dot_t(du, up[...])
    norm_param_grads(acc, FFB, da, kept)
    dx3 = dx4 + norm_grad(da, kept, v(FFB))
    dx3_o[...] = dx3
    dc = dx3.astype(BF)
    hc_all[at, :] = hc
    dc_all[at, :] = dc
    dy = dot_t(dc, p2[...]) * slope_c.astype(F32)
    dy_o[...] = dy
    acc[BATCH_BIAS] += fold_rows(dy)
    acc[BATCH_GAIN] += fold_rows(dy * z)

    @pl.when(step == pl.num_programs(0) - 1)
    def _():
        acc[BATCH_BIAS] *= 0.5
        acc[BATCH_GAIN] *= 0.5
        settle(acc, vec_o)
        for row, source in ((0, BATCH_BIAS), (2, BATCH_GAIN)):
            line = vec_o[pl.ds(source, 1), :]
            for t in range(2):
                sums_o[pl.ds(row + t, 1), :] = line[:, t * LANES : (t + 1) * LANES]

    @pl.when(step == pl.num_programs(0) - 1)
    def _():
        greeted_all(total)
        share_start(total, sums_o.at[pl.ds(0, 4)], inbox, ss, rs)

        @pl.loop(0, pl.num_programs(0))
        def _(k):
            at = pl.ds(pl.multiple_of(k * tokens, tokens), tokens)
            ddn_o[...] += t_dot(do_all[at, :], h_all[at, :])
            dup_o[...] += t_dot(a_all[at, :], du_all[at, :])
            dp2_o[...] += t_dot(hc_all[at, :], dc_all[at, :])

        moves = [
            pltpu.make_async_copy(here, there, out_sem.at[j])
            for j, (here, there) in enumerate(((dup_o, dup_far), (ddn_o, ddn_far), (dp2_o, dp2_far)))
        ]
        for move in moves:
            move.start()
        share_finish(total, sums_o.at[pl.ds(0, 4)], inbox, ss, rs)
        sums = jnp.sum(inbox[...], 0)
        keep_o[...] = keep[...]
        keep_o[pl.ds(3, 1), :] = jnp.concatenate([sums[0:1], sums[1:2]], 1)
        keep_o[pl.ds(4, 1), :] = jnp.concatenate([sums[2:3], sums[3:4]], 1)
        for move in moves:
            move.wait()


def phase_c_kernel(
    seqs, steps, sizes, lengths, keep, xw_far, back_far, short_far, long_far, e_far, late_far, kept1_far,
    p1, wo, wqkv, dn, up, vec, dup2, ddn2, dp2, vec2,
    dx0_o, sum_o,
    dp1_o, dwo_o, dqkv_o, dup_o, ddn_o, vec_o, rel_o, dx1_buf, mine,
    acc, padw, padg, grads, w_b, back_b, short_b, long_b, e_b, late_b, kept1_b, in_sem, *refs,
):
    step = pl.program_id(0)
    length = dx0_o.shape[1]
    side = lax.rem(step, 2)
    cut = 3 * DP

    def fetch(k, names):
        to = lax.rem(k, 2)
        size = seqs * length
        rows = pl.ds(pl.multiple_of(k * size, size), size)
        make = pltpu.make_async_copy
        every = (
            lambda j: make(xw_far.at[rows, pl.ds(DP, DP)], w_b.at[to], in_sem.at[to, j]),
            lambda j: make(back_far.at[rows], back_b.at[to], in_sem.at[to, j]),
            lambda j: make(short_far.at[rows, pl.ds(0, cut)], short_b.at[to, :, pl.ds(0, cut)], in_sem.at[to, j]),
            lambda j: make(
                short_far.at[rows, pl.ds(cut, short_b.shape[2] - cut)],
                short_b.at[to, :, pl.ds(cut, short_b.shape[2] - cut)],
                in_sem.at[to, j],
            ),
            lambda j: make(long_far.at[rows], long_b.at[to], in_sem.at[to, j]),
            lambda j: make(e_far.at[pl.ds(k * seqs, seqs)], e_b.at[to], in_sem.at[to, j]),
            lambda j: make(late_far.at[rows], late_b.at[to], in_sem.at[to, j]),
            lambda j: make(kept1_far.at[rows], kept1_b.at[to], in_sem.at[to, j]),
        )
        return [every[j](j) for j in names]

    conv_names, rest_names, late_names = (0, 1, 2), (3, 4, 5), (6, 7)

    @pl.when(step == 0)
    def _():
        for move in fetch(step, conv_names + rest_names):
            move.start()

    @pl.when(step < steps - 1)
    def _():
        for move in fetch(step + 1, conv_names + rest_names):
            move.start()

    @pl.when(step == steps - 1)
    def _():
        for move in fetch(step * 0, late_names):
            move.start()

    @pl.when((step >= steps) & (step < 2 * steps - 1))
    def _():
        for move in fetch(step + 1 - steps, late_names):
            move.start()

    w, back, short, long, e_all = (ref.at[side] for ref in (w_b, back_b, short_b, long_b, e_b))
    late_side = lax.rem(jnp.maximum(step - steps, 0), 2)
    late, kept1 = late_b.at[late_side], kept1_b.at[late_side]
    flat = Flat(*sizes, refs[:5])
    nz = sizes[0] // 4
    scatter = Scatter(nz, flat.hr, flat.sr, mine, refs[5:])
    one, two, rest, shared_two, shared_rest = flat.groups()
    dy, dx3 = columns(back, PAIR)
    gl, f1, f2, a3, qkv, m, a2, h = columns(short, SHORT)
    kept3, kept2, rl = columns(long, LONG)
    slope, a1 = columns(late, LATE)

    @pl.when(step == 0)
    def _():
        greet(nz, scatter.me, scatter.core, scatter.zc, scatter.yc, scatter.xc)
        for ref in (dp1_o, dwo_o, dqkv_o, dup_o, ddn_o, acc, rel_o, padw, padg):
            ref[...] = jnp.zeros(ref.shape, F32)
        flat.clear_unused()
        flat.up(dup2, "up2", "upb2")
        flat.down(ddn2, "dn2", DOWNB_TWO)
        for z in one:
            flat.slots(scatter.g, z, 0)
        greeted(nz)
        for z in one:
            scatter.stage_core(z, 0)

    @pl.when(step < steps)
    def _():
        def ready(names):
            for move in fetch(step, names):
                move.wait()

        ready(conv_names)
        phase_c_first(
            functools.partial(ready, rest_names), seqs, step, steps, length, lengths, keep, w, dy, dx3, gl, f1, f2, a3, kept3, qkv, e_all, rl, m, a2, kept2,
            h, p1, wo, wqkv, vec, dp1_o, dwo_o, dqkv_o, ddn_o, rel_o, dx1_buf, acc, padw, padg, grads,
        )

    @pl.when(step == steps)
    def _():
        flat.attention(dqkv_o, dwo_o, rel_o)
        flat.down(ddn_o, "dn1", DOWNB_ONE)
        for z in two:
            flat.slots(scatter.g, z, 0)
            scatter.stage_core(z, 0)
        settle(acc, vec_o)
        flat.points(dp1_o, dp2)
        flat.vectors(vec_o, vec2)
        for z in shared_two:
            flat.slots(scatter.g, z, 1)
            scatter.stage_core(z, 1)

    last_rows = pl.ds(pl.multiple_of(jnp.maximum(step - steps, 0) * (seqs * length), seqs * length), seqs * length)

    @pl.when(step >= steps)
    def _():
        for move in fetch(step - steps, late_names):
            move.wait()
        dx1 = dx1_buf[last_rows, :]
        du = dot_t(dx1.astype(BF), dn[...]).astype(BF) * slope[...]
        slope[...] = du
        dup_o[...] += t_dot(a1[...], du)

    @pl.when(step == 2 * steps - 1)
    def _():
        flat.up(dup_o, "up1", "upb1")
        for z in rest:
            flat.slots(scatter.g, z, 0)
            scatter.stage_core(z, 0)

    @pl.when(step >= steps)
    def _():
        da = dot_t(slope[...], up[...])
        norm_param_grads(acc, FFA, da, kept1[...])
        dx0 = dx1_buf[last_rows, :] + norm_grad(da, kept1[...], vec[pl.ds(FFA, 1), :])
        dx0_o[...] = dx0[:, :D].reshape(seqs, length, D)

    stages = (scatter.stage_first, scatter.stage_second, scatter.stage_third)
    for at, heads, shared in (((1, 2, 3), one, []), (tuple(steps + k for k in TWO_AT), two, shared_two)):
        for when, stage in zip(at, stages):
            @pl.when(step == when)
            def _():
                for z in heads:
                    stage(z, 0)
                for z in shared:
                    stage(z, 1)

    @pl.when(step == 2 * steps - 1)
    def _():
        settle(acc, vec_o)
        flat.first_norm(vec_o)
        for z in shared_rest:
            flat.slots(scatter.g, z, 1)
            scatter.stage_core(z, 1)
        waiting = [(stage, two, shared_two) for stage in stages[len(TWO_AT) :]]
        last = [(stage, rest, shared_rest) for stage in stages]
        for stage, heads, shared in [x for pair in zip(waiting, last) for x in pair] + last[len(waiting) :]:
            for z in heads:
                stage(z, 0)
            for z in shared:
                stage(z, 1)
        scatter.finish(sum_o)


def phase_c_first(
    ready, seqs, step, steps, length, lengths, keep, w, dy, dx3, gl, f1, f2, a3, kept3, qkv, e_all, rl, m, a2, kept2,
    h, p1, wo, wqkv, vec, dp1_o, dwo_o, dqkv_o, ddn_o, rel_o, dx1_buf, acc, padw, padg, grads,
):
    first_seq = lax.axis_index("head") * (seqs * steps) + step * seqs
    half = KW // 2

    def v(row):
        return vec[pl.ds(row, 1), :]

    mean, inv_batch, count = (keep[pl.ds(row, 1), :] for row in range(3))
    scale = v(BATCH_GAIN) * inv_batch
    cross = inv_batch * scale * keep[pl.ds(4, 1), :] / count
    plain = scale * keep[pl.ds(3, 1), :] / count - mean * cross
    scale = 0.5 * scale
    for b in range(seqs):
        rows = pl.ds(b * length, length)
        valid = jnp.where(valid_rows(lengths, first_seq + b, length), 1.0, 0.0)
        dw = dy[rows, :] * scale - valid * (plain + w[rows, :] * cross)
        acc[DEPTH_BIAS] += fold_rows(dw)
        for t in range(2):
            cols = pl.ds(t * LANES, LANES)
            here = dw[:, t * LANES : (t + 1) * LANES]
            padw[b, t, pl.ds(8, length), :] = here
            padg[b, t, pl.ds(8, length), :] = gl[rows, cols].astype(F32)
            total = jnp.zeros((length, LANES), F32)
            for r in range(KW):
                total = total + padw[b, t, pl.ds(8 + half - r, length), :] * vec[pl.ds(TAPS + r, 1), cols]
                tap = here * padg[b, t, pl.ds(8 - half + r, length), :]
                acc[TAPS + r, :, cols] += fold_rows(tap)
            grads[rows, cols] = (total * f1[rows, cols].astype(F32)).astype(BF)
            grads[rows, pl.ds(DP + t * LANES, LANES)] = (total * f2[rows, cols].astype(F32)).astype(BF)
    ready()
    de = grads[:, pl.ds(0, 2 * DP)]
    dp1_o[...] += t_dot(a3[...], de)
    da = dot_t(de, p1[...])
    kept = kept3[...].astype(F32)
    norm_param_grads(acc, CNV, da, kept)
    dx2 = dx3[...] + norm_grad(da, kept, v(CNV))
    db = dx2.astype(BF)
    dwo_o[...] += t_dot(m[...], db)
    dm = dot_t(db, wo[...])
    first, second, special = head_lanes()
    source = lax.broadcasted_iota(jnp.int32, (LANES, 2 * LANES), 0)
    target = lane_iota((LANES, 2 * LANES)) // LANES
    spread = jnp.where((source >= target * HD) & (source < (target + 1) * HD), 1.0, 0.0).astype(BF)
    for b in range(seqs):
        rows = pl.ds(b * length, length)
        for g in range(2):
            cols = pl.ds(g * LANES, LANES)
            q = qkv[rows, cols]
            k = qkv[rows, pl.ds(DP + g * LANES, LANES)]
            vv = qkv[rows, pl.ds(2 * DP + g * LANES, LANES)]
            dmb = (dm[b * length : (b + 1) * length, g * LANES : (g + 1) * LANES] * rl[rows, cols].astype(F32)).astype(BF)
            level = dot(dmb * m[rows, cols], spread)
            level = jnp.concatenate([level[:, :LANES], level[:, LANES:]], 0)
            zero = jnp.zeros_like(q)
            dm_pair = jnp.concatenate([jnp.where(first, dmb, zero), jnp.where(second, dmb, zero)], 0)
            q_pair = jnp.concatenate([jnp.where(first, q, zero), jnp.where(second, q, zero)], 0)
            at = pl.ds(2 * g * length, 2 * length)
            e = e_all[b, at, :]
            dp = dot_t(dm_pair, vv)
            ds = e.astype(F32) * (dp - jnp.concatenate([level, level[:, : length - LANES]], 1))
            rel_o[at, :] += ds
            ds = ds.astype(BF)
            dq = dot(ds, k)
            dq = jnp.where(second, dq[length:], dq[:length])
            grads[rows, cols] = (dq * SCALE).astype(BF)
            grads[rows, pl.ds(DP + g * LANES, LANES)] = (t_dot(ds, q_pair) * LN2).astype(BF)
            grads[rows, pl.ds(2 * DP + g * LANES, LANES)] = t_dot(e, dm_pair).astype(BF)
    dqkv = grads[...]
    dqkv_o[...] += t_dot(a2[...], dqkv)
    da = dot_t(dqkv, wqkv[...])
    kept = kept2[...].astype(F32)
    norm_param_grads(acc, ATT, da, kept)
    dx1 = dx2 + norm_grad(da, kept, v(ATT))
    at = pl.ds(pl.multiple_of(step * (seqs * length), seqs * length), seqs * length)
    dx1_buf[at, :] = dx1
    ddn_o[...] += t_dot(dx1.astype(BF), h[...])


def layer_call(body, steps, ins, outs, scratch, name, collective_id=None):
    def spec(item):
        kind, shape = item
        if kind == "far":
            return pl.BlockSpec(memory_space=pl.ANY)
        if kind == "smem":
            return pl.BlockSpec(memory_space=pltpu.SMEM)
        if kind == "tile":
            return pl.BlockSpec(shape, lambda i: (i,) + (0,) * (len(shape) - 1))
        if kind == "early":
            return pl.BlockSpec(shape, lambda i: (jnp.minimum(i, steps // 2 - 1),) + (0,) * (len(shape) - 1))
        if kind == "late":
            return pl.BlockSpec(shape, lambda i: (jnp.maximum(i - steps // 2, 0),) + (0,) * (len(shape) - 1))
        return pl.BlockSpec(shape, lambda i: (0,) * len(shape))

    arrays = [a for _, _, a in ins]
    return pl.pallas_call(
        body,
        grid=(steps,),
        out_shape=tuple(jax.ShapeDtypeStruct(full, dtype) for _, _, full, dtype in outs),
        in_specs=[spec((kind, block)) for kind, block, _ in ins],
        out_specs=tuple(spec((kind, block)) for kind, block, _, _ in outs),
        scratch_shapes=list(scratch),
        compiler_params=pltpu.CompilerParams(
            vmem_limit_bytes=BIG,
            dimension_semantics=("arbitrary",),
            collective_id=collective_id,
            has_side_effects=collective_id is not None,
        ),
        name=name,
    )(*arrays)


def tile_in(array, steps, kind="tile"):
    return (kind, (array.shape[0] // steps,) + array.shape[1:], array)


def whole_in(array):
    return ("whole", array.shape, array)


def tile_out(steps, shape, dtype, kind="tile"):
    return (kind, (shape[0] // steps,) + shape[1:], shape, dtype)


def far_in(array):
    return ("far", None, array)


def far_out(shape, dtype):
    return ("far", None, shape, dtype)


def whole_out(shape, dtype=F32):
    return ("whole", shape, shape, dtype)


SEQS_A = 4
SEQS_B = 4
SEQS_C = 4
TWO_AT = (1,)


def per_device(
    frames, cotangent, lengths, head_params, shared_params, head_first, head_second, shared_first, shared_second
):
    seq_here, length, _ = frames.shape
    tokens = seq_here * length
    dp = lax.axis_size("dp")
    head_size, shared_size = head_params.shape[1], shared_params.shape[0]
    rows = slot_rows(head_size) + slot_rows(shared_size)
    vm = pltpu.VMEM
    dma = pltpu.SemaphoreType.DMA
    sharing = [vm((8, LANES), F32), vm((2 * dp, 4, LANES), F32), dma((2 * dp,)), dma((2 * dp,))]
    steps = seq_here // SEQS_A
    block = SEQS_A * length
    t = functools.partial(tile_out, steps)
    (
        short, late, long, kept1, xw, e_all, keep,
        up1, dn1, up2, dn2, wqkv, wo, p1, p2, vec, rel
    ) = layer_call(
        functools.partial(phase_a_kernel, SEQS_A, (dp, head_size, shared_size)),
        steps,
        [("smem", None, lengths), tile_in(frames, steps), whole_in(head_params), whole_in(shared_params)],
        [
            far_out((tokens, sum(SHORT) * DP), BF), far_out((tokens, sum(LATE) * DP), BF),
            far_out((tokens, sum(LONG) * DP), BF), far_out((tokens, DP), F32), far_out((tokens, sum(PAIR) * DP), F32),
            far_out((seq_here, HEADS * length, length), BF),
            whole_out((8, DP)),
            whole_out((DP, FFP), BF), whole_out((FFP, DP), BF), whole_out((DP, FFP), BF), whole_out((FFP, DP), BF),
            whole_out((DP, 3 * DP), BF), whole_out((DP, DP), BF), whole_out((DP, 2 * DP), BF), whole_out((DP, DP), BF),
            whole_out((VEC_ROWS, DP)), whole_out((HEADS * length, length)),
        ],
        [vm((SEQS_A, 2, length + 16, LANES), F32)]
        + sharing
        + [vm((rows, LANES), BF), vm((dp, 2, rows, LANES), BF)]
        + Flat.scratch(dp, head_size, shared_size)
        + [
            vm((2, block, sum(SHORT) * DP), BF), vm((2, block, sum(LATE) * DP), BF), vm((2, block, sum(LONG) * DP), BF),
            vm((2, block, DP), F32), vm((2, block, sum(PAIR) * DP), F32), vm((2, SEQS_A, HEADS * length, length), BF),
            dma((2, 6)),
        ]
        + gather_sems(dp // 4),
        "phase_a",
        1,
    )
    steps = seq_here // SEQS_B
    t = functools.partial(tile_out, steps)
    early, back, dup2, ddn2, dp2, vec_b, keep = layer_call(
        functools.partial(phase_b_kernel, SEQS_B),
        steps,
        [whole_in(keep), tile_in(xw, steps), tile_in(cotangent, steps)]
        + [whole_in(x) for x in (p2, up2, dn2, vec)],
        [
            t((seq_here, length, D), BF), t((tokens, sum(PAIR) * DP), F32),
            far_out((DP, FFP), F32), far_out((DP, FFP), F32), far_out((DP, DP), F32), whole_out((VEC_ROWS, DP)),
            whole_out((8, DP)),
        ],
        [
            vm((DP, FFP), F32), vm((DP, FFP), F32), vm((DP, DP), F32), dma((3,)),
            vm((VEC_ROWS, 8, DP), F32), vm((tokens, DP), BF), vm((tokens, FFP), BF), vm((tokens, DP), BF),
            vm((tokens, FFP), BF), vm((tokens, DP), BF), vm((tokens, DP), BF),
        ]
        + sharing,
        "phase_b",
        3,
    )
    steps = seq_here // SEQS_C
    slot = (slot_rows(head_size), slot_rows(shared_size))
    block = SEQS_C * length
    input_grad, summed = layer_call(
        functools.partial(phase_c_kernel, SEQS_C, steps, (dp, head_size, shared_size)),
        2 * steps,
        [("smem", None, lengths), whole_in(keep)]
        + [far_in(x) for x in (xw, back, short, long, e_all, late, kept1)]
        + [whole_in(x) for x in (p1, wo, wqkv, dn1, up1, vec, dup2, ddn2, dp2, vec_b)],
        [tile_out(steps, (seq_here, length, D), F32, "late"), whole_out((rows, LANES))],
        [
            vm((DP, 2 * DP), F32), vm((DP, DP), F32), vm((DP, 3 * DP), F32), vm((DP, FFP), F32), vm((DP, FFP), F32),
            vm((VEC_ROWS, DP), F32), vm((HEADS * length, length), F32), vm((tokens, DP), F32), vm((rows, LANES), F32),
            vm((VEC_ROWS, 8, DP), F32),
            vm((SEQS_C, 2, length + 16, LANES), F32),
            vm((SEQS_C, 2, length + 16, LANES), F32),
            vm((block, 3 * DP), BF),
            vm((2, block, DP), F32), vm((2, block, sum(PAIR) * DP), F32), vm((2, block, sum(SHORT) * DP), BF),
            vm((2, block, sum(LONG) * DP), BF), vm((2, SEQS_C, HEADS * length, length), BF),
            vm((2, block, sum(LATE) * DP), BF), vm((2, block, DP), F32), dma((2, 8)),
        ]
        + Flat.scratch(dp, head_size, shared_size)
        + Scatter.scratch(dp, *slot),
        "phase_c",
        4,
    )
    h_shape, s_shape = head_params.shape, shared_params.shape
    steps = 2
    return layer_call(
        adam_kernel,
        steps,
        [tile_in(x, steps) for x in (early, input_grad)]
        + [whole_in(x) for x in (summed, head_params, head_first, head_second, shared_params, shared_first, shared_second)],
        [tile_out(steps, early.shape, BF), tile_out(steps, early.shape, F32)]
        + [whole_out(h_shape)] * 3
        + [whole_out(h_shape, BF)]
        + [whole_out(s_shape)] * 3
        + [whole_out(s_shape, BF)],
        [],
        "adam",
    )


def solution(mesh):
    frames = P(("dp", "head"), None, None)
    heads = P("head", "dp")
    shared = P(("dp", "head"))
    return jax.shard_map(
        per_device,
        mesh=mesh,
        in_specs=(frames, frames, P("dp"), heads, shared, heads, heads, shared, shared),
        out_specs=(frames, frames) + (heads,) * 4 + (shared,) * 4,
        check_vma=False,
    )
```

```python
import functools
import math

import jax
import jax.numpy as jnp
from jax import lax
from jax.experimental import pallas as pl
from jax.experimental.pallas import tpu as pltpu
from jax.sharding import PartitionSpec as P

BF = jnp.bfloat16
F32 = jnp.float32
LANES = 128


def up_to(count, unit):
    return -(-count // unit) * unit


def grid_place(nz):
    me = lax.axis_index("dp")
    core = lax.axis_index("head")
    zc = me // 4
    rest = me - 4 * zc
    yc = rest // 2
    xc = rest - 2 * yc
    return me, core, zc, yc, xc


def remote(src, dst, send, recv, dp, head):
    return pltpu.make_async_remote_copy(
        src_ref=src,
        dst_ref=dst,
        send_sem=send,
        recv_sem=recv,
        device_id={"dp": dp, "head": head},
        device_id_type=pl.DeviceIdType.MESH,
    )


def greet(nz, me, core, zc, yc, xc):
    barrier = pltpu.get_barrier_semaphore()

    def hello(dp, head):
        pl.semaphore_signal(
            barrier, inc=1, device_id={"dp": dp, "head": head}, device_id_type=pl.DeviceIdType.MESH
        )

    for k in range(1, nz):
        hello(lax.rem(zc + k, nz) * 4 + 2 * yc + xc, core)
    hello(4 * zc + 2 * (1 - yc) + xc, core)
    hello(4 * zc + 2 * yc + 1 - xc, core)
    hello(me, 1 - core)


def greeted(nz):
    pl.semaphore_wait(pltpu.get_barrier_semaphore(), nz + 2)


def gather(nz, src, out, sems, merge):
    sz, rz, s1, r1, s2, r2, sc, rc = sems
    rows = src.shape[0]
    row_a = up_to(rows // 2, 16)
    parts = (pl.ds(0, row_a), pl.ds(row_a, rows - row_a))
    me, core, zc, yc, xc = grid_place(nz)
    out[me, core] = src[...]
    y_peer = 4 * zc + 2 * (1 - yc) + xc
    x_peer = 4 * zc + 2 * yc + 1 - xc
    firsts = (y_peer, x_peer)
    seconds = (x_peer, y_peer)
    pending = []

    def send(slot, p, send_sem, recv_sem, dp, head):
        block = out.at[slot, core, parts[p]]
        copy = remote(block, block, send_sem, recv_sem, dp, head)
        copy.start()
        pending.append(copy)

    def arrived(slot, which, p, send_sem, recv_sem):
        block = out.at[slot, which, parts[p]]
        remote(block, block, send_sem, recv_sem, me, 1 - core).wait_recv()

    zs = [lax.rem(zc + k, nz) for k in range(nz)]
    here = 2 * yc + xc
    first_here = (2 * (1 - yc) + xc, 2 * yc + 1 - xc)
    second_here = ((2 * yc + 1 - xc, 2 * (1 - yc) + 1 - xc), (2 * (1 - yc) + xc, 2 * (1 - yc) + 1 - xc))
    for k in range(1, nz):
        for p in (0, 1):
            send(me, p, sz.at[p, k], rz.at[p, zc], zs[k] * 4 + here, core)
    for k in range(nz):
        z = zs[k]
        slot = 4 * z + here
        for p in (0, 1):
            if k:
                arrived(slot, core, p, sz.at[p, k], rz.at[p, z])
            send(slot, p, s1.at[p, k], r1.at[p, z], firsts[p], core)
            send(slot, p, s2.at[p, k, 0], r2.at[p, z, 0], seconds[p], core)
            send(slot, p, sc.at[p, k, 0], rc.at[p, z, 0], me, 1 - core)
    for k in range(nz):
        for p in (0, 1):
            merge(4 * zs[k] + here, core, p)
    for k in range(nz):
        z = zs[k]
        for p in (0, 1):
            slot = 4 * z + first_here[p]
            arrived(slot, core, p, s1.at[p, k], r1.at[p, z])
            send(slot, p, s2.at[p, k, 1], r2.at[p, z, 1], seconds[p], core)
            send(slot, p, sc.at[p, k, 1], rc.at[p, z, 1], me, 1 - core)
    for k in range(nz):
        for p in (0, 1):
            merge(4 * zs[k] + first_here[p], core, p)
    for k in range(nz):
        z = zs[k]
        for b in (0, 1):
            for p in (0, 1):
                slot = 4 * z + second_here[p][b]
                arrived(slot, core, p, s2.at[p, k, b], r2.at[p, z, b])
                send(slot, p, sc.at[p, k, 2 + b], rc.at[p, z, 2 + b], me, 1 - core)
        for b in (0, 1):
            for p in (0, 1):
                merge(4 * z + second_here[p][b], core, p)
    for k in range(nz):
        z = zs[k]
        for p in (0, 1):
            for b, at in enumerate((here, first_here[p]) + second_here[p]):
                arrived(4 * z + at, 1 - core, p, sc.at[p, k, b], rc.at[p, z, b])
                merge(4 * z + at, 1 - core, p)
    for copy in pending:
        copy.wait_send()


def gather_sems(nz):
    dma = pltpu.SemaphoreType.DMA
    return [
        dma((2, nz)), dma((2, nz)), dma((2, nz)), dma((2, nz)),
        dma((2, nz, 2)), dma((2, nz, 2)), dma((2, nz, 4)), dma((2, nz, 4)),
    ]


class Scatter:
    @staticmethod
    def scratch(dp, hr, sr):
        nz, rows = dp // 4, hr + sr
        dma, vm = pltpu.SemaphoreType.DMA, pltpu.VMEM
        return [
            vm((2, dp, rows, LANES), BF), vm((dp, rows, LANES), BF),
            vm((nz, 2, rows, LANES), BF), vm((nz, 2, rows, LANES), BF),
            vm((nz, rows, LANES), BF), vm((nz, rows, LANES), BF),
            vm((nz, rows, LANES), BF), vm((nz, rows, LANES), BF),
            dma((nz, 2)), dma((nz, 2)), dma((3, nz)), dma((3, nz)), dma((3, nz)), dma((3, nz)), dma((3, nz)), dma((3, nz)),
        ]

    def __init__(self, nz, hr, sr, mine, refs):
        self.nz, self.mine = nz, mine
        (
            self.g, self.c1, self.t1, self.rx1, self.t2, self.rx2, self.t3, self.rx3,
            self.sc, self.rc, self.s1, self.r1, self.s2, self.r2, self.s3, self.r3,
        ) = refs
        ha = up_to(hr // 2, 16)
        self.parts = (pl.ds(0, ha), pl.ds(ha, hr - ha), pl.ds(hr, sr))
        self.kinds = (pl.ds(0, hr), pl.ds(hr, sr))
        self.me, self.core, self.zc, self.yc, self.xc = grid_place(nz)
        zc, yc, xc = self.zc, self.yc, self.xc
        y_peer = 4 * zc + 2 * (1 - yc) + xc
        x_peer = 4 * zc + 2 * yc + 1 - xc
        self.firsts = (x_peer, y_peer, x_peer)
        self.seconds = (y_peer, x_peer, y_peer)
        self.second_give = (1 - yc, 1 - xc, 1 - yc)
        self.second_keep = (yc, xc, yc)

    def core_copy(self, z, kind):
        group, rows = pl.ds(4 * z, 4), self.kinds[kind]
        return remote(
            self.g.at[1 - self.core, group, rows], self.c1.at[group, rows],
            self.sc.at[z, kind], self.rc.at[z, kind], self.me, 1 - self.core,
        )

    def first_copy(self, z, p):
        rows = self.parts[p]
        return remote(
            self.t1.at[z, :, rows], self.rx1.at[z, :, rows], self.s1.at[p, z], self.r1.at[p, z], self.firsts[p], self.core
        )

    def second_copy(self, z, p):
        rows = self.parts[p]
        return remote(
            self.t2.at[z, rows], self.rx2.at[z, rows], self.s2.at[p, z], self.r2.at[p, z], self.seconds[p], self.core
        )

    def third_copy(self, z, p):
        rows = self.parts[p]
        return remote(
            self.t3.at[z, rows], self.rx3.at[self.zc, rows], self.s3.at[p, z], self.r3.at[p, self.zc],
            4 * z + 2 * self.yc + self.xc, self.core,
        )

    def place(self, p, z, b):
        return 4 * z + (2 * self.yc + b if p == 1 else 2 * b + self.xc)

    def held(self, z, p, slot):
        rows = self.parts[p]
        return self.g[self.core, slot, rows].astype(F32) + self.c1[slot, rows].astype(F32)

    def partial(self, z, p, b):
        return self.held(z, p, self.place(p, z, b)) + self.rx1[z, b, self.parts[p]].astype(F32)

    def stage_core(self, z, kind):
        self.core_copy(z, kind).start()

    def stage_first(self, z, kind):
        self.core_copy(z, kind).wait_recv()
        for p in ((0, 1), (2,))[kind]:
            for b in (0, 1):
                slot = 4 * z + (2 * (1 - self.yc) + b if p == 1 else 2 * b + 1 - self.xc)
                self.t1[z, b, self.parts[p]] = self.held(z, p, slot).astype(BF)
            self.first_copy(z, p).start()

    def stage_second(self, z, kind):
        for p in ((0, 1), (2,))[kind]:
            self.first_copy(z, p).wait_recv()
            self.t2[z, self.parts[p]] = self.partial(z, p, self.second_give[p]).astype(BF)
            self.second_copy(z, p).start()

    def stage_third(self, z, kind):
        for p in ((0, 1), (2,))[kind]:
            rows = self.parts[p]
            self.second_copy(z, p).wait_recv()
            total = self.partial(z, p, self.second_keep[p]) + self.rx2[z, rows].astype(F32)

            @pl.when(self.zc == z)
            def _():
                self.mine[rows, :] = total

            @pl.when(self.zc != z)
            def _():
                self.t3[z, rows] = total.astype(BF)
                self.third_copy(z, p).start()

    def finish(self, out):
        total = self.mine[...]
        for k in range(1, self.nz):
            sender = lax.rem(self.zc + k, self.nz)
            for p in range(3):
                rows = self.parts[p]
                remote(
                    self.t3.at[sender, rows], self.rx3.at[sender, rows], self.s3.at[p, sender], self.r3.at[p, sender],
                    self.me, 1 - self.core,
                ).wait_recv()
            total = total + self.rx3[sender].astype(F32)
        out[...] = total
        for z in range(self.nz):
            for kind in range(2):
                self.core_copy(z, kind).wait_send()
            for p in range(3):
                self.first_copy(z, p).wait_send()
                self.second_copy(z, p).wait_send()

            @pl.when(self.zc != z)
            def _():
                for p in range(3):
                    self.third_copy(z, p).wait_send()


def peer_of(own, total, k):
    other = lax.rem(own + k, total)
    dp = other // 2
    return other, dp, other - 2 * dp


def own_number():
    return 2 * lax.axis_index("dp") + lax.axis_index("head")


def greet_all(total):
    barrier = pltpu.get_barrier_semaphore()
    own = own_number()

    @pl.loop(1, total)
    def _(k):
        _, dp, head = peer_of(own, total, k)
        pl.semaphore_signal(
            barrier, inc=1, device_id={"dp": dp, "head": head}, device_id_type=pl.DeviceIdType.MESH
        )


def greeted_all(total):
    pl.semaphore_wait(pltpu.get_barrier_semaphore(), total - 1)


def share_start(total, src, inbox, ss, rs):
    own = own_number()
    inbox[own] = src[...]

    @pl.loop(1, total)
    def _(k):
        _, dp, head = peer_of(own, total, k)
        remote(src, inbox.at[own], ss.at[k], rs.at[own], dp, head).start()


def share_finish(total, src, inbox, ss, rs):
    own = own_number()

    @pl.loop(1, total)
    def _(k):
        other, dp, head = peer_of(own, total, k)
        remote(src, inbox.at[other], ss.at[k], rs.at[other], dp, head).wait()


HEADS = 4
HD = 60
FF = 960
KW = 15
STEP = 10
KREL = 383
NORM_EPS = 1e-05
BETA_ONE = 0.9
BETA_TWO = 0.999
LEARN_RATE = 0.1
WEIGHT_DECAY = 0.01
ADAM_EPS = 1e-08
LOG2E = 1.4426950408889634
LN2 = 0.6931471805599453
SCALE = HD ** (-0.5)
UNIT = 1.28125
D = 240
DP = 256
HF = 480
HFP = 512
FFP = 1024
HC = 120
MASK_LANE = 120
NEG = -1e30
FFA, ATT, CNV, FFB, OUT = 0, 2, 4, 6, 8
DOWNB_ONE, DOWNB_TWO, B_OUT, BATCH_GAIN, BATCH_BIAS, TAPS, DEPTH_BIAS = 10, 11, 12, 13, 14, 16, 31
VEC_ROWS = 32
BIG = 60 << 20


def head_places():
    out, at = {}, 0
    for name, size in (
        ("up1", D * HF), ("upb1", HF), ("dn1", HF * D), ("up2", D * HF), ("upb2", HF), ("dn2", HF * D),
        ("wq", D * HC), ("wk", D * HC), ("wv", D * HC), ("bq", HC), ("bv", HC),
        ("rel", 2 * KREL), ("wo", HC * D),
    ):
        out[name] = at
        at += size
    return out, at


def shared_places():
    out, at = {}, 0
    for name, size in (
        ("vec", 13 * D), ("p1", 2 * D * D), ("pb1", 2 * D), ("taps", KW * D), ("db", D),
        ("bg", D), ("bb", D), ("p2", D * D), ("pb2", D),
    ):
        out[name] = at
        at += size
    return out, at


def lane_iota(shape):
    return lax.broadcasted_iota(jnp.int32, shape, len(shape) - 1)


def slot_rows(size):
    return up_to(-(-(size + LANES - 1) // LANES), 16)


def dot(a, b):
    return jnp.dot(a, b, preferred_element_type=F32)


def dot_t(a, b):
    return lax.dot_general(a, b, (((1,), (1,)), ((), ())), preferred_element_type=F32)


def t_dot(a, b):
    return lax.dot_general(a, b, (((0,), (0,)), ((), ())), preferred_element_type=F32)


def vmem_call(body, outs, ins, scratch=(), name=None, limit=BIG):
    return pl.pallas_call(
        body,
        out_shape=outs,
        in_specs=[pl.BlockSpec(memory_space=pltpu.VMEM) for _ in ins],
        out_specs=jax.tree.map(lambda _: pl.BlockSpec(memory_space=pltpu.VMEM), outs),
        scratch_shapes=list(scratch),
        compiler_params=pltpu.CompilerParams(vmem_limit_bytes=limit),
        name=name,
    )(*ins)


def own_offsets(head_size, shared_size):
    me = lax.axis_index("dp")
    core = lax.axis_index("head")
    return lax.rem(me * head_size, LANES), lax.rem((2 * me + core) * shared_size, LANES)


def push_lanes(x, shift):
    rolled = pltpu.roll(x, shift, 1)
    before = jnp.concatenate([jnp.zeros((1, LANES), F32), rolled[:-1]], 0)
    return jnp.where(lane_iota(x.shape) >= shift, rolled, before)


def pull_lanes(x, shift):
    rolled = pltpu.roll(x, lax.rem(LANES - shift, LANES), 1)
    after = jnp.concatenate([rolled[1:], jnp.zeros((1, LANES), F32)], 0)
    return jnp.where(lane_iota(x.shape) < LANES - shift, rolled, after)


def align(head_ref, shared_ref, out):
    head_size, shared_size = head_ref.shape[1], shared_ref.shape[0]
    hr, sr = slot_rows(head_size), slot_rows(shared_size)
    ho, so = own_offsets(head_size, shared_size)
    x = jnp.concatenate([head_ref[...], jnp.zeros((1, hr * LANES - head_size), F32)], 1)
    out[pl.ds(0, hr), :] = push_lanes(x.reshape(hr, LANES), ho).astype(BF)
    x = shared_ref[...].reshape(1, shared_size)
    x = jnp.concatenate([x, jnp.zeros((1, sr * LANES - shared_size), F32)], 1)
    out[pl.ds(hr, sr), :] = push_lanes(x.reshape(sr, LANES), so).astype(BF)


def adam_kernel(
    early, grad, g_ref, hp, hf, hs, sp, sf, ss, out_o, grad_o, hf_o, hs_o, hp_o, hc_o, sf_o, ss_o, sp_o, sc_o
):
    out_o[...] = early[...]
    grad_o[...] = grad[...]

    @pl.when(pl.program_id(0) == 0)
    def _():
        adam_update(g_ref, hp, hf, hs, sp, sf, ss, hf_o, hs_o, hp_o, hc_o, sf_o, ss_o, sp_o, sc_o)


def adam_update(g_ref, hp, hf, hs, sp, sf, ss, hf_o, hs_o, hp_o, hc_o, sf_o, ss_o, sp_o, sc_o):
    head_size, shared_size = hp.shape[1], sp.shape[0]
    hr, sr = slot_rows(head_size), slot_rows(shared_size)
    ho, so = own_offsets(head_size, shared_size)

    def update(master, g, first, second):
        first_new = BETA_ONE * first + (1.0 - BETA_ONE) * g
        second_new = BETA_TWO * second + (1.0 - BETA_TWO) * g * g
        first_hat = first_new * (1.0 / (1.0 - BETA_ONE**STEP))
        second_hat = second_new * (1.0 / (1.0 - BETA_TWO**STEP))
        new = master - LEARN_RATE * (first_hat / (jnp.sqrt(second_hat) + ADAM_EPS) + WEIGHT_DECAY * master)
        return first_new, second_new, new

    g = pull_lanes(g_ref[pl.ds(0, hr), :], ho).reshape(1, hr * LANES)[:, :head_size]
    one, two, new = update(hp[...], g, hf[...], hs[...])
    hf_o[...] = one
    hs_o[...] = two
    hp_o[...] = new
    hc_o[...] = new.astype(BF)
    g = pull_lanes(g_ref[pl.ds(hr, sr), :], so).reshape(sr * LANES)[:shared_size]
    one, two, new = update(sp[...], g, sf[...], ss[...])
    sf_o[...] = one
    ss_o[...] = two
    sp_o[...] = new
    sc_o[...] = new.astype(BF)


def row_phases(rows, pitch):
    if rows == 1:
        return 1, 1, 0
    period = LANES // math.gcd(pitch, LANES)
    return period, rows // period, period * pitch // LANES


def take(flat, at, rows, pitch, col, width, dst, row0, lane0):
    period, count, stride = row_phases(rows, pitch)
    lane = lane_iota((count, LANES))
    for j in range(period):
        start = at + j * pitch + col
        q, l = divmod(start, LANES)

        def load(t):
            if count == 1:
                return flat[pl.ds(q + t, 1), :]
            return flat[pl.ds(q + t, count, stride), :]

        pieces = [load(t) for t in range(-(-(l + width) // LANES))]
        if l:
            pieces = [pltpu.roll(x, LANES - l, 1) for x in pieces]
        for t in range(-(-width // LANES)):
            value = pieces[t]
            if l and t + 1 < len(pieces):
                value = jnp.where(lane < LANES - l, value, pieces[t + 1])
            left = width - t * LANES
            if left < LANES:
                value = jnp.where(lane < left, value, 0.0)
            rows_at = pl.ds(row0 + j, 1) if count == 1 else pl.ds(row0 + j, count, period)
            dst[lane0 // LANES + t, rows_at, :] = value


def give(flat, at, rows, pitch, col, width, src, row0, lane0):
    period, count, stride = row_phases(rows, pitch)
    lane = lane_iota((count, LANES))
    for j in range(period):
        start = at + j * pitch + col
        q, l = divmod(start, LANES)
        rows_at = pl.ds(row0 + j, 1) if count == 1 else pl.ds(row0 + j, count, period)
        pieces = [src[lane0 // LANES + t, rows_at, :] for t in range(-(-width // LANES))]
        if l:
            pieces = [pltpu.roll(x, l, 1) for x in pieces]
        total = -(-(l + width) // LANES)
        for t in range(total):
            here = pl.ds(q + t, 1) if count == 1 else pl.ds(q + t, count, stride)
            if not l:
                value = pieces[t]
            elif t == 0:
                value = pieces[0]
            elif t == len(pieces):
                value = pieces[t - 1]
            else:
                value = jnp.where(lane >= l, pieces[t], pieces[t - 1])
            lo = l if t == 0 else 0
            hi = min(LANES, l + width - t * LANES)
            if lo or hi < LANES:
                keep = (lane >= lo) & (lane < hi)
                value = jnp.where(keep, value, flat[here, :])
            flat[here, :] = value


def spill(tiles, rows, dst, factor=None):
    for t in range(dst.shape[1] // LANES):
        value = tiles[t, pl.ds(0, rows), :]
        if factor:
            value = factor * value
        dst[:, pl.ds(t * LANES, LANES)] = value.astype(dst.dtype)


def load_tiles(src, tiles, factor=None):
    for t in range(src.shape[1] // LANES):
        value = src[:, pl.ds(t * LANES, LANES)]
        tiles[t, pl.ds(0, src.shape[0]), :] = factor * value if factor else value


def flat_rows(total, size):
    return up_to(total // LANES + slot_rows(size) + 16, 16)


class Weights:
    def __init__(self, dp, head_size, shared_size, got, refs):
        self.dp, self.head_size, self.shared_size, self.got = dp, head_size, shared_size, got
        self.hr, self.sr = slot_rows(head_size), slot_rows(shared_size)
        self.fh, self.fs, self.wide, self.tall, self.tmp = refs
        self.hp, _ = head_places()
        self.sp, _ = shared_places()

    def clear_flat(self):
        self.fh[...] = jnp.zeros(self.fh.shape, F32)
        self.fs[...] = jnp.zeros(self.fs.shape, F32)

    def merge(self, slot, core, p):
        rows = self.hr + self.sr
        cut = up_to(rows // 2, 16)
        first = (slot * self.head_size) // LANES
        low, high = ((0, min(cut, self.hr)), (min(cut, self.hr), self.hr))[p]
        if high > low:
            at = pl.ds(first + low, high - low)
            self.fh[core, at, :] += self.got[slot, core, pl.ds(low, high - low), :].astype(F32)
        low, high = ((self.hr, max(cut, self.hr)), (max(cut, self.hr), rows))[p]
        if high > low:
            at = pl.ds(((2 * slot + core) * self.shared_size) // LANES + low - self.hr, high - low)
            self.fs[at, :] += self.got[slot, core, pl.ds(low, high - low), :].astype(F32)

    def clear(self, tiles, count, row, size):
        for t in range(count):
            tiles[t, pl.ds(row, size), :] = jnp.zeros((size, LANES), F32)

    def patch(self, tiles, tile, row, where, value):
        part = tiles[tile, pl.ds(row, 1), :]
        tiles[tile, pl.ds(row, 1), :] = jnp.where(where, value, part)

    def ffn(self, up, dn, up_place, bias_place, dn_place, row):
        wide, tall, hp = self.wide, self.tall, self.hp
        self.clear(wide, 8, 240, 16)
        for g in range(2):
            take(self.fh.at[g], hp[up_place], D, HF, 0, HF, wide, 0, g * HFP)
            take(self.fh.at[g], hp[bias_place], 1, HF, 0, HF, wide, 240, g * HFP)
        self.patch(wide, 3, 240, lane_iota((1, LANES)) == HF - 3 * LANES, UNIT)
        spill(wide, DP, up, 0.5)
        for g in range(2):
            self.clear(tall, 2, g * HFP + HF, 32)
            take(self.fh.at[g], hp[dn_place], HF, D, 0, D, tall, g * HFP, 0)
        take(self.fs, self.sp["vec"] + row * D, 1, D, 0, D, tall, HF, 0)
        spill(tall, FFP, dn, 0.5)

    def point_two(self, p2):
        self.clear(self.tall, 2, 240, 16)
        take(self.fs, self.sp["p2"], D, D, 0, D, self.tall, 0, 0)
        take(self.fs, self.sp["pb2"], 1, D, 0, D, self.tall, 240, 0)
        spill(self.tall, DP, p2)

    def others(self, qkv, wo, p1, vec, rel):
        wide, tall, tmp, fh, fs, hp, sp = self.wide, self.tall, self.tmp, self.fh, self.fs, self.hp, self.sp
        lane = lane_iota((1, LANES))
        self.clear(wide, 6, 240, 16)
        for g in range(2):
            for which, (place, bplace) in enumerate((("wq", "bq"), ("wk", None), ("wv", "bv"))):
                lane0 = which * DP + g * LANES
                take(fh.at[g], hp[place], D, HC, 0, HC, wide, 0, lane0)
                if bplace:
                    take(fh.at[g], hp[bplace], 1, HC, 0, HC, wide, 240, lane0)
        for tile in (0, 1, 4, 5):
            self.patch(wide, tile, 240, lane == MASK_LANE, 1.0)
        spill(wide, DP, qkv)
        self.clear(tall, 2, 0, DP)
        for g in range(2):
            take(fh.at[g], hp["wo"], HC, D, 0, D, tall, g * LANES, 0)
        take(fs, sp["vec"] + B_OUT * D, 1, D, 0, D, tall, MASK_LANE, 0)
        spill(tall, DP, wo)
        self.clear(wide, 4, 240, 16)
        for half in range(2):
            take(fs, sp["p1"], D, 2 * D, half * D, D, wide, 0, half * DP)
            take(fs, sp["pb1"] + half * D, 1, D, 0, D, wide, 240, half * DP)
        spill(wide, DP, p1)
        take(fs, sp["vec"], 16, D, 0, D, tall, 0, 0)
        take(fs, sp["taps"], 16, D, 0, D, tall, TAPS, 0)
        take(fs, sp["bg"], 1, D, 0, D, tall, BATCH_GAIN, 0)
        take(fs, sp["bb"], 1, D, 0, D, tall, BATCH_BIAS, 0)
        for row, value in ((FFA + 1, 1.0), (ATT + 1, 1.0), (CNV + 1, 1.0), (FFB + 1, 1.0), (BATCH_BIAS, UNIT)):
            self.patch(tall, 1, row, lane == D - LANES, value)
        spill(tall, VEC_ROWS, vec)
        length = rel.shape[1]
        for n in range(HEADS):
            take(fh.at[n // 2], hp["rel"] + (n % 2) * KREL, 1, KREL, 0, KREL, tmp, 0, 0)
            row = jnp.concatenate([tmp[t, pl.ds(0, 1), :] for t in range(3)] + [jnp.zeros((1, LANES), F32)], 1)
            rows = jnp.broadcast_to(row, (length, 4 * LANES))
            rows = pltpu.roll(rows, 4 * LANES - (length - 1), 1, stride=1, stride_axis=0)
            rel[pl.ds(n * length, length), :] = rows[:, :length] * LOG2E


class Flat:
    @staticmethod
    def scratch(dp, head_size, shared_size):
        vm = pltpu.VMEM
        return [
            vm((2, flat_rows(head_size * dp, head_size), LANES), F32),
            vm((flat_rows(shared_size * 2 * dp, shared_size), LANES), F32),
            vm((8, DP, LANES), F32),
            vm((2, FFP, LANES), F32),
            vm((4, 8, LANES), F32),
        ]

    def __init__(self, dp, head_size, shared_size, refs):
        self.dp, self.head_size, self.shared_size = dp, head_size, shared_size
        self.hr, self.sr = slot_rows(head_size), slot_rows(shared_size)
        self.fh, self.fs, self.wide, self.tall, self.tmp = refs
        self.hp, self.used_h = head_places()
        self.sp, self.used_s = shared_places()

    def clear_unused(self):
        for g in range(2):
            first = self.used_h // LANES // 8 * 8
            count = self.fh.shape[1] - first
            self.fh[g, pl.ds(first, count), :] = jnp.zeros((count, LANES), F32)
        first = self.used_s // LANES // 8 * 8
        count = self.fs.shape[0] - first
        self.fs[pl.ds(first, count), :] = jnp.zeros((count, LANES), F32)

    def head(self, g, place, rows, pitch, src, row0, lane0):
        give(self.fh.at[g], self.hp[place], rows, pitch, 0, pitch, src, row0, lane0)

    def shared(self, place, at, rows, pitch, col, src, row0, lane0):
        give(self.fs, self.sp[place] + at, rows, pitch, col, D, src, row0, lane0)

    def up(self, up, place, bias_place):
        load_tiles(up, self.wide, 0.5)
        for g in range(2):
            self.head(g, place, D, HF, self.wide, 0, g * HFP)
            self.head(g, bias_place, 1, HF, self.wide, 240, g * HFP)

    def down(self, dn, place, row):
        for t in range(2):
            self.tall[t] = (0.5 * dn[pl.ds(t * LANES, LANES), :]).astype(BF).T.astype(F32)
        for g in range(2):
            self.head(g, place, HF, D, self.tall, g * HFP, 0)
        self.shared("vec", row * D, 1, D, 0, self.tall, HF, 0)

    def attention(self, qkv, wo, rel):
        load_tiles(qkv, self.wide)
        load_tiles(wo, self.tall)
        length = rel.shape[0] // HEADS
        for g in range(2):
            for which, (place, bplace) in enumerate((("wq", "bq"), ("wk", None), ("wv", "bv"))):
                lane0 = which * DP + g * LANES
                self.head(g, place, D, HC, self.wide, 0, lane0)
                if bplace:
                    self.head(g, bplace, 1, HC, self.wide, 240, lane0)
            self.head(g, "wo", HC, D, self.tall, g * LANES, 0)
        for n in range(HEADS):
            total = jnp.zeros((8, 4 * LANES), F32)
            for block in range(length // 8):
                rows = rel[pl.ds(n * length + 8 * block, 8), :]
                rows = jnp.concatenate([rows, jnp.zeros((8, 4 * LANES - length), F32)], 1)
                total = total + pltpu.roll(rows, length - 8 - 8 * block, 1)
            row = total[7:8]
            for i in range(7):
                row = row + pltpu.roll(total[i : i + 1], 7 - i, 1)
            for t in range(4):
                self.tmp[t, pl.ds(0, 1), :] = row[:, t * LANES : (t + 1) * LANES]
            give(self.fh.at[n // 2], self.hp["rel"] + (n % 2) * KREL, 1, KREL, 0, KREL, self.tmp, 0, 0)
        self.shared("vec", B_OUT * D, 1, D, 0, self.tall, MASK_LANE, 0)

    def points(self, p1, p2):
        load_tiles(p1, self.wide)
        load_tiles(p2, self.tall)
        for half in range(2):
            self.shared("p1", 0, D, 2 * D, half * D, self.wide, 0, half * DP)
            self.shared("pb1", half * D, 1, D, 0, self.wide, 240, half * DP)
        self.shared("p2", 0, D, D, 0, self.tall, 0, 0)
        self.shared("pb2", 0, 1, D, 0, self.tall, 240, 0)

    def vectors(self, vec, vec2):
        for t in range(2):
            cols = pl.ds(t * LANES, LANES)
            self.tall[t, pl.ds(0, VEC_ROWS), :] = vec[:, cols] + vec2[:, cols]
        for row in range(2, 10):
            self.shared("vec", row * D, 1, D, 0, self.tall, row, 0)
        self.shared("taps", 0, 16, D, 0, self.tall, TAPS, 0)
        self.shared("bg", 0, 1, D, 0, self.tall, BATCH_GAIN, 0)
        self.shared("bb", 0, 1, D, 0, self.tall, BATCH_BIAS, 0)

    def first_norm(self, vec):
        for t in range(2):
            self.tall[t, pl.ds(0, 8), :] = vec[pl.ds(0, 8), pl.ds(t * LANES, LANES)]
        for row in (FFA, FFA + 1):
            self.shared("vec", row * D, 1, D, 0, self.tall, row, 0)

    def slots(self, out, z, kind):
        for i in range(4 * z, 4 * z + 4):
            for g in range(2):
                if kind == 0:
                    out[g, i, pl.ds(0, self.hr), :] = self.fh[g, pl.ds(i * self.head_size // LANES, self.hr), :].astype(BF)
                else:
                    at = (2 * i + g) * self.shared_size // LANES
                    out[g, i, pl.ds(self.hr, self.sr), :] = self.fs[pl.ds(at, self.sr), :].astype(BF)

    def groups(self):
        size = 4 * self.head_size
        every = range(self.dp // 4)
        one = [z for z in every if z * size >= self.hp["up2"] and (z + 1) * size <= self.hp["wq"]]
        two = [z for z in every if z * size >= self.hp["dn1"] and z not in one]
        late = [z for z in every if 8 * z * self.shared_size < 2 * D]
        return one, two, [z for z in every if z not in one and z not in two], [z for z in every if z not in late], late


def row_sum(x):
    return jnp.sum(x, -1, keepdims=True)


def halves(x):
    return x[:, :LANES], x[:, LANES:]


def both(lo, hi):
    return jnp.concatenate([lo, hi], 1)


def norm(x, gain, bias):
    lane = lane_iota((1, LANES))
    lo, hi = halves(x)
    mean = row_sum(lo + hi) * (1.0 / D)
    lo = lo - mean
    hi = jnp.where(lane < D - LANES, hi - mean, 0.0)
    inv = lax.rsqrt(row_sum(lo * lo + hi * hi) * (1.0 / D) + NORM_EPS)
    lo, hi = lo * inv, hi * inv
    return both(lo, hi) * gain + bias, both(lo, jnp.where(lane == LANES - 1, inv, hi))


def norm_grad(grad, kept, gain):
    dg = grad * gain
    inv = kept[:, DP - 1 :]
    first = row_sum(dg) * (1.0 / D)
    second = row_sum(dg * kept) * (1.0 / D)
    return inv * (dg - first - kept * second)


def fold_rows(x):
    return jnp.sum(x.reshape(x.shape[0] // 8, 8, x.shape[1]), 0)


def norm_param_grads(acc, row, grad, kept):
    acc[row] += fold_rows(grad * kept)
    acc[row + 1] += fold_rows(grad)


def settle(acc, out):
    for row in range(acc.shape[0]):
        out[pl.ds(row, 1), :] = jnp.sum(acc[row], 0, keepdims=True)


def silu_pair(y):
    p = jnp.tanh(y) + 1.0
    h = (y * p).astype(BF)
    p = p.astype(BF)
    return h, p + h * (2.0 - p)


def widen(x):
    rows = x.shape[0]
    return jnp.concatenate([x.astype(F32), jnp.zeros((rows, DP - D), F32)], 1)


SHORT = (1, 1, 1, 1, 3, 1, 1, 4)
LATE = (4, 1)
LONG = (1, 1, 1)
PAIR = (1, 1)


def columns(ref, widths):
    out, at = [], 0
    for width in widths:
        out.append(ref.at[:, pl.ds(at * DP, width * DP)])
        at += width
    return out


def head_lanes():
    lane = lane_iota((1, LANES))
    return lane < HD, (lane >= HD) & (lane < 2 * HD), lane == MASK_LANE


def valid_rows(lengths, at, length):
    return lax.broadcasted_iota(jnp.int32, (length, 1), 0) < lengths[at]


def phase_a_kernel(
    seqs, sizes, lengths, frames, head_ref, shared_ref,
    short_far, late_far, long_far, kept1_far, xw_far, e_far, keep_o, up, dn, up2, dn2, wqkv, wo, p1, p2, vec, rel,
    pad, stats_o, inbox, ss, rs, own_slot, got, fh, fs, wide, tall, tmp,
    short_b, late_b, long_b, kept1_b, xw_b, e_b, out_sem, *sems,
):
    step = pl.program_id(0)
    slot = lax.rem(step, 2)
    far = (short_far, late_far, long_far, kept1_far, xw_far, e_far)
    near = (short_b, late_b, long_b, kept1_b, xw_b, e_b)

    def moves(k):
        side = lax.rem(k, 2)
        out = []
        for j, (here, there) in enumerate(zip(near, far)):
            size = here.shape[1]
            rows = pl.ds(pl.multiple_of(k * size, size), size)
            out.append(pltpu.make_async_copy(here.at[side], there.at[rows], out_sem.at[side, j]))
        return out

    @pl.when(step >= 2)
    def _():
        for move in moves(step - 2):
            move.wait()

    short_o, late_o, long_o, kept1_o, xw_o, e_o = (ref.at[slot] for ref in near)
    total = inbox.shape[0]
    weights = Weights(*sizes, got, (fh, fs, wide, tall, tmp))
    gl_o, f1_o, f2_o, a3_o, qkv_o, m_o, a2_o, h_o = columns(short_o, SHORT)
    sp_o, a1_o = columns(late_o, LATE)
    kept3_o, kept2_o, rl_o = columns(long_o, LONG)
    x2_o, w_o = columns(xw_o, PAIR)

    @pl.when(step == 0)
    def _():
        greet_all(total)
        align(head_ref, shared_ref, own_slot)
        weights.clear_flat()
        greeted_all(total)
        gather(sizes[0] // 4, own_slot, got, sems, weights.merge)
        weights.ffn(up, dn, "up1", "upb1", "dn1", DOWNB_ONE)
        weights.others(wqkv, wo, p1, vec, rel)

    length = frames.shape[1]
    tokens = seqs * length
    first_seq = lax.axis_index("head") * (seqs * pl.num_programs(0)) + step * seqs

    def v(row):
        return vec[pl.ds(row, 1), :]

    x0 = widen(frames[...].reshape(tokens, D))
    a, kept1_o[...] = norm(x0, v(FFA), v(FFA + 1))
    a = a.astype(BF)
    a1_o[...] = a
    h, slope = silu_pair(dot(a, up[...]))
    h_o[...] = h
    sp_o[...] = slope
    x1 = x0 + dot(h, dn[...])
    a, kept = norm(x1, v(ATT), v(ATT + 1))
    kept2_o[...] = kept.astype(BF)
    a = a.astype(BF)
    a2_o[...] = a
    qkv = dot(a, wqkv[...])
    first, second, special = head_lanes()
    for b in range(seqs):
        rows = pl.ds(b * length, length)
        fence = jnp.where(valid_rows(lengths, first_seq + b, length), 0.0, NEG)
        for g in range(2):
            def piece(which):
                at = which * DP + g * LANES
                return qkv[b * length : (b + 1) * length, at : at + LANES]

            q = (piece(0) * (SCALE * LOG2E)).astype(BF)
            k = jnp.where(special, fence, piece(1)).astype(BF)
            vv = piece(2).astype(BF)
            qkv_o[rows, pl.ds(g * LANES, LANES)] = q
            qkv_o[rows, pl.ds(DP + g * LANES, LANES)] = k
            qkv_o[rows, pl.ds(2 * DP + g * LANES, LANES)] = vv
            zero = jnp.zeros_like(q)
            pair = jnp.concatenate([jnp.where(first | special, q, zero), jnp.where(second | special, q, zero)], 0)
            at = pl.ds(2 * g * length, 2 * length)
            s = dot_t(pair, k) + rel[at, :]
            e = jnp.exp2(s - jnp.max(s, -1, keepdims=True)).astype(BF)
            e_o[b, at, :] = e
            o = dot(e, vv)
            r = 1.0 / o[:, MASK_LANE : MASK_LANE + 1]
            shares = jnp.where(second, r[length:], r[:length])
            rl_o[rows, pl.ds(g * LANES, LANES)] = shares.astype(BF)
            m_o[rows, pl.ds(g * LANES, LANES)] = (jnp.where(second, o[length:], o[:length]) * shares).astype(BF)
    x2 = x1 + dot(m_o[...], wo[...])
    x2_o[...] = x2
    a, kept = norm(x2, v(CNV), v(CNV + 1))
    kept3_o[...] = kept.astype(BF)
    a = a.astype(BF)
    a3_o[...] = a
    e = dot(a, p1[...])
    half = KW // 2

    @pl.when(step == 0)
    def _():
        pad[...] = jnp.zeros(pad.shape, F32)
        stats_o[...] = jnp.zeros(stats_o.shape, F32)

    count = jnp.float32(0.0)
    summed = jnp.zeros((1, DP), F32)
    for b in range(seqs):
        rows = pl.ds(b * length, length)
        valid = jnp.where(valid_rows(lengths, first_seq + b, length), 1.0, 0.0)
        linear = e[b * length : (b + 1) * length, :DP]
        gate = 0.5 * jnp.tanh(0.5 * e[b * length : (b + 1) * length, DP:]) + 0.5
        f1 = gate * valid
        gl = linear * f1
        f1_o[rows, :] = f1.astype(BF)
        f2_o[rows, :] = (gl * (1.0 - gate)).astype(BF)
        gl_o[rows, :] = gl.astype(BF)
        for t in range(2):
            cols = pl.ds(t * LANES, LANES)
            pad[b, t, pl.ds(8, length), :] = gl[:, t * LANES : (t + 1) * LANES]
            acc = jnp.broadcast_to(vec[pl.ds(DEPTH_BIAS, 1), cols], (length, LANES))
            for r in range(KW):
                acc = acc + pad[b, t, pl.ds(8 - half + r, length), :] * vec[pl.ds(TAPS + r, 1), cols]
            w_o[rows, cols] = acc
        summed = summed + jnp.sum(w_o[rows, :] * valid, 0, keepdims=True)
        count = count + lengths[first_seq + b].astype(F32)
    mean = summed / count
    square = jnp.zeros((1, DP), F32)
    for b in range(seqs):
        valid = jnp.where(valid_rows(lengths, first_seq + b, length), 1.0, 0.0)
        centre = (w_o[pl.ds(b * length, length), :] - mean) * valid
        square = square + jnp.sum(centre * centre, 0, keepdims=True)
    old = stats_o[pl.ds(4, 1), :]
    new = old + count
    for t in range(2):
        cols = slice(t * LANES, (t + 1) * LANES)
        before = stats_o[pl.ds(t, 1), :]
        delta = mean[:, cols] - before
        stats_o[pl.ds(t, 1), :] = before + delta * (count / new)
        stats_o[pl.ds(2 + t, 1), :] += square[:, cols] + delta * delta * (old * count / new)
    stats_o[pl.ds(4, 1), :] = new
    for move in moves(step):
        move.start()

    @pl.when(step == pl.num_programs(0) - 1)
    def _():
        unused = lane_iota((1, LANES)) == LANES - 1
        stats_o[pl.ds(1, 1), :] = jnp.where(unused, stats_o[pl.ds(4, 1), :], stats_o[pl.ds(1, 1), :])
        share_start(total, stats_o.at[pl.ds(0, 4)], inbox, ss, rs)
        weights.ffn(up2, dn2, "up2", "upb2", "dn2", DOWNB_TWO)
        weights.point_two(p2)
        share_finish(total, stats_o.at[pl.ds(0, 4)], inbox, ss, rs)
        batch_stats(inbox[...], keep_o)
        for move in moves(step - 1) + moves(step):
            move.wait()


def batch_stats(shared, keep):
    counts = jnp.broadcast_to(shared[:, 1:2, LANES - 1 :], (shared.shape[0], 1, LANES))
    total = jnp.sum(counts, 0)
    means, spreads = [], []
    for t in range(2):
        each = shared[:, t : t + 1, :]
        mean = jnp.sum(each * counts, 0) / total
        spread = (jnp.sum(shared[:, 2 + t : 3 + t, :], 0) + jnp.sum(counts * (each - mean) ** 2, 0)) / total
        means.append(mean)
        spreads.append(spread)
    keep[pl.ds(0, 1), :] = jnp.concatenate(means, 1)
    keep[pl.ds(1, 1), :] = lax.rsqrt(jnp.concatenate(spreads, 1) + NORM_EPS)
    keep[pl.ds(2, 1), :] = jnp.concatenate([total, total], 1)
    keep[pl.ds(3, 5), :] = jnp.zeros((5, DP), F32)


def phase_b_kernel(
    seqs, keep, xw, cotangent, p2, up, dn, vec,
    out_o, back_o, dup_far, ddn_far, dp2_far, vec_o, keep_o,
    dup_o, ddn_o, dp2_o, out_sem, acc, a_all, du_all, do_all, h_all, hc_all, dc_all, sums_o, inbox, ss, rs,
):
    step = pl.program_id(0)
    total = inbox.shape[0]
    length = cotangent.shape[1]
    tokens = seqs * length
    at = pl.ds(pl.multiple_of(step * tokens, tokens), tokens)
    x2, w = columns(xw, PAIR)
    dy_o, dx3_o = columns(back_o, PAIR)

    @pl.when(step == 0)
    def _():
        greet_all(total)
        for ref in (dup_o, ddn_o, dp2_o, acc):
            ref[...] = jnp.zeros(ref.shape, F32)

    def v(row):
        return vec[pl.ds(row, 1), :]

    mean, inv_batch = keep[pl.ds(0, 1), :], keep[pl.ds(1, 1), :]
    z = (w[...] - mean) * inv_batch
    hc, slope_c = silu_pair(z * (0.5 * v(BATCH_GAIN)) + 0.5 * v(BATCH_BIAS))
    x3 = x2[...] + dot(hc, p2[...])
    a, kept = norm(x3, v(FFB), v(FFB + 1))
    a = a.astype(BF)
    h, slope = silu_pair(dot(a, up[...]))
    x4 = x3 + dot(h, dn[...])
    final, kept4 = norm(x4, v(OUT), v(OUT + 1))
    out_o[...] = final[:, :D].astype(BF).reshape(seqs, length, D)
    g = widen(cotangent[...].reshape(tokens, D))
    norm_param_grads(acc, OUT, g, kept4)
    dx4 = norm_grad(g, kept4, v(OUT))
    do = dx4.astype(BF)
    do_all[at, :] = do
    h_all[at, :] = h
    du = dot_t(do, dn[...]).astype(BF) * slope
    a_all[at, :] = a
    du_all[at, :] = du
    da = dot_t(du, up[...])
    norm_param_grads(acc, FFB, da, kept)
    dx3 = dx4 + norm_grad(da, kept, v(FFB))
    dx3_o[...] = dx3
    dc = dx3.astype(BF)
    hc_all[at, :] = hc
    dc_all[at, :] = dc
    dy = dot_t(dc, p2[...]) * slope_c.astype(F32)
    dy_o[...] = dy
    acc[BATCH_BIAS] += fold_rows(dy)
    acc[BATCH_GAIN] += fold_rows(dy * z)

    @pl.when(step == pl.num_programs(0) - 1)
    def _():
        acc[BATCH_BIAS] *= 0.5
        acc[BATCH_GAIN] *= 0.5
        settle(acc, vec_o)
        for row, source in ((0, BATCH_BIAS), (2, BATCH_GAIN)):
            line = vec_o[pl.ds(source, 1), :]
            for t in range(2):
                sums_o[pl.ds(row + t, 1), :] = line[:, t * LANES : (t + 1) * LANES]

    @pl.when(step == pl.num_programs(0) - 1)
    def _():
        greeted_all(total)
        share_start(total, sums_o.at[pl.ds(0, 4)], inbox, ss, rs)

        @pl.loop(0, pl.num_programs(0))
        def _(k):
            at = pl.ds(pl.multiple_of(k * tokens, tokens), tokens)
            ddn_o[...] += t_dot(do_all[at, :], h_all[at, :])
            dup_o[...] += t_dot(a_all[at, :], du_all[at, :])
            dp2_o[...] += t_dot(hc_all[at, :], dc_all[at, :])

        moves = [
            pltpu.make_async_copy(here, there, out_sem.at[j])
            for j, (here, there) in enumerate(((dup_o, dup_far), (ddn_o, ddn_far), (dp2_o, dp2_far)))
        ]
        for move in moves:
            move.start()
        share_finish(total, sums_o.at[pl.ds(0, 4)], inbox, ss, rs)
        sums = jnp.sum(inbox[...], 0)
        keep_o[...] = keep[...]
        keep_o[pl.ds(3, 1), :] = jnp.concatenate([sums[0:1], sums[1:2]], 1)
        keep_o[pl.ds(4, 1), :] = jnp.concatenate([sums[2:3], sums[3:4]], 1)
        for move in moves:
            move.wait()


def phase_c_kernel(
    seqs, steps, sizes, lengths, keep, xw_far, back_far, short_far, long_far, e_far, late_far, kept1_far,
    p1, wo, wqkv, dn, up, vec, dup2, ddn2, dp2, vec2,
    dx0_o, sum_o,
    dp1_o, dwo_o, dqkv_o, dup_o, ddn_o, vec_o, rel_o, dx1_buf, mine,
    acc, padw, padg, grads, w_b, back_b, short_b, long_b, e_b, late_b, kept1_b, in_sem, *refs,
):
    step = pl.program_id(0)
    length = dx0_o.shape[1]
    side = lax.rem(step, 2)
    cut = 3 * DP

    def fetch(k, names):
        to = lax.rem(k, 2)
        size = seqs * length
        rows = pl.ds(pl.multiple_of(k * size, size), size)
        make = pltpu.make_async_copy
        every = (
            lambda j: make(xw_far.at[rows, pl.ds(DP, DP)], w_b.at[to], in_sem.at[to, j]),
            lambda j: make(back_far.at[rows], back_b.at[to], in_sem.at[to, j]),
            lambda j: make(short_far.at[rows, pl.ds(0, cut)], short_b.at[to, :, pl.ds(0, cut)], in_sem.at[to, j]),
            lambda j: make(
                short_far.at[rows, pl.ds(cut, short_b.shape[2] - cut)],
                short_b.at[to, :, pl.ds(cut, short_b.shape[2] - cut)],
                in_sem.at[to, j],
            ),
            lambda j: make(long_far.at[rows], long_b.at[to], in_sem.at[to, j]),
            lambda j: make(e_far.at[pl.ds(k * seqs, seqs)], e_b.at[to], in_sem.at[to, j]),
            lambda j: make(late_far.at[rows], late_b.at[to], in_sem.at[to, j]),
            lambda j: make(kept1_far.at[rows], kept1_b.at[to], in_sem.at[to, j]),
        )
        return [every[j](j) for j in names]

    conv_names, rest_names, late_names = (0, 1, 2), (3, 4, 5), (6, 7)

    @pl.when(step == 0)
    def _():
        for move in fetch(step, conv_names + rest_names):
            move.start()

    @pl.when(step < steps - 1)
    def _():
        for move in fetch(step + 1, conv_names + rest_names):
            move.start()

    @pl.when(step == steps - 1)
    def _():
        for move in fetch(step * 0, late_names):
            move.start()

    @pl.when((step >= steps) & (step < 2 * steps - 1))
    def _():
        for move in fetch(step + 1 - steps, late_names):
            move.start()

    w, back, short, long, e_all = (ref.at[side] for ref in (w_b, back_b, short_b, long_b, e_b))
    late_side = lax.rem(jnp.maximum(step - steps, 0), 2)
    late, kept1 = late_b.at[late_side], kept1_b.at[late_side]
    flat = Flat(*sizes, refs[:5])
    nz = sizes[0] // 4
    scatter = Scatter(nz, flat.hr, flat.sr, mine, refs[5:])
    one, two, rest, shared_two, shared_rest = flat.groups()
    dy, dx3 = columns(back, PAIR)
    gl, f1, f2, a3, qkv, m, a2, h = columns(short, SHORT)
    kept3, kept2, rl = columns(long, LONG)
    slope, a1 = columns(late, LATE)

    @pl.when(step == 0)
    def _():
        greet(nz, scatter.me, scatter.core, scatter.zc, scatter.yc, scatter.xc)
        for ref in (dp1_o, dwo_o, dqkv_o, dup_o, ddn_o, acc, rel_o, padw, padg):
            ref[...] = jnp.zeros(ref.shape, F32)
        flat.clear_unused()
        flat.up(dup2, "up2", "upb2")
        flat.down(ddn2, "dn2", DOWNB_TWO)
        for z in one:
            flat.slots(scatter.g, z, 0)
        greeted(nz)
        for z in one:
            scatter.stage_core(z, 0)

    @pl.when(step < steps)
    def _():
        def ready(names):
            for move in fetch(step, names):
                move.wait()

        ready(conv_names)
        phase_c_first(
            functools.partial(ready, rest_names), seqs, step, steps, length, lengths, keep, w, dy, dx3, gl, f1, f2, a3, kept3, qkv, e_all, rl, m, a2, kept2,
            h, p1, wo, wqkv, vec, dp1_o, dwo_o, dqkv_o, ddn_o, rel_o, dx1_buf, acc, padw, padg, grads,
        )

    @pl.when(step == steps)
    def _():
        flat.attention(dqkv_o, dwo_o, rel_o)
        flat.down(ddn_o, "dn1", DOWNB_ONE)
        for z in two:
            flat.slots(scatter.g, z, 0)
            scatter.stage_core(z, 0)
        settle(acc, vec_o)
        flat.points(dp1_o, dp2)
        flat.vectors(vec_o, vec2)
        for z in shared_two:
            flat.slots(scatter.g, z, 1)
            scatter.stage_core(z, 1)

    last_rows = pl.ds(pl.multiple_of(jnp.maximum(step - steps, 0) * (seqs * length), seqs * length), seqs * length)

    @pl.when(step >= steps)
    def _():
        for move in fetch(step - steps, late_names):
            move.wait()
        dx1 = dx1_buf[last_rows, :]
        du = dot_t(dx1.astype(BF), dn[...]).astype(BF) * slope[...]
        slope[...] = du
        dup_o[...] += t_dot(a1[...], du)

    @pl.when(step == 2 * steps - 1)
    def _():
        flat.up(dup_o, "up1", "upb1")
        for z in rest:
            flat.slots(scatter.g, z, 0)
            scatter.stage_core(z, 0)

    @pl.when(step >= steps)
    def _():
        da = dot_t(slope[...], up[...])
        norm_param_grads(acc, FFA, da, kept1[...])
        dx0 = dx1_buf[last_rows, :] + norm_grad(da, kept1[...], vec[pl.ds(FFA, 1), :])
        dx0_o[...] = dx0[:, :D].reshape(seqs, length, D)

    stages = (scatter.stage_first, scatter.stage_second, scatter.stage_third)
    for at, heads, shared in (((1, 2, 3), one, []), (tuple(steps + k for k in TWO_AT), two, shared_two)):
        for when, stage in zip(at, stages):
            @pl.when(step == when)
            def _():
                for z in heads:
                    stage(z, 0)
                for z in shared:
                    stage(z, 1)

    @pl.when(step == 2 * steps - 1)
    def _():
        settle(acc, vec_o)
        flat.first_norm(vec_o)
        for z in shared_rest:
            flat.slots(scatter.g, z, 1)
            scatter.stage_core(z, 1)
        waiting = [(stage, two, shared_two) for stage in stages[len(TWO_AT) :]]
        last = [(stage, rest, shared_rest) for stage in stages]
        for stage, heads, shared in [x for pair in zip(waiting, last) for x in pair] + last[len(waiting) :]:
            for z in heads:
                stage(z, 0)
            for z in shared:
                stage(z, 1)
        scatter.finish(sum_o)


def phase_c_first(
    ready, seqs, step, steps, length, lengths, keep, w, dy, dx3, gl, f1, f2, a3, kept3, qkv, e_all, rl, m, a2, kept2,
    h, p1, wo, wqkv, vec, dp1_o, dwo_o, dqkv_o, ddn_o, rel_o, dx1_buf, acc, padw, padg, grads,
):
    first_seq = lax.axis_index("head") * (seqs * steps) + step * seqs
    half = KW // 2

    def v(row):
        return vec[pl.ds(row, 1), :]

    mean, inv_batch, count = (keep[pl.ds(row, 1), :] for row in range(3))
    scale = v(BATCH_GAIN) * inv_batch
    cross = inv_batch * scale * keep[pl.ds(4, 1), :] / count
    plain = scale * keep[pl.ds(3, 1), :] / count - mean * cross
    scale = 0.5 * scale
    for b in range(seqs):
        rows = pl.ds(b * length, length)
        valid = jnp.where(valid_rows(lengths, first_seq + b, length), 1.0, 0.0)
        dw = dy[rows, :] * scale - valid * (plain + w[rows, :] * cross)
        acc[DEPTH_BIAS] += fold_rows(dw)
        for t in range(2):
            cols = pl.ds(t * LANES, LANES)
            here = dw[:, t * LANES : (t + 1) * LANES]
            padw[b, t, pl.ds(8, length), :] = here
            padg[b, t, pl.ds(8, length), :] = gl[rows, cols].astype(F32)
            total = jnp.zeros((length, LANES), F32)
            for r in range(KW):
                total = total + padw[b, t, pl.ds(8 + half - r, length), :] * vec[pl.ds(TAPS + r, 1), cols]
                tap = here * padg[b, t, pl.ds(8 - half + r, length), :]
                acc[TAPS + r, :, cols] += fold_rows(tap)
            grads[rows, cols] = (total * f1[rows, cols].astype(F32)).astype(BF)
            grads[rows, pl.ds(DP + t * LANES, LANES)] = (total * f2[rows, cols].astype(F32)).astype(BF)
    ready()
    de = grads[:, pl.ds(0, 2 * DP)]
    dp1_o[...] += t_dot(a3[...], de)
    da = dot_t(de, p1[...])
    kept = kept3[...].astype(F32)
    norm_param_grads(acc, CNV, da, kept)
    dx2 = dx3[...] + norm_grad(da, kept, v(CNV))
    db = dx2.astype(BF)
    dwo_o[...] += t_dot(m[...], db)
    dm = dot_t(db, wo[...])
    first, second, special = head_lanes()
    source = lax.broadcasted_iota(jnp.int32, (LANES, 2 * LANES), 0)
    target = lane_iota((LANES, 2 * LANES)) // LANES
    spread = jnp.where((source >= target * HD) & (source < (target + 1) * HD), 1.0, 0.0).astype(BF)
    for b in range(seqs):
        rows = pl.ds(b * length, length)
        for g in range(2):
            cols = pl.ds(g * LANES, LANES)
            q = qkv[rows, cols]
            k = qkv[rows, pl.ds(DP + g * LANES, LANES)]
            vv = qkv[rows, pl.ds(2 * DP + g * LANES, LANES)]
            dmb = (dm[b * length : (b + 1) * length, g * LANES : (g + 1) * LANES] * rl[rows, cols].astype(F32)).astype(BF)
            level = dot(dmb * m[rows, cols], spread)
            level = jnp.concatenate([level[:, :LANES], level[:, LANES:]], 0)
            zero = jnp.zeros_like(q)
            dm_pair = jnp.concatenate([jnp.where(first, dmb, zero), jnp.where(second, dmb, zero)], 0)
            q_pair = jnp.concatenate([jnp.where(first, q, zero), jnp.where(second, q, zero)], 0)
            at = pl.ds(2 * g * length, 2 * length)
            e = e_all[b, at, :]
            dp = dot_t(dm_pair, vv)
            ds = e.astype(F32) * (dp - jnp.concatenate([level, level[:, : length - LANES]], 1))
            rel_o[at, :] += ds
            ds = ds.astype(BF)
            dq = dot(ds, k)
            dq = jnp.where(second, dq[length:], dq[:length])
            grads[rows, cols] = (dq * SCALE).astype(BF)
            grads[rows, pl.ds(DP + g * LANES, LANES)] = (t_dot(ds, q_pair) * LN2).astype(BF)
            grads[rows, pl.ds(2 * DP + g * LANES, LANES)] = t_dot(e, dm_pair).astype(BF)
    dqkv = grads[...]
    dqkv_o[...] += t_dot(a2[...], dqkv)
    da = dot_t(dqkv, wqkv[...])
    kept = kept2[...].astype(F32)
    norm_param_grads(acc, ATT, da, kept)
    dx1 = dx2 + norm_grad(da, kept, v(ATT))
    at = pl.ds(pl.multiple_of(step * (seqs * length), seqs * length), seqs * length)
    dx1_buf[at, :] = dx1
    ddn_o[...] += t_dot(dx1.astype(BF), h[...])


def layer_call(body, steps, ins, outs, scratch, name, collective_id=None):
    def spec(item):
        kind, shape = item
        if kind == "far":
            return pl.BlockSpec(memory_space=pl.ANY)
        if kind == "smem":
            return pl.BlockSpec(memory_space=pltpu.SMEM)
        if kind == "tile":
            return pl.BlockSpec(shape, lambda i: (i,) + (0,) * (len(shape) - 1))
        if kind == "early":
            return pl.BlockSpec(shape, lambda i: (jnp.minimum(i, steps // 2 - 1),) + (0,) * (len(shape) - 1))
        if kind == "late":
            return pl.BlockSpec(shape, lambda i: (jnp.maximum(i - steps // 2, 0),) + (0,) * (len(shape) - 1))
        return pl.BlockSpec(shape, lambda i: (0,) * len(shape))

    arrays = [a for _, _, a in ins]
    return pl.pallas_call(
        body,
        grid=(steps,),
        out_shape=tuple(jax.ShapeDtypeStruct(full, dtype) for _, _, full, dtype in outs),
        in_specs=[spec((kind, block)) for kind, block, _ in ins],
        out_specs=tuple(spec((kind, block)) for kind, block, _, _ in outs),
        scratch_shapes=list(scratch),
        compiler_params=pltpu.CompilerParams(
            vmem_limit_bytes=BIG,
            dimension_semantics=("arbitrary",),
            collective_id=collective_id,
            has_side_effects=collective_id is not None,
        ),
        name=name,
    )(*arrays)


def tile_in(array, steps, kind="tile"):
    return (kind, (array.shape[0] // steps,) + array.shape[1:], array)


def whole_in(array):
    return ("whole", array.shape, array)


def tile_out(steps, shape, dtype, kind="tile"):
    return (kind, (shape[0] // steps,) + shape[1:], shape, dtype)


def far_in(array):
    return ("far", None, array)


def far_out(shape, dtype):
    return ("far", None, shape, dtype)


def whole_out(shape, dtype=F32):
    return ("whole", shape, shape, dtype)


SEQS_A = 4
SEQS_B = 4
SEQS_C = 4
TWO_AT = (0,)


def per_device(
    frames, cotangent, lengths, head_params, shared_params, head_first, head_second, shared_first, shared_second
):
    seq_here, length, _ = frames.shape
    tokens = seq_here * length
    dp = lax.axis_size("dp")
    head_size, shared_size = head_params.shape[1], shared_params.shape[0]
    rows = slot_rows(head_size) + slot_rows(shared_size)
    vm = pltpu.VMEM
    dma = pltpu.SemaphoreType.DMA
    sharing = [vm((8, LANES), F32), vm((2 * dp, 4, LANES), F32), dma((2 * dp,)), dma((2 * dp,))]
    steps = seq_here // SEQS_A
    block = SEQS_A * length
    t = functools.partial(tile_out, steps)
    (
        short, late, long, kept1, xw, e_all, keep,
        up1, dn1, up2, dn2, wqkv, wo, p1, p2, vec, rel
    ) = layer_call(
        functools.partial(phase_a_kernel, SEQS_A, (dp, head_size, shared_size)),
        steps,
        [("smem", None, lengths), tile_in(frames, steps), whole_in(head_params), whole_in(shared_params)],
        [
            far_out((tokens, sum(SHORT) * DP), BF), far_out((tokens, sum(LATE) * DP), BF),
            far_out((tokens, sum(LONG) * DP), BF), far_out((tokens, DP), F32), far_out((tokens, sum(PAIR) * DP), F32),
            far_out((seq_here, HEADS * length, length), BF),
            whole_out((8, DP)),
            whole_out((DP, FFP), BF), whole_out((FFP, DP), BF), whole_out((DP, FFP), BF), whole_out((FFP, DP), BF),
            whole_out((DP, 3 * DP), BF), whole_out((DP, DP), BF), whole_out((DP, 2 * DP), BF), whole_out((DP, DP), BF),
            whole_out((VEC_ROWS, DP)), whole_out((HEADS * length, length)),
        ],
        [vm((SEQS_A, 2, length + 16, LANES), F32)]
        + sharing
        + [vm((rows, LANES), BF), vm((dp, 2, rows, LANES), BF)]
        + Flat.scratch(dp, head_size, shared_size)
        + [
            vm((2, block, sum(SHORT) * DP), BF), vm((2, block, sum(LATE) * DP), BF), vm((2, block, sum(LONG) * DP), BF),
            vm((2, block, DP), F32), vm((2, block, sum(PAIR) * DP), F32), vm((2, SEQS_A, HEADS * length, length), BF),
            dma((2, 6)),
        ]
        + gather_sems(dp // 4),
        "phase_a",
        1,
    )
    steps = seq_here // SEQS_B
    t = functools.partial(tile_out, steps)
    early, back, dup2, ddn2, dp2, vec_b, keep = layer_call(
        functools.partial(phase_b_kernel, SEQS_B),
        steps,
        [whole_in(keep), tile_in(xw, steps), tile_in(cotangent, steps)]
        + [whole_in(x) for x in (p2, up2, dn2, vec)],
        [
            t((seq_here, length, D), BF), t((tokens, sum(PAIR) * DP), F32),
            far_out((DP, FFP), F32), far_out((DP, FFP), F32), far_out((DP, DP), F32), whole_out((VEC_ROWS, DP)),
            whole_out((8, DP)),
        ],
        [
            vm((DP, FFP), F32), vm((DP, FFP), F32), vm((DP, DP), F32), dma((3,)),
            vm((VEC_ROWS, 8, DP), F32), vm((tokens, DP), BF), vm((tokens, FFP), BF), vm((tokens, DP), BF),
            vm((tokens, FFP), BF), vm((tokens, DP), BF), vm((tokens, DP), BF),
        ]
        + sharing,
        "phase_b",
        3,
    )
    steps = seq_here // SEQS_C
    slot = (slot_rows(head_size), slot_rows(shared_size))
    block = SEQS_C * length
    input_grad, summed = layer_call(
        functools.partial(phase_c_kernel, SEQS_C, steps, (dp, head_size, shared_size)),
        2 * steps,
        [("smem", None, lengths), whole_in(keep)]
        + [far_in(x) for x in (xw, back, short, long, e_all, late, kept1)]
        + [whole_in(x) for x in (p1, wo, wqkv, dn1, up1, vec, dup2, ddn2, dp2, vec_b)],
        [tile_out(steps, (seq_here, length, D), F32, "late"), whole_out((rows, LANES))],
        [
            vm((DP, 2 * DP), F32), vm((DP, DP), F32), vm((DP, 3 * DP), F32), vm((DP, FFP), F32), vm((DP, FFP), F32),
            vm((VEC_ROWS, DP), F32), vm((HEADS * length, length), F32), vm((tokens, DP), F32), vm((rows, LANES), F32),
            vm((VEC_ROWS, 8, DP), F32),
            vm((SEQS_C, 2, length + 16, LANES), F32),
            vm((SEQS_C, 2, length + 16, LANES), F32),
            vm((block, 3 * DP), BF),
            vm((2, block, DP), F32), vm((2, block, sum(PAIR) * DP), F32), vm((2, block, sum(SHORT) * DP), BF),
            vm((2, block, sum(LONG) * DP), BF), vm((2, SEQS_C, HEADS * length, length), BF),
            vm((2, block, sum(LATE) * DP), BF), vm((2, block, DP), F32), dma((2, 8)),
        ]
        + Flat.scratch(dp, head_size, shared_size)
        + Scatter.scratch(dp, *slot),
        "phase_c",
        4,
    )
    h_shape, s_shape = head_params.shape, shared_params.shape
    steps = 2
    return layer_call(
        adam_kernel,
        steps,
        [tile_in(x, steps) for x in (early, input_grad)]
        + [whole_in(x) for x in (summed, head_params, head_first, head_second, shared_params, shared_first, shared_second)],
        [tile_out(steps, early.shape, BF), tile_out(steps, early.shape, F32)]
        + [whole_out(h_shape)] * 3
        + [whole_out(h_shape, BF)]
        + [whole_out(s_shape)] * 3
        + [whole_out(s_shape, BF)],
        [],
        "adam",
    )


def solution(mesh):
    frames = P(("dp", "head"), None, None)
    heads = P("head", "dp")
    shared = P(("dp", "head"))
    return jax.shard_map(
        per_device,
        mesh=mesh,
        in_specs=(frames, frames, P("dp"), heads, shared, heads, heads, shared, shared),
        out_specs=(frames, frames) + (heads,) * 4 + (shared,) * 4,
        check_vma=False,
    )
```
